32 devices in a mesh: gx: 4 (over x, core), gy: 2 (over y), gz: 4 (over z).
Axes of the slice: x: 2, y: 2, z: 4, core: 2. Of those that a mesh axis runs over, the one named last changes fastest.
Arguments:
- primal_states: float32 [2, 19, 16, 32, 512], P(None, None, 'gx', 'gy', 'gz'), as said below
- adjoint_last: float32 [19, 16, 32, 512], P(None, 'gx', 'gy', 'gz'), may hold values from -6 to 6
- porosity: float32 [16, 32, 512], P('gx', 'gy', 'gz'), may hold values from 0 to 0.9
- solid_mask: int32 [16, 32, 512], P('gx', 'gy', 'gz'), may hold values from 0 to 1, as said below
Outputs:
- adjoint_first: float32 [19, 16, 32, 512], P(None, 'gx', 'gy', 'gz')
- porosity_grad: float32 [16, 32, 512], P('gx', 'gy', 'gz')
- drag: float32 [], replicated
The draws below stay inside these ranges and needn't reach their ends.
Inputs may be any that keep to these rules, and one draw needn't show every extreme that they name: `primal_states`: every population is positive. `solid_mask`: every cell on the planes y = 0 and y = 31 is solid; elsewhere cells are solid at random.
All inputs are finite; a program needn't handle non-finite values.
Results may differ from the reference program's by a relative error of at most 0.00013.
Values sent between devices are 32-bit elements; how exact they have to be, the bound alone decides.
No kernel may reach another device: no remote copies, remote signals or barrier semaphores. Data moves between devices by JAX's collectives and lax.ppermute only.
A program may use at most 128 MiB of HBM per device.

```python
import jax
import jax.numpy as jnp
import numpy as np
from jax import lax

WINDOW = 2
NX = 16
NY = 32
NZ = 512


def lattice_parts():
    velocity = np.array([(0, 0, 0), (1, 0, 0), (-1, 0, 0), (0, 1, 0), (0, -1, 0), (0, 0, 1), (0, 0, -1), (1, 1, 0), (-1, -1, 0), (1, -1, 0), (-1, 1, 0), (1, 0, 1), (-1, 0, -1), (1, 0, -1), (-1, 0, 1), (0, 1, 1), (0, -1, -1), (0, 1, -1), (0, -1, 1)]) * 1.0
    speeds = np.sum(np.abs(velocity), axis=1)
    weights = np.where(speeds == 0, 1.0 / 3.0, np.where(speeds == 1, 1.0 / 18.0, 1.0 / 36.0))
    return (velocity, weights)


def draw_primal_states(key, part):
    velocity, weights = lattice_parts()
    key_rho, key_vel, key_noise = jax.random.split(key, 3)
    shape = (WINDOW, 1, NX, NY, NZ)
    density = 1.0 + 0.1 * jax.random.uniform(key_rho, shape, jnp.float32, -1.0, 1.0)
    speed = 0.03 * jnp.clip(jax.random.normal(key_vel, (3,) + shape, jnp.float32), -3.0, 3.0)
    speed = speed.at[0].add(0.1)
    noise = 0.05 * jnp.clip(jax.random.normal(key_noise, (WINDOW, 19, NX, NY, NZ), jnp.float32), -3.0, 3.0)
    shaped = (1, 19, 1, 1, 1)
    along = jnp.asarray(velocity[:, 0], jnp.float32).reshape(shaped) * speed[0] + jnp.asarray(velocity[:, 1], jnp.float32).reshape(shaped) * speed[1] + jnp.asarray(velocity[:, 2], jnp.float32).reshape(shaped) * speed[2]
    usquare = speed[0] * speed[0] + speed[1] * speed[1] + speed[2] * speed[2]
    equilibrium = jnp.asarray(weights, jnp.float32).reshape(shaped) * density * (1.0 + 3.0 * along + 4.5 * along * along - 1.5 * usquare)
    return (equilibrium * (1.0 + noise)).astype(jnp.float32)


def draw_solid_mask(key, part):
    picks = jax.random.randint(key, (NX, NY, NZ), 0, 8)
    rows_y = lax.broadcasted_iota(jnp.int32, (NX, NY, NZ), 1)
    solid = (picks == 0) | (rows_y == 0) | (rows_y == NY - 1)
    return jnp.where(solid, 1, 0).astype(jnp.int32)


def level_of(stream_key, extent, cuts, low, largest):
    gain = 1.0
    for dim, shards_of in cuts:
        heights = jax.random.uniform(jax.random.fold_in(jax.random.fold_in(stream_key, 6), dim), (shards_of,), jnp.float32, low / len(cuts), largest / len(cuts))
        gain = gain * jnp.repeat(jnp.exp(heights), extent[dim] // shards_of).reshape((-1,) + (1,) * (len(extent) - 1 - dim))
    return gain


def centred(stream_key, extent, deviation, reach, shards=(), kind=jnp.bfloat16):
    drawn = deviation * jax.random.normal(stream_key, extent, jnp.float32)
    if shards:
        drawn = drawn * level_of(stream_key, extent, shards, -0.22, 0.18)
    return jnp.clip(drawn, -reach, reach).astype(kind)


def setup_inputs(seed: int = 0) -> dict:
    streams_of = jax.random.split(jax.random.key(seed), 5)
    primal_states = draw_primal_states(jax.random.fold_in(streams_of[4], 71), 0)
    adjoint_last = centred(streams_of[1], (19, NX, NY, NZ), 1.0, 6.0, ((1, 4), (2, 2), (3, 4)), jnp.float32)
    porosity = jnp.clip(0.9 * jax.random.uniform(streams_of[2], (NX, NY, NZ), jnp.float32) ** level_of(streams_of[2], (NX, NY, NZ), ((0, 4), (1, 2), (2, 4)), -0.2, 0.2), 0.0, 0.9)
    solid_mask = draw_solid_mask(jax.random.fold_in(streams_of[4], 71), 0)
    return dict(primal_states=primal_states, adjoint_last=adjoint_last, porosity=porosity, solid_mask=solid_mask)


def orthonormal_rows(monomials):
    rows = []
    for column in range(monomials.shape[1]):
        vector = monomials[:, column] * 1.0
        for sweep in range(2):
            for earlier in rows:
                vector = vector - np.dot(earlier, vector) * earlier
        vector = vector / np.sqrt(np.dot(vector, vector))
        rows.append(vector)
    return np.stack(rows)

def lattice_tables():
    velocity = np.array([(0, 0, 0), (1, 0, 0), (-1, 0, 0), (0, 1, 0), (0, -1, 0), (0, 0, 1), (0, 0, -1), (1, 1, 0), (-1, -1, 0), (1, -1, 0), (-1, 1, 0), (1, 0, 1), (-1, 0, -1), (1, 0, -1), (-1, 0, 1), (0, 1, 1), (0, -1, -1), (0, 1, -1), (0, -1, 1)]) * 1.0
    speeds = np.sum(np.abs(velocity), axis=1)
    weights = np.where(speeds == 0, 1.0 / 3.0, np.where(speeds == 1, 1.0 / 18.0, 1.0 / 36.0))
    opposite = np.zeros((19, 19))
    for member in range(19):
        for other in range(19):
            if np.all(velocity[other] == -velocity[member]):
                opposite[member, other] = 1.0
    vx = velocity[:, 0]
    vy = velocity[:, 1]
    vz = velocity[:, 2]
    columns = [np.ones(19), vx, vy, vz, vx * vx, vy * vy, vz * vz, vx * vy, vx * vz, vy * vz, vx * vy * vy, vx * vz * vz, vy * vx * vx, vy * vz * vz, vz * vx * vx, vz * vy * vy, vx * vx * vy * vy, vx * vx * vz * vz, vy * vy * vz * vz]
    monomials = np.stack(columns, axis=1)
    basis = orthonormal_rows(monomials)
    rates = np.array([0.0] * 4 + [1.6] * 6 + [1.2] * 9)
    return (velocity, weights, opposite, basis, rates)

def collide(state, blocking):
    velocity, weights, opposite, basis, rates = lattice_tables()
    highest = lax.Precision.HIGHEST
    vel = jnp.asarray(velocity, jnp.float32)
    density = lax.optimization_barrier(jnp.sum(state, axis=0))
    momentum = jnp.dot(vel.T, state, precision=highest)
    speed = momentum / density[None, :]
    along = jnp.dot(vel, speed, precision=highest)
    usquare = lax.optimization_barrier(jnp.sum(speed * speed, axis=0))
    equilibrium = jnp.asarray(weights, jnp.float32)[:, None] * density[None, :] * (1.0 + 3.0 * along + 4.5 * along * along - 1.5 * usquare[None, :])
    basis_rows = jnp.asarray(basis, jnp.float32)
    moments = jnp.dot(basis_rows, state - equilibrium, precision=highest)
    relaxed = jnp.asarray(rates, jnp.float32)[:, None] * moments
    post = state - jnp.dot(basis_rows.T, relaxed, precision=highest)
    bounced = jnp.dot(jnp.asarray(opposite, jnp.float32), state, precision=highest)
    return (1.0 - blocking[None, :]) * post + blocking[None, :] * bounced

def adjoint_step(read, state, blocking):
    velocity = jnp.asarray(lattice_tables()[0], jnp.float32)
    unused, pull = jax.vjp(collide, state, blocking)
    d_state, d_block = pull(read)
    flux_x = jnp.dot(velocity[:, 0], state, precision=lax.Precision.HIGHEST)
    adjoint = d_state + velocity[:, 0:1] * blocking[None, :]
    return (adjoint, d_block + flux_x, jnp.sum(blocking * flux_x))

def reference(primal_states, adjoint_last, porosity, solid_mask):
    velocity = lattice_tables()[0]
    fluid = solid_mask == 0
    blocking = jnp.where(fluid, porosity, jnp.ones_like(porosity))
    adjoint = adjoint_last
    gradient = jnp.zeros_like(porosity)
    total = jnp.zeros((), jnp.float32)
    for instant in (1, 0):
        read = jnp.stack([jnp.roll(adjoint[member], (-int(velocity[member, 0]), -int(velocity[member, 1]), -int(velocity[member, 2])), axis=(0, 1, 2)) for member in range(19)])
        items = (jnp.moveaxis(read, 1, 0).reshape(NX, 19, NY * NZ), jnp.moveaxis(primal_states[instant], 1, 0).reshape(NX, 19, NY * NZ), blocking.reshape(NX, NY * NZ))

        def plane(pieces):
            return adjoint_step(pieces[0], pieces[1], pieces[2])
        fresh, d_block, drag_parts = lax.map(plane, items)
        adjoint = jnp.moveaxis(fresh.reshape(NX, 19, NY, NZ), 0, 1)
        gradient = gradient + d_block.reshape(NX, NY, NZ)
        total = total + jnp.sum(drag_parts)
    porosity_grad = jnp.where(fluid, gradient, jnp.zeros_like(gradient))
    return (adjoint, porosity_grad, total / (NX * NY * NZ))
```

```python
import functools

import jax
import jax.numpy as jnp
import numpy as np
from jax import lax
from jax.experimental import pallas as pl
from jax.experimental.pallas import tpu as pltpu
from jax.sharding import PartitionSpec as P

VEL = (
    (0, 0, 0),
    (1, 0, 0),
    (-1, 0, 0),
    (0, 1, 0),
    (0, -1, 0),
    (0, 0, 1),
    (0, 0, -1),
    (1, 1, 0),
    (-1, -1, 0),
    (1, -1, 0),
    (-1, 1, 0),
    (1, 0, 1),
    (-1, 0, -1),
    (1, 0, -1),
    (-1, 0, 1),
    (0, 1, 1),
    (0, -1, -1),
    (0, 1, -1),
    (0, -1, 1),
)
PAIRS = tuple((i, i + 1) for i in range(1, 19, 2))
AXES = ("gx", "gy", "gz")
UB = (19, 20, 21, 22)


def near(axis, sign):
    return tuple(i for i in range(19) if VEL[i][axis] * sign >= 0) + UB


def far(axis, sign):
    return tuple(i for i in range(19) if VEL[i][axis] == sign)


NSLOT = 23
ZGROUPS = (
    tuple(i for i in range(19) if VEL[i][2] == -1),
    tuple(i for i in range(19) if VEL[i][2] == 1),
    tuple(i for i in range(19) if VEL[i][2] == 0)[:8],
    tuple(i for i in range(19) if VEL[i][2] == 0)[8:] + UB,
)
ZSLOT = {q: (g, k) for g, group in enumerate(ZGROUPS) for k, q in enumerate(group)}


def pairs_of(values):
    s = [values[a] + values[b] for a, b in PAIRS]
    d = [values[a] - values[b] for a, b in PAIRS]
    return s, d


def moments(v0, s, d):
    sx, sy, sz, sp, sq, sr, ss, st, su = s
    dx, dy, dz, dp, dq, dr, ds, dt, du = d
    ex = sp + sq
    ez = sr + ss
    ey = st + su
    faces = sx + sy + sz
    edges = ex + ez + ey
    exx = ex + ez
    eyy = ex + ey
    ezz = ez + ey
    fx = (dp + dq) + (dr + ds)
    fy = (dp - dq) + (dt + du)
    fz = (dr - ds) + (dt - du)
    return dict(
        rest=v0,
        faces=faces,
        edges=edges,
        total=v0 + faces + edges,
        face1=(dx, dy, dz),
        edge1=(fx, fy, fz),
        one=(dx + fx, dy + fy, dz + fz),
        face2=(sx, sy, sz),
        edge2=(exx, eyy, ezz),
        two=(sx + exx, sy + eyy, sz + ezz),
        cross=(sp - sq, sr - ss, st - su),
    )


def adjoint_cell(g, u, b, drive):
    s, d = pairs_of(g)
    m = moments(g[0], s, d)
    total = m["total"]
    trace = m["faces"] + 2.0 * m["edges"] - (30.0 / 19.0) * total
    p0 = (-1.2 / 19.0) * total - (2.0 / 21.0) * trace
    q = [
        (0.4 / 6.0) * (two - (10.0 / 19.0) * total) + (0.8 / 21.0) * trace
        for two in m["two"]
    ]
    qsum = q[0] + q[1] + q[2]
    qab = [0.1 * c for c in m["cross"]]
    p1 = [-0.12 * one for one in m["one"]]
    h0 = (
        0.4 * m["rest"]
        + (1.2 / 18.0) * m["faces"]
        + (1.2 / 36.0) * m["edges"]
        + p0
        + (1.0 / 3.0) * qsum
    )
    h1 = [
        (1.2 / 18.0) * f + (1.2 / 36.0) * e + (1.0 / 3.0) * p
        for f, e, p in zip(m["face1"], m["edge1"], p1)
    ]
    base = (1.0 / 3.0) * p0 + (1.0 / 9.0) * qsum
    haa = [
        (1.2 / 18.0) * f + (1.2 / 36.0) * e + (2.0 / 9.0) * qa + base
        for f, e, qa in zip(m["face2"], m["edge2"], q)
    ]
    hxy, hxz, hyz = [(2.0 / 45.0) * c for c in m["cross"]]
    ux, uy, uz = u
    v = (
        haa[0] * ux + hxy * uy + hxz * uz,
        hxy * ux + haa[1] * uy + hyz * uz,
        hxz * ux + hyz * uy + haa[2] * uz,
    )
    uv = ux * v[0] + uy * v[1] + uz * v[2]
    uu = ux * ux + uy * uy + uz * uz
    uuh = 1.5 * uu * h0
    a = h0 + uuh - 4.5 * uv
    nb = 1.0 - b
    e0 = nb * (a - p0)
    nq = [nb * x for x in q]
    nxy, nxz, nyz = [nb * x for x in qab]
    o = [
        nb * (3.0 * h1[k] + 9.0 * v[k] - 3.0 * u[k] * h0 - p1[k]) for k in range(3)
    ]
    o[0] = o[0] + b * drive
    alpha = -0.2 * nb
    half_s = 0.5 * (alpha + b)
    half_d = 0.5 * (alpha - b)
    exy = e0 - nq[0] - nq[1]
    exz = e0 - nq[0] - nq[2]
    eyz = e0 - nq[1] - nq[2]
    even = (
        e0 - nq[0],
        e0 - nq[1],
        e0 - nq[2],
        exy - nxy,
        exy + nxy,
        exz - nxz,
        exz + nxz,
        eyz - nyz,
        eyz + nyz,
    )
    odd = (
        o[0],
        o[1],
        o[2],
        o[0] + o[1],
        o[0] - o[1],
        o[0] + o[2],
        o[0] - o[2],
        o[1] + o[2],
        o[1] - o[2],
    )
    out = [(alpha + b) * g[0] + e0]
    for k in range(9):
        even_k = half_s * s[k] + even[k]
        odd_k = half_d * d[k] + odd[k]
        out.append(even_k + odd_k)
        out.append(even_k - odd_k)
    kept = dict(
        s=s, d=d, g0=g[0], p0=p0, p1=p1, q=q, qab=qab, h0=h0, h1=h1, uv=uv, uuh=uuh
    )
    return out, kept


def gradient_cell(kept, f0, fs, fd, fm, u):
    rho = fm["total"]
    even = fs[0] * kept["s"][0]
    odd = fd[0] * kept["d"][0]
    for k in range(1, 9):
        even = even + fs[k] * kept["s"][k]
        odd = odd + fd[k] * kept["d"][k]
    hf = kept["p0"] * rho
    for k in range(3):
        hf = hf + kept["p1"][k] * fm["one"][k] + kept["q"][k] * fm["two"][k]
        hf = hf + kept["qab"][k] * fm["cross"][k]
    uh1 = u[0] * kept["h1"][0] + u[1] * kept["h1"][1] + u[2] * kept["h1"][2]
    hfeq = rho * (kept["h0"] - kept["uuh"] + 3.0 * uh1 + 4.5 * kept["uv"])
    pairs = 1.2 * f0 * kept["g0"] + 0.6 * even - 0.4 * odd
    return pairs + hf - hfeq + fm["one"][0]


def state_of(ref, index):
    f = [ref[(index[0], i) + index[1:]] for i in range(19)]
    s, d = pairs_of(f)
    m = moments(f[0], s, d)
    inverse = 1.0 / m["total"]
    u = [one * inverse for one in m["one"]]
    return f[0], s, d, m, u


def pack_x_kernel(
    par_ref, states_ref, adj_ref, por_ref, mask_ref, a_ref, b_ref, ub_ref, drag_ref
):
    nx, ny, nz = por_ref.shape
    tiles = ny // 8

    def cells(n, drag):
        x = n // tiles
        rows = pl.ds(pl.multiple_of((n % tiles) * 8, 8), 8)
        blocking = jnp.where(mask_ref[x, rows, :] == 0, por_ref[x, rows, :], 1.0)
        f0, s, d, m, u = state_of(states_ref, (1, x, rows))
        flux = m["one"][0]
        for a, b in PAIRS:
            if VEL[a][0]:
                flux = flux + (states_ref[0, a, x, rows, :] - states_ref[0, b, x, rows, :])
        for k in range(3):
            ub_ref[k, x, rows, :] = u[k]
        ub_ref[3, x, rows, :] = blocking
        return drag + blocking * flux

    drag = lax.fori_loop(0, nx * tiles, cells, jnp.zeros((8, nz), jnp.float32))
    drag_ref[...] = drag

    def fill(out_ref, sign):
        first, second = (0, 1) if sign > 0 else (nx - 1, nx - 2)
        for k, q in enumerate(near(0, sign)):
            out_ref[k * ny : (k + 1) * ny] = (
                adj_ref[q, first] if q < 19 else ub_ref[q - 19, first]
            )
        for k, q in enumerate(far(0, sign)):
            k += 18
            out_ref[k * ny : (k + 1) * ny] = adj_ref[q, second]
        out_ref[NSLOT * ny : NSLOT * ny + 8] = drag

    @pl.when(par_ref[0] == 0)
    def _():
        fill(a_ref, -1)
        fill(b_ref, 1)

    @pl.when(par_ref[0] == 1)
    def _():
        fill(a_ref, 1)
        fill(b_ref, -1)


def total_of(mode, tiles):
    if mode == "pair":
        return tiles[0] + tiles[1]
    if mode == "four":
        return (tiles[0] + tiles[1]) + (tiles[2] + tiles[3])
    return tiles[3]


def pack_y_kernel(
    mode,
    par_ref,
    adj_ref,
    ub_ref,
    xa_ref,
    xb_ref,
    drag_ref,
    extra_ref,
    out_ref,
):
    nx, ny = adj_ref.shape[1:3]
    even = par_ref[0] == 0
    row_sets = {
        1: (near(1, 1), 0, far(1, 1), 1),
        -1: (near(1, -1), ny - 1, far(1, -1), ny - 2),
    }

    def fill(place, sign):
        first_q, first_row, second_q, second_row = row_sets[sign]
        entries = [(q, first_row) for q in first_q] + [(q, second_row) for q in second_q]
        for k, (q, row) in enumerate(entries):
            where = slice(k * 8, k * 8 + 8)
            rows = []
            for s in range(nx + 4):
                if 2 <= s < nx + 2:
                    rows.append(
                        adj_ref[q, s - 2, row : row + 1, :]
                        if q < 19
                        else ub_ref[q - 19, s - 2, row : row + 1, :]
                    )
                    continue
                side = -1 if s < 2 else 1
                if s in (1, nx + 2):
                    names, offset = near(0, side), 0
                else:
                    names, offset = far(0, side), 18
                if q in names:
                    start = (names.index(q) + offset) * ny + row
                    va = xa_ref[start : start + 1, :]
                    vb = xb_ref[start : start + 1, :]
                    rows.append(
                        jnp.where(even, va, vb) if side > 0 else jnp.where(even, vb, va)
                    )
                else:
                    rows.append(None)
            for s, value in enumerate(rows):
                if value is not None:
                    out_ref[place, k * 8 + s : k * 8 + s + 1, :] = value
                else:
                    out_ref[place, k * 8 + s : k * 8 + s + 1, :] = jnp.zeros(
                        (1, out_ref.shape[2]), jnp.float32
                    )

    @pl.when(par_ref[1] == 0)
    def _():
        fill(0, -1)
        fill(1, 1)

    @pl.when(par_ref[1] == 1)
    def _():
        fill(0, 1)
        fill(1, -1)

    last = slice(NSLOT * ny, NSLOT * ny + 8)
    drag = total_of(
        mode, (drag_ref[...], xa_ref[last], xb_ref[last], extra_ref[...])
    )
    out_ref[0, NSLOT * 8 : NSLOT * 8 + 8, :] = drag
    out_ref[1, NSLOT * 8 : NSLOT * 8 + 8, :] = drag


def pack_z_kernel(
    mode,
    par_ref,
    adj_ref,
    ub_ref,
    xa_ref,
    xb_ref,
    ya_ref,
    yb_ref,
    ysent_ref,
    extra_ref,
    read_ref,
    zmsg_ref,
    drag_ref,
    ext,
):
    nx, ny, nz = adj_ref.shape[1:]
    even_x = par_ref[0] == 0
    even_y = par_ref[1] == 0
    base = 16

    def copy(q, carry):
        return carry

    for q in range(NSLOT):
        for x in range(nx):
            ext[q, x + 2, base : base + ny, :] = (
                adj_ref[q, x] if q < 19 else ub_ref[q - 19, x]
            )
    for sign in (1, -1):
        one, two = (nx + 2, nx + 3) if sign > 0 else (1, 0)
        for names, plane, offset in ((near(0, sign), one, 0), (far(0, sign), two, 18)):
            for k, q in enumerate(names):
                rows = slice((k + offset) * ny, (k + offset + 1) * ny)
                first, second = (xa_ref, xb_ref) if sign > 0 else (xb_ref, xa_ref)
                ext[q, plane, base : base + ny, :] = jnp.where(
                    even_x, first[rows], second[rows]
                )
        one, two = (base + ny, base + ny + 1) if sign > 0 else (base - 1, base - 2)
        first, second = (ya_ref, yb_ref) if sign > 0 else (yb_ref, ya_ref)
        for names, row, offset in ((near(1, sign), one, 0), (far(1, sign), two, 18)):
            for k, q in enumerate(names):
                start = (k + offset) * 8
                tile = jnp.where(
                    even_y, first[start : start + 8], second[start : start + 8]
                )
                for s in range(nx + 4):
                    ext[q, s, row : row + 1, :] = tile[s : s + 1]

    lane = lax.broadcasted_iota(jnp.int32, (8, nz), 1)
    sub = lax.broadcasted_iota(jnp.int32, (8, nz), 0)
    pair = lane // 2
    tiles = ny // 8
    for g, group in enumerate(ZGROUPS):
        acc = [jnp.zeros((8, nz), jnp.float32) for t in range(tiles + 1)]
        for k, q in enumerate(group):
            cx, cy, cz = VEL[q] if q < 19 else (0, 0, 0)
            for p in range(nx + 2):
                plane = p + 1 + cx
                start = 16 * k + 2 * p
                mask = pair == start // 2
                for t in range(tiles + 1):
                    if t < tiles:
                        low = base + 8 * t + cy
                        value = ext[q, plane, low : low + 8, :]
                    else:
                        high = base + ny + cy
                        low = base - 8 + cy
                        value = jnp.where(
                            sub < 4,
                            ext[q, plane, high : high + 8, :],
                            ext[q, plane, low : low + 8, :],
                        )
                    read_ref[q, p, 8 * t : 8 * t + 8, :] = value
                    shift = start + (2 if cz < 0 else 1 if cz == 0 else 0)
                    moved = pltpu.roll(value, shift % nz, 1)
                    acc[t] = jnp.where(mask, moved, acc[t])
        for t in range(tiles + 1):
            row = (g * (tiles + 1) + t) * 8
            zmsg_ref[row : row + 8, :] = acc[t]
    last = slice(NSLOT * 8, NSLOT * 8 + 8)
    drag = total_of(mode, (ysent_ref[0, last, :], ya_ref[last], yb_ref[last], extra_ref[...]))
    drag_ref[...] = drag
    row = 4 * (tiles + 1) * 8
    zmsg_ref[row : row + 8, :] = drag


def levels_kernel(
    mode,
    whole_cells,
    par_ref,
    states_ref,
    mask_ref,
    read_ref,
    zown_ref,
    za_ref,
    zb_ref,
    extra_ref,
    out_ref,
    grad_ref,
    drag_ref,
    lo_ref,
    hi_ref,
    slab_ref,
    mid,
    zmid,
):
    nx, ny, nz = mask_ref.shape
    tiles = ny // 8
    height = (tiles + 1) * 8
    even = par_ref[2] == 0
    lane = lax.broadcasted_iota(jnp.int32, (8, nz), 1)
    side = lane % 2
    first_lane = lane == 0
    last_lane = lane == nz - 1

    for g in range(4):
        for t in range(tiles + 1):
            rows = slice((g * (tiles + 1) + t) * 8, (g * (tiles + 1) + t) * 8 + 8)
            va = za_ref[rows]
            vb = zb_ref[rows]
            high = jnp.where(even, va, vb)
            low = jnp.where(even, vb, va)
            lo_ref[rows] = low
            hi_ref[rows] = high
            own = zown_ref[rows]
            slab_ref[rows] = jnp.where(
                side == 0, own if g == 1 else low, own if g == 0 else high
            )

    last = slice(4 * height, 4 * height + 8)
    drag = total_of(mode, (zown_ref[last], za_ref[last], zb_ref[last], extra_ref[...]))
    summed = jnp.sum(jnp.sum(drag, axis=1, keepdims=True), axis=0, keepdims=True)
    drag_ref[...] = summed / whole_cells

    def rolled(value, shift):
        return pltpu.roll(value, lax.rem(shift + 2 * nz, nz), 1)

    def z_slab(t, carry):
        row = pl.multiple_of(t * 8, 8)
        got = []
        for q in range(NSLOT):
            g, k = ZSLOT[q]
            tile = slab_ref[pl.ds(pl.multiple_of(g * height + row, 8), 8), :]
            got.append(tile if k == 0 else pltpu.roll(tile, nz - 16 * k, 1))
        out, kept = adjoint_cell(got[:19], got[19:22], got[22], 1.0)
        for n, i in enumerate(ZGROUPS[0] + ZGROUPS[1]):
            if_last = t == tiles

            zmid[n, pl.ds(pl.multiple_of(row + 8, 8), 8), :] = out[i]

            @pl.when(if_last)
            def _():
                zmid[n, 0:8, :] = out[i]

        return carry

    lax.fori_loop(0, tiles + 1, z_slab, 0)

    def first_reads(p, t):
        rows = pl.ds(pl.multiple_of(t * 8, 8), 8)
        got = []
        for i in range(19):
            value = read_ref[i, p, rows, :]
            cz = VEL[i][2]
            if cz:
                g, k = ZSLOT[i]
                zrows = pl.ds(pl.multiple_of(g * height + t * 8, 8), 8)
                value = pltpu.roll(value, 1 if cz < 0 else nz - 1, 1)
                if cz < 0:
                    edge = rolled(lo_ref[zrows, :], -(16 * k + 2 * p + 1))
                    value = jnp.where(first_lane, edge, value)
                else:
                    edge = rolled(hi_ref[zrows, :], nz - 1 - 16 * k - 2 * p)
                    value = jnp.where(last_lane, edge, value)
            got.append(value)
        ub = [read_ref[19 + k, p, rows, :] for k in range(4)]
        return got, ub[:3], ub[3]

    def store_mid(out, p, t):
        for i in range(19):
            mid[i, p, pl.ds(pl.multiple_of(t * 8 + 8, 8), 8), :] = out[i]

    def inner(n, carry):
        x = n // tiles
        t = n % tiles
        got, u, b = first_reads(x + 1, t)
        out, kept = adjoint_cell(got, u, b, 1.0)
        store_mid(out, x + 1, t)
        rows = pl.ds(pl.multiple_of(t * 8, 8), 8)
        f0, fs, fd, fm, _ = state_of(states_ref, (1, x, rows))
        grad_ref[x, rows, :] = gradient_cell(kept, f0, fs, fd, fm, u)
        return carry

    lax.fori_loop(0, nx * tiles, inner, 0)

    def outer(n, carry):
        faces = 2 * (tiles + 1)
        p = jnp.where(n < faces, (nx + 1) * (n // (tiles + 1)), n - faces + 1)
        t = jnp.where(n < faces, n % (tiles + 1), tiles)
        got, u, b = first_reads(p, t)
        out, kept = adjoint_cell(got, u, b, 1.0)
        store_mid(out, p, t)

        @pl.when(t == tiles)
        def _():
            for i in range(19):
                mid[i, p, 0:8, :] = out[i]

        return carry

    lax.fori_loop(0, 2 * (tiles + 1) + nx, outer, 0)

    edge_pops = ZGROUPS[0] + ZGROUPS[1]

    def second(x, carry):
        for t in range(tiles):
            rows = slice(t * 8, t * 8 + 8)
            got = []
            for i in range(19):
                cx, cy, cz = VEL[i]
                low = 8 + 8 * t + cy
                value = mid[i, x + 1 + cx, low : low + 8, :]
                if cz:
                    value = pltpu.roll(value, 1 if cz < 0 else nz - 1, 1)
                    edge = zmid[edge_pops.index(i), low : low + 8, :]
                    at = 2 * (x + 1 + cx)
                    if cz < 0:
                        value = jnp.where(first_lane, rolled(edge, -at), value)
                    else:
                        value = jnp.where(
                            last_lane, rolled(edge, nz - 2 - at), value
                        )
                got.append(value)
            f0, fs, fd, fm, u = state_of(states_ref, (0, x, rows))
            b = read_ref[22, x + 1, rows, :]
            out, kept = adjoint_cell(got, u, b, 1.0)
            for i in range(19):
                out_ref[i, x, rows, :] = out[i]
            grad = grad_ref[x, rows, :] + gradient_cell(kept, f0, fs, fd, fm, u)
            grad_ref[x, rows, :] = jnp.where(mask_ref[x, rows, :] == 0, grad, 0.0)
        return carry

    lax.fori_loop(0, nx, second, 0)


def swaps(count):
    first = [(i, i ^ 1) for i in range(count)]
    second = [(i, (((i + 1) % count) ^ 1) - 1) for i in range(count)]
    second = [(i, j % count) for i, j in second]
    return first, second


def drag_extra(tile, axis, count):
    if count == 2:
        return "pair", tile
    if count == 4:
        return "four", lax.ppermute(tile, axis, [(i, (i + 2) % 4) for i in range(4)])
    return "whole", lax.psum(tile, axis)


VMEM = pl.BlockSpec(memory_space=pltpu.VMEM)
SMEM = pl.BlockSpec(memory_space=pltpu.SMEM)
PARAMS = pltpu.CompilerParams(vmem_limit_bytes=48 * 2**20)


def call(kernel, inputs, shapes, scratch=()):
    return pl.pallas_call(
        kernel,
        out_shape=[jax.ShapeDtypeStruct(s, jnp.float32) for s in shapes],
        in_specs=[SMEM] + [VMEM] * (len(inputs) - 1),
        out_specs=[VMEM] * len(shapes),
        scratch_shapes=[pltpu.VMEM(s, jnp.float32) for s in scratch],
        compiler_params=PARAMS,
    )(*inputs)


def body(primal_states, adjoint_last, porosity, solid_mask):
    nx, ny, nz = porosity.shape
    counts = [lax.axis_size(axis) for axis in AXES]
    pairings = [swaps(count) for count in counts]
    parity = jnp.stack([lax.axis_index(axis) & 1 for axis in AXES]).astype(jnp.int32)
    tiles = ny // 8
    height = (tiles + 1) * 8

    rows_x = NSLOT * ny + 8
    xa, xb, ub, drag = call(
        pack_x_kernel,
        (parity, primal_states, adjoint_last, porosity, solid_mask),
        [(rows_x, nz), (rows_x, nz), (4, nx, ny, nz), (8, nz)],
    )
    xb = lax.ppermute(xb, "gx", pairings[0][1])
    xa = lax.ppermute(xa, "gx", pairings[0][0])
    mode, extra = drag_extra(drag, "gx", counts[0])

    rows_y = NSLOT * 8 + 8
    (ysent,) = call(
        functools.partial(pack_y_kernel, mode),
        (parity, adjoint_last, ub, xa, xb, drag, extra),
        [(2, rows_y, nz)],
    )
    drag_y = ysent[0, NSLOT * 8 :] if counts[1] > 2 else drag
    if counts[1] == 2:
        ygot = lax.ppermute(ysent, "gy", pairings[1][0])
        ya, yb = ygot[0], ygot[1]
    else:
        ya = lax.ppermute(ysent[0], "gy", pairings[1][0])
        yb = lax.ppermute(ysent[1], "gy", pairings[1][1])
    mode, extra = drag_extra(drag_y, "gy", counts[1])

    read, zmsg, drag = call(
        functools.partial(pack_z_kernel, mode),
        (parity, adjoint_last, ub, xa, xb, ya, yb, ysent, extra),
        [(NSLOT, nx + 2, height, nz), (4 * height + 8, nz), (8, nz)],
        [(NSLOT, nx + 4, ny + 32, nz)],
    )
    zb = lax.ppermute(zmsg, "gz", pairings[2][1])
    za = lax.ppermute(zmsg, "gz", pairings[2][0])
    mode, extra = drag_extra(drag, "gz", counts[2])
    whole_cells = nx * ny * nz * counts[0] * counts[1] * counts[2]

    first, gradient, total = call(
        functools.partial(levels_kernel, mode, float(whole_cells)),
        (parity, primal_states, solid_mask, read, zmsg, za, zb, extra),
        [(19, nx, ny, nz), (nx, ny, nz), (1, 1)],
        [
            (4 * height, nz),
            (4 * height, nz),
            (4 * height, nz),
            (19, nx + 2, height + 8, nz),
            (10, height + 8, nz),
        ],
    )
    return (first, gradient, total.reshape(()))


def solution(mesh):
    return jax.shard_map(
        body,
        mesh=mesh,
        in_specs=(
            P(None, None, "gx", "gy", "gz"),
            P(None, "gx", "gy", "gz"),
            P("gx", "gy", "gz"),
            P("gx", "gy", "gz"),
        ),
        out_specs=(P(None, "gx", "gy", "gz"), P("gx", "gy", "gz"), P()),
        check_vma=False,
    )
```

```python
import functools

import jax
import jax.numpy as jnp
import numpy as np
from jax import lax
from jax.experimental import pallas as pl
from jax.experimental.pallas import tpu as pltpu
from jax.sharding import PartitionSpec as P

VEL = (
    (0, 0, 0),
    (1, 0, 0),
    (-1, 0, 0),
    (0, 1, 0),
    (0, -1, 0),
    (0, 0, 1),
    (0, 0, -1),
    (1, 1, 0),
    (-1, -1, 0),
    (1, -1, 0),
    (-1, 1, 0),
    (1, 0, 1),
    (-1, 0, -1),
    (1, 0, -1),
    (-1, 0, 1),
    (0, 1, 1),
    (0, -1, -1),
    (0, 1, -1),
    (0, -1, 1),
)
PAIRS = tuple((i, i + 1) for i in range(1, 19, 2))
AXES = ("gx", "gy", "gz")
UB = (19, 20, 21, 22)


def near(axis, sign):
    return tuple(i for i in range(19) if VEL[i][axis] * sign >= 0) + UB


def far(axis, sign):
    return tuple(i for i in range(19) if VEL[i][axis] == sign)


NSLOT = 23
CORNER = 24


def y_rows(nx):
    return -(-NSLOT * nx // 8) * 8


ZGROUPS = (
    tuple(i for i in range(19) if VEL[i][2] == -1),
    tuple(i for i in range(19) if VEL[i][2] == 1),
    tuple(i for i in range(19) if VEL[i][2] == 0)[:8],
    tuple(i for i in range(19) if VEL[i][2] == 0)[8:] + UB,
)
ZSLOT = {q: (g, k) for g, group in enumerate(ZGROUPS) for k, q in enumerate(group)}


def pairs_of(values):
    s = [values[a] + values[b] for a, b in PAIRS]
    d = [values[a] - values[b] for a, b in PAIRS]
    return s, d


def moments(v0, s, d):
    sx, sy, sz, sp, sq, sr, ss, st, su = s
    dx, dy, dz, dp, dq, dr, ds, dt, du = d
    ex = sp + sq
    ez = sr + ss
    ey = st + su
    faces = sx + sy + sz
    edges = ex + ez + ey
    exx = ex + ez
    eyy = ex + ey
    ezz = ez + ey
    fx = (dp + dq) + (dr + ds)
    fy = (dp - dq) + (dt + du)
    fz = (dr - ds) + (dt - du)
    return dict(
        rest=v0,
        faces=faces,
        edges=edges,
        total=v0 + faces + edges,
        face1=(dx, dy, dz),
        edge1=(fx, fy, fz),
        one=(dx + fx, dy + fy, dz + fz),
        face2=(sx, sy, sz),
        edge2=(exx, eyy, ezz),
        two=(sx + exx, sy + eyy, sz + ezz),
        cross=(sp - sq, sr - ss, st - su),
    )


def adjoint_cell(g, u, b, drive):
    s, d = pairs_of(g)
    m = moments(g[0], s, d)
    total = m["total"]
    trace = m["faces"] + 2.0 * m["edges"] - (30.0 / 19.0) * total
    p0 = (-1.2 / 19.0) * total - (2.0 / 21.0) * trace
    q = [
        (0.4 / 6.0) * (two - (10.0 / 19.0) * total) + (0.8 / 21.0) * trace
        for two in m["two"]
    ]
    qsum = q[0] + q[1] + q[2]
    qab = [0.1 * c for c in m["cross"]]
    p1 = [-0.12 * one for one in m["one"]]
    h0 = (
        0.4 * m["rest"]
        + (1.2 / 18.0) * m["faces"]
        + (1.2 / 36.0) * m["edges"]
        + p0
        + (1.0 / 3.0) * qsum
    )
    h1 = [
        (1.2 / 18.0) * f + (1.2 / 36.0) * e + (1.0 / 3.0) * p
        for f, e, p in zip(m["face1"], m["edge1"], p1)
    ]
    base = (1.0 / 3.0) * p0 + (1.0 / 9.0) * qsum
    haa = [
        (1.2 / 18.0) * f + (1.2 / 36.0) * e + (2.0 / 9.0) * qa + base
        for f, e, qa in zip(m["face2"], m["edge2"], q)
    ]
    hxy, hxz, hyz = [(2.0 / 45.0) * c for c in m["cross"]]
    ux, uy, uz = u
    v = (
        haa[0] * ux + hxy * uy + hxz * uz,
        hxy * ux + haa[1] * uy + hyz * uz,
        hxz * ux + hyz * uy + haa[2] * uz,
    )
    uv = ux * v[0] + uy * v[1] + uz * v[2]
    uu = ux * ux + uy * uy + uz * uz
    uuh = 1.5 * uu * h0
    a = h0 + uuh - 4.5 * uv
    nb = 1.0 - b
    e0 = nb * (a - p0)
    nq = [nb * x for x in q]
    nxy, nxz, nyz = [nb * x for x in qab]
    o = [
        nb * (3.0 * h1[k] + 9.0 * v[k] - 3.0 * u[k] * h0 - p1[k]) for k in range(3)
    ]
    o[0] = o[0] + b * drive
    alpha = -0.2 * nb
    half_s = 0.5 * (alpha + b)
    half_d = 0.5 * (alpha - b)
    exy = e0 - nq[0] - nq[1]
    exz = e0 - nq[0] - nq[2]
    eyz = e0 - nq[1] - nq[2]
    even = (
        e0 - nq[0],
        e0 - nq[1],
        e0 - nq[2],
        exy - nxy,
        exy + nxy,
        exz - nxz,
        exz + nxz,
        eyz - nyz,
        eyz + nyz,
    )
    odd = (
        o[0],
        o[1],
        o[2],
        o[0] + o[1],
        o[0] - o[1],
        o[0] + o[2],
        o[0] - o[2],
        o[1] + o[2],
        o[1] - o[2],
    )
    out = [(alpha + b) * g[0] + e0]
    for k in range(9):
        even_k = half_s * s[k] + even[k]
        odd_k = half_d * d[k] + odd[k]
        out.append(even_k + odd_k)
        out.append(even_k - odd_k)
    kept = dict(
        s=s, d=d, g0=g[0], p0=p0, p1=p1, q=q, qab=qab, h0=h0, h1=h1, uv=uv, uuh=uuh
    )
    return out, kept


def gradient_cell(kept, f0, fs, fd, fm, u):
    rho = fm["total"]
    even = fs[0] * kept["s"][0]
    odd = fd[0] * kept["d"][0]
    for k in range(1, 9):
        even = even + fs[k] * kept["s"][k]
        odd = odd + fd[k] * kept["d"][k]
    hf = kept["p0"] * rho
    for k in range(3):
        hf = hf + kept["p1"][k] * fm["one"][k] + kept["q"][k] * fm["two"][k]
        hf = hf + kept["qab"][k] * fm["cross"][k]
    uh1 = u[0] * kept["h1"][0] + u[1] * kept["h1"][1] + u[2] * kept["h1"][2]
    hfeq = rho * (kept["h0"] - kept["uuh"] + 3.0 * uh1 + 4.5 * kept["uv"])
    pairs = 1.2 * f0 * kept["g0"] + 0.6 * even - 0.4 * odd
    return pairs + hf - hfeq + fm["one"][0]


def state_of(ref, index):
    f = [ref[(index[0], i) + index[1:]] for i in range(19)]
    s, d = pairs_of(f)
    m = moments(f[0], s, d)
    inverse = 1.0 / m["total"]
    u = [one * inverse for one in m["one"]]
    return f[0], s, d, m, u


def corner_rows(sx, sy):
    rows = []
    for dx, dy in ((0, 0), (1, 0), (0, 1), (1, 1)):
        for i in near(0, sx) if dx == 0 else far(0, sx):
            if i in (near(1, sy) if dy == 0 else far(1, sy)):
                rows.append((i, dx, dy))
    return rows


def cell_rows(adj_ref, ub_ref, q, x, rows):
    return adj_ref[q, x, rows, :] if q < 19 else ub_ref[q - 19, x, rows, :]


def pack_x_kernel(
    par_ref,
    states_hbm,
    adj_hbm,
    por_hbm,
    mask_hbm,
    a_ref,
    b_ref,
    ub_ref,
    drag_ref,
    states_ref,
    adj_ref,
    por_ref,
    mask_ref,
    sems,
):
    nx, ny, nz = por_ref.shape
    tiles = ny // 8
    copies = [
        pltpu.make_async_copy(src, dst, sems.at[k])
        for k, (src, dst) in enumerate(
            (
                (states_hbm.at[1], states_ref.at[1]),
                (por_hbm, por_ref),
                (mask_hbm, mask_ref),
                (states_hbm.at[0, 1:3], states_ref.at[0, 1:3]),
                (states_hbm.at[0, 7:15], states_ref.at[0, 7:15]),
                (adj_hbm, adj_ref),
            )
        )
    ]
    for copy in copies:
        copy.start()
    for copy in copies[:5]:
        copy.wait()

    def cells(n, carry):
        x = n // tiles
        rows = pl.ds(pl.multiple_of((n % tiles) * 8, 8), 8)
        blocking = jnp.where(mask_ref[x, rows, :] == 0, por_ref[x, rows, :], 1.0)
        f0, s, d, m, u = state_of(states_ref, (1, x, rows))
        flux = m["one"][0]
        for a, b in PAIRS:
            if VEL[a][0]:
                flux = flux + (states_ref[0, a, x, rows, :] - states_ref[0, b, x, rows, :])
        for k in range(3):
            ub_ref[k, x, rows, :] = u[k]
        ub_ref[3, x, rows, :] = blocking
        return carry + blocking * flux

    drag = lax.fori_loop(0, nx * tiles, cells, jnp.zeros((8, nz), jnp.float32))
    drag_ref[...] = drag
    a_ref[NSLOT * ny :] = drag
    b_ref[NSLOT * ny :] = drag
    copies[5].wait()

    def fill_x(out_ref, sign):
        for names, offset, x in (
            (near(0, sign), 0, 0 if sign > 0 else nx - 1),
            (far(0, sign), 18, 1 if sign > 0 else nx - 2),
        ):
            for k, q in enumerate(names):
                k += offset
                out_ref[k * ny : (k + 1) * ny] = cell_rows(
                    adj_ref, ub_ref, q, x, slice(0, ny)
                )

    for px in (0, 1):

        @pl.when(par_ref[0] == px)
        def _():
            sa = 1 if px else -1
            fill_x(a_ref, sa)
            fill_x(b_ref, -sa)


def pack_y_kernel(par_ref, adj_ref, ub_ref, drag_ref, y_ref, ya_ref, yb_ref):
    nx, ny, nz = adj_ref.shape[1:]

    def fill_y(place, sign):
        for names, offset, y in (
            (near(1, sign), 0, 0 if sign > 0 else ny - 1),
            (far(1, sign), 18, 1 if sign > 0 else ny - 2),
        ):
            for k, q in enumerate(names):
                for x in range(nx):
                    row = place * y_rows(nx) + (k + offset) * nx + x
                    y_ref[row : row + 1] = cell_rows(
                        adj_ref, ub_ref, q, x, slice(y, y + 1)
                    )

    def fill_corner(out_ref, place, sx, sy):
        names = corner_rows(sx, sy)
        for k, (q, dx, dy) in enumerate(names):
            x = dx if sx > 0 else nx - 1 - dx
            y = dy if sy > 0 else ny - 1 - dy
            row = place * CORNER + k
            out_ref[row : row + 1] = cell_rows(adj_ref, ub_ref, q, x, slice(y, y + 1))
        row = place * CORNER + len(names)
        out_ref[row : (place + 1) * CORNER] = jnp.zeros(
            ((place + 1) * CORNER - row, nz), jnp.float32
        )

    drag = drag_ref[...]
    y_ref[2 * y_rows(nx) :] = drag
    ya_ref[2 * CORNER :] = drag
    yb_ref[2 * CORNER :] = drag
    for py in (0, 1):

        @pl.when(par_ref[1] == py)
        def _():
            s0 = 1 if py else -1
            fill_y(0, s0)
            fill_y(1, -s0)

    for px in (0, 1):
        for py in (0, 1):

            @pl.when((par_ref[0] == px) & (par_ref[1] == py))
            def _():
                sa = 1 if px else -1
                s0 = 1 if py else -1
                for out_ref, sx in ((ya_ref, sa), (yb_ref, -sa)):
                    fill_corner(out_ref, 0, sx, s0)
                    fill_corner(out_ref, 1, sx, -s0)


def pack_z_kernel(
    par_ref,
    adj_ref,
    ub_ref,
    xa_ref,
    xb_ref,
    y_ref,
    ya_ref,
    yb_ref,
    own_ref,
    read_ref,
    zmsg_ref,
    drag_ref,
    ext,
):
    nx, ny, nz = adj_ref.shape[1:]
    even_x = par_ref[0] == 0
    even_y = par_ref[1] == 0
    base = 16

    for q in range(NSLOT):
        for x in range(nx):
            ext[q, x + 2, base : base + ny, :] = (
                adj_ref[q, x] if q < 19 else ub_ref[q - 19, x]
            )
    planes = {1: (nx + 2, nx + 3), -1: (1, 0)}
    lines = {1: (base + ny, base + ny + 1), -1: (base - 1, base - 2)}
    for sign in (1, -1):
        first, second = (xa_ref, xb_ref) if sign > 0 else (xb_ref, xa_ref)
        for names, depth, offset in ((near(0, sign), 0, 0), (far(0, sign), 1, 18)):
            for k, q in enumerate(names):
                rows = slice((k + offset) * ny, (k + offset + 1) * ny)
                ext[q, planes[sign][depth], base : base + ny, :] = jnp.where(
                    even_x, first[rows], second[rows]
                )
        block = y_rows(nx)
        first, second = (0, block) if sign > 0 else (block, 0)
        per = 8 // nx if nx < 8 else 1
        for names, depth, offset in ((near(1, sign), 0, 0), (far(1, sign), 1, 18)):
            line = lines[sign][depth]
            for k, q in enumerate(names):
                row = (k + offset) * nx
                got = jnp.where(
                    even_y,
                    y_ref[first + row : first + row + nx],
                    y_ref[second + row : second + row + nx],
                )
                for x in range(nx):
                    ext[q, x + 2, line : line + 1, :] = got[x : x + 1]
        for sx in (1, -1):
            xs = (ya_ref, yb_ref) if sx > 0 else (yb_ref, ya_ref)
            ys = (0, CORNER) if sign > 0 else (CORNER, 0)
            low, high = [
                jnp.where(even_x, xs[0][r : r + CORNER], xs[1][r : r + CORNER])
                for r in ys
            ]
            got = jnp.where(even_y, low, high)
            for k, (q, dx, dy) in enumerate(corner_rows(sx, sign)):
                line = lines[sign][dy]
                ext[q, planes[sx][dx], line : line + 1, :] = got[k : k + 1]

    lane = lax.broadcasted_iota(jnp.int32, (8, nz), 1)
    sub = lax.broadcasted_iota(jnp.int32, (8, nz), 0)
    pair = lane // 2
    tiles = ny // 8
    for g, group in enumerate(ZGROUPS):
        acc = [jnp.zeros((8, nz), jnp.float32) for t in range(tiles + 1)]
        for k, q in enumerate(group):
            cx, cy, cz = VEL[q] if q < 19 else (0, 0, 0)
            for p in range(nx + 2):
                plane = p + 1 + cx
                start = 16 * k + 2 * p
                mask = pair == start // 2
                for t in range(tiles + 1):
                    if t < tiles:
                        low = base + 8 * t + cy
                        value = ext[q, plane, low : low + 8, :]
                    else:
                        high = base + ny + cy
                        low = base - 8 + cy
                        value = jnp.where(
                            sub < 4,
                            ext[q, plane, high : high + 8, :],
                            ext[q, plane, low : low + 8, :],
                        )
                    read_ref[q, p, 8 * t : 8 * t + 8, :] = value
                    shift = start + (2 if cz < 0 else 1 if cz == 0 else 0)
                    moved = pltpu.roll(value, shift % nz, 1)
                    acc[t] = jnp.where(mask, moved, acc[t])
        for t in range(tiles + 1):
            row = (g * (tiles + 1) + t) * 8
            zmsg_ref[row : row + 8, :] = acc[t]
    drags = [
        own_ref[...] + y_ref[2 * y_rows(nx) :],
        xa_ref[NSLOT * ny :] + ya_ref[2 * CORNER :],
        xb_ref[NSLOT * ny :] + yb_ref[2 * CORNER :],
    ]
    row = 4 * (tiles + 1) * 8
    for k, drag in enumerate(drags):
        drag_ref[8 * k : 8 * k + 8, :] = drag
        zmsg_ref[row + 8 * k : row + 8 * k + 8, :] = drag


def levels_kernel(
    par_ref,
    states_ref,
    mask_ref,
    read_ref,
    zown_ref,
    za_ref,
    zb_ref,
    out_ref,
    grad_ref,
    lo_ref,
    hi_ref,
    slab_ref,
    mid,
    zmid,
):
    nx, ny, nz = mask_ref.shape
    tiles = ny // 8
    height = (tiles + 1) * 8
    even = par_ref[2] == 0
    lane = lax.broadcasted_iota(jnp.int32, (8, nz), 1)
    side = lane % 2
    first_lane = lane == 0
    last_lane = lane == nz - 1

    for g in range(4):
        for t in range(tiles + 1):
            rows = slice((g * (tiles + 1) + t) * 8, (g * (tiles + 1) + t) * 8 + 8)
            va = za_ref[rows]
            vb = zb_ref[rows]
            high = jnp.where(even, va, vb)
            low = jnp.where(even, vb, va)
            lo_ref[rows] = low
            hi_ref[rows] = high
            own = zown_ref[rows]
            slab_ref[rows] = jnp.where(
                side == 0, own if g == 1 else low, own if g == 0 else high
            )

    def rolled(value, shift):
        return pltpu.roll(value, lax.rem(shift + 2 * nz, nz), 1)

    def z_slab(t, carry):
        row = pl.multiple_of(t * 8, 8)
        got = []
        for q in range(NSLOT):
            g, k = ZSLOT[q]
            tile = slab_ref[pl.ds(pl.multiple_of(g * height + row, 8), 8), :]
            got.append(tile if k == 0 else pltpu.roll(tile, nz - 16 * k, 1))
        out, kept = adjoint_cell(got[:19], got[19:22], got[22], 1.0)
        for n, i in enumerate(ZGROUPS[0] + ZGROUPS[1]):
            if_last = t == tiles

            zmid[n, pl.ds(pl.multiple_of(row + 8, 8), 8), :] = out[i]

            @pl.when(if_last)
            def _():
                zmid[n, 0:8, :] = out[i]

        return carry

    lax.fori_loop(0, tiles + 1, z_slab, 0)

    def first_reads(p, t):
        rows = pl.ds(pl.multiple_of(t * 8, 8), 8)
        got = []
        for i in range(19):
            value = read_ref[i, p, rows, :]
            cz = VEL[i][2]
            if cz:
                g, k = ZSLOT[i]
                zrows = pl.ds(pl.multiple_of(g * height + t * 8, 8), 8)
                value = pltpu.roll(value, 1 if cz < 0 else nz - 1, 1)
                if cz < 0:
                    edge = rolled(lo_ref[zrows, :], -(16 * k + 2 * p + 1))
                    value = jnp.where(first_lane, edge, value)
                else:
                    edge = rolled(hi_ref[zrows, :], nz - 1 - 16 * k - 2 * p)
                    value = jnp.where(last_lane, edge, value)
            got.append(value)
        ub = [read_ref[19 + k, p, rows, :] for k in range(4)]
        return got, ub[:3], ub[3]

    def store_mid(out, p, t):
        for i in range(19):
            mid[i, p, pl.ds(pl.multiple_of(t * 8 + 8, 8), 8), :] = out[i]

    def inner(n, carry):
        x = n // tiles
        t = n % tiles
        got, u, b = first_reads(x + 1, t)
        out, kept = adjoint_cell(got, u, b, 1.0)
        store_mid(out, x + 1, t)
        rows = pl.ds(pl.multiple_of(t * 8, 8), 8)
        f0, fs, fd, fm, _ = state_of(states_ref, (1, x, rows))
        grad_ref[x, rows, :] = gradient_cell(kept, f0, fs, fd, fm, u)
        return carry

    lax.fori_loop(0, nx * tiles, inner, 0)

    def outer(n, carry):
        faces = 2 * (tiles + 1)
        p = jnp.where(n < faces, (nx + 1) * (n // (tiles + 1)), n - faces + 1)
        t = jnp.where(n < faces, n % (tiles + 1), tiles)
        got, u, b = first_reads(p, t)
        out, kept = adjoint_cell(got, u, b, 1.0)
        store_mid(out, p, t)

        @pl.when(t == tiles)
        def _():
            for i in range(19):
                mid[i, p, 0:8, :] = out[i]

        return carry

    lax.fori_loop(0, 2 * (tiles + 1) + nx, outer, 0)

    edge_pops = ZGROUPS[0] + ZGROUPS[1]

    def second(x, carry):
        for t in range(tiles):
            rows = slice(t * 8, t * 8 + 8)
            got = []
            for i in range(19):
                cx, cy, cz = VEL[i]
                low = 8 + 8 * t + cy
                value = mid[i, x + 1 + cx, low : low + 8, :]
                if cz:
                    value = pltpu.roll(value, 1 if cz < 0 else nz - 1, 1)
                    edge = zmid[edge_pops.index(i), low : low + 8, :]
                    at = 2 * (x + 1 + cx)
                    if cz < 0:
                        value = jnp.where(first_lane, rolled(edge, -at), value)
                    else:
                        value = jnp.where(
                            last_lane, rolled(edge, nz - 2 - at), value
                        )
                got.append(value)
            f0, fs, fd, fm, u = state_of(states_ref, (0, x, rows))
            b = read_ref[22, x + 1, rows, :]
            out, kept = adjoint_cell(got, u, b, 1.0)
            for i in range(19):
                out_ref[i, x, rows, :] = out[i]
            grad = grad_ref[x, rows, :] + gradient_cell(kept, f0, fs, fd, fm, u)
            grad_ref[x, rows, :] = jnp.where(mask_ref[x, rows, :] == 0, grad, 0.0)
        return carry

    lax.fori_loop(0, nx, second, 0)


def swaps(count):
    first = [(i, i ^ 1) for i in range(count)]
    second = [(i, (((i + 1) % count) ^ 1) - 1) for i in range(count)]
    second = [(i, j % count) for i, j in second]
    return first, second


VMEM = pl.BlockSpec(memory_space=pltpu.VMEM)
SMEM = pl.BlockSpec(memory_space=pltpu.SMEM)
HBM = pl.BlockSpec(memory_space=pltpu.HBM)
PARAMS = pltpu.CompilerParams(vmem_limit_bytes=48 * 2**20)


def call(kernel, inputs, shapes, scratch=(), space=VMEM, micros=1):
    if space is HBM:
        inputs = inputs[:1] + tuple(
            pltpu.with_memory_space_constraint(x, pltpu.HBM) for x in inputs[1:]
        )
    return pl.pallas_call(
        kernel,
        out_shape=[jax.ShapeDtypeStruct(s, jnp.float32) for s in shapes],
        in_specs=[SMEM] + [space] * (len(inputs) - 1),
        out_specs=[VMEM] * len(shapes),
        scratch_shapes=list(scratch),
        compiler_params=PARAMS,
        cost_estimate=pl.CostEstimate(
            flops=0, bytes_accessed=int(3.6e6 * micros), transcendentals=0
        ),
    )(*inputs)


def body(primal_states, adjoint_last, porosity, solid_mask):
    nx, ny, nz = porosity.shape
    gx, gy, gz = [lax.axis_size(axis) for axis in AXES]
    x_first, x_second = swaps(gx)
    y_first, y_second = swaps(gy)
    z_first, z_second = swaps(gz)
    parity = jnp.stack([lax.axis_index(axis) & 1 for axis in AXES]).astype(jnp.int32)
    tiles = ny // 8
    height = (tiles + 1) * 8
    f32 = jnp.float32

    def diagonal(message, x_pairs, y_pairs):
        pairs = [(a * gy + c, b * gy + d) for a, b in x_pairs for c, d in y_pairs]
        return lax.ppermute(message, ("gx", "gy"), pairs)

    rows_x = NSLOT * ny + 8
    rows_y = 2 * y_rows(nx) + 8
    rows_c = 2 * CORNER + 8
    xa, xb, ub, drag = call(
        pack_x_kernel,
        (parity, primal_states, adjoint_last, porosity, solid_mask),
        [(rows_x, nz), (rows_x, nz), (4, nx, ny, nz), (8, nz)],
        [
            pltpu.VMEM((2, 19, nx, ny, nz), f32),
            pltpu.VMEM((19, nx, ny, nz), f32),
            pltpu.VMEM((nx, ny, nz), f32),
            pltpu.VMEM((nx, ny, nz), jnp.int32),
            pltpu.SemaphoreType.DMA((6,)),
        ],
        HBM,
    )
    y, ya, yb = call(
        pack_y_kernel,
        (parity, adjoint_last, ub, drag),
        [(rows_y, nz), (rows_c, nz), (rows_c, nz)],
        micros=4,
    )
    xb = lax.ppermute(xb, "gx", x_second)
    if gy == 2:
        y = lax.ppermute(y, "gy", y_first)
        yb = diagonal(yb, x_second, y_first)
        ya = diagonal(ya, x_first, y_first)
    else:

        def both(message, block, send):
            parts = [message[:block], message[block : 2 * block], message[2 * block :]]
            return jnp.concatenate(
                [send(parts[0], y_first), send(parts[1], y_second), parts[2]]
            )

        y = both(y, y_rows(nx), lambda m, pairs: lax.ppermute(m, "gy", pairs))
        yb = both(yb, CORNER, lambda m, pairs: diagonal(m, x_second, pairs))
        ya = both(ya, CORNER, lambda m, pairs: diagonal(m, x_first, pairs))
    xa = lax.ppermute(xa, "gx", x_first)

    read, zmsg, drags = call(
        pack_z_kernel,
        (parity, adjoint_last, ub, xa, xb, y, ya, yb, drag),
        [(NSLOT, nx + 2, height, nz), (4 * height + 24, nz), (24, nz)],
        [pltpu.VMEM((NSLOT, nx + 4, ny + 32, nz), f32)],
    )
    zb = lax.ppermute(zmsg, "gz", z_second)
    za = lax.ppermute(zmsg, "gz", z_first)
    if (gx, gy, gz) == (4, 2, 4):
        across = lax.ppermute(drags, "gz", [(i, i ^ 2) for i in range(gz)])
        drags = (drags + across) + (za[4 * height :] + zb[4 * height :])
        fourth = lax.ppermute(drags[16:], "gx", x_first)
        drag = jnp.sum(drags[:8] + drags[8:16] + drags[16:] + fourth)
    else:
        drag = lax.psum(jnp.sum(drag), AXES)

    first, gradient = call(
        levels_kernel,
        (parity, primal_states, solid_mask, read, zmsg, za, zb),
        [(19, nx, ny, nz), (nx, ny, nz)],
        [
            pltpu.VMEM((4 * height, nz), f32),
            pltpu.VMEM((4 * height, nz), f32),
            pltpu.VMEM((4 * height, nz), f32),
            pltpu.VMEM((19, nx + 2, height + 8, nz), f32),
            pltpu.VMEM((10, height + 8, nz), f32),
        ],
        micros=4,
    )
    return (first, gradient, drag / (nx * ny * nz * gx * gy * gz))


def solution(mesh):
    return jax.shard_map(
        body,
        mesh=mesh,
        in_specs=(
            P(None, None, "gx", "gy", "gz"),
            P(None, "gx", "gy", "gz"),
            P("gx", "gy", "gz"),
            P("gx", "gy", "gz"),
        ),
        out_specs=(P(None, "gx", "gy", "gz"), P("gx", "gy", "gz"), P()),
        check_vma=False,
    )
```

```python
import functools

import jax
import jax.numpy as jnp
import numpy as np
from jax import lax
from jax.experimental import pallas as pl
from jax.experimental.pallas import tpu as pltpu
from jax.sharding import PartitionSpec as P

VEL = (
    (0, 0, 0),
    (1, 0, 0),
    (-1, 0, 0),
    (0, 1, 0),
    (0, -1, 0),
    (0, 0, 1),
    (0, 0, -1),
    (1, 1, 0),
    (-1, -1, 0),
    (1, -1, 0),
    (-1, 1, 0),
    (1, 0, 1),
    (-1, 0, -1),
    (1, 0, -1),
    (-1, 0, 1),
    (0, 1, 1),
    (0, -1, -1),
    (0, 1, -1),
    (0, -1, 1),
)
PAIRS = tuple((i, i + 1) for i in range(1, 19, 2))
AXES = ("gx", "gy", "gz")
UB = (19, 20, 21, 22)


def near(axis, sign):
    return tuple(i for i in range(19) if VEL[i][axis] * sign >= 0) + UB


def far(axis, sign):
    return tuple(i for i in range(19) if VEL[i][axis] == sign)


NSLOT = 23
CORNER = 24


def y_rows(nx):
    return -(-NSLOT * nx // 8) * 8


ZGROUPS = (
    tuple(i for i in range(19) if VEL[i][2] == -1),
    tuple(i for i in range(19) if VEL[i][2] == 1),
    tuple(i for i in range(19) if VEL[i][2] == 0)[:8],
    tuple(i for i in range(19) if VEL[i][2] == 0)[8:] + UB,
)
ZSLOT = {q: (g, k) for g, group in enumerate(ZGROUPS) for k, q in enumerate(group)}


def pairs_of(values):
    s = [values[a] + values[b] for a, b in PAIRS]
    d = [values[a] - values[b] for a, b in PAIRS]
    return s, d


def moments(v0, s, d):
    sx, sy, sz, sp, sq, sr, ss, st, su = s
    dx, dy, dz, dp, dq, dr, ds, dt, du = d
    ex = sp + sq
    ez = sr + ss
    ey = st + su
    faces = sx + sy + sz
    edges = ex + ez + ey
    exx = ex + ez
    eyy = ex + ey
    ezz = ez + ey
    fx = (dp + dq) + (dr + ds)
    fy = (dp - dq) + (dt + du)
    fz = (dr - ds) + (dt - du)
    return dict(
        rest=v0,
        faces=faces,
        edges=edges,
        total=v0 + faces + edges,
        face1=(dx, dy, dz),
        edge1=(fx, fy, fz),
        one=(dx + fx, dy + fy, dz + fz),
        face2=(sx, sy, sz),
        edge2=(exx, eyy, ezz),
        two=(sx + exx, sy + eyy, sz + ezz),
        cross=(sp - sq, sr - ss, st - su),
    )


def adjoint_cell(g, u, b, drive):
    s, d = pairs_of(g)
    m = moments(g[0], s, d)
    total = m["total"]
    trace = m["faces"] + 2.0 * m["edges"] - (30.0 / 19.0) * total
    p0 = (-1.2 / 19.0) * total - (2.0 / 21.0) * trace
    q = [
        (0.4 / 6.0) * (two - (10.0 / 19.0) * total) + (0.8 / 21.0) * trace
        for two in m["two"]
    ]
    qsum = q[0] + q[1] + q[2]
    qab = [0.1 * c for c in m["cross"]]
    p1 = [-0.12 * one for one in m["one"]]
    h0 = (
        0.4 * m["rest"]
        + (1.2 / 18.0) * m["faces"]
        + (1.2 / 36.0) * m["edges"]
        + p0
        + (1.0 / 3.0) * qsum
    )
    h1 = [
        (1.2 / 18.0) * f + (1.2 / 36.0) * e + (1.0 / 3.0) * p
        for f, e, p in zip(m["face1"], m["edge1"], p1)
    ]
    base = (1.0 / 3.0) * p0 + (1.0 / 9.0) * qsum
    haa = [
        (1.2 / 18.0) * f + (1.2 / 36.0) * e + (2.0 / 9.0) * qa + base
        for f, e, qa in zip(m["face2"], m["edge2"], q)
    ]
    hxy, hxz, hyz = [(2.0 / 45.0) * c for c in m["cross"]]
    ux, uy, uz = u
    v = (
        haa[0] * ux + hxy * uy + hxz * uz,
        hxy * ux + haa[1] * uy + hyz * uz,
        hxz * ux + hyz * uy + haa[2] * uz,
    )
    uv = ux * v[0] + uy * v[1] + uz * v[2]
    uu = ux * ux + uy * uy + uz * uz
    uuh = 1.5 * uu * h0
    a = h0 + uuh - 4.5 * uv
    nb = 1.0 - b
    e0 = nb * (a - p0)
    nq = [nb * x for x in q]
    nxy, nxz, nyz = [nb * x for x in qab]
    o = [
        nb * (3.0 * h1[k] + 9.0 * v[k] - 3.0 * u[k] * h0 - p1[k]) for k in range(3)
    ]
    o[0] = o[0] + b * drive
    alpha = -0.2 * nb
    half_s = 0.5 * (alpha + b)
    half_d = 0.5 * (alpha - b)
    exy = e0 - nq[0] - nq[1]
    exz = e0 - nq[0] - nq[2]
    eyz = e0 - nq[1] - nq[2]
    even = (
        e0 - nq[0],
        e0 - nq[1],
        e0 - nq[2],
        exy - nxy,
        exy + nxy,
        exz - nxz,
        exz + nxz,
        eyz - nyz,
        eyz + nyz,
    )
    odd = (
        o[0],
        o[1],
        o[2],
        o[0] + o[1],
        o[0] - o[1],
        o[0] + o[2],
        o[0] - o[2],
        o[1] + o[2],
        o[1] - o[2],
    )
    out = [(alpha + b) * g[0] + e0]
    for k in range(9):
        even_k = half_s * s[k] + even[k]
        odd_k = half_d * d[k] + odd[k]
        out.append(even_k + odd_k)
        out.append(even_k - odd_k)
    kept = dict(
        s=s, d=d, g0=g[0], p0=p0, p1=p1, q=q, qab=qab, h0=h0, h1=h1, uv=uv, uuh=uuh
    )
    return out, kept


def gradient_cell(kept, f0, fs, fd, fm, u):
    rho = fm["total"]
    even = fs[0] * kept["s"][0]
    odd = fd[0] * kept["d"][0]
    for k in range(1, 9):
        even = even + fs[k] * kept["s"][k]
        odd = odd + fd[k] * kept["d"][k]
    hf = kept["p0"] * rho
    for k in range(3):
        hf = hf + kept["p1"][k] * fm["one"][k] + kept["q"][k] * fm["two"][k]
        hf = hf + kept["qab"][k] * fm["cross"][k]
    uh1 = u[0] * kept["h1"][0] + u[1] * kept["h1"][1] + u[2] * kept["h1"][2]
    hfeq = rho * (kept["h0"] - kept["uuh"] + 3.0 * uh1 + 4.5 * kept["uv"])
    pairs = 1.2 * f0 * kept["g0"] + 0.6 * even - 0.4 * odd
    return pairs + hf - hfeq + fm["one"][0]


def state_of(ref, index):
    f = [ref[(index[0], i) + index[1:]] for i in range(19)]
    s, d = pairs_of(f)
    m = moments(f[0], s, d)
    inverse = 1.0 / m["total"]
    u = [one * inverse for one in m["one"]]
    return f[0], s, d, m, u


def corner_rows(sx, sy):
    rows = []
    for dx, dy in ((0, 0), (1, 0), (0, 1), (1, 1)):
        for i in near(0, sx) if dx == 0 else far(0, sx):
            if i in (near(1, sy) if dy == 0 else far(1, sy)):
                rows.append((i, dx, dy))
    return rows


def cell_rows(adj_ref, ub_ref, q, x, rows):
    return adj_ref[q, x, rows, :] if q < 19 else ub_ref[q - 19, x, rows, :]


def pack_x_kernel(
    par_ref,
    states_hbm,
    adj_hbm,
    por_hbm,
    mask_hbm,
    a_ref,
    b_ref,
    ub_ref,
    drag_ref,
    states_ref,
    adj_ref,
    por_ref,
    mask_ref,
    sems,
):
    nx, ny, nz = por_ref.shape
    tiles = ny // 8
    copies = [
        pltpu.make_async_copy(src, dst, sems.at[k])
        for k, (src, dst) in enumerate(
            (
                (states_hbm.at[1], states_ref.at[1]),
                (por_hbm, por_ref),
                (mask_hbm, mask_ref),
                (states_hbm.at[0, 1:3], states_ref.at[0, 1:3]),
                (states_hbm.at[0, 7:15], states_ref.at[0, 7:15]),
                (adj_hbm, adj_ref),
            )
        )
    ]
    for copy in copies:
        copy.start()
    for copy in copies[:5]:
        copy.wait()

    def cells(n, carry):
        x = n // tiles
        rows = pl.ds(pl.multiple_of((n % tiles) * 8, 8), 8)
        blocking = jnp.where(mask_ref[x, rows, :] == 0, por_ref[x, rows, :], 1.0)
        f0, s, d, m, u = state_of(states_ref, (1, x, rows))
        flux = m["one"][0]
        for a, b in PAIRS:
            if VEL[a][0]:
                flux = flux + (states_ref[0, a, x, rows, :] - states_ref[0, b, x, rows, :])
        for k in range(3):
            ub_ref[k, x, rows, :] = u[k]
        ub_ref[3, x, rows, :] = blocking
        return carry + blocking * flux

    drag = lax.fori_loop(0, nx * tiles, cells, jnp.zeros((8, nz), jnp.float32))
    drag_ref[...] = drag
    a_ref[NSLOT * ny :] = drag
    b_ref[NSLOT * ny :] = drag
    copies[5].wait()

    def fill_x(out_ref, sign):
        for names, offset, x in (
            (near(0, sign), 0, 0 if sign > 0 else nx - 1),
            (far(0, sign), 18, 1 if sign > 0 else nx - 2),
        ):
            for k, q in enumerate(names):
                k += offset
                out_ref[k * ny : (k + 1) * ny] = cell_rows(
                    adj_ref, ub_ref, q, x, slice(0, ny)
                )

    for px in (0, 1):

        @pl.when(par_ref[0] == px)
        def _():
            sa = 1 if px else -1
            fill_x(a_ref, sa)
            fill_x(b_ref, -sa)


def pack_y_kernel(par_ref, adj_ref, ub_ref, drag_ref, y_ref, ya_ref, yb_ref):
    nx, ny, nz = adj_ref.shape[1:]

    def fill_y(place, sign):
        for names, offset, y in (
            (near(1, sign), 0, 0 if sign > 0 else ny - 1),
            (far(1, sign), 18, 1 if sign > 0 else ny - 2),
        ):
            for k, q in enumerate(names):
                for x in range(nx):
                    row = place * y_rows(nx) + (k + offset) * nx + x
                    y_ref[row : row + 1] = cell_rows(
                        adj_ref, ub_ref, q, x, slice(y, y + 1)
                    )

    def fill_corner(out_ref, place, sx, sy):
        names = corner_rows(sx, sy)
        for k, (q, dx, dy) in enumerate(names):
            x = dx if sx > 0 else nx - 1 - dx
            y = dy if sy > 0 else ny - 1 - dy
            row = place * CORNER + k
            out_ref[row : row + 1] = cell_rows(adj_ref, ub_ref, q, x, slice(y, y + 1))
        row = place * CORNER + len(names)
        out_ref[row : (place + 1) * CORNER] = jnp.zeros(
            ((place + 1) * CORNER - row, nz), jnp.float32
        )

    drag = drag_ref[...]
    y_ref[2 * y_rows(nx) :] = drag
    ya_ref[2 * CORNER :] = drag
    yb_ref[2 * CORNER :] = drag
    for py in (0, 1):

        @pl.when(par_ref[1] == py)
        def _():
            s0 = 1 if py else -1
            fill_y(0, s0)
            fill_y(1, -s0)

    for px in (0, 1):
        for py in (0, 1):

            @pl.when((par_ref[0] == px) & (par_ref[1] == py))
            def _():
                sa = 1 if px else -1
                s0 = 1 if py else -1
                for out_ref, sx in ((ya_ref, sa), (yb_ref, -sa)):
                    fill_corner(out_ref, 0, sx, s0)
                    fill_corner(out_ref, 1, sx, -s0)


def pack_z_kernel(
    par_ref,
    adj_ref,
    ub_ref,
    xa_ref,
    xb_ref,
    y_ref,
    ya_ref,
    yb_ref,
    own_ref,
    read_ref,
    zmsg_ref,
    drag_ref,
    ext,
):
    nx, ny, nz = adj_ref.shape[1:]
    even_x = par_ref[0] == 0
    even_y = par_ref[1] == 0
    base = 16

    for q in range(NSLOT):
        for x in range(nx):
            ext[q, x + 2, base : base + ny, :] = (
                adj_ref[q, x] if q < 19 else ub_ref[q - 19, x]
            )
    planes = {1: (nx + 2, nx + 3), -1: (1, 0)}
    lines = {1: (base + ny, base + ny + 1), -1: (base - 1, base - 2)}
    for sign in (1, -1):
        first, second = (xa_ref, xb_ref) if sign > 0 else (xb_ref, xa_ref)
        for names, depth, offset in ((near(0, sign), 0, 0), (far(0, sign), 1, 18)):
            for k, q in enumerate(names):
                rows = slice((k + offset) * ny, (k + offset + 1) * ny)
                ext[q, planes[sign][depth], base : base + ny, :] = jnp.where(
                    even_x, first[rows], second[rows]
                )
        block = y_rows(nx)
        first, second = (0, block) if sign > 0 else (block, 0)
        per = 8 // nx if nx < 8 else 1
        for names, depth, offset in ((near(1, sign), 0, 0), (far(1, sign), 1, 18)):
            line = lines[sign][depth]
            for k, q in enumerate(names):
                row = (k + offset) * nx
                got = jnp.where(
                    even_y,
                    y_ref[first + row : first + row + nx],
                    y_ref[second + row : second + row + nx],
                )
                for x in range(nx):
                    ext[q, x + 2, line : line + 1, :] = got[x : x + 1]
        for sx in (1, -1):
            xs = (ya_ref, yb_ref) if sx > 0 else (yb_ref, ya_ref)
            ys = (0, CORNER) if sign > 0 else (CORNER, 0)
            low, high = [
                jnp.where(even_x, xs[0][r : r + CORNER], xs[1][r : r + CORNER])
                for r in ys
            ]
            got = jnp.where(even_y, low, high)
            for k, (q, dx, dy) in enumerate(corner_rows(sx, sign)):
                line = lines[sign][dy]
                ext[q, planes[sx][dx], line : line + 1, :] = got[k : k + 1]

    lane = lax.broadcasted_iota(jnp.int32, (8, nz), 1)
    sub = lax.broadcasted_iota(jnp.int32, (8, nz), 0)
    pair = lane // 2
    tiles = ny // 8
    for g, group in enumerate(ZGROUPS):
        acc = [jnp.zeros((8, nz), jnp.float32) for t in range(tiles + 1)]
        for k, q in enumerate(group):
            cx, cy, cz = VEL[q] if q < 19 else (0, 0, 0)
            for p in range(nx + 2):
                plane = p + 1 + cx
                start = 32 * (k // 2) + 4 * p + 2 * (k % 2)
                mask = pair == start // 2
                for t in range(tiles + 1):
                    if t < tiles:
                        low = base + 8 * t + cy
                        value = ext[q, plane, low : low + 8, :]
                    else:
                        high = base + ny + cy
                        low = base - 8 + cy
                        value = jnp.where(
                            sub < 4,
                            ext[q, plane, high : high + 8, :],
                            ext[q, plane, low : low + 8, :],
                        )
                    read_ref[q, p, 8 * t : 8 * t + 8, :] = value
                    shift = start + (2 if cz < 0 else 1 if cz == 0 else 0)
                    moved = pltpu.roll(value, shift % nz, 1)
                    acc[t] = jnp.where(mask, moved, acc[t])
        for t in range(tiles + 1):
            row = (g * (tiles + 1) + t) * 8
            zmsg_ref[row : row + 8, :] = acc[t]
    drags = [
        own_ref[...] + y_ref[2 * y_rows(nx) :],
        xa_ref[NSLOT * ny :] + ya_ref[2 * CORNER :],
        xb_ref[NSLOT * ny :] + yb_ref[2 * CORNER :],
    ]
    row = 4 * (tiles + 1) * 8
    for k, drag in enumerate(drags):
        drag_ref[8 * k : 8 * k + 8, :] = drag
        zmsg_ref[row + 8 * k : row + 8 * k + 8, :] = drag


def pack_state_kernel(states_ref, ub_ref, f0_ref, f1_ref):
    nx, ny, nz = ub_ref.shape[1:]
    lane = lax.broadcasted_iota(jnp.int32, (8, nz), 1)
    slot = lane // 4

    def tile(t, carry):
        rows = pl.ds(pl.multiple_of(t * 8, 8), 8)
        for i in range(20):
            for out_ref, level, first in ((f0_ref, 0, 0), (f1_ref, 1, 1)):
                if i == 19 and level == 1:
                    continue
                acc = jnp.zeros((8, nz), jnp.float32)
                for x in range(nx):
                    value = (
                        states_ref[level, i, x, rows, :]
                        if i < 19
                        else ub_ref[3, x, rows, :]
                    )
                    p = x + first
                    acc = jnp.where(slot == p, pltpu.roll(value, 4 * p + 2, 1), acc)
                out_ref[i, rows, :] = acc
        return carry

    lax.fori_loop(0, ny // 8, tile, 0)


def turn(value, shift):
    nz = value.shape[1]
    return pltpu.roll(value, shift % nz, 1) if shift % nz else value


def z_shifted(value, cz):
    return turn(value, -cz) if cz else value


def inner_kernel(states_ref, read_ref, out_ref, grad1_ref, grad_ref, pack_ref, mid):
    nx, ny, nz = grad_ref.shape
    tiles = ny // 8
    lane = lax.broadcasted_iota(jnp.int32, (8, nz), 1)
    slot = lane // 4

    def first_level(p, t):
        rows = pl.ds(pl.multiple_of(t * 8, 8), 8)
        got = [z_shifted(read_ref[i, p, rows, :], VEL[i][2]) for i in range(19)]
        ub = [read_ref[19 + k, p, rows, :] for k in range(4)]
        out, kept = adjoint_cell(got, ub[:3], ub[3], 1.0)
        for i in range(19):
            mid[i, p, pl.ds(pl.multiple_of(t * 8 + 8, 8), 8), :] = out[i]
        return out, kept, ub[:3]

    def inside(n, carry):
        x = n // tiles
        t = n % tiles
        out, kept, u = first_level(x + 1, t)
        rows = pl.ds(pl.multiple_of(t * 8, 8), 8)
        f0, fs, fd, fm, _ = state_of(states_ref, (1, x, rows))
        grad1_ref[x, rows, :] = gradient_cell(kept, f0, fs, fd, fm, u)
        return carry

    lax.fori_loop(0, nx * tiles, inside, 0)

    def halo(n, carry):
        faces = 2 * (tiles + 1)
        p = jnp.where(n < faces, (nx + 1) * (n // (tiles + 1)), n - faces + 1)
        t = jnp.where(n < faces, n % (tiles + 1), tiles)
        out, _, _ = first_level(p, t)

        @pl.when(t == tiles)
        def _():
            for i in range(19):
                mid[i, p, 0:8, :] = out[i]

        return carry

    lax.fori_loop(0, 2 * (tiles + 1) + nx, halo, 0)

    def second_level(x, carry):
        for t in range(tiles):
            rows = slice(t * 8, t * 8 + 8)
            got = []
            for i in range(19):
                cx, cy, cz = VEL[i]
                low = 8 + 8 * t + cy
                value = z_shifted(mid[i, x + 1 + cx, low : low + 8, :], cz)
                got.append(value)
                pack_ref[i, rows, :] = jnp.where(
                    slot == x, pltpu.roll(value, 4 * x + 2, 1), pack_ref[i, rows, :]
                )
            f0, fs, fd, fm, u = state_of(states_ref, (0, x, rows))
            b = read_ref[22, x + 1, rows, :]
            out, kept = adjoint_cell(got, u, b, 1.0)
            for i in range(19):
                out_ref[i, x, rows, :] = out[i]
            grad_ref[x, rows, :] = grad1_ref[x, rows, :] + gradient_cell(
                kept, f0, fs, fd, fm, u
            )
        return carry

    lax.fori_loop(0, nx, second_level, 0)


def edge_kernel(
    par_ref,
    mask_ref,
    zown_ref,
    za_ref,
    zb_ref,
    pack_ref,
    f0_ref,
    f1_ref,
    inner_ref,
    grad1_ref,
    inner_grad_ref,
    out_ref,
    grad_ref,
    first_ref,
    second_ref,
    zmid,
    zout,
):
    nx, ny, nz = mask_ref.shape
    tiles = ny // 8
    height = (tiles + 1) * 8
    even = par_ref[2] == 0
    lane = lax.broadcasted_iota(jnp.int32, (8, nz), 1)
    even_lane = lane % 2 == 0
    low_pair = lane % 4 < 2

    def swapped(value):
        return jnp.where(even_lane, turn(value, -1), turn(value, 1))

    for g in range(4):
        for t in range(tiles + 1):
            rows = slice((g * (tiles + 1) + t) * 8, (g * (tiles + 1) + t) * 8 + 8)
            va = za_ref[rows]
            vb = zb_ref[rows]
            high = jnp.where(even, va, vb)
            low = jnp.where(even, vb, va)
            own = zown_ref[rows]
            if g == 0:
                head, tail = own, low
            elif g == 1:
                head, tail = high, own
            else:
                head, tail = jnp.where(even_lane, own, high), jnp.where(even_lane, low, own)
            head = swapped(head)
            tail = swapped(tail)
            first_ref[rows] = jnp.where(low_pair, head, turn(tail, 2))
            second_ref[rows] = jnp.where(low_pair, turn(head, -2), tail)

    slab_grad = []
    for t in range(tiles + 1):
        got = []
        for q in range(NSLOT):
            g, k = ZSLOT[q]
            row = g * height + t * 8
            ref = second_ref if k % 2 else first_ref
            got.append(turn(ref[row : row + 8, :], -32 * (k // 2)))
        out, kept = adjoint_cell(got[:19], got[19:22], got[22], 1.0)
        for i in range(19):
            zmid[i, 8 * t + 8 : 8 * t + 16, :] = out[i]
            if t == tiles:
                zmid[i, 0:8, :] = out[i]
        if t < tiles:
            f = [f1_ref[i, 8 * t : 8 * t + 8, :] for i in range(19)]
            fs, fd = pairs_of(f)
            fm = moments(f[0], fs, fd)
            grad = gradient_cell(kept, f[0], fs, fd, fm, got[19:22])
            slab_grad.append(turn(grad, -4))

    at = lane % 4
    for t in range(tiles):
        rows = slice(8 * t, 8 * t + 8)
        got = []
        for i in range(19):
            cx, cy, cz = VEL[i]
            value = pack_ref[i, rows, :]
            edge = zmid[i, 8 + 8 * t + cy : 16 + 8 * t + cy, :]
            back = -4 * (1 + cx)
            if cz == 0:
                value = jnp.where((at == 1) | (at == 2), turn(edge, back), value)
            else:
                near_lane = 2 if cz < 0 else 0
                value = jnp.where(at == near_lane, turn(edge, back - 1), value)
                value = jnp.where(at == near_lane + 1, turn(edge, back + 1), value)
            got.append(value)
        f = [f0_ref[i, rows, :] for i in range(19)]
        fs, fd = pairs_of(f)
        fm = moments(f[0], fs, fd)
        inverse = 1.0 / fm["total"]
        u = [one * inverse for one in fm["one"]]
        out, kept = adjoint_cell(got, u, f0_ref[19, rows, :], 1.0)
        for i in range(19):
            zout[i, rows, :] = out[i]
        zout[19, rows, :] = gradient_cell(kept, f[0], fs, fd, fm, u)
        zout[20, rows, :] = slab_grad[t]

    outer = (lane < 2) | (lane >= nz - 2)
    ends = (lane < 1) | (lane >= nz - 1)
    for x in range(nx):
        for t in range(tiles):
            rows = slice(8 * t, 8 * t + 8)
            for i in range(19):
                out_ref[i, x, rows, :] = jnp.where(
                    outer, turn(zout[i, rows, :], -2 - 4 * x), inner_ref[i, x, rows, :]
                )
            level1 = jnp.where(
                ends, turn(zout[20, rows, :], -2 - 4 * x), grad1_ref[x, rows, :]
            )
            edge = turn(zout[19, rows, :], -2 - 4 * x) + level1
            grad = jnp.where(outer, edge, inner_grad_ref[x, rows, :])
            grad_ref[x, rows, :] = jnp.where(mask_ref[x, rows, :] == 0, grad, 0.0)


def swaps(count):
    first = [(i, i ^ 1) for i in range(count)]
    second = [(i, (((i + 1) % count) ^ 1) - 1) for i in range(count)]
    second = [(i, j % count) for i, j in second]
    return first, second


VMEM = pl.BlockSpec(memory_space=pltpu.VMEM)
SMEM = pl.BlockSpec(memory_space=pltpu.SMEM)
HBM = pl.BlockSpec(memory_space=pltpu.HBM)
PARAMS = pltpu.CompilerParams(vmem_limit_bytes=48 * 2**20)


def call(kernel, inputs, shapes, scratch=(), space=VMEM, micros=1):
    if space is HBM:
        inputs = inputs[:1] + tuple(
            pltpu.with_memory_space_constraint(x, pltpu.HBM) for x in inputs[1:]
        )
    return pl.pallas_call(
        kernel,
        out_shape=[jax.ShapeDtypeStruct(s, jnp.float32) for s in shapes],
        in_specs=[SMEM if x.dtype == jnp.int32 and x.ndim == 1 else space for x in inputs],
        out_specs=[VMEM] * len(shapes),
        scratch_shapes=list(scratch),
        compiler_params=PARAMS,
        cost_estimate=pl.CostEstimate(
            flops=0, bytes_accessed=int(3.6e6 * micros), transcendentals=0
        ),
    )(*inputs)


def body(primal_states, adjoint_last, porosity, solid_mask):
    nx, ny, nz = porosity.shape
    gx, gy, gz = [lax.axis_size(axis) for axis in AXES]
    x_first, x_second = swaps(gx)
    y_first, y_second = swaps(gy)
    z_first, z_second = swaps(gz)
    parity = jnp.stack([lax.axis_index(axis) & 1 for axis in AXES]).astype(jnp.int32)
    tiles = ny // 8
    height = (tiles + 1) * 8
    f32 = jnp.float32

    def diagonal(message, x_pairs, y_pairs):
        pairs = [(a * gy + c, b * gy + d) for a, b in x_pairs for c, d in y_pairs]
        return lax.ppermute(message, ("gx", "gy"), pairs)

    rows_x = NSLOT * ny + 8
    rows_y = 2 * y_rows(nx) + 8
    rows_c = 2 * CORNER + 8
    xa, xb, ub, drag = call(
        pack_x_kernel,
        (parity, primal_states, adjoint_last, porosity, solid_mask),
        [(rows_x, nz), (rows_x, nz), (4, nx, ny, nz), (8, nz)],
        [
            pltpu.VMEM((2, 19, nx, ny, nz), f32),
            pltpu.VMEM((19, nx, ny, nz), f32),
            pltpu.VMEM((nx, ny, nz), f32),
            pltpu.VMEM((nx, ny, nz), jnp.int32),
            pltpu.SemaphoreType.DMA((6,)),
        ],
        HBM,
    )
    y, ya, yb = call(
        pack_y_kernel,
        (parity, adjoint_last, ub, drag),
        [(rows_y, nz), (rows_c, nz), (rows_c, nz)],
        micros=4,
    )
    xb = lax.ppermute(xb, "gx", x_second)
    if gy == 2:
        y = lax.ppermute(y, "gy", y_first)
        yb = diagonal(yb, x_second, y_first)
        ya = diagonal(ya, x_first, y_first)
    else:

        def both(message, block, send):
            parts = [message[:block], message[block : 2 * block], message[2 * block :]]
            return jnp.concatenate(
                [send(parts[0], y_first), send(parts[1], y_second), parts[2]]
            )

        y = both(y, y_rows(nx), lambda m, pairs: lax.ppermute(m, "gy", pairs))
        yb = both(yb, CORNER, lambda m, pairs: diagonal(m, x_second, pairs))
        ya = both(ya, CORNER, lambda m, pairs: diagonal(m, x_first, pairs))
    xa = lax.ppermute(xa, "gx", x_first)

    f0, f1 = call(
        pack_state_kernel, (primal_states, ub), [(20, ny, nz), (19, ny, nz)]
    )
    drag, f1 = lax.optimization_barrier((drag, f1))

    read, zmsg, drags = call(
        pack_z_kernel,
        (parity, adjoint_last, ub, xa, xb, y, ya, yb, drag),
        [(NSLOT, nx + 2, height, nz), (4 * height + 24, nz), (24, nz)],
        [pltpu.VMEM((NSLOT, nx + 4, ny + 32, nz), f32)],
    )
    zb = lax.ppermute(zmsg, "gz", z_second)
    za = lax.ppermute(zmsg, "gz", z_first)
    inner, grad1, inner_grad, pack = call(
        inner_kernel,
        (primal_states, read),
        [(19, nx, ny, nz), (nx, ny, nz), (nx, ny, nz), (19, ny, nz)],
        [pltpu.VMEM((19, nx + 2, height + 8, nz), f32)],
        micros=4,
    )
    if (gx, gy, gz) == (4, 2, 4):
        across = lax.ppermute(drags, "gz", [(i, i ^ 2) for i in range(gz)])
        drags, grad1 = lax.optimization_barrier((drags, grad1))
        drags = (drags + across) + (za[4 * height :] + zb[4 * height :])
        fourth = lax.ppermute(drags[16:], "gx", x_first)
        drag = jnp.sum(drags[:8] + drags[8:16] + drags[16:] + fourth)
    else:
        drag = lax.psum(jnp.sum(drag), AXES)

    first, gradient = call(
        edge_kernel,
        (parity, solid_mask, zmsg, za, zb, pack, f0, f1, inner, grad1, inner_grad),
        [(19, nx, ny, nz), (nx, ny, nz)],
        [
            pltpu.VMEM((4 * height, nz), f32),
            pltpu.VMEM((4 * height, nz), f32),
            pltpu.VMEM((19, height + 8, nz), f32),
            pltpu.VMEM((21, ny, nz), f32),
        ],
    )
    return (first, gradient, drag / (nx * ny * nz * gx * gy * gz))


def solution(mesh):
    return jax.shard_map(
        body,
        mesh=mesh,
        in_specs=(
            P(None, None, "gx", "gy", "gz"),
            P(None, "gx", "gy", "gz"),
            P("gx", "gy", "gz"),
            P("gx", "gy", "gz"),
        ),
        out_specs=(P(None, "gx", "gy", "gz"), P("gx", "gy", "gz"), P()),
        check_vma=False,
    )
```

```python
import functools

import jax
import jax.numpy as jnp
import numpy as np
from jax import lax
from jax.experimental import pallas as pl
from jax.experimental.pallas import tpu as pltpu
from jax.sharding import PartitionSpec as P

VEL = (
    (0, 0, 0),
    (1, 0, 0),
    (-1, 0, 0),
    (0, 1, 0),
    (0, -1, 0),
    (0, 0, 1),
    (0, 0, -1),
    (1, 1, 0),
    (-1, -1, 0),
    (1, -1, 0),
    (-1, 1, 0),
    (1, 0, 1),
    (-1, 0, -1),
    (1, 0, -1),
    (-1, 0, 1),
    (0, 1, 1),
    (0, -1, -1),
    (0, 1, -1),
    (0, -1, 1),
)
PAIRS = tuple((i, i + 1) for i in range(1, 19, 2))
AXES = ("gx", "gy", "gz")
UB = (19, 20, 21, 22)


def near(axis, sign):
    return tuple(i for i in range(19) if VEL[i][axis] * sign >= 0) + UB


def far(axis, sign):
    return tuple(i for i in range(19) if VEL[i][axis] == sign)


NSLOT = 23
CORNER = 24
EDGE_ROWS = 8


def y_rows(nx):
    return -(-NSLOT * nx // 8) * 8


ZGROUPS = (
    tuple(i for i in range(19) if VEL[i][2] == -1),
    tuple(i for i in range(19) if VEL[i][2] == 1),
    tuple(i for i in range(19) if VEL[i][2] == 0)[:8],
    tuple(i for i in range(19) if VEL[i][2] == 0)[8:] + UB,
)
ZSLOT = {q: (g, k) for g, group in enumerate(ZGROUPS) for k, q in enumerate(group)}


def pairs_of(values):
    s = [values[a] + values[b] for a, b in PAIRS]
    d = [values[a] - values[b] for a, b in PAIRS]
    return s, d


def moments(v0, s, d):
    sx, sy, sz, sp, sq, sr, ss, st, su = s
    dx, dy, dz, dp, dq, dr, ds, dt, du = d
    ex = sp + sq
    ez = sr + ss
    ey = st + su
    faces = sx + sy + sz
    edges = ex + ez + ey
    exx = ex + ez
    eyy = ex + ey
    ezz = ez + ey
    fx = (dp + dq) + (dr + ds)
    fy = (dp - dq) + (dt + du)
    fz = (dr - ds) + (dt - du)
    return dict(
        rest=v0,
        faces=faces,
        edges=edges,
        total=v0 + faces + edges,
        face1=(dx, dy, dz),
        edge1=(fx, fy, fz),
        one=(dx + fx, dy + fy, dz + fz),
        face2=(sx, sy, sz),
        edge2=(exx, eyy, ezz),
        two=(sx + exx, sy + eyy, sz + ezz),
        cross=(sp - sq, sr - ss, st - su),
    )


def adjoint_cell(g, u, b, drive):
    s, d = pairs_of(g)
    m = moments(g[0], s, d)
    total = m["total"]
    trace = m["faces"] + 2.0 * m["edges"] - (30.0 / 19.0) * total
    p0 = (-1.2 / 19.0) * total - (2.0 / 21.0) * trace
    q = [
        (0.4 / 6.0) * (two - (10.0 / 19.0) * total) + (0.8 / 21.0) * trace
        for two in m["two"]
    ]
    qsum = q[0] + q[1] + q[2]
    qab = [0.1 * c for c in m["cross"]]
    p1 = [-0.12 * one for one in m["one"]]
    h0 = (
        0.4 * m["rest"]
        + (1.2 / 18.0) * m["faces"]
        + (1.2 / 36.0) * m["edges"]
        + p0
        + (1.0 / 3.0) * qsum
    )
    h1 = [
        (1.2 / 18.0) * f + (1.2 / 36.0) * e + (1.0 / 3.0) * p
        for f, e, p in zip(m["face1"], m["edge1"], p1)
    ]
    base = (1.0 / 3.0) * p0 + (1.0 / 9.0) * qsum
    haa = [
        (1.2 / 18.0) * f + (1.2 / 36.0) * e + (2.0 / 9.0) * qa + base
        for f, e, qa in zip(m["face2"], m["edge2"], q)
    ]
    hxy, hxz, hyz = [(2.0 / 45.0) * c for c in m["cross"]]
    ux, uy, uz = u
    v = (
        haa[0] * ux + hxy * uy + hxz * uz,
        hxy * ux + haa[1] * uy + hyz * uz,
        hxz * ux + hyz * uy + haa[2] * uz,
    )
    uv = ux * v[0] + uy * v[1] + uz * v[2]
    uu = ux * ux + uy * uy + uz * uz
    uuh = 1.5 * uu * h0
    a = h0 + uuh - 4.5 * uv
    nb = 1.0 - b
    e0 = nb * (a - p0)
    nq = [nb * x for x in q]
    nxy, nxz, nyz = [nb * x for x in qab]
    o = [
        nb * (3.0 * h1[k] + 9.0 * v[k] - 3.0 * u[k] * h0 - p1[k]) for k in range(3)
    ]
    o[0] = o[0] + b * drive
    alpha = -0.2 * nb
    half_s = 0.5 * (alpha + b)
    half_d = 0.5 * (alpha - b)
    exy = e0 - nq[0] - nq[1]
    exz = e0 - nq[0] - nq[2]
    eyz = e0 - nq[1] - nq[2]
    even = (
        e0 - nq[0],
        e0 - nq[1],
        e0 - nq[2],
        exy - nxy,
        exy + nxy,
        exz - nxz,
        exz + nxz,
        eyz - nyz,
        eyz + nyz,
    )
    odd = (
        o[0],
        o[1],
        o[2],
        o[0] + o[1],
        o[0] - o[1],
        o[0] + o[2],
        o[0] - o[2],
        o[1] + o[2],
        o[1] - o[2],
    )
    out = [(alpha + b) * g[0] + e0]
    for k in range(9):
        even_k = half_s * s[k] + even[k]
        odd_k = half_d * d[k] + odd[k]
        out.append(even_k + odd_k)
        out.append(even_k - odd_k)
    kept = dict(
        s=s, d=d, g0=g[0], p0=p0, p1=p1, q=q, qab=qab, h0=h0, h1=h1, uv=uv, uuh=uuh
    )
    return out, kept


def gradient_cell(kept, f0, fs, fd, fm, u):
    rho = fm["total"]
    even = fs[0] * kept["s"][0]
    odd = fd[0] * kept["d"][0]
    for k in range(1, 9):
        even = even + fs[k] * kept["s"][k]
        odd = odd + fd[k] * kept["d"][k]
    hf = kept["p0"] * rho
    for k in range(3):
        hf = hf + kept["p1"][k] * fm["one"][k] + kept["q"][k] * fm["two"][k]
        hf = hf + kept["qab"][k] * fm["cross"][k]
    uh1 = u[0] * kept["h1"][0] + u[1] * kept["h1"][1] + u[2] * kept["h1"][2]
    hfeq = rho * (kept["h0"] - kept["uuh"] + 3.0 * uh1 + 4.5 * kept["uv"])
    pairs = 1.2 * f0 * kept["g0"] + 0.6 * even - 0.4 * odd
    return pairs + hf - hfeq + fm["one"][0]


def state_of(ref, index):
    f = [ref[(index[0], i) + index[1:]] for i in range(19)]
    s, d = pairs_of(f)
    m = moments(f[0], s, d)
    inverse = 1.0 / m["total"]
    u = [one * inverse for one in m["one"]]
    return f[0], s, d, m, u


def corner_rows(sx, sy):
    rows = []
    for dx, dy in ((0, 0), (1, 0), (0, 1), (1, 1)):
        for i in near(0, sx) if dx == 0 else far(0, sx):
            if i in (near(1, sy) if dy == 0 else far(1, sy)):
                rows.append((i, dx, dy))
    return rows


def cell_rows(adj_ref, ub_ref, q, x, rows):
    return adj_ref[q, x, rows, :] if q < 19 else ub_ref[q - 19, x, rows, :]


def pack_x_kernel(
    par_ref,
    states_hbm,
    adj_hbm,
    por_hbm,
    mask_hbm,
    a_ref,
    b_ref,
    cols_ref,
    ub_ref,
    drag_ref,
    states_ref,
    adj_ref,
    por_ref,
    mask_ref,
    sems,
):
    nx, ny, nz = por_ref.shape
    tiles = ny // 8
    copies = [
        pltpu.make_async_copy(src, dst, sems.at[k])
        for k, (src, dst) in enumerate(
            (
                (adj_hbm, adj_ref),
                (states_hbm.at[1], states_ref.at[1]),
                (por_hbm, por_ref),
                (mask_hbm, mask_ref),
                (states_hbm.at[0, 1:3], states_ref.at[0, 1:3]),
                (states_hbm.at[0, 7:15], states_ref.at[0, 7:15]),
            )
        )
    ]
    for copy in copies:
        copy.start()
    copies[0].wait()

    pair = lax.broadcasted_iota(jnp.int32, (8, nz), 1) // 2

    def columns(acc, g, t, wanted):
        for k, q in enumerate(ZGROUPS[g]):
            if q not in wanted:
                continue
            cz = VEL[q][2] if q < 19 else 0
            for x in range(nx):
                start = 32 * (k // 2) + 4 * (x + 2) + 2 * (k % 2)
                value = cell_rows(adj_ref, ub_ref, q, x, slice(8 * t, 8 * t + 8))
                acc = jnp.where(pair == start // 2, turn(value, start + 1 - cz), acc)
        row = g * ny + 8 * t
        cols_ref[row : row + 8] = acc
        a_ref[NSLOT * ny + row : NSLOT * ny + row + 8] = acc

    for g in range(4):
        for t in range(tiles):
            columns(jnp.zeros((8, nz), jnp.float32), g, t, range(19))
    for copy in copies[1:]:
        copy.wait()

    def cells(x, carry):
        for t in range(tiles):
            rows = slice(8 * t, 8 * t + 8)
            blocking = jnp.where(mask_ref[x, rows, :] == 0, por_ref[x, rows, :], 1.0)
            f0, s, d, m, u = state_of(states_ref, (1, x, rows))
            flux = m["one"][0]
            for a, b in PAIRS:
                if VEL[a][0]:
                    flux = flux + (
                        states_ref[0, a, x, rows, :] - states_ref[0, b, x, rows, :]
                    )
            for k in range(3):
                ub_ref[k, x, rows, :] = u[k]
            ub_ref[3, x, rows, :] = blocking
            carry = carry + blocking * flux
        return carry

    drag = lax.fori_loop(0, nx, cells, jnp.zeros((8, nz), jnp.float32))
    drag_ref[...] = drag
    for t in range(tiles):
        row = 3 * ny + 8 * t
        columns(cols_ref[row : row + 8], 3, t, UB)
    cols_ref[4 * ny :] = drag
    a_ref[(NSLOT + 4) * ny :] = drag

    def fill_x(out_ref, sign):
        for names, offset, x in (
            (near(0, sign), 0, 0 if sign > 0 else nx - 1),
            (far(0, sign), 18, 1 if sign > 0 else nx - 2),
        ):
            for k, q in enumerate(names):
                k += offset
                out_ref[k * ny : (k + 1) * ny] = cell_rows(
                    adj_ref, ub_ref, q, x, slice(0, ny)
                )

    for px in (0, 1):

        @pl.when(par_ref[0] == px)
        def _():
            sa = 1 if px else -1
            fill_x(a_ref, sa)
            fill_x(b_ref, -sa)


def pack_y_kernel(par_ref, adj_ref, ub_ref, cols_ref, y_ref, ya_ref, yb_ref):
    nx, ny, nz = adj_ref.shape[1:]
    y_block = y_rows(nx) + EDGE_ROWS
    corner_block = CORNER + EDGE_ROWS

    def fill_edges(place, sign):
        for g in range(4):
            for d in range(2):
                y = d if sign > 0 else ny - 1 - d
                line = cols_ref[g * ny + y : g * ny + y + 1]
                row = place * y_block + y_rows(nx) + 2 * g + d
                y_ref[row : row + 1] = line
                row = place * corner_block + CORNER + 2 * g + d
                ya_ref[row : row + 1] = line
                yb_ref[row : row + 1] = line

    def fill_y(place, sign):
        for names, offset, y in (
            (near(1, sign), 0, 0 if sign > 0 else ny - 1),
            (far(1, sign), 18, 1 if sign > 0 else ny - 2),
        ):
            for k, q in enumerate(names):
                for x in range(nx):
                    row = place * y_block + (k + offset) * nx + x
                    y_ref[row : row + 1] = cell_rows(
                        adj_ref, ub_ref, q, x, slice(y, y + 1)
                    )

    def fill_corner(out_ref, place, sx, sy):
        names = corner_rows(sx, sy)
        for k, (q, dx, dy) in enumerate(names):
            x = dx if sx > 0 else nx - 1 - dx
            y = dy if sy > 0 else ny - 1 - dy
            row = place * corner_block + k
            out_ref[row : row + 1] = cell_rows(adj_ref, ub_ref, q, x, slice(y, y + 1))
        row = place * corner_block + len(names)
        last = place * corner_block + CORNER
        out_ref[row:last] = jnp.zeros((last - row, nz), jnp.float32)

    drag = cols_ref[4 * ny :]
    y_ref[2 * y_block :] = drag
    ya_ref[2 * corner_block :] = drag
    yb_ref[2 * corner_block :] = drag
    for py in (0, 1):

        @pl.when(par_ref[1] == py)
        def _():
            s0 = 1 if py else -1
            fill_y(0, s0)
            fill_y(1, -s0)
            fill_edges(0, s0)
            fill_edges(1, -s0)

    for px in (0, 1):
        for py in (0, 1):

            @pl.when((par_ref[0] == px) & (par_ref[1] == py))
            def _():
                sa = 1 if px else -1
                s0 = 1 if py else -1
                for out_ref, sx in ((ya_ref, sa), (yb_ref, -sa)):
                    fill_corner(out_ref, 0, sx, s0)
                    fill_corner(out_ref, 1, sx, -s0)


def pack_z_kernel(
    par_ref,
    cols_ref,
    xa_ref,
    xc_ref,
    y_ref,
    ya_ref,
    yb_ref,
    zown_ref,
    za_ref,
    zb_ref,
    drag_ref,
    ext,
):
    ny = (cols_ref.shape[0] - 8) // 4
    nz = cols_ref.shape[1]
    tiles = ny // 8
    base = 16
    even_x = par_ref[0] == 0
    even_y = par_ref[1] == 0
    lane = lax.broadcasted_iota(jnp.int32, (8, nz), 1)
    sub = lax.broadcasted_iota(jnp.int32, (8, nz), 0)
    plane = (lane % 32) // 4
    slot = 2 * (lane // 32) + (lane % 4) // 2

    def along_x(own, va, vb):
        low = turn(jnp.where(even_x, vb, va), -16)
        high = turn(jnp.where(even_x, va, vb), 16)
        return jnp.where(plane < 2, low, jnp.where(plane > 5, high, own))

    offset = xa_ref.shape[0] - 8 - 4 * ny
    for g in range(4):
        for t in range(tiles):
            row = g * ny + 8 * t
            ext[g, base + 8 * t : base + 8 * t + 8, :] = along_x(
                cols_ref[row : row + 8],
                xa_ref[offset + row : offset + row + 8],
                xc_ref[row : row + 8],
            )
    y_block = (y_ref.shape[0] - 8) // 2
    corner_block = CORNER + EDGE_ROWS

    def edges(ref, block, place):
        return ref[(place + 1) * block - EDGE_ROWS : (place + 1) * block]

    first, second = [
        along_x(
            edges(y_ref, y_block, place),
            edges(ya_ref, corner_block, place),
            edges(yb_ref, corner_block, place),
        )
        for place in range(2)
    ]
    high = jnp.where(even_y, first, second)
    low = jnp.where(even_y, second, first)
    for g in range(4):
        for d in range(2):
            row = 2 * g + d
            ext[g, base + ny + d : base + ny + d + 1, :] = high[row : row + 1]
            ext[g, base - 1 - d : base - d, :] = low[row : row + 1]

    packed = []
    for g, group in enumerate(ZGROUPS):
        moves = {}
        for k, q in enumerate(group):
            cx, cy, _ = VEL[q] if q < 19 else (0, 0, 0)
            moves.setdefault((cx, cy), []).append(k)
        acc = [jnp.zeros((8, nz), jnp.float32) for t in range(tiles + 1)]
        for (cx, cy), slots in moves.items():
            mask = slot == slots[0]
            for k in slots[1:]:
                mask = mask | (slot == k)
            for t in range(tiles + 1):
                if t < tiles:
                    row = base + 8 * t + cy
                    value = ext[g, row : row + 8, :]
                else:
                    above = base + ny + cy
                    below = base - 8 + cy
                    value = jnp.where(
                        sub < 4, ext[g, above : above + 8, :], ext[g, below : below + 8, :]
                    )
                acc[t] = jnp.where(mask, turn(value, -4 * cx), acc[t])
        packed.append(acc)
        for t in range(tiles + 1):
            row = (g * (tiles + 1) + t) * 8
            zown_ref[row : row + 8, :] = acc[t]
    up_first = par_ref[2] == 0
    even_lane = lane % 2 == 0
    for t in range(tiles + 1):
        two, three = packed[2][t], packed[3][t]
        up = (packed[0][t], jnp.where(even_lane, two, pltpu.roll(three, 1, 1)))
        down = (packed[1][t], jnp.where(even_lane, pltpu.roll(two, nz - 1, 1), three))
        for g in range(2):
            row = (g * (tiles + 1) + t) * 8
            za_ref[row : row + 8, :] = jnp.where(up_first, up[g], down[g])
            zb_ref[row : row + 8, :] = jnp.where(up_first, down[g], up[g])
    drag = cols_ref[4 * ny :] + y_ref[2 * y_block :]
    for x_ref, c_ref in ((xa_ref, ya_ref), (xc_ref, yb_ref)):
        drag = drag + (x_ref[x_ref.shape[0] - 8 :] + c_ref[2 * corner_block :])
    drag_ref[...] = drag


OUT_GROUPS = ((0, 7), (7, 13), (13, 17), (17, 19))


def turn(value, shift):
    nz = value.shape[1]
    return pltpu.roll(value, shift % nz, 1) if shift % nz else value


def z_shifted(value, cz):
    return turn(value, -cz) if cz else value


def inner_kernel(
    par_ref,
    states_ref,
    adj_ref,
    ub_ref,
    xa_ref,
    xb_ref,
    y_ref,
    ya_ref,
    yb_ref,
    out_ref,
    grad1_ref,
    grad_ref,
    pack_ref,
    f0_ref,
    f1_ref,
    ext,
    mid,
):
    nx, ny, nz = grad_ref.shape
    tiles = ny // 8
    lane = lax.broadcasted_iota(jnp.int32, (8, nz), 1)
    slot = lane // 4
    sub = lax.broadcasted_iota(jnp.int32, (8, nz), 0)
    even_x = par_ref[0] == 0
    even_y = par_ref[1] == 0
    base = 16

    for q in range(NSLOT):
        for x in range(nx):
            ext[q, x + 2, base : base + ny, :] = (
                adj_ref[q, x] if q < 19 else ub_ref[q - 19, x]
            )
    planes = {1: (nx + 2, nx + 3), -1: (1, 0)}
    lines = {1: (base + ny, base + ny + 1), -1: (base - 1, base - 2)}
    for sign in (1, -1):
        first, second = (xa_ref, xb_ref) if sign > 0 else (xb_ref, xa_ref)
        for names, depth, offset in ((near(0, sign), 0, 0), (far(0, sign), 1, 18)):
            for k, q in enumerate(names):
                rows = slice((k + offset) * ny, (k + offset + 1) * ny)
                ext[q, planes[sign][depth], base : base + ny, :] = jnp.where(
                    even_x, first[rows], second[rows]
                )
        block = y_rows(nx) + EDGE_ROWS
        first, second = (0, block) if sign > 0 else (block, 0)
        for names, depth, offset in ((near(1, sign), 0, 0), (far(1, sign), 1, 18)):
            line = lines[sign][depth]
            for k, q in enumerate(names):
                row = (k + offset) * nx
                got = jnp.where(
                    even_y,
                    y_ref[first + row : first + row + nx],
                    y_ref[second + row : second + row + nx],
                )
                for x in range(nx):
                    ext[q, x + 2, line : line + 1, :] = got[x : x + 1]
        for sx in (1, -1):
            xs = (ya_ref, yb_ref) if sx > 0 else (yb_ref, ya_ref)
            block = CORNER + EDGE_ROWS
            ys = (0, block) if sign > 0 else (block, 0)
            low, high = [
                jnp.where(even_x, xs[0][r : r + CORNER], xs[1][r : r + CORNER])
                for r in ys
            ]
            got = jnp.where(even_y, low, high)
            for k, (q, dx, dy) in enumerate(corner_rows(sx, sign)):
                line = lines[sign][dy]
                ext[q, planes[sx][dx], line : line + 1, :] = got[k : k + 1]

    def near_cells(q, plane, t, cy):
        if t < tiles:
            row = base + 8 * t + cy
            return ext[q, plane, row : row + 8, :]
        above = base + ny + cy
        below = base - 8 + cy
        return jnp.where(
            sub < 4, ext[q, plane, above : above + 8, :], ext[q, plane, below : below + 8, :]
        )

    def first_level(p, t, kinds):
        got = []
        for i in range(19):
            cx, cy, cz = VEL[i]
            got.append(z_shifted(near_cells(i, p + 1 + cx, t, cy), cz))
        ub = [near_cells(19 + k, p + 1, t, 0) for k in range(4)]
        out, kept = adjoint_cell(got, ub[:3], ub[3], 1.0)
        for i in kinds:
            if t < tiles:
                mid[i, p, t * 8 + 8 : t * 8 + 16, :] = out[i]
            elif VEL[i][1] > 0:
                mid[i, p, t * 8 + 8 : t * 8 + 16, :] = out[i]
            elif VEL[i][1] < 0:
                mid[i, p, 0:8, :] = out[i]
        return kept, ub[:3]

    def inside(x, carry):
        for t in range(tiles):
            kept, u = first_level(x + 1, t, range(19))
            rows = slice(t * 8, t * 8 + 8)
            f0, fs, fd, fm, _ = state_of(states_ref, (1, x, rows))
            grad1_ref[x, rows, :] = gradient_cell(kept, f0, fs, fd, fm, u)
        return carry

    lax.fori_loop(0, nx, inside, 0)
    for t in range(tiles):
        first_level(0, t, far(0, -1))
        first_level(nx + 1, t, far(0, 1))

    def rim(n, carry):
        for p in (2 * n, 2 * n + 1):
            first_level(p, tiles, far(1, -1) + far(1, 1))
        return carry

    lax.fori_loop(0, (nx + 2) // 2, rim, 0)

    def second_level(x, carry):
        for t in range(tiles):
            rows = slice(t * 8, t * 8 + 8)
            got = []
            for i in range(19):
                cx, cy, cz = VEL[i]
                low = 8 + 8 * t + cy
                value = z_shifted(mid[i, x + 1 + cx, low : low + 8, :], cz)
                got.append(value)
                pack_ref[i, rows, :] = jnp.where(
                    slot == x, pltpu.roll(value, 4 * x + 2, 1), pack_ref[i, rows, :]
                )
            f0, fs, fd, fm, u = state_of(states_ref, (0, x, rows))
            b = ub_ref[3, x, rows, :]
            out, kept = adjoint_cell(got, u, b, 1.0)
            for i in range(19):
                out_ref[i, x, rows, :] = out[i]
            grad_ref[x, rows, :] = grad1_ref[x, rows, :] + gradient_cell(
                kept, f0, fs, fd, fm, u
            )
        return carry

    lax.fori_loop(0, nx, second_level, 0)

    def tile(t, carry):
        rows = pl.ds(pl.multiple_of(t * 8, 8), 8)
        for i in range(20):
            for out_ref, level, first in ((f0_ref, 0, 0), (f1_ref, 1, 2)):
                if i == 19 and level == 1:
                    continue
                acc = jnp.zeros((8, nz), jnp.float32)
                for x in range(nx):
                    value = (
                        states_ref[level, i, x, rows, :]
                        if i < 19
                        else ub_ref[3, x, rows, :]
                    )
                    p = x + first
                    acc = jnp.where(slot == p, pltpu.roll(value, 4 * p + 2, 1), acc)
                out_ref[i, rows, :] = acc
        return carry

    lax.fori_loop(0, ny // 8, tile, 0)


def edge_kernel(
    par_ref,
    mask_ref,
    zown_ref,
    za_ref,
    zb_ref,
    pack_ref,
    f0_ref,
    f1_ref,
    inner_ref,
    grad1_ref,
    inner_grad_ref,
    out_hbm,
    grad_hbm,
    tail_ref,
    first_ref,
    second_ref,
    zmid,
    zout,
    out_ref,
    grad_ref,
    sems,
):
    nx, ny, nz = mask_ref.shape
    tiles = ny // 8
    height = (tiles + 1) * 8
    even = par_ref[2] == 0
    lane = lax.broadcasted_iota(jnp.int32, (8, nz), 1)
    even_lane = lane % 2 == 0
    low_pair = lane % 4 < 2

    last = slice(2 * height, 2 * height + 8)
    tail_ref[...] = za_ref[last] + zb_ref[last]

    def swapped(value):
        return jnp.where(even_lane, turn(value, -1), turn(value, 1))

    for t in range(tiles + 1):
        received = []
        for g in range(2):
            row = (g * (tiles + 1) + t) * 8
            va = za_ref[row : row + 8, :]
            vb = zb_ref[row : row + 8, :]
            received.append((jnp.where(even, va, vb), jnp.where(even, vb, va)))
        (high0, low0), (high1, low1) = received
        for g in range(4):
            row = (g * (tiles + 1) + t) * 8
            rows = slice(row, row + 8)
            own = zown_ref[rows]
            if g == 0:
                head, tail = own, low0
            elif g == 1:
                head, tail = high0, own
            elif g == 2:
                head = jnp.where(even_lane, own, turn(high1, 1))
                tail = jnp.where(even_lane, low1, own)
            else:
                head = jnp.where(even_lane, own, high1)
                tail = jnp.where(even_lane, turn(low1, -1), own)
            head = swapped(head)
            tail = swapped(tail)
            first_ref[rows] = jnp.where(low_pair, head, turn(tail, 2))
            second_ref[rows] = jnp.where(low_pair, turn(head, -2), tail)

    slab_grad = []
    for t in range(tiles + 1):
        got = []
        for q in range(NSLOT):
            g, k = ZSLOT[q]
            row = g * height + t * 8
            ref = second_ref if k % 2 else first_ref
            got.append(turn(ref[row : row + 8, :], -32 * (k // 2)))
        out, kept = adjoint_cell(got[:19], got[19:22], got[22], 1.0)
        for i in range(19):
            zmid[i, 8 * t + 8 : 8 * t + 16, :] = out[i]
            if t == tiles:
                zmid[i, 0:8, :] = out[i]
        if t < tiles:
            f = [f1_ref[i, 8 * t : 8 * t + 8, :] for i in range(19)]
            fs, fd = pairs_of(f)
            fm = moments(f[0], fs, fd)
            grad = gradient_cell(kept, f[0], fs, fd, fm, got[19:22])
            slab_grad.append(turn(grad, -8))

    at = lane % 4
    for t in range(tiles):
        rows = slice(8 * t, 8 * t + 8)
        got = []
        for i in range(19):
            cx, cy, cz = VEL[i]
            value = pack_ref[i, rows, :]
            edge = zmid[i, 8 + 8 * t + cy : 16 + 8 * t + cy, :]
            back = -4 * (2 + cx)
            if cz == 0:
                value = jnp.where((at == 1) | (at == 2), turn(edge, back), value)
            else:
                near_lane = 2 if cz < 0 else 0
                value = jnp.where(at == near_lane, turn(edge, back - 1), value)
                value = jnp.where(at == near_lane + 1, turn(edge, back + 1), value)
            got.append(value)
        f = [f0_ref[i, rows, :] for i in range(19)]
        fs, fd = pairs_of(f)
        fm = moments(f[0], fs, fd)
        inverse = 1.0 / fm["total"]
        u = [one * inverse for one in fm["one"]]
        out, kept = adjoint_cell(got, u, f0_ref[19, rows, :], 1.0)
        for i in range(19):
            zout[i, rows, :] = out[i]
        zout[19, rows, :] = gradient_cell(kept, f[0], fs, fd, fm, u)
        zout[20, rows, :] = slab_grad[t]

    def out_copy(k):
        part = slice(*OUT_GROUPS[k])
        return pltpu.make_async_copy(out_ref.at[part], out_hbm.at[part], sems.at[k])

    outer = (lane < 2) | (lane >= nz - 2)
    ends = (lane < 1) | (lane >= nz - 1)
    for x in range(nx):
        for t in range(tiles):
            rows = slice(8 * t, 8 * t + 8)
            level1 = jnp.where(
                ends, turn(zout[20, rows, :], -2 - 4 * x), grad1_ref[x, rows, :]
            )
            edge = turn(zout[19, rows, :], -2 - 4 * x) + level1
            grad = jnp.where(outer, edge, inner_grad_ref[x, rows, :])
            grad_ref[x, rows, :] = jnp.where(mask_ref[x, rows, :] == 0, grad, 0.0)
    grad_copy = pltpu.make_async_copy(grad_ref, grad_hbm, sems.at[len(OUT_GROUPS)])
    grad_copy.start()
    for k, group in enumerate(OUT_GROUPS):
        for i in range(*group):
            for x in range(nx):
                for t in range(tiles):
                    rows = slice(8 * t, 8 * t + 8)
                    out_ref[i, x, rows, :] = jnp.where(
                        outer,
                        turn(zout[i, rows, :], -2 - 4 * x),
                        inner_ref[i, x, rows, :],
                    )
        out_copy(k).start()
    grad_copy.wait()
    for k in range(len(OUT_GROUPS)):
        out_copy(k).wait()


def drag_kernel(whole_cells, *refs):
    total = refs[0][...]
    for ref in refs[1:-1]:
        total = total + ref[...]
    summed = jnp.sum(jnp.sum(total, axis=1, keepdims=True), axis=0, keepdims=True)
    refs[-1][...] = summed / whole_cells


def swaps(count):
    first = [(i, i ^ 1) for i in range(count)]
    second = [(i, (((i + 1) % count) ^ 1) - 1) for i in range(count)]
    second = [(i, j % count) for i, j in second]
    return first, second


VMEM = pl.BlockSpec(memory_space=pltpu.VMEM)
SMEM = pl.BlockSpec(memory_space=pltpu.SMEM)
HBM = pl.BlockSpec(memory_space=pltpu.HBM)
PARAMS = pltpu.CompilerParams(vmem_limit_bytes=48 * 2**20)


def call(kernel, inputs, shapes, scratch=(), space=VMEM, micros=1, outs=None):
    if space is HBM:
        inputs = inputs[:1] + tuple(
            pltpu.with_memory_space_constraint(x, pltpu.HBM) for x in inputs[1:]
        )
    return pl.pallas_call(
        kernel,
        out_shape=[jax.ShapeDtypeStruct(s, jnp.float32) for s in shapes],
        in_specs=[SMEM if x.dtype == jnp.int32 and x.ndim == 1 else space for x in inputs],
        out_specs=outs or [VMEM] * len(shapes),
        scratch_shapes=list(scratch),
        compiler_params=PARAMS,
        cost_estimate=pl.CostEstimate(
            flops=0, bytes_accessed=int(3.6e6 * micros), transcendentals=0
        ),
    )(*inputs)


def body(primal_states, adjoint_last, porosity, solid_mask):
    nx, ny, nz = porosity.shape
    gx, gy, gz = [lax.axis_size(axis) for axis in AXES]
    x_first, x_second = swaps(gx)
    y_first, y_second = swaps(gy)
    z_first, z_second = swaps(gz)
    parity = jnp.stack([lax.axis_index(axis) & 1 for axis in AXES]).astype(jnp.int32)
    tiles = ny // 8
    height = (tiles + 1) * 8
    f32 = jnp.float32

    def diagonal(message, x_pairs, y_pairs):
        pairs = [(a * gy + c, b * gy + d) for a, b in x_pairs for c, d in y_pairs]
        return lax.ppermute(message, ("gx", "gy"), pairs)

    rows_x = NSLOT * ny
    rows_y = 2 * (y_rows(nx) + EDGE_ROWS) + 8
    rows_c = 2 * (CORNER + EDGE_ROWS) + 8
    rows_z = 2 * height + 8
    rides = (gx, gy, gz) == (4, 2, 4)
    xa, xb, cols, ub, drag = call(
        pack_x_kernel,
        (parity, primal_states, adjoint_last, porosity, solid_mask),
        [
            (rows_x + 4 * ny + 8, nz),
            (rows_x, nz),
            (4 * ny + 8, nz),
            (4, nx, ny, nz),
            (8, nz),
        ],
        [
            pltpu.VMEM((2, 19, nx, ny, nz), f32),
            pltpu.VMEM((19, nx, ny, nz), f32),
            pltpu.VMEM((nx, ny, nz), f32),
            pltpu.VMEM((nx, ny, nz), jnp.int32),
            pltpu.SemaphoreType.DMA((6,)),
        ],
        HBM,
    )
    y, ya, yb = call(
        pack_y_kernel,
        (parity, adjoint_last, ub, cols),
        [(rows_y, nz), (rows_c, nz), (rows_c, nz)],
        micros=4,
    )
    xc = lax.ppermute(cols, "gx", x_second)
    xa = lax.ppermute(xa, "gx", x_first)
    if gy == 2:
        y = lax.ppermute(y, "gy", y_first)
        yb = diagonal(yb, x_second, y_first)
        ya = diagonal(ya, x_first, y_first)
    else:

        def both(message, block, send):
            parts = [message[:block], message[block : 2 * block], message[2 * block :]]
            return jnp.concatenate(
                [send(parts[0], y_first), send(parts[1], y_second), parts[2]]
            )

        block = y_rows(nx) + EDGE_ROWS
        y = both(y, block, lambda m, pairs: lax.ppermute(m, "gy", pairs))
        block = CORNER + EDGE_ROWS
        yb = both(yb, block, lambda m, pairs: diagonal(m, x_second, pairs))
        ya = both(ya, block, lambda m, pairs: diagonal(m, x_first, pairs))
    xb, xa = lax.optimization_barrier((xb, xa))
    xb = lax.ppermute(xb, "gx", x_second)

    zown, za, zb, drag_xy = call(
        pack_z_kernel,
        (parity, cols, xa, xc, y, ya, yb),
        [(4 * height, nz), (rows_z, nz), (rows_z, nz), (8, nz)],
        [pltpu.VMEM((4, ny + 32, nz), f32)],
    )
    if rides:
        second = xc[4 * ny :] + yb[rows_c - 8 :]
        drag_xy = drag_xy + lax.ppermute(second, "gx", x_first)
        za = za.at[2 * height :].set(drag_xy)
        zb = zb.at[2 * height :].set(drag_xy)
    zb = lax.ppermute(zb, "gz", z_second)
    za = lax.ppermute(za, "gz", z_first)
    inner, grad1, inner_grad, pack, f0, f1 = call(
        inner_kernel,
        (parity, primal_states, adjoint_last, ub, xa, xb, y, ya, yb),
        [
            (19, nx, ny, nz),
            (nx, ny, nz),
            (nx, ny, nz),
            (19, ny, nz),
            (20, ny, nz),
            (19, ny, nz),
        ],
        [
            pltpu.VMEM((NSLOT, nx + 4, ny + 32, nz), f32),
            pltpu.VMEM((19, nx + 2, height + 8, nz), f32),
        ],
        micros=4,
    )
    if rides:
        zhalf = lax.ppermute(drag_xy, "gz", [(i, i ^ 2) for i in range(gz)])
        drags = (drag_xy, zhalf)
    else:
        drags = (lax.psum(drag, AXES),)

    first, gradient, tails = call(
        edge_kernel,
        (parity, solid_mask, zown, za, zb, pack, f0, f1, inner, grad1, inner_grad),
        [(19, nx, ny, nz), (nx, ny, nz), (8, nz)],
        [
            pltpu.VMEM((4 * height, nz), f32),
            pltpu.VMEM((4 * height, nz), f32),
            pltpu.VMEM((19, height + 8, nz), f32),
            pltpu.VMEM((21, ny, nz), f32),
            pltpu.VMEM((19, nx, ny, nz), f32),
            pltpu.VMEM((nx, ny, nz), f32),
            pltpu.SemaphoreType.DMA((len(OUT_GROUPS) + 1,)),
        ],
        outs=[HBM, HBM, VMEM],
    )
    if rides:
        drags += (tails,)
    whole_cells = float(nx * ny * nz * gx * gy * gz)
    (drag,) = call(functools.partial(drag_kernel, whole_cells), drags, [(1, 1)])
    return (first, gradient, drag.reshape(()))


def solution(mesh):
    return jax.shard_map(
        body,
        mesh=mesh,
        in_specs=(
            P(None, None, "gx", "gy", "gz"),
            P(None, "gx", "gy", "gz"),
            P("gx", "gy", "gz"),
            P("gx", "gy", "gz"),
        ),
        out_specs=(P(None, "gx", "gy", "gz"), P("gx", "gy", "gz"), P()),
        check_vma=False,
    )
```

```python
import functools

import jax
import jax.numpy as jnp
import numpy as np
from jax import lax
from jax.experimental import pallas as pl
from jax.experimental.pallas import tpu as pltpu
from jax.sharding import PartitionSpec as P

VEL = (
    (0, 0, 0),
    (1, 0, 0),
    (-1, 0, 0),
    (0, 1, 0),
    (0, -1, 0),
    (0, 0, 1),
    (0, 0, -1),
    (1, 1, 0),
    (-1, -1, 0),
    (1, -1, 0),
    (-1, 1, 0),
    (1, 0, 1),
    (-1, 0, -1),
    (1, 0, -1),
    (-1, 0, 1),
    (0, 1, 1),
    (0, -1, -1),
    (0, 1, -1),
    (0, -1, 1),
)
PAIRS = tuple((i, i + 1) for i in range(1, 19, 2))
AXES = ("gx", "gy", "gz")
UB = (19, 20, 21, 22)


def near(axis, sign):
    return tuple(i for i in range(19) if VEL[i][axis] * sign >= 0) + UB


def far(axis, sign):
    return tuple(i for i in range(19) if VEL[i][axis] == sign)


NSLOT = 23
CORNER = 24
EDGE_ROWS = 8


def y_rows(nx):
    return -(-NSLOT * nx // 8) * 8


ZGROUPS = (
    tuple(i for i in range(19) if VEL[i][2] == -1),
    tuple(i for i in range(19) if VEL[i][2] == 1),
    tuple(i for i in range(19) if VEL[i][2] == 0)[:8],
    tuple(i for i in range(19) if VEL[i][2] == 0)[8:] + UB,
)
ZSLOT = {q: (g, k) for g, group in enumerate(ZGROUPS) for k, q in enumerate(group)}


def pairs_of(values):
    s = [values[a] + values[b] for a, b in PAIRS]
    d = [values[a] - values[b] for a, b in PAIRS]
    return s, d


def moments(v0, s, d):
    sx, sy, sz, sp, sq, sr, ss, st, su = s
    dx, dy, dz, dp, dq, dr, ds, dt, du = d
    ex = sp + sq
    ez = sr + ss
    ey = st + su
    faces = sx + sy + sz
    edges = ex + ez + ey
    exx = ex + ez
    eyy = ex + ey
    ezz = ez + ey
    fx = (dp + dq) + (dr + ds)
    fy = (dp - dq) + (dt + du)
    fz = (dr - ds) + (dt - du)
    return dict(
        rest=v0,
        faces=faces,
        edges=edges,
        total=v0 + faces + edges,
        face1=(dx, dy, dz),
        edge1=(fx, fy, fz),
        one=(dx + fx, dy + fy, dz + fz),
        face2=(sx, sy, sz),
        edge2=(exx, eyy, ezz),
        two=(sx + exx, sy + eyy, sz + ezz),
        cross=(sp - sq, sr - ss, st - su),
    )


def adjoint_cell(g, u, b, drive):
    s, d = pairs_of(g)
    m = moments(g[0], s, d)
    total = m["total"]
    trace = m["faces"] + 2.0 * m["edges"] - (30.0 / 19.0) * total
    p0 = (-1.2 / 19.0) * total - (2.0 / 21.0) * trace
    q = [
        (0.4 / 6.0) * (two - (10.0 / 19.0) * total) + (0.8 / 21.0) * trace
        for two in m["two"]
    ]
    qsum = q[0] + q[1] + q[2]
    qab = [0.1 * c for c in m["cross"]]
    p1 = [-0.12 * one for one in m["one"]]
    h0 = (
        0.4 * m["rest"]
        + (1.2 / 18.0) * m["faces"]
        + (1.2 / 36.0) * m["edges"]
        + p0
        + (1.0 / 3.0) * qsum
    )
    h1 = [
        (1.2 / 18.0) * f + (1.2 / 36.0) * e + (1.0 / 3.0) * p
        for f, e, p in zip(m["face1"], m["edge1"], p1)
    ]
    base = (1.0 / 3.0) * p0 + (1.0 / 9.0) * qsum
    haa = [
        (1.2 / 18.0) * f + (1.2 / 36.0) * e + (2.0 / 9.0) * qa + base
        for f, e, qa in zip(m["face2"], m["edge2"], q)
    ]
    hxy, hxz, hyz = [(2.0 / 45.0) * c for c in m["cross"]]
    ux, uy, uz = u
    v = (
        haa[0] * ux + hxy * uy + hxz * uz,
        hxy * ux + haa[1] * uy + hyz * uz,
        hxz * ux + hyz * uy + haa[2] * uz,
    )
    uv = ux * v[0] + uy * v[1] + uz * v[2]
    uu = ux * ux + uy * uy + uz * uz
    uuh = 1.5 * uu * h0
    a = h0 + uuh - 4.5 * uv
    nb = 1.0 - b
    e0 = nb * (a - p0)
    nq = [nb * x for x in q]
    nxy, nxz, nyz = [nb * x for x in qab]
    o = [
        nb * (3.0 * h1[k] + 9.0 * v[k] - 3.0 * u[k] * h0 - p1[k]) for k in range(3)
    ]
    o[0] = o[0] + b * drive
    alpha = -0.2 * nb
    half_s = 0.5 * (alpha + b)
    half_d = 0.5 * (alpha - b)
    exy = e0 - nq[0] - nq[1]
    exz = e0 - nq[0] - nq[2]
    eyz = e0 - nq[1] - nq[2]
    even = (
        e0 - nq[0],
        e0 - nq[1],
        e0 - nq[2],
        exy - nxy,
        exy + nxy,
        exz - nxz,
        exz + nxz,
        eyz - nyz,
        eyz + nyz,
    )
    odd = (
        o[0],
        o[1],
        o[2],
        o[0] + o[1],
        o[0] - o[1],
        o[0] + o[2],
        o[0] - o[2],
        o[1] + o[2],
        o[1] - o[2],
    )
    out = [(alpha + b) * g[0] + e0]
    for k in range(9):
        even_k = half_s * s[k] + even[k]
        odd_k = half_d * d[k] + odd[k]
        out.append(even_k + odd_k)
        out.append(even_k - odd_k)
    kept = dict(
        s=s, d=d, g0=g[0], p0=p0, p1=p1, q=q, qab=qab, h0=h0, h1=h1, uv=uv, uuh=uuh
    )
    return out, kept


def gradient_cell(kept, f0, fs, fd, fm, u):
    rho = fm["total"]
    even = fs[0] * kept["s"][0]
    odd = fd[0] * kept["d"][0]
    for k in range(1, 9):
        even = even + fs[k] * kept["s"][k]
        odd = odd + fd[k] * kept["d"][k]
    hf = kept["p0"] * rho
    for k in range(3):
        hf = hf + kept["p1"][k] * fm["one"][k] + kept["q"][k] * fm["two"][k]
        hf = hf + kept["qab"][k] * fm["cross"][k]
    uh1 = u[0] * kept["h1"][0] + u[1] * kept["h1"][1] + u[2] * kept["h1"][2]
    hfeq = rho * (kept["h0"] - kept["uuh"] + 3.0 * uh1 + 4.5 * kept["uv"])
    pairs = 1.2 * f0 * kept["g0"] + 0.6 * even - 0.4 * odd
    return pairs + hf - hfeq + fm["one"][0]


def state_of(ref, index):
    f = [ref[(index[0], i) + index[1:]] for i in range(19)]
    s, d = pairs_of(f)
    m = moments(f[0], s, d)
    inverse = 1.0 / m["total"]
    u = [one * inverse for one in m["one"]]
    return f[0], s, d, m, u


def corner_rows(sx, sy):
    rows = []
    for dx, dy in ((0, 0), (1, 0), (0, 1), (1, 1)):
        for i in near(0, sx) if dx == 0 else far(0, sx):
            if i in (near(1, sy) if dy == 0 else far(1, sy)):
                rows.append((i, dx, dy))
    return rows


def cell_rows(adj_ref, ub_ref, q, x, rows):
    return adj_ref[q, x, rows, :] if q < 19 else ub_ref[q - 19, x, rows, :]


def pack_x_kernel(
    par_ref,
    states_hbm,
    adj_hbm,
    por_hbm,
    mask_hbm,
    a_ref,
    b_ref,
    ub_ref,
    drag_ref,
    states_ref,
    adj_ref,
    por_ref,
    mask_ref,
    sems,
):
    nx, ny, nz = por_ref.shape
    tiles = ny // 8
    copies = [
        pltpu.make_async_copy(src, dst, sems.at[k])
        for k, (src, dst) in enumerate(
            (
                (states_hbm.at[1], states_ref.at[1]),
                (por_hbm, por_ref),
                (mask_hbm, mask_ref),
                (states_hbm.at[0, 1:3], states_ref.at[0, 1:3]),
                (states_hbm.at[0, 7:15], states_ref.at[0, 7:15]),
                (adj_hbm, adj_ref),
            )
        )
    ]
    for copy in copies:
        copy.start()
    for copy in copies[:5]:
        copy.wait()

    def cells(x, carry):
        for t in range(tiles):
            rows = slice(8 * t, 8 * t + 8)
            blocking = jnp.where(mask_ref[x, rows, :] == 0, por_ref[x, rows, :], 1.0)
            f0, s, d, m, u = state_of(states_ref, (1, x, rows))
            flux = m["one"][0]
            for a, b in PAIRS:
                if VEL[a][0]:
                    flux = flux + (
                        states_ref[0, a, x, rows, :] - states_ref[0, b, x, rows, :]
                    )
            for k in range(3):
                ub_ref[k, x, rows, :] = u[k]
            ub_ref[3, x, rows, :] = blocking
            carry = carry + blocking * flux
        return carry

    drag = lax.fori_loop(0, nx, cells, jnp.zeros((8, nz), jnp.float32))
    drag_ref[...] = drag
    a_ref[NSLOT * ny :] = drag
    b_ref[NSLOT * ny :] = drag
    copies[5].wait()

    def fill_x(out_ref, sign):
        for names, offset, x in (
            (near(0, sign), 0, 0 if sign > 0 else nx - 1),
            (far(0, sign), 18, 1 if sign > 0 else nx - 2),
        ):
            for k, q in enumerate(names):
                k += offset
                out_ref[k * ny : (k + 1) * ny] = cell_rows(
                    adj_ref, ub_ref, q, x, slice(0, ny)
                )

    for px in (0, 1):

        @pl.when(par_ref[0] == px)
        def _():
            sa = 1 if px else -1
            fill_x(a_ref, sa)
            fill_x(b_ref, -sa)


def column_pair(acc, value, pair, q, k, plane):
    start = 32 * (k // 2) + 4 * plane + 2 * (k % 2)
    cz = VEL[q][2] if q < 19 else 0
    return jnp.where(pair == start // 2, turn(value, start + 1 - cz), acc)


def pack_y_kernel(
    par_ref, adj_ref, ub_ref, drag_ref, cols_ref, y_ref, ya_ref, yb_ref
):
    nx, ny, nz = adj_ref.shape[1:]
    pair = lax.broadcasted_iota(jnp.int32, (8, nz), 1) // 2
    for g, group in enumerate(ZGROUPS):
        for t in range(ny // 8):
            acc = jnp.zeros((8, nz), jnp.float32)
            for k, q in enumerate(group):
                for x in range(nx):
                    value = cell_rows(adj_ref, ub_ref, q, x, slice(8 * t, 8 * t + 8))
                    acc = column_pair(acc, value, pair, q, k, x + 2)
            row = g * ny + 8 * t
            cols_ref[row : row + 8] = acc
    y_block = y_rows(nx) + EDGE_ROWS
    corner_block = CORNER + EDGE_ROWS

    def fill_edges(place, sign):
        for g in range(4):
            for d in range(2):
                y = d if sign > 0 else ny - 1 - d
                line = cols_ref[g * ny + y : g * ny + y + 1]
                row = place * y_block + y_rows(nx) + 2 * g + d
                y_ref[row : row + 1] = line
                row = place * corner_block + CORNER + 2 * g + d
                ya_ref[row : row + 1] = line
                yb_ref[row : row + 1] = line

    def fill_y(place, sign):
        for names, offset, y in (
            (near(1, sign), 0, 0 if sign > 0 else ny - 1),
            (far(1, sign), 18, 1 if sign > 0 else ny - 2),
        ):
            for k, q in enumerate(names):
                for x in range(nx):
                    row = place * y_block + (k + offset) * nx + x
                    y_ref[row : row + 1] = cell_rows(
                        adj_ref, ub_ref, q, x, slice(y, y + 1)
                    )

    def fill_corner(out_ref, place, sx, sy):
        names = corner_rows(sx, sy)
        for k, (q, dx, dy) in enumerate(names):
            x = dx if sx > 0 else nx - 1 - dx
            y = dy if sy > 0 else ny - 1 - dy
            row = place * corner_block + k
            out_ref[row : row + 1] = cell_rows(adj_ref, ub_ref, q, x, slice(y, y + 1))
        row = place * corner_block + len(names)
        last = place * corner_block + CORNER
        out_ref[row:last] = jnp.zeros((last - row, nz), jnp.float32)

    drag = drag_ref[...]
    cols_ref[4 * ny :] = drag
    y_ref[2 * y_block :] = drag
    ya_ref[2 * corner_block :] = drag
    yb_ref[2 * corner_block :] = drag
    for py in (0, 1):

        @pl.when(par_ref[1] == py)
        def _():
            s0 = 1 if py else -1
            fill_y(0, s0)
            fill_y(1, -s0)
            fill_edges(0, s0)
            fill_edges(1, -s0)

    for px in (0, 1):
        for py in (0, 1):

            @pl.when((par_ref[0] == px) & (par_ref[1] == py))
            def _():
                sa = 1 if px else -1
                s0 = 1 if py else -1
                for out_ref, sx in ((ya_ref, sa), (yb_ref, -sa)):
                    fill_corner(out_ref, 0, sx, s0)
                    fill_corner(out_ref, 1, sx, -s0)


def pack_z_kernel(
    par_ref,
    cols_ref,
    xa_ref,
    xc_ref,
    y_ref,
    ya_ref,
    yb_ref,
    zown_ref,
    za_ref,
    zb_ref,
    drag_ref,
    ext,
):
    ny = (cols_ref.shape[0] - 8) // 4
    nz = cols_ref.shape[1]
    tiles = ny // 8
    base = 16
    even_x = par_ref[0] == 0
    even_y = par_ref[1] == 0
    lane = lax.broadcasted_iota(jnp.int32, (8, nz), 1)
    sub = lax.broadcasted_iota(jnp.int32, (8, nz), 0)
    plane = (lane % 32) // 4
    slot = 2 * (lane // 32) + (lane % 4) // 2

    def along_x(own, va, vb):
        low = turn(jnp.where(even_x, vb, va), -16)
        high = turn(jnp.where(even_x, va, vb), 16)
        return jnp.where(plane < 2, low, jnp.where(plane > 5, high, own))

    pair = lane // 2

    def fill_main(sign):
        halo = {}
        for names, offset, p in (
            (near(0, sign), 0, 6 if sign > 0 else 1),
            (far(0, sign), 18, 7 if sign > 0 else 0),
        ):
            for k, q in enumerate(names):
                halo.setdefault(q, []).append((k + offset, p))
        for g, group in enumerate(ZGROUPS):
            for t in range(tiles):
                rows = slice(g * ny + 8 * t, g * ny + 8 * t + 8)
                acc = jnp.where(
                    plane < 2 if sign > 0 else plane > 5,
                    turn(xc_ref[rows], -16 * sign),
                    cols_ref[rows],
                )
                for k, q in enumerate(group):
                    for at, p in halo.get(q, ()):
                        row = at * ny + 8 * t
                        acc = column_pair(acc, xa_ref[row : row + 8], pair, q, k, p)
                ext[g, base + 8 * t : base + 8 * t + 8, :] = acc

    @pl.when(par_ref[0] == 0)
    def _():
        fill_main(1)

    @pl.when(par_ref[0] == 1)
    def _():
        fill_main(-1)

    y_block = (y_ref.shape[0] - 8) // 2
    corner_block = CORNER + EDGE_ROWS

    def edges(ref, block, place):
        return ref[(place + 1) * block - EDGE_ROWS : (place + 1) * block]

    first, second = [
        along_x(
            edges(y_ref, y_block, place),
            edges(ya_ref, corner_block, place),
            edges(yb_ref, corner_block, place),
        )
        for place in range(2)
    ]
    high = jnp.where(even_y, first, second)
    low = jnp.where(even_y, second, first)
    for g in range(4):
        for d in range(2):
            row = 2 * g + d
            ext[g, base + ny + d : base + ny + d + 1, :] = high[row : row + 1]
            ext[g, base - 1 - d : base - d, :] = low[row : row + 1]

    packed = []
    for g, group in enumerate(ZGROUPS):
        moves = {}
        for k, q in enumerate(group):
            cx, cy, _ = VEL[q] if q < 19 else (0, 0, 0)
            moves.setdefault((cx, cy), []).append(k)
        acc = [jnp.zeros((8, nz), jnp.float32) for t in range(tiles + 1)]
        for (cx, cy), slots in moves.items():
            mask = slot == slots[0]
            for k in slots[1:]:
                mask = mask | (slot == k)
            for t in range(tiles + 1):
                if t < tiles:
                    row = base + 8 * t + cy
                    value = ext[g, row : row + 8, :]
                else:
                    above = base + ny + cy
                    below = base - 8 + cy
                    value = jnp.where(
                        sub < 4, ext[g, above : above + 8, :], ext[g, below : below + 8, :]
                    )
                acc[t] = jnp.where(mask, turn(value, -4 * cx), acc[t])
        packed.append(acc)
        for t in range(tiles + 1):
            row = (g * (tiles + 1) + t) * 8
            zown_ref[row : row + 8, :] = acc[t]
    up_first = par_ref[2] == 0
    even_lane = lane % 2 == 0
    for t in range(tiles + 1):
        two, three = packed[2][t], packed[3][t]
        up = (packed[0][t], jnp.where(even_lane, two, pltpu.roll(three, 1, 1)))
        down = (packed[1][t], jnp.where(even_lane, pltpu.roll(two, nz - 1, 1), three))
        for g in range(2):
            row = (g * (tiles + 1) + t) * 8
            za_ref[row : row + 8, :] = jnp.where(up_first, up[g], down[g])
            zb_ref[row : row + 8, :] = jnp.where(up_first, down[g], up[g])
    drag = cols_ref[4 * ny :] + y_ref[2 * y_block :]
    for x_ref, c_ref in ((xa_ref, ya_ref), (xc_ref, yb_ref)):
        drag = drag + (x_ref[x_ref.shape[0] - 8 :] + c_ref[2 * corner_block :])
    drag_ref[...] = drag


OUT_GROUPS = ((0, 7), (7, 13), (13, 17), (17, 19))


def turn(value, shift):
    nz = value.shape[1]
    return pltpu.roll(value, shift % nz, 1) if shift % nz else value


def z_shifted(value, cz):
    return turn(value, -cz) if cz else value


def inner_kernel(
    par_ref,
    states_ref,
    adj_ref,
    ub_ref,
    xa_ref,
    xb_ref,
    y_ref,
    ya_ref,
    yb_ref,
    out_ref,
    grad1_ref,
    grad_ref,
    pack_ref,
    f0_ref,
    f1_ref,
    ext,
    mid,
):
    nx, ny, nz = grad_ref.shape
    tiles = ny // 8
    lane = lax.broadcasted_iota(jnp.int32, (8, nz), 1)
    slot = lane // 4
    sub = lax.broadcasted_iota(jnp.int32, (8, nz), 0)
    even_x = par_ref[0] == 0
    even_y = par_ref[1] == 0
    base = 16

    for q in range(NSLOT):
        for x in range(nx):
            ext[q, x + 2, base : base + ny, :] = (
                adj_ref[q, x] if q < 19 else ub_ref[q - 19, x]
            )
    planes = {1: (nx + 2, nx + 3), -1: (1, 0)}
    lines = {1: (base + ny, base + ny + 1), -1: (base - 1, base - 2)}
    for sign in (1, -1):
        first, second = (xa_ref, xb_ref) if sign > 0 else (xb_ref, xa_ref)
        for names, depth, offset in ((near(0, sign), 0, 0), (far(0, sign), 1, 18)):
            for k, q in enumerate(names):
                rows = slice((k + offset) * ny, (k + offset + 1) * ny)
                ext[q, planes[sign][depth], base : base + ny, :] = jnp.where(
                    even_x, first[rows], second[rows]
                )
        block = y_rows(nx) + EDGE_ROWS
        first, second = (0, block) if sign > 0 else (block, 0)
        for names, depth, offset in ((near(1, sign), 0, 0), (far(1, sign), 1, 18)):
            line = lines[sign][depth]
            for k, q in enumerate(names):
                row = (k + offset) * nx
                got = jnp.where(
                    even_y,
                    y_ref[first + row : first + row + nx],
                    y_ref[second + row : second + row + nx],
                )
                for x in range(nx):
                    ext[q, x + 2, line : line + 1, :] = got[x : x + 1]
        for sx in (1, -1):
            xs = (ya_ref, yb_ref) if sx > 0 else (yb_ref, ya_ref)
            block = CORNER + EDGE_ROWS
            ys = (0, block) if sign > 0 else (block, 0)
            low, high = [
                jnp.where(even_x, xs[0][r : r + CORNER], xs[1][r : r + CORNER])
                for r in ys
            ]
            got = jnp.where(even_y, low, high)
            for k, (q, dx, dy) in enumerate(corner_rows(sx, sign)):
                line = lines[sign][dy]
                ext[q, planes[sx][dx], line : line + 1, :] = got[k : k + 1]

    def near_cells(q, plane, t, cy):
        if t < tiles:
            row = base + 8 * t + cy
            return ext[q, plane, row : row + 8, :]
        above = base + ny + cy
        below = base - 8 + cy
        return jnp.where(
            sub < 4, ext[q, plane, above : above + 8, :], ext[q, plane, below : below + 8, :]
        )

    def first_level(p, t, kinds):
        got = []
        for i in range(19):
            cx, cy, cz = VEL[i]
            got.append(z_shifted(near_cells(i, p + 1 + cx, t, cy), cz))
        ub = [near_cells(19 + k, p + 1, t, 0) for k in range(4)]
        out, kept = adjoint_cell(got, ub[:3], ub[3], 1.0)
        for i in kinds:
            if t < tiles:
                mid[i, p, t * 8 + 8 : t * 8 + 16, :] = out[i]
            elif VEL[i][1] > 0:
                mid[i, p, t * 8 + 8 : t * 8 + 16, :] = out[i]
            elif VEL[i][1] < 0:
                mid[i, p, 0:8, :] = out[i]
        return kept, ub[:3]

    def inside(x, carry):
        for t in range(tiles):
            kept, u = first_level(x + 1, t, range(19))
            rows = slice(t * 8, t * 8 + 8)
            f0, fs, fd, fm, _ = state_of(states_ref, (1, x, rows))
            grad1_ref[x, rows, :] = gradient_cell(kept, f0, fs, fd, fm, u)
        return carry

    lax.fori_loop(0, nx, inside, 0)
    for t in range(tiles):
        first_level(0, t, far(0, -1))
        first_level(nx + 1, t, far(0, 1))

    def rim(n, carry):
        for p in (2 * n, 2 * n + 1):
            first_level(p, tiles, far(1, -1) + far(1, 1))
        return carry

    lax.fori_loop(0, (nx + 2) // 2, rim, 0)

    def second_level(x, carry):
        for t in range(tiles):
            rows = slice(t * 8, t * 8 + 8)
            got = []
            for i in range(19):
                cx, cy, cz = VEL[i]
                low = 8 + 8 * t + cy
                value = z_shifted(mid[i, x + 1 + cx, low : low + 8, :], cz)
                got.append(value)
                pack_ref[i, rows, :] = jnp.where(
                    slot == x, pltpu.roll(value, 4 * x + 2, 1), pack_ref[i, rows, :]
                )
            f0, fs, fd, fm, u = state_of(states_ref, (0, x, rows))
            b = ub_ref[3, x, rows, :]
            out, kept = adjoint_cell(got, u, b, 1.0)
            for i in range(19):
                out_ref[i, x, rows, :] = out[i]
            grad_ref[x, rows, :] = grad1_ref[x, rows, :] + gradient_cell(
                kept, f0, fs, fd, fm, u
            )
        return carry

    lax.fori_loop(0, nx, second_level, 0)

    def tile(t, carry):
        rows = pl.ds(pl.multiple_of(t * 8, 8), 8)
        for i in range(20):
            for out_ref, level, first in ((f0_ref, 0, 0), (f1_ref, 1, 2)):
                if i == 19 and level == 1:
                    continue
                acc = jnp.zeros((8, nz), jnp.float32)
                for x in range(nx):
                    value = (
                        states_ref[level, i, x, rows, :]
                        if i < 19
                        else ub_ref[3, x, rows, :]
                    )
                    p = x + first
                    acc = jnp.where(slot == p, pltpu.roll(value, 4 * p + 2, 1), acc)
                out_ref[i, rows, :] = acc
        return carry

    lax.fori_loop(0, ny // 8, tile, 0)


def edge_kernel(
    par_ref,
    mask_ref,
    zown_ref,
    za_ref,
    zb_ref,
    pack_ref,
    f0_ref,
    f1_ref,
    inner_ref,
    grad1_ref,
    inner_grad_ref,
    out_hbm,
    grad_hbm,
    tail_ref,
    first_ref,
    second_ref,
    zmid,
    zout,
    out_ref,
    grad_ref,
    sems,
):
    nx, ny, nz = mask_ref.shape
    tiles = ny // 8
    height = (tiles + 1) * 8
    even = par_ref[2] == 0
    lane = lax.broadcasted_iota(jnp.int32, (8, nz), 1)
    even_lane = lane % 2 == 0
    low_pair = lane % 4 < 2

    last = slice(2 * height, 2 * height + 8)
    tail_ref[...] = za_ref[last] + zb_ref[last]

    def swapped(value):
        return jnp.where(even_lane, turn(value, -1), turn(value, 1))

    for t in range(tiles + 1):
        received = []
        for g in range(2):
            row = (g * (tiles + 1) + t) * 8
            va = za_ref[row : row + 8, :]
            vb = zb_ref[row : row + 8, :]
            received.append((jnp.where(even, va, vb), jnp.where(even, vb, va)))
        (high0, low0), (high1, low1) = received
        for g in range(4):
            row = (g * (tiles + 1) + t) * 8
            rows = slice(row, row + 8)
            own = zown_ref[rows]
            if g == 0:
                head, tail = own, low0
            elif g == 1:
                head, tail = high0, own
            elif g == 2:
                head = jnp.where(even_lane, own, turn(high1, 1))
                tail = jnp.where(even_lane, low1, own)
            else:
                head = jnp.where(even_lane, own, high1)
                tail = jnp.where(even_lane, turn(low1, -1), own)
            head = swapped(head)
            tail = swapped(tail)
            first_ref[rows] = jnp.where(low_pair, head, turn(tail, 2))
            second_ref[rows] = jnp.where(low_pair, turn(head, -2), tail)

    slab_grad = []
    for t in range(tiles + 1):
        got = []
        for q in range(NSLOT):
            g, k = ZSLOT[q]
            row = g * height + t * 8
            ref = second_ref if k % 2 else first_ref
            got.append(turn(ref[row : row + 8, :], -32 * (k // 2)))
        out, kept = adjoint_cell(got[:19], got[19:22], got[22], 1.0)
        for i in range(19):
            zmid[i, 8 * t + 8 : 8 * t + 16, :] = out[i]
            if t == tiles:
                zmid[i, 0:8, :] = out[i]
        if t < tiles:
            f = [f1_ref[i, 8 * t : 8 * t + 8, :] for i in range(19)]
            fs, fd = pairs_of(f)
            fm = moments(f[0], fs, fd)
            grad = gradient_cell(kept, f[0], fs, fd, fm, got[19:22])
            slab_grad.append(turn(grad, -8))

    at = lane % 4
    for t in range(tiles):
        rows = slice(8 * t, 8 * t + 8)
        got = []
        for i in range(19):
            cx, cy, cz = VEL[i]
            value = pack_ref[i, rows, :]
            edge = zmid[i, 8 + 8 * t + cy : 16 + 8 * t + cy, :]
            back = -4 * (2 + cx)
            if cz == 0:
                value = jnp.where((at == 1) | (at == 2), turn(edge, back), value)
            else:
                near_lane = 2 if cz < 0 else 0
                value = jnp.where(at == near_lane, turn(edge, back - 1), value)
                value = jnp.where(at == near_lane + 1, turn(edge, back + 1), value)
            got.append(value)
        f = [f0_ref[i, rows, :] for i in range(19)]
        fs, fd = pairs_of(f)
        fm = moments(f[0], fs, fd)
        inverse = 1.0 / fm["total"]
        u = [one * inverse for one in fm["one"]]
        out, kept = adjoint_cell(got, u, f0_ref[19, rows, :], 1.0)
        for i in range(19):
            zout[i, rows, :] = out[i]
        zout[19, rows, :] = gradient_cell(kept, f[0], fs, fd, fm, u)
        zout[20, rows, :] = slab_grad[t]

    def out_copy(k):
        part = slice(*OUT_GROUPS[k])
        return pltpu.make_async_copy(out_ref.at[part], out_hbm.at[part], sems.at[k])

    outer = (lane < 2) | (lane >= nz - 2)
    ends = (lane < 1) | (lane >= nz - 1)
    for x in range(nx):
        for t in range(tiles):
            rows = slice(8 * t, 8 * t + 8)
            level1 = jnp.where(
                ends, turn(zout[20, rows, :], -2 - 4 * x), grad1_ref[x, rows, :]
            )
            edge = turn(zout[19, rows, :], -2 - 4 * x) + level1
            grad = jnp.where(outer, edge, inner_grad_ref[x, rows, :])
            grad_ref[x, rows, :] = jnp.where(mask_ref[x, rows, :] == 0, grad, 0.0)
    grad_copy = pltpu.make_async_copy(grad_ref, grad_hbm, sems.at[len(OUT_GROUPS)])
    grad_copy.start()
    for k, group in enumerate(OUT_GROUPS):
        for i in range(*group):
            for x in range(nx):
                for t in range(tiles):
                    rows = slice(8 * t, 8 * t + 8)
                    out_ref[i, x, rows, :] = jnp.where(
                        outer,
                        turn(zout[i, rows, :], -2 - 4 * x),
                        inner_ref[i, x, rows, :],
                    )
        out_copy(k).start()
    grad_copy.wait()
    for k in range(len(OUT_GROUPS)):
        out_copy(k).wait()


def drag_kernel(whole_cells, *refs):
    total = refs[0][...]
    for ref in refs[1:-1]:
        total = total + ref[...]
    summed = jnp.sum(jnp.sum(total, axis=1, keepdims=True), axis=0, keepdims=True)
    refs[-1][...] = summed / whole_cells


def swaps(count):
    first = [(i, i ^ 1) for i in range(count)]
    second = [(i, (((i + 1) % count) ^ 1) - 1) for i in range(count)]
    second = [(i, j % count) for i, j in second]
    return first, second


VMEM = pl.BlockSpec(memory_space=pltpu.VMEM)
SMEM = pl.BlockSpec(memory_space=pltpu.SMEM)
HBM = pl.BlockSpec(memory_space=pltpu.HBM)
PARAMS = pltpu.CompilerParams(vmem_limit_bytes=48 * 2**20)


def call(kernel, inputs, shapes, scratch=(), space=VMEM, micros=1, outs=None):
    if space is HBM:
        inputs = inputs[:1] + tuple(
            pltpu.with_memory_space_constraint(x, pltpu.HBM) for x in inputs[1:]
        )
    return pl.pallas_call(
        kernel,
        out_shape=[jax.ShapeDtypeStruct(s, jnp.float32) for s in shapes],
        in_specs=[SMEM if x.dtype == jnp.int32 and x.ndim == 1 else space for x in inputs],
        out_specs=outs or [VMEM] * len(shapes),
        scratch_shapes=list(scratch),
        compiler_params=PARAMS,
        cost_estimate=pl.CostEstimate(
            flops=0, bytes_accessed=int(3.6e6 * micros), transcendentals=0
        ),
    )(*inputs)


def body(primal_states, adjoint_last, porosity, solid_mask):
    nx, ny, nz = porosity.shape
    gx, gy, gz = [lax.axis_size(axis) for axis in AXES]
    x_first, x_second = swaps(gx)
    y_first, y_second = swaps(gy)
    z_first, z_second = swaps(gz)
    parity = jnp.stack([lax.axis_index(axis) & 1 for axis in AXES]).astype(jnp.int32)
    tiles = ny // 8
    height = (tiles + 1) * 8
    f32 = jnp.float32

    def diagonal(message, x_pairs, y_pairs):
        pairs = [(a * gy + c, b * gy + d) for a, b in x_pairs for c, d in y_pairs]
        return lax.ppermute(message, ("gx", "gy"), pairs)

    rows_x = NSLOT * ny + 8
    rows_y = 2 * (y_rows(nx) + EDGE_ROWS) + 8
    rows_c = 2 * (CORNER + EDGE_ROWS) + 8
    rows_z = 2 * height + 8
    rides = (gx, gy, gz) == (4, 2, 4)
    xa, xb, ub, drag = call(
        pack_x_kernel,
        (parity, primal_states, adjoint_last, porosity, solid_mask),
        [(rows_x, nz), (rows_x, nz), (4, nx, ny, nz), (8, nz)],
        [
            pltpu.VMEM((2, 19, nx, ny, nz), f32),
            pltpu.VMEM((19, nx, ny, nz), f32),
            pltpu.VMEM((nx, ny, nz), f32),
            pltpu.VMEM((nx, ny, nz), jnp.int32),
            pltpu.SemaphoreType.DMA((6,)),
        ],
        HBM,
    )
    cols, y, ya, yb = call(
        pack_y_kernel,
        (parity, adjoint_last, ub, drag),
        [(4 * ny + 8, nz), (rows_y, nz), (rows_c, nz), (rows_c, nz)],
        micros=4,
    )
    xc = lax.ppermute(cols, "gx", x_second)
    xa = lax.ppermute(xa, "gx", x_first)
    if gy == 2:
        y = lax.ppermute(y, "gy", y_first)
        yb = diagonal(yb, x_second, y_first)
        ya = diagonal(ya, x_first, y_first)
    else:

        def both(message, block, send):
            parts = [message[:block], message[block : 2 * block], message[2 * block :]]
            return jnp.concatenate(
                [send(parts[0], y_first), send(parts[1], y_second), parts[2]]
            )

        block = y_rows(nx) + EDGE_ROWS
        y = both(y, block, lambda m, pairs: lax.ppermute(m, "gy", pairs))
        block = CORNER + EDGE_ROWS
        yb = both(yb, block, lambda m, pairs: diagonal(m, x_second, pairs))
        ya = both(ya, block, lambda m, pairs: diagonal(m, x_first, pairs))
    xb, yb = lax.optimization_barrier((xb, yb))
    xb = lax.ppermute(xb, "gx", x_second)

    zown, za, zb, drag_xy = call(
        pack_z_kernel,
        (parity, cols, xa, xc, y, ya, yb),
        [(4 * height, nz), (rows_z, nz), (rows_z, nz), (8, nz)],
        [pltpu.VMEM((4, ny + 32, nz), f32)],
    )
    if rides:
        second = xc[4 * ny :] + yb[rows_c - 8 :]
        drag_xy = drag_xy + lax.ppermute(second, "gx", x_first)
        za = za.at[2 * height :].set(drag_xy)
        zb = zb.at[2 * height :].set(drag_xy)
    zb = lax.ppermute(zb, "gz", z_second)
    za = lax.ppermute(za, "gz", z_first)
    inner, grad1, inner_grad, pack, f0, f1 = call(
        inner_kernel,
        (parity, primal_states, adjoint_last, ub, xa, xb, y, ya, yb),
        [
            (19, nx, ny, nz),
            (nx, ny, nz),
            (nx, ny, nz),
            (19, ny, nz),
            (20, ny, nz),
            (19, ny, nz),
        ],
        [
            pltpu.VMEM((NSLOT, nx + 4, ny + 32, nz), f32),
            pltpu.VMEM((19, nx + 2, height + 8, nz), f32),
        ],
        micros=4,
    )
    if rides:
        zhalf = lax.ppermute(drag_xy, "gz", [(i, i ^ 2) for i in range(gz)])
        drags = (drag_xy, zhalf)
    else:
        drags = (lax.psum(drag, AXES),)

    first, gradient, tails = call(
        edge_kernel,
        (parity, solid_mask, zown, za, zb, pack, f0, f1, inner, grad1, inner_grad),
        [(19, nx, ny, nz), (nx, ny, nz), (8, nz)],
        [
            pltpu.VMEM((4 * height, nz), f32),
            pltpu.VMEM((4 * height, nz), f32),
            pltpu.VMEM((19, height + 8, nz), f32),
            pltpu.VMEM((21, ny, nz), f32),
            pltpu.VMEM((19, nx, ny, nz), f32),
            pltpu.VMEM((nx, ny, nz), f32),
            pltpu.SemaphoreType.DMA((len(OUT_GROUPS) + 1,)),
        ],
        outs=[HBM, HBM, VMEM],
    )
    if rides:
        drags += (tails,)
    whole_cells = float(nx * ny * nz * gx * gy * gz)
    (drag,) = call(functools.partial(drag_kernel, whole_cells), drags, [(1, 1)])
    return (first, gradient, drag.reshape(()))


def solution(mesh):
    return jax.shard_map(
        body,
        mesh=mesh,
        in_specs=(
            P(None, None, "gx", "gy", "gz"),
            P(None, "gx", "gy", "gz"),
            P("gx", "gy", "gz"),
            P("gx", "gy", "gz"),
        ),
        out_specs=(P(None, "gx", "gy", "gz"), P("gx", "gy", "gz"), P()),
        check_vma=False,
    )
```

```python
import functools

import jax
import jax.numpy as jnp
import numpy as np
from jax import lax
from jax.experimental import pallas as pl
from jax.experimental.pallas import tpu as pltpu
from jax.sharding import PartitionSpec as P

VEL = (
    (0, 0, 0),
    (1, 0, 0),
    (-1, 0, 0),
    (0, 1, 0),
    (0, -1, 0),
    (0, 0, 1),
    (0, 0, -1),
    (1, 1, 0),
    (-1, -1, 0),
    (1, -1, 0),
    (-1, 1, 0),
    (1, 0, 1),
    (-1, 0, -1),
    (1, 0, -1),
    (-1, 0, 1),
    (0, 1, 1),
    (0, -1, -1),
    (0, 1, -1),
    (0, -1, 1),
)
PAIRS = tuple((i, i + 1) for i in range(1, 19, 2))
AXES = ("gx", "gy", "gz")
UB = (19, 20, 21, 22)


def near(axis, sign):
    return tuple(i for i in range(19) if VEL[i][axis] * sign >= 0) + UB


def far(axis, sign):
    return tuple(i for i in range(19) if VEL[i][axis] == sign)


NSLOT = 23
CORNER = 24
EDGE_ROWS = 8


def y_rows(nx):
    return -(-NSLOT * nx // 8) * 8


ZGROUPS = (
    tuple(i for i in range(19) if VEL[i][2] == -1),
    tuple(i for i in range(19) if VEL[i][2] == 1),
    tuple(i for i in range(19) if VEL[i][2] == 0)[:8],
    tuple(i for i in range(19) if VEL[i][2] == 0)[8:] + UB,
)
ZSLOT = {q: (g, k) for g, group in enumerate(ZGROUPS) for k, q in enumerate(group)}


def pairs_of(values):
    s = [values[a] + values[b] for a, b in PAIRS]
    d = [values[a] - values[b] for a, b in PAIRS]
    return s, d


def moments(v0, s, d):
    sx, sy, sz, sp, sq, sr, ss, st, su = s
    dx, dy, dz, dp, dq, dr, ds, dt, du = d
    ex = sp + sq
    ez = sr + ss
    ey = st + su
    faces = sx + sy + sz
    edges = ex + ez + ey
    exx = ex + ez
    eyy = ex + ey
    ezz = ez + ey
    fx = (dp + dq) + (dr + ds)
    fy = (dp - dq) + (dt + du)
    fz = (dr - ds) + (dt - du)
    return dict(
        rest=v0,
        faces=faces,
        edges=edges,
        total=v0 + faces + edges,
        face1=(dx, dy, dz),
        edge1=(fx, fy, fz),
        one=(dx + fx, dy + fy, dz + fz),
        face2=(sx, sy, sz),
        edge2=(exx, eyy, ezz),
        two=(sx + exx, sy + eyy, sz + ezz),
        cross=(sp - sq, sr - ss, st - su),
    )


def adjoint_cell(g, u, b, drive):
    s, d = pairs_of(g)
    m = moments(g[0], s, d)
    total = m["total"]
    trace = m["faces"] + 2.0 * m["edges"] - (30.0 / 19.0) * total
    p0 = (-1.2 / 19.0) * total - (2.0 / 21.0) * trace
    q = [
        (0.4 / 6.0) * (two - (10.0 / 19.0) * total) + (0.8 / 21.0) * trace
        for two in m["two"]
    ]
    qsum = q[0] + q[1] + q[2]
    qab = [0.1 * c for c in m["cross"]]
    p1 = [-0.12 * one for one in m["one"]]
    h0 = (
        0.4 * m["rest"]
        + (1.2 / 18.0) * m["faces"]
        + (1.2 / 36.0) * m["edges"]
        + p0
        + (1.0 / 3.0) * qsum
    )
    h1 = [
        (1.2 / 18.0) * f + (1.2 / 36.0) * e + (1.0 / 3.0) * p
        for f, e, p in zip(m["face1"], m["edge1"], p1)
    ]
    base = (1.0 / 3.0) * p0 + (1.0 / 9.0) * qsum
    haa = [
        (1.2 / 18.0) * f + (1.2 / 36.0) * e + (2.0 / 9.0) * qa + base
        for f, e, qa in zip(m["face2"], m["edge2"], q)
    ]
    hxy, hxz, hyz = [(2.0 / 45.0) * c for c in m["cross"]]
    ux, uy, uz = u
    v = (
        haa[0] * ux + hxy * uy + hxz * uz,
        hxy * ux + haa[1] * uy + hyz * uz,
        hxz * ux + hyz * uy + haa[2] * uz,
    )
    uv = ux * v[0] + uy * v[1] + uz * v[2]
    uu = ux * ux + uy * uy + uz * uz
    uuh = 1.5 * uu * h0
    a = h0 + uuh - 4.5 * uv
    nb = 1.0 - b
    e0 = nb * (a - p0)
    nq = [nb * x for x in q]
    nxy, nxz, nyz = [nb * x for x in qab]
    o = [
        nb * (3.0 * h1[k] + 9.0 * v[k] - 3.0 * u[k] * h0 - p1[k]) for k in range(3)
    ]
    o[0] = o[0] + b * drive
    alpha = -0.2 * nb
    half_s = 0.5 * (alpha + b)
    half_d = 0.5 * (alpha - b)
    exy = e0 - nq[0] - nq[1]
    exz = e0 - nq[0] - nq[2]
    eyz = e0 - nq[1] - nq[2]
    even = (
        e0 - nq[0],
        e0 - nq[1],
        e0 - nq[2],
        exy - nxy,
        exy + nxy,
        exz - nxz,
        exz + nxz,
        eyz - nyz,
        eyz + nyz,
    )
    odd = (
        o[0],
        o[1],
        o[2],
        o[0] + o[1],
        o[0] - o[1],
        o[0] + o[2],
        o[0] - o[2],
        o[1] + o[2],
        o[1] - o[2],
    )
    out = [(alpha + b) * g[0] + e0]
    for k in range(9):
        even_k = half_s * s[k] + even[k]
        odd_k = half_d * d[k] + odd[k]
        out.append(even_k + odd_k)
        out.append(even_k - odd_k)
    kept = dict(
        s=s, d=d, g0=g[0], p0=p0, p1=p1, q=q, qab=qab, h0=h0, h1=h1, uv=uv, uuh=uuh
    )
    return out, kept


def gradient_cell(kept, f0, fs, fd, fm, u):
    rho = fm["total"]
    even = fs[0] * kept["s"][0]
    odd = fd[0] * kept["d"][0]
    for k in range(1, 9):
        even = even + fs[k] * kept["s"][k]
        odd = odd + fd[k] * kept["d"][k]
    hf = kept["p0"] * rho
    for k in range(3):
        hf = hf + kept["p1"][k] * fm["one"][k] + kept["q"][k] * fm["two"][k]
        hf = hf + kept["qab"][k] * fm["cross"][k]
    uh1 = u[0] * kept["h1"][0] + u[1] * kept["h1"][1] + u[2] * kept["h1"][2]
    hfeq = rho * (kept["h0"] - kept["uuh"] + 3.0 * uh1 + 4.5 * kept["uv"])
    pairs = 1.2 * f0 * kept["g0"] + 0.6 * even - 0.4 * odd
    return pairs + hf - hfeq + fm["one"][0]


def state_of(ref, index):
    f = [ref[(index[0], i) + index[1:]] for i in range(19)]
    s, d = pairs_of(f)
    m = moments(f[0], s, d)
    inverse = 1.0 / m["total"]
    u = [one * inverse for one in m["one"]]
    return f[0], s, d, m, u


def corner_rows(sx, sy):
    rows = []
    for dx, dy in ((0, 0), (1, 0), (0, 1), (1, 1)):
        for i in near(0, sx) if dx == 0 else far(0, sx):
            if i in (near(1, sy) if dy == 0 else far(1, sy)):
                rows.append((i, dx, dy))
    return rows


def parity(axis):
    return lax.axis_index(axis) % 2


def cell_rows(adj_ref, ub_ref, q, x, rows):
    return adj_ref[q, x, rows, :] if q < 19 else ub_ref[q - 19, x, rows, :]


def pack_x_kernel(
    states_hbm,
    adj_hbm,
    por_hbm,
    mask_hbm,
    a_ref,
    b_ref,
    ub_ref,
    drag_ref,
    states_ref,
    adj_ref,
    por_ref,
    mask_ref,
    sems,
):
    nx, ny, nz = por_ref.shape
    tiles = ny // 8
    copies = [
        pltpu.make_async_copy(src, dst, sems.at[k])
        for k, (src, dst) in enumerate(
            (
                (states_hbm.at[1], states_ref.at[1]),
                (por_hbm, por_ref),
                (mask_hbm, mask_ref),
                (states_hbm.at[0, 1:3], states_ref.at[0, 1:3]),
                (states_hbm.at[0, 7:15], states_ref.at[0, 7:15]),
                (adj_hbm, adj_ref),
            )
        )
    ]
    for copy in copies:
        copy.start()
    for copy in copies[:5]:
        copy.wait()

    def cells(x, carry):
        for t in range(tiles):
            rows = slice(8 * t, 8 * t + 8)
            blocking = jnp.where(mask_ref[x, rows, :] == 0, por_ref[x, rows, :], 1.0)
            f0, s, d, m, u = state_of(states_ref, (1, x, rows))
            flux = m["one"][0]
            for a, b in PAIRS:
                if VEL[a][0]:
                    flux = flux + (
                        states_ref[0, a, x, rows, :] - states_ref[0, b, x, rows, :]
                    )
            for k in range(3):
                ub_ref[k, x, rows, :] = u[k]
            ub_ref[3, x, rows, :] = blocking
            carry = carry + blocking * flux
        return carry

    drag = lax.fori_loop(0, nx, cells, jnp.zeros((8, nz), jnp.float32))
    drag_ref[...] = drag
    a_ref[NSLOT * ny :] = drag
    b_ref[NSLOT * ny :] = drag
    copies[5].wait()

    def fill_x(out_ref, sign):
        for names, offset, x in (
            (near(0, sign), 0, 0 if sign > 0 else nx - 1),
            (far(0, sign), 18, 1 if sign > 0 else nx - 2),
        ):
            for k, q in enumerate(names):
                k += offset
                out_ref[k * ny : (k + 1) * ny] = cell_rows(
                    adj_ref, ub_ref, q, x, slice(0, ny)
                )

    for px in (0, 1):

        @pl.when(parity("gx") == px)
        def _():
            sa = 1 if px else -1
            fill_x(a_ref, sa)
            fill_x(b_ref, -sa)


def column_pair(acc, value, pair, q, k, plane):
    start = 32 * (k // 2) + 4 * plane + 2 * (k % 2)
    cz = VEL[q][2] if q < 19 else 0
    return jnp.where(pair == start // 2, turn(value, start + 1 - cz), acc)


def pack_y_kernel(
    adj_ref, ub_ref, drag_ref, cols_ref, y_ref, ya_ref, yb_ref
):
    nx, ny, nz = adj_ref.shape[1:]
    pair = lax.broadcasted_iota(jnp.int32, (8, nz), 1) // 2
    for g, group in enumerate(ZGROUPS):
        for t in range(ny // 8):
            acc = jnp.zeros((8, nz), jnp.float32)
            for k, q in enumerate(group):
                for x in range(nx):
                    value = cell_rows(adj_ref, ub_ref, q, x, slice(8 * t, 8 * t + 8))
                    acc = column_pair(acc, value, pair, q, k, x + 2)
            row = g * ny + 8 * t
            cols_ref[row : row + 8] = acc
    y_block = y_rows(nx) + EDGE_ROWS
    corner_block = CORNER + EDGE_ROWS

    def fill_edges(place, sign):
        for g in range(4):
            for d in range(2):
                y = d if sign > 0 else ny - 1 - d
                line = cols_ref[g * ny + y : g * ny + y + 1]
                row = place * y_block + y_rows(nx) + 2 * g + d
                y_ref[row : row + 1] = line
                row = place * corner_block + CORNER + 2 * g + d
                ya_ref[row : row + 1] = line
                yb_ref[row : row + 1] = line

    def fill_y(place, sign):
        for names, offset, y in (
            (near(1, sign), 0, 0 if sign > 0 else ny - 1),
            (far(1, sign), 18, 1 if sign > 0 else ny - 2),
        ):
            for k, q in enumerate(names):
                for x in range(nx):
                    row = place * y_block + (k + offset) * nx + x
                    y_ref[row : row + 1] = cell_rows(
                        adj_ref, ub_ref, q, x, slice(y, y + 1)
                    )

    def fill_corner(out_ref, place, sx, sy):
        names = corner_rows(sx, sy)
        for k, (q, dx, dy) in enumerate(names):
            x = dx if sx > 0 else nx - 1 - dx
            y = dy if sy > 0 else ny - 1 - dy
            row = place * corner_block + k
            out_ref[row : row + 1] = cell_rows(adj_ref, ub_ref, q, x, slice(y, y + 1))
        row = place * corner_block + len(names)
        last = place * corner_block + CORNER
        out_ref[row:last] = jnp.zeros((last - row, nz), jnp.float32)

    drag = drag_ref[...]
    cols_ref[4 * ny :] = drag
    y_ref[2 * y_block :] = drag
    ya_ref[2 * corner_block :] = drag
    yb_ref[2 * corner_block :] = drag
    for py in (0, 1):

        @pl.when(parity("gy") == py)
        def _():
            s0 = 1 if py else -1
            fill_y(0, s0)
            fill_y(1, -s0)
            fill_edges(0, s0)
            fill_edges(1, -s0)

    for px in (0, 1):
        for py in (0, 1):

            @pl.when((parity("gx") == px) & (parity("gy") == py))
            def _():
                sa = 1 if px else -1
                s0 = 1 if py else -1
                for out_ref, sx in ((ya_ref, sa), (yb_ref, -sa)):
                    fill_corner(out_ref, 0, sx, s0)
                    fill_corner(out_ref, 1, sx, -s0)


def pack_z_kernel(
    cols_ref,
    xa_ref,
    xc_ref,
    y_ref,
    ya_ref,
    yb_ref,
    zown_ref,
    za_ref,
    zb_ref,
    drag_ref,
    ext,
):
    ny = (cols_ref.shape[0] - 8) // 4
    nz = cols_ref.shape[1]
    tiles = ny // 8
    base = 16
    even_x = parity("gx") == 0
    even_y = parity("gy") == 0
    lane = lax.broadcasted_iota(jnp.int32, (8, nz), 1)
    sub = lax.broadcasted_iota(jnp.int32, (8, nz), 0)
    plane = (lane % 32) // 4
    slot = 2 * (lane // 32) + (lane % 4) // 2

    def along_x(own, va, vb):
        low = turn(jnp.where(even_x, vb, va), -16)
        high = turn(jnp.where(even_x, va, vb), 16)
        return jnp.where(plane < 2, low, jnp.where(plane > 5, high, own))

    pair = lane // 2

    def fill_main(sign):
        halo = {}
        for names, offset, p in (
            (near(0, sign), 0, 6 if sign > 0 else 1),
            (far(0, sign), 18, 7 if sign > 0 else 0),
        ):
            for k, q in enumerate(names):
                halo.setdefault(q, []).append((k + offset, p))
        for g, group in enumerate(ZGROUPS):
            for t in range(tiles):
                rows = slice(g * ny + 8 * t, g * ny + 8 * t + 8)
                acc = jnp.where(
                    plane < 2 if sign > 0 else plane > 5,
                    turn(xc_ref[rows], -16 * sign),
                    cols_ref[rows],
                )
                for k, q in enumerate(group):
                    for at, p in halo.get(q, ()):
                        row = at * ny + 8 * t
                        acc = column_pair(acc, xa_ref[row : row + 8], pair, q, k, p)
                ext[g, base + 8 * t : base + 8 * t + 8, :] = acc

    @pl.when(parity("gx") == 0)
    def _():
        fill_main(1)

    @pl.when(parity("gx") == 1)
    def _():
        fill_main(-1)

    y_block = (y_ref.shape[0] - 8) // 2
    corner_block = CORNER + EDGE_ROWS

    def edges(ref, block, place):
        return ref[(place + 1) * block - EDGE_ROWS : (place + 1) * block]

    first, second = [
        along_x(
            edges(y_ref, y_block, place),
            edges(ya_ref, corner_block, place),
            edges(yb_ref, corner_block, place),
        )
        for place in range(2)
    ]
    high = jnp.where(even_y, first, second)
    low = jnp.where(even_y, second, first)
    for g in range(4):
        for d in range(2):
            row = 2 * g + d
            ext[g, base + ny + d : base + ny + d + 1, :] = high[row : row + 1]
            ext[g, base - 1 - d : base - d, :] = low[row : row + 1]

    packed = []
    for g, group in enumerate(ZGROUPS):
        moves = {}
        for k, q in enumerate(group):
            cx, cy, _ = VEL[q] if q < 19 else (0, 0, 0)
            moves.setdefault((cx, cy), []).append(k)
        acc = [jnp.zeros((8, nz), jnp.float32) for t in range(tiles + 1)]
        for (cx, cy), slots in moves.items():
            mask = slot == slots[0]
            for k in slots[1:]:
                mask = mask | (slot == k)
            for t in range(tiles + 1):
                if t < tiles:
                    row = base + 8 * t + cy
                    value = ext[g, row : row + 8, :]
                else:
                    above = base + ny + cy
                    below = base - 8 + cy
                    value = jnp.where(
                        sub < 4, ext[g, above : above + 8, :], ext[g, below : below + 8, :]
                    )
                acc[t] = jnp.where(mask, turn(value, -4 * cx), acc[t])
        packed.append(acc)
        for t in range(tiles + 1):
            row = (g * (tiles + 1) + t) * 8
            zown_ref[row : row + 8, :] = acc[t]
    up_first = parity("gz") == 0
    even_lane = lane % 2 == 0
    for t in range(tiles + 1):
        two, three = packed[2][t], packed[3][t]
        up = (packed[0][t], jnp.where(even_lane, two, pltpu.roll(three, 1, 1)))
        down = (packed[1][t], jnp.where(even_lane, pltpu.roll(two, nz - 1, 1), three))
        for g in range(2):
            row = (g * (tiles + 1) + t) * 8
            za_ref[row : row + 8, :] = jnp.where(up_first, up[g], down[g])
            zb_ref[row : row + 8, :] = jnp.where(up_first, down[g], up[g])
    drag = cols_ref[4 * ny :] + y_ref[2 * y_block :]
    for x_ref, c_ref in ((xa_ref, ya_ref), (xc_ref, yb_ref)):
        drag = drag + (x_ref[x_ref.shape[0] - 8 :] + c_ref[2 * corner_block :])
    drag_ref[...] = drag


OUT_GROUPS = ((0, 7), (7, 13), (13, 17), (17, 19))


def turn(value, shift):
    nz = value.shape[1]
    return pltpu.roll(value, shift % nz, 1) if shift % nz else value


def z_shifted(value, cz):
    return turn(value, -cz) if cz else value


def inner_kernel(
    states_ref,
    adj_ref,
    ub_ref,
    xa_ref,
    xb_ref,
    y_ref,
    ya_ref,
    yb_ref,
    out_ref,
    grad1_ref,
    grad_ref,
    pack_ref,
    f0_ref,
    f1_ref,
    ext,
    mid,
):
    nx, ny, nz = grad_ref.shape
    tiles = ny // 8
    lane = lax.broadcasted_iota(jnp.int32, (8, nz), 1)
    slot = lane // 4
    sub = lax.broadcasted_iota(jnp.int32, (8, nz), 0)
    even_x = parity("gx") == 0
    even_y = parity("gy") == 0
    base = 16

    for q in range(NSLOT):
        for x in range(nx):
            ext[q, x + 2, base : base + ny, :] = (
                adj_ref[q, x] if q < 19 else ub_ref[q - 19, x]
            )
    planes = {1: (nx + 2, nx + 3), -1: (1, 0)}
    lines = {1: (base + ny, base + ny + 1), -1: (base - 1, base - 2)}
    for sign in (1, -1):
        first, second = (xa_ref, xb_ref) if sign > 0 else (xb_ref, xa_ref)
        for names, depth, offset in ((near(0, sign), 0, 0), (far(0, sign), 1, 18)):
            for k, q in enumerate(names):
                rows = slice((k + offset) * ny, (k + offset + 1) * ny)
                ext[q, planes[sign][depth], base : base + ny, :] = jnp.where(
                    even_x, first[rows], second[rows]
                )
        block = y_rows(nx) + EDGE_ROWS
        first, second = (0, block) if sign > 0 else (block, 0)
        for names, depth, offset in ((near(1, sign), 0, 0), (far(1, sign), 1, 18)):
            line = lines[sign][depth]
            for k, q in enumerate(names):
                row = (k + offset) * nx
                got = jnp.where(
                    even_y,
                    y_ref[first + row : first + row + nx],
                    y_ref[second + row : second + row + nx],
                )
                for x in range(nx):
                    ext[q, x + 2, line : line + 1, :] = got[x : x + 1]
        for sx in (1, -1):
            xs = (ya_ref, yb_ref) if sx > 0 else (yb_ref, ya_ref)
            block = CORNER + EDGE_ROWS
            ys = (0, block) if sign > 0 else (block, 0)
            low, high = [
                jnp.where(even_x, xs[0][r : r + CORNER], xs[1][r : r + CORNER])
                for r in ys
            ]
            got = jnp.where(even_y, low, high)
            for k, (q, dx, dy) in enumerate(corner_rows(sx, sign)):
                line = lines[sign][dy]
                ext[q, planes[sx][dx], line : line + 1, :] = got[k : k + 1]

    def near_cells(q, plane, t, cy):
        if t < tiles:
            row = base + 8 * t + cy
            return ext[q, plane, row : row + 8, :]
        above = base + ny + cy
        below = base - 8 + cy
        return jnp.where(
            sub < 4, ext[q, plane, above : above + 8, :], ext[q, plane, below : below + 8, :]
        )

    def first_level(p, t, kinds):
        got = []
        for i in range(19):
            cx, cy, cz = VEL[i]
            got.append(z_shifted(near_cells(i, p + 1 + cx, t, cy), cz))
        ub = [near_cells(19 + k, p + 1, t, 0) for k in range(4)]
        out, kept = adjoint_cell(got, ub[:3], ub[3], 1.0)
        for i in kinds:
            if t < tiles:
                mid[i, p, t * 8 + 8 : t * 8 + 16, :] = out[i]
            elif VEL[i][1] > 0:
                mid[i, p, t * 8 + 8 : t * 8 + 16, :] = out[i]
            elif VEL[i][1] < 0:
                mid[i, p, 0:8, :] = out[i]
        return kept, ub[:3]

    def inside(x, carry):
        for t in range(tiles):
            kept, u = first_level(x + 1, t, range(19))
            rows = slice(t * 8, t * 8 + 8)
            f0, fs, fd, fm, _ = state_of(states_ref, (1, x, rows))
            grad1_ref[x, rows, :] = gradient_cell(kept, f0, fs, fd, fm, u)
        return carry

    lax.fori_loop(0, nx, inside, 0)
    for t in range(tiles):
        first_level(0, t, far(0, -1))
        first_level(nx + 1, t, far(0, 1))

    def rim(n, carry):
        for p in (2 * n, 2 * n + 1):
            first_level(p, tiles, far(1, -1) + far(1, 1))
        return carry

    lax.fori_loop(0, (nx + 2) // 2, rim, 0)

    def second_level(x, carry):
        for t in range(tiles):
            rows = slice(t * 8, t * 8 + 8)
            got = []
            for i in range(19):
                cx, cy, cz = VEL[i]
                low = 8 + 8 * t + cy
                value = z_shifted(mid[i, x + 1 + cx, low : low + 8, :], cz)
                got.append(value)
                pack_ref[i, rows, :] = jnp.where(
                    slot == x, pltpu.roll(value, 4 * x + 2, 1), pack_ref[i, rows, :]
                )
            f0, fs, fd, fm, u = state_of(states_ref, (0, x, rows))
            b = ub_ref[3, x, rows, :]
            out, kept = adjoint_cell(got, u, b, 1.0)
            for i in range(19):
                out_ref[i, x, rows, :] = out[i]
            grad_ref[x, rows, :] = grad1_ref[x, rows, :] + gradient_cell(
                kept, f0, fs, fd, fm, u
            )
        return carry

    lax.fori_loop(0, nx, second_level, 0)

    def tile(t, carry):
        rows = pl.ds(pl.multiple_of(t * 8, 8), 8)
        for i in range(20):
            for out_ref, level, first in ((f0_ref, 0, 0), (f1_ref, 1, 2)):
                if i == 19 and level == 1:
                    continue
                acc = jnp.zeros((8, nz), jnp.float32)
                for x in range(nx):
                    value = (
                        states_ref[level, i, x, rows, :]
                        if i < 19
                        else ub_ref[3, x, rows, :]
                    )
                    p = x + first
                    acc = jnp.where(slot == p, pltpu.roll(value, 4 * p + 2, 1), acc)
                out_ref[i, rows, :] = acc
        return carry

    lax.fori_loop(0, ny // 8, tile, 0)


def edge_kernel(
    mask_ref,
    zown_ref,
    za_ref,
    zb_ref,
    pack_ref,
    f0_ref,
    f1_ref,
    inner_ref,
    grad1_ref,
    inner_grad_ref,
    out_hbm,
    grad_hbm,
    tail_ref,
    first_ref,
    second_ref,
    zmid,
    zout,
    out_ref,
    grad_ref,
    sems,
):
    nx, ny, nz = mask_ref.shape
    tiles = ny // 8
    height = (tiles + 1) * 8
    even = parity("gz") == 0
    lane = lax.broadcasted_iota(jnp.int32, (8, nz), 1)
    even_lane = lane % 2 == 0
    low_pair = lane % 4 < 2

    last = slice(2 * height, 2 * height + 8)
    tail_ref[...] = za_ref[last] + zb_ref[last]

    def swapped(value):
        return jnp.where(even_lane, turn(value, -1), turn(value, 1))

    for t in range(tiles + 1):
        received = []
        for g in range(2):
            row = (g * (tiles + 1) + t) * 8
            va = za_ref[row : row + 8, :]
            vb = zb_ref[row : row + 8, :]
            received.append((jnp.where(even, va, vb), jnp.where(even, vb, va)))
        (high0, low0), (high1, low1) = received
        for g in range(4):
            row = (g * (tiles + 1) + t) * 8
            rows = slice(row, row + 8)
            own = zown_ref[rows]
            if g == 0:
                head, tail = own, low0
            elif g == 1:
                head, tail = high0, own
            elif g == 2:
                head = jnp.where(even_lane, own, turn(high1, 1))
                tail = jnp.where(even_lane, low1, own)
            else:
                head = jnp.where(even_lane, own, high1)
                tail = jnp.where(even_lane, turn(low1, -1), own)
            head = swapped(head)
            tail = swapped(tail)
            first_ref[rows] = jnp.where(low_pair, head, turn(tail, 2))
            second_ref[rows] = jnp.where(low_pair, turn(head, -2), tail)

    slab_grad = []
    for t in range(tiles + 1):
        got = []
        for q in range(NSLOT):
            g, k = ZSLOT[q]
            row = g * height + t * 8
            ref = second_ref if k % 2 else first_ref
            got.append(turn(ref[row : row + 8, :], -32 * (k // 2)))
        out, kept = adjoint_cell(got[:19], got[19:22], got[22], 1.0)
        for i in range(19):
            zmid[i, 8 * t + 8 : 8 * t + 16, :] = out[i]
            if t == tiles:
                zmid[i, 0:8, :] = out[i]
        if t < tiles:
            f = [f1_ref[i, 8 * t : 8 * t + 8, :] for i in range(19)]
            fs, fd = pairs_of(f)
            fm = moments(f[0], fs, fd)
            grad = gradient_cell(kept, f[0], fs, fd, fm, got[19:22])
            slab_grad.append(turn(grad, -8))

    at = lane % 4
    for t in range(tiles):
        rows = slice(8 * t, 8 * t + 8)
        got = []
        for i in range(19):
            cx, cy, cz = VEL[i]
            value = pack_ref[i, rows, :]
            edge = zmid[i, 8 + 8 * t + cy : 16 + 8 * t + cy, :]
            back = -4 * (2 + cx)
            if cz == 0:
                value = jnp.where((at == 1) | (at == 2), turn(edge, back), value)
            else:
                near_lane = 2 if cz < 0 else 0
                value = jnp.where(at == near_lane, turn(edge, back - 1), value)
                value = jnp.where(at == near_lane + 1, turn(edge, back + 1), value)
            got.append(value)
        f = [f0_ref[i, rows, :] for i in range(19)]
        fs, fd = pairs_of(f)
        fm = moments(f[0], fs, fd)
        inverse = 1.0 / fm["total"]
        u = [one * inverse for one in fm["one"]]
        out, kept = adjoint_cell(got, u, f0_ref[19, rows, :], 1.0)
        for i in range(19):
            zout[i, rows, :] = out[i]
        zout[19, rows, :] = gradient_cell(kept, f[0], fs, fd, fm, u)
        zout[20, rows, :] = slab_grad[t]

    def out_copy(k):
        part = slice(*OUT_GROUPS[k])
        return pltpu.make_async_copy(out_ref.at[part], out_hbm.at[part], sems.at[k])

    outer = (lane < 2) | (lane >= nz - 2)
    ends = (lane < 1) | (lane >= nz - 1)
    for x in range(nx):
        for t in range(tiles):
            rows = slice(8 * t, 8 * t + 8)
            level1 = jnp.where(
                ends, turn(zout[20, rows, :], -2 - 4 * x), grad1_ref[x, rows, :]
            )
            edge = turn(zout[19, rows, :], -2 - 4 * x) + level1
            grad = jnp.where(outer, edge, inner_grad_ref[x, rows, :])
            grad_ref[x, rows, :] = jnp.where(mask_ref[x, rows, :] == 0, grad, 0.0)
    grad_copy = pltpu.make_async_copy(grad_ref, grad_hbm, sems.at[len(OUT_GROUPS)])
    grad_copy.start()
    for k, group in enumerate(OUT_GROUPS):
        for i in range(*group):
            for x in range(nx):
                for t in range(tiles):
                    rows = slice(8 * t, 8 * t + 8)
                    out_ref[i, x, rows, :] = jnp.where(
                        outer,
                        turn(zout[i, rows, :], -2 - 4 * x),
                        inner_ref[i, x, rows, :],
                    )
        out_copy(k).start()
    grad_copy.wait()
    for k in range(len(OUT_GROUPS)):
        out_copy(k).wait()


def drag_kernel(whole_cells, *refs):
    total = refs[0][...]
    for ref in refs[1:-1]:
        total = total + ref[...]
    summed = jnp.sum(jnp.sum(total, axis=1, keepdims=True), axis=0, keepdims=True)
    refs[-1][...] = summed / whole_cells


def swaps(count):
    first = [(i, i ^ 1) for i in range(count)]
    second = [(i, (((i + 1) % count) ^ 1) - 1) for i in range(count)]
    second = [(i, j % count) for i, j in second]
    return first, second


VMEM = pl.BlockSpec(memory_space=pltpu.VMEM)
HBM = pl.BlockSpec(memory_space=pltpu.HBM)
PARAMS = pltpu.CompilerParams(vmem_limit_bytes=48 * 2**20)


def call(kernel, inputs, shapes, scratch=(), space=VMEM, micros=1, outs=None):
    if space is HBM:
        inputs = [pltpu.with_memory_space_constraint(x, pltpu.HBM) for x in inputs]
    return pl.pallas_call(
        kernel,
        out_shape=[jax.ShapeDtypeStruct(s, jnp.float32) for s in shapes],
        in_specs=[space] * len(inputs),
        out_specs=outs or [VMEM] * len(shapes),
        scratch_shapes=list(scratch),
        compiler_params=PARAMS,
        cost_estimate=pl.CostEstimate(
            flops=0, bytes_accessed=int(3.6e6 * micros), transcendentals=0
        ),
    )(*inputs)


def body(primal_states, adjoint_last, porosity, solid_mask):
    nx, ny, nz = porosity.shape
    gx, gy, gz = [lax.axis_size(axis) for axis in AXES]
    x_first, x_second = swaps(gx)
    y_first, y_second = swaps(gy)
    z_first, z_second = swaps(gz)
    tiles = ny // 8
    height = (tiles + 1) * 8
    f32 = jnp.float32

    def diagonal(message, x_pairs, y_pairs):
        pairs = [(a * gy + c, b * gy + d) for a, b in x_pairs for c, d in y_pairs]
        return lax.ppermute(message, ("gx", "gy"), pairs)

    rows_x = NSLOT * ny + 8
    rows_y = 2 * (y_rows(nx) + EDGE_ROWS) + 8
    rows_c = 2 * (CORNER + EDGE_ROWS) + 8
    rows_z = 2 * height + 8
    rides = (gx, gy, gz) == (4, 2, 4)
    xa, xb, ub, drag = call(
        pack_x_kernel,
        (primal_states, adjoint_last, porosity, solid_mask),
        [(rows_x, nz), (rows_x, nz), (4, nx, ny, nz), (8, nz)],
        [
            pltpu.VMEM((2, 19, nx, ny, nz), f32),
            pltpu.VMEM((19, nx, ny, nz), f32),
            pltpu.VMEM((nx, ny, nz), f32),
            pltpu.VMEM((nx, ny, nz), jnp.int32),
            pltpu.SemaphoreType.DMA((6,)),
        ],
        HBM,
    )
    cols, y, ya, yb = call(
        pack_y_kernel,
        (adjoint_last, ub, drag),
        [(4 * ny + 8, nz), (rows_y, nz), (rows_c, nz), (rows_c, nz)],
        micros=4,
    )
    xc = lax.ppermute(cols, "gx", x_second)
    xa = lax.ppermute(xa, "gx", x_first)
    if gy == 2:
        y = lax.ppermute(y, "gy", y_first)
        yb = diagonal(yb, x_second, y_first)
        ya = diagonal(ya, x_first, y_first)
    else:

        def both(message, block, send):
            parts = [message[:block], message[block : 2 * block], message[2 * block :]]
            return jnp.concatenate(
                [send(parts[0], y_first), send(parts[1], y_second), parts[2]]
            )

        block = y_rows(nx) + EDGE_ROWS
        y = both(y, block, lambda m, pairs: lax.ppermute(m, "gy", pairs))
        block = CORNER + EDGE_ROWS
        yb = both(yb, block, lambda m, pairs: diagonal(m, x_second, pairs))
        ya = both(ya, block, lambda m, pairs: diagonal(m, x_first, pairs))
    xb, yb = lax.optimization_barrier((xb, yb))
    xb = lax.ppermute(xb, "gx", x_second)

    zown, za, zb, drag_xy = call(
        pack_z_kernel,
        (cols, xa, xc, y, ya, yb),
        [(4 * height, nz), (rows_z, nz), (rows_z, nz), (8, nz)],
        [pltpu.VMEM((4, ny + 32, nz), f32)],
    )
    if rides:
        second = xc[4 * ny :] + yb[rows_c - 8 :]
        drag_xy = drag_xy + lax.ppermute(second, "gx", x_first)
        za = za.at[2 * height :].set(drag_xy)
        zb = zb.at[2 * height :].set(drag_xy)
    zb = lax.ppermute(zb, "gz", z_second)
    za = lax.ppermute(za, "gz", z_first)
    inner, grad1, inner_grad, pack, f0, f1 = call(
        inner_kernel,
        (primal_states, adjoint_last, ub, xa, xb, y, ya, yb),
        [
            (19, nx, ny, nz),
            (nx, ny, nz),
            (nx, ny, nz),
            (19, ny, nz),
            (20, ny, nz),
            (19, ny, nz),
        ],
        [
            pltpu.VMEM((NSLOT, nx + 4, ny + 32, nz), f32),
            pltpu.VMEM((19, nx + 2, height + 8, nz), f32),
        ],
        micros=4,
    )
    if rides:
        zhalf = lax.ppermute(drag_xy, "gz", [(i, i ^ 2) for i in range(gz)])
        drags = (drag_xy, zhalf)
    else:
        drags = (lax.psum(drag, AXES),)

    first, gradient, tails = call(
        edge_kernel,
        (solid_mask, zown, za, zb, pack, f0, f1, inner, grad1, inner_grad),
        [(19, nx, ny, nz), (nx, ny, nz), (8, nz)],
        [
            pltpu.VMEM((4 * height, nz), f32),
            pltpu.VMEM((4 * height, nz), f32),
            pltpu.VMEM((19, height + 8, nz), f32),
            pltpu.VMEM((21, ny, nz), f32),
            pltpu.VMEM((19, nx, ny, nz), f32),
            pltpu.VMEM((nx, ny, nz), f32),
            pltpu.SemaphoreType.DMA((len(OUT_GROUPS) + 1,)),
        ],
        outs=[HBM, HBM, VMEM],
    )
    if rides:
        drags += (tails,)
    whole_cells = float(nx * ny * nz * gx * gy * gz)
    (drag,) = call(functools.partial(drag_kernel, whole_cells), drags, [(1, 1)])
    return (first, gradient, drag.reshape(()))


def solution(mesh):
    return jax.shard_map(
        body,
        mesh=mesh,
        in_specs=(
            P(None, None, "gx", "gy", "gz"),
            P(None, "gx", "gy", "gz"),
            P("gx", "gy", "gz"),
            P("gx", "gy", "gz"),
        ),
        out_specs=(P(None, "gx", "gy", "gz"), P("gx", "gy", "gz"), P()),
        check_vma=False,
    )
```

```python
import functools

import jax
import jax.numpy as jnp
import numpy as np
from jax import lax
from jax.experimental import pallas as pl
from jax.experimental.pallas import tpu as pltpu
from jax.sharding import PartitionSpec as P

VEL = (
    (0, 0, 0),
    (1, 0, 0),
    (-1, 0, 0),
    (0, 1, 0),
    (0, -1, 0),
    (0, 0, 1),
    (0, 0, -1),
    (1, 1, 0),
    (-1, -1, 0),
    (1, -1, 0),
    (-1, 1, 0),
    (1, 0, 1),
    (-1, 0, -1),
    (1, 0, -1),
    (-1, 0, 1),
    (0, 1, 1),
    (0, -1, -1),
    (0, 1, -1),
    (0, -1, 1),
)
PAIRS = tuple((i, i + 1) for i in range(1, 19, 2))
AXES = ("gx", "gy", "gz")
UB = (19, 20, 21, 22)


def near(axis, sign):
    return tuple(i for i in range(19) if VEL[i][axis] * sign >= 0) + UB


def far(axis, sign):
    return tuple(i for i in range(19) if VEL[i][axis] == sign)


NSLOT = 23
CORNER = 24
EDGE_ROWS = 8


def y_rows(nx):
    return -(-NSLOT * nx // 8) * 8


ZGROUPS = (
    tuple(i for i in range(19) if VEL[i][2] == -1),
    tuple(i for i in range(19) if VEL[i][2] == 1),
    tuple(i for i in range(19) if VEL[i][2] == 0)[:8],
    tuple(i for i in range(19) if VEL[i][2] == 0)[8:] + UB,
)
ZSLOT = {q: (g, k) for g, group in enumerate(ZGROUPS) for k, q in enumerate(group)}


def pairs_of(values):
    s = [values[a] + values[b] for a, b in PAIRS]
    d = [values[a] - values[b] for a, b in PAIRS]
    return s, d


def moments(v0, s, d):
    sx, sy, sz, sp, sq, sr, ss, st, su = s
    dx, dy, dz, dp, dq, dr, ds, dt, du = d
    ex = sp + sq
    ez = sr + ss
    ey = st + su
    faces = sx + sy + sz
    edges = ex + ez + ey
    exx = ex + ez
    eyy = ex + ey
    ezz = ez + ey
    fx = (dp + dq) + (dr + ds)
    fy = (dp - dq) + (dt + du)
    fz = (dr - ds) + (dt - du)
    return dict(
        rest=v0,
        faces=faces,
        edges=edges,
        total=v0 + faces + edges,
        face1=(dx, dy, dz),
        edge1=(fx, fy, fz),
        one=(dx + fx, dy + fy, dz + fz),
        face2=(sx, sy, sz),
        edge2=(exx, eyy, ezz),
        two=(sx + exx, sy + eyy, sz + ezz),
        cross=(sp - sq, sr - ss, st - su),
    )


def adjoint_cell(g, u, b, drive):
    s, d = pairs_of(g)
    m = moments(g[0], s, d)
    total = m["total"]
    trace = m["faces"] + 2.0 * m["edges"] - (30.0 / 19.0) * total
    p0 = (-1.2 / 19.0) * total - (2.0 / 21.0) * trace
    q = [
        (0.4 / 6.0) * (two - (10.0 / 19.0) * total) + (0.8 / 21.0) * trace
        for two in m["two"]
    ]
    qsum = q[0] + q[1] + q[2]
    qab = [0.1 * c for c in m["cross"]]
    p1 = [-0.12 * one for one in m["one"]]
    h0 = (
        0.4 * m["rest"]
        + (1.2 / 18.0) * m["faces"]
        + (1.2 / 36.0) * m["edges"]
        + p0
        + (1.0 / 3.0) * qsum
    )
    h1 = [
        (1.2 / 18.0) * f + (1.2 / 36.0) * e + (1.0 / 3.0) * p
        for f, e, p in zip(m["face1"], m["edge1"], p1)
    ]
    base = (1.0 / 3.0) * p0 + (1.0 / 9.0) * qsum
    haa = [
        (1.2 / 18.0) * f + (1.2 / 36.0) * e + (2.0 / 9.0) * qa + base
        for f, e, qa in zip(m["face2"], m["edge2"], q)
    ]
    hxy, hxz, hyz = [(2.0 / 45.0) * c for c in m["cross"]]
    ux, uy, uz = u
    v = (
        haa[0] * ux + hxy * uy + hxz * uz,
        hxy * ux + haa[1] * uy + hyz * uz,
        hxz * ux + hyz * uy + haa[2] * uz,
    )
    uv = ux * v[0] + uy * v[1] + uz * v[2]
    uu = ux * ux + uy * uy + uz * uz
    uuh = 1.5 * uu * h0
    a = h0 + uuh - 4.5 * uv
    nb = 1.0 - b
    e0 = nb * (a - p0)
    nq = [nb * x for x in q]
    nxy, nxz, nyz = [nb * x for x in qab]
    o = [
        nb * (3.0 * h1[k] + 9.0 * v[k] - 3.0 * u[k] * h0 - p1[k]) for k in range(3)
    ]
    o[0] = o[0] + b * drive
    alpha = -0.2 * nb
    half_s = 0.5 * (alpha + b)
    half_d = 0.5 * (alpha - b)
    exy = e0 - nq[0] - nq[1]
    exz = e0 - nq[0] - nq[2]
    eyz = e0 - nq[1] - nq[2]
    even = (
        e0 - nq[0],
        e0 - nq[1],
        e0 - nq[2],
        exy - nxy,
        exy + nxy,
        exz - nxz,
        exz + nxz,
        eyz - nyz,
        eyz + nyz,
    )
    odd = (
        o[0],
        o[1],
        o[2],
        o[0] + o[1],
        o[0] - o[1],
        o[0] + o[2],
        o[0] - o[2],
        o[1] + o[2],
        o[1] - o[2],
    )
    out = [(alpha + b) * g[0] + e0]
    for k in range(9):
        even_k = half_s * s[k] + even[k]
        odd_k = half_d * d[k] + odd[k]
        out.append(even_k + odd_k)
        out.append(even_k - odd_k)
    kept = dict(
        s=s, d=d, g0=g[0], p0=p0, p1=p1, q=q, qab=qab, h0=h0, h1=h1, uv=uv, uuh=uuh
    )
    return out, kept


def gradient_cell(kept, f0, fs, fd, fm, u):
    rho = fm["total"]
    even = fs[0] * kept["s"][0]
    odd = fd[0] * kept["d"][0]
    for k in range(1, 9):
        even = even + fs[k] * kept["s"][k]
        odd = odd + fd[k] * kept["d"][k]
    hf = kept["p0"] * rho
    for k in range(3):
        hf = hf + kept["p1"][k] * fm["one"][k] + kept["q"][k] * fm["two"][k]
        hf = hf + kept["qab"][k] * fm["cross"][k]
    uh1 = u[0] * kept["h1"][0] + u[1] * kept["h1"][1] + u[2] * kept["h1"][2]
    hfeq = rho * (kept["h0"] - kept["uuh"] + 3.0 * uh1 + 4.5 * kept["uv"])
    pairs = 1.2 * f0 * kept["g0"] + 0.6 * even - 0.4 * odd
    return pairs + hf - hfeq + fm["one"][0]


def state_of(ref, index):
    f = [ref[(index[0], i) + index[1:]] for i in range(19)]
    s, d = pairs_of(f)
    m = moments(f[0], s, d)
    inverse = 1.0 / m["total"]
    u = [one * inverse for one in m["one"]]
    return f[0], s, d, m, u


def corner_rows(sx, sy):
    rows = []
    for dx, dy in ((0, 0), (1, 0), (0, 1), (1, 1)):
        for i in near(0, sx) if dx == 0 else far(0, sx):
            if i in (near(1, sy) if dy == 0 else far(1, sy)):
                rows.append((i, dx, dy))
    return rows


def parity(axis):
    return lax.axis_index(axis) % 2


def cell_rows(adj_ref, ub_ref, q, x, rows):
    return adj_ref[q, x, rows, :] if q < 19 else ub_ref[q - 19, x, rows, :]


def state_kernel(
    states_hbm,
    por_hbm,
    mask_hbm,
    ub_ref,
    drag_ref,
    states_ref,
    por_ref,
    mask_ref,
    sems,
):
    nx, ny, nz = por_ref.shape
    tiles = ny // 8
    copies = [
        pltpu.make_async_copy(src, dst, sems.at[k])
        for k, (src, dst) in enumerate(
            (
                (states_hbm.at[1], states_ref.at[1]),
                (por_hbm, por_ref),
                (mask_hbm, mask_ref),
                (states_hbm.at[0, 1:3], states_ref.at[0, 1:3]),
                (states_hbm.at[0, 7:15], states_ref.at[0, 7:15]),
            )
        )
    ]
    for copy in copies:
        copy.start()
    for copy in copies[:3]:
        copy.wait()

    def cells(x, carry):
        for t in range(tiles):
            rows = slice(8 * t, 8 * t + 8)
            blocking = jnp.where(mask_ref[x, rows, :] == 0, por_ref[x, rows, :], 1.0)
            f0, s, d, m, u = state_of(states_ref, (1, x, rows))
            for k in range(3):
                ub_ref[k, x, rows, :] = u[k]
            ub_ref[3, x, rows, :] = blocking
            carry = carry + blocking * m["one"][0]
        return carry

    drag = lax.fori_loop(0, nx, cells, jnp.zeros((8, nz), jnp.float32))
    for copy in copies[3:]:
        copy.wait()

    def flux_cells(x, carry):
        for t in range(tiles):
            rows = slice(8 * t, 8 * t + 8)
            flux = 0.0
            for a, b in PAIRS:
                if VEL[a][0]:
                    flux = flux + (
                        states_ref[0, a, x, rows, :] - states_ref[0, b, x, rows, :]
                    )
            carry = carry + ub_ref[3, x, rows, :] * flux
        return carry

    drag = lax.fori_loop(0, nx, flux_cells, drag)
    drag_ref[...] = drag


def pack_x_kernel(adj_ref, ub_ref, drag_ref, a_ref, b_ref):
    nx, ny = adj_ref.shape[1:3]
    drag = drag_ref[...]
    a_ref[NSLOT * ny :] = drag
    b_ref[NSLOT * ny :] = drag

    def fill_x(out_ref, sign):
        for names, offset, x in (
            (near(0, sign), 0, 0 if sign > 0 else nx - 1),
            (far(0, sign), 18, 1 if sign > 0 else nx - 2),
        ):
            for k, q in enumerate(names):
                k += offset
                out_ref[k * ny : (k + 1) * ny] = cell_rows(
                    adj_ref, ub_ref, q, x, slice(0, ny)
                )

    for px in (0, 1):

        @pl.when(parity("gx") == px)
        def _():
            sa = 1 if px else -1
            fill_x(a_ref, sa)
            fill_x(b_ref, -sa)


def column_pair(acc, value, pair, q, k, plane):
    start = 32 * (k // 2) + 4 * plane + 2 * (k % 2)
    cz = VEL[q][2] if q < 19 else 0
    return jnp.where(pair == start // 2, turn(value, start + 1 - cz), acc)


def pack_y_kernel(
    adj_ref, ub_ref, drag_ref, cols_ref, y_ref, ya_ref, yb_ref
):
    nx, ny, nz = adj_ref.shape[1:]
    pair = lax.broadcasted_iota(jnp.int32, (8, nz), 1) // 2
    for g, group in enumerate(ZGROUPS):
        for t in range(ny // 8):
            acc = jnp.zeros((8, nz), jnp.float32)
            for k, q in enumerate(group):
                for x in range(nx):
                    value = cell_rows(adj_ref, ub_ref, q, x, slice(8 * t, 8 * t + 8))
                    acc = column_pair(acc, value, pair, q, k, x + 2)
            row = g * ny + 8 * t
            cols_ref[row : row + 8] = acc
    y_block = y_rows(nx) + EDGE_ROWS
    corner_block = CORNER + EDGE_ROWS

    def fill_edges(place, sign):
        for g in range(4):
            for d in range(2):
                y = d if sign > 0 else ny - 1 - d
                line = cols_ref[g * ny + y : g * ny + y + 1]
                row = place * y_block + y_rows(nx) + 2 * g + d
                y_ref[row : row + 1] = line
                row = place * corner_block + CORNER + 2 * g + d
                ya_ref[row : row + 1] = line
                yb_ref[row : row + 1] = line

    def fill_y(place, sign):
        for names, offset, y in (
            (near(1, sign), 0, 0 if sign > 0 else ny - 1),
            (far(1, sign), 18, 1 if sign > 0 else ny - 2),
        ):
            for k, q in enumerate(names):
                for x in range(nx):
                    row = place * y_block + (k + offset) * nx + x
                    y_ref[row : row + 1] = cell_rows(
                        adj_ref, ub_ref, q, x, slice(y, y + 1)
                    )

    def fill_corner(out_ref, place, sx, sy):
        names = corner_rows(sx, sy)
        for k, (q, dx, dy) in enumerate(names):
            x = dx if sx > 0 else nx - 1 - dx
            y = dy if sy > 0 else ny - 1 - dy
            row = place * corner_block + k
            out_ref[row : row + 1] = cell_rows(adj_ref, ub_ref, q, x, slice(y, y + 1))
        row = place * corner_block + len(names)
        last = place * corner_block + CORNER
        out_ref[row:last] = jnp.zeros((last - row, nz), jnp.float32)

    drag = drag_ref[...]
    cols_ref[4 * ny :] = drag
    y_ref[2 * y_block :] = drag
    ya_ref[2 * corner_block :] = drag
    yb_ref[2 * corner_block :] = drag
    for py in (0, 1):

        @pl.when(parity("gy") == py)
        def _():
            s0 = 1 if py else -1
            fill_y(0, s0)
            fill_y(1, -s0)
            fill_edges(0, s0)
            fill_edges(1, -s0)

    for px in (0, 1):
        for py in (0, 1):

            @pl.when((parity("gx") == px) & (parity("gy") == py))
            def _():
                sa = 1 if px else -1
                s0 = 1 if py else -1
                for out_ref, sx in ((ya_ref, sa), (yb_ref, -sa)):
                    fill_corner(out_ref, 0, sx, s0)
                    fill_corner(out_ref, 1, sx, -s0)


def pack_z_kernel(
    cols_ref,
    xa_ref,
    xc_ref,
    y_ref,
    ya_ref,
    yb_ref,
    zown_ref,
    za_ref,
    zb_ref,
    drag_ref,
    ext,
):
    ny = (cols_ref.shape[0] - 8) // 4
    nz = cols_ref.shape[1]
    tiles = ny // 8
    base = 16
    even_x = parity("gx") == 0
    even_y = parity("gy") == 0
    lane = lax.broadcasted_iota(jnp.int32, (8, nz), 1)
    sub = lax.broadcasted_iota(jnp.int32, (8, nz), 0)
    plane = (lane % 32) // 4
    slot = 2 * (lane // 32) + (lane % 4) // 2

    def along_x(own, va, vb):
        low = turn(jnp.where(even_x, vb, va), -16)
        high = turn(jnp.where(even_x, va, vb), 16)
        return jnp.where(plane < 2, low, jnp.where(plane > 5, high, own))

    pair = lane // 2

    def fill_main(sign):
        halo = {}
        for names, offset, p in (
            (near(0, sign), 0, 6 if sign > 0 else 1),
            (far(0, sign), 18, 7 if sign > 0 else 0),
        ):
            for k, q in enumerate(names):
                halo.setdefault(q, []).append((k + offset, p))
        for g, group in enumerate(ZGROUPS):
            for t in range(tiles):
                rows = slice(g * ny + 8 * t, g * ny + 8 * t + 8)
                acc = jnp.where(
                    plane < 2 if sign > 0 else plane > 5,
                    turn(xc_ref[rows], -16 * sign),
                    cols_ref[rows],
                )
                for k, q in enumerate(group):
                    for at, p in halo.get(q, ()):
                        row = at * ny + 8 * t
                        acc = column_pair(acc, xa_ref[row : row + 8], pair, q, k, p)
                ext[g, base + 8 * t : base + 8 * t + 8, :] = acc

    @pl.when(parity("gx") == 0)
    def _():
        fill_main(1)

    @pl.when(parity("gx") == 1)
    def _():
        fill_main(-1)

    y_block = (y_ref.shape[0] - 8) // 2
    corner_block = CORNER + EDGE_ROWS

    def edges(ref, block, place):
        return ref[(place + 1) * block - EDGE_ROWS : (place + 1) * block]

    first, second = [
        along_x(
            edges(y_ref, y_block, place),
            edges(ya_ref, corner_block, place),
            edges(yb_ref, corner_block, place),
        )
        for place in range(2)
    ]
    high = jnp.where(even_y, first, second)
    low = jnp.where(even_y, second, first)
    for g in range(4):
        for d in range(2):
            row = 2 * g + d
            ext[g, base + ny + d : base + ny + d + 1, :] = high[row : row + 1]
            ext[g, base - 1 - d : base - d, :] = low[row : row + 1]

    packed = []
    for g, group in enumerate(ZGROUPS):
        moves = {}
        for k, q in enumerate(group):
            cx, cy, _ = VEL[q] if q < 19 else (0, 0, 0)
            moves.setdefault((cx, cy), []).append(k)
        acc = [jnp.zeros((8, nz), jnp.float32) for t in range(tiles + 1)]
        for (cx, cy), slots in moves.items():
            mask = slot == slots[0]
            for k in slots[1:]:
                mask = mask | (slot == k)
            for t in range(tiles + 1):
                if t < tiles:
                    row = base + 8 * t + cy
                    value = ext[g, row : row + 8, :]
                else:
                    above = base + ny + cy
                    below = base - 8 + cy
                    value = jnp.where(
                        sub < 4, ext[g, above : above + 8, :], ext[g, below : below + 8, :]
                    )
                acc[t] = jnp.where(mask, turn(value, -4 * cx), acc[t])
        packed.append(acc)
        for t in range(tiles + 1):
            row = (g * (tiles + 1) + t) * 8
            zown_ref[row : row + 8, :] = acc[t]
    up_first = parity("gz") == 0
    even_lane = lane % 2 == 0
    for t in range(tiles + 1):
        two, three = packed[2][t], packed[3][t]
        up = (packed[0][t], jnp.where(even_lane, two, pltpu.roll(three, 1, 1)))
        down = (packed[1][t], jnp.where(even_lane, pltpu.roll(two, nz - 1, 1), three))
        for g in range(2):
            row = (g * (tiles + 1) + t) * 8
            za_ref[row : row + 8, :] = jnp.where(up_first, up[g], down[g])
            zb_ref[row : row + 8, :] = jnp.where(up_first, down[g], up[g])
    drag = cols_ref[4 * ny :] + y_ref[2 * y_block :]
    for x_ref, c_ref in ((xa_ref, ya_ref), (xc_ref, yb_ref)):
        drag = drag + (x_ref[x_ref.shape[0] - 8 :] + c_ref[2 * corner_block :])
    drag_ref[...] = drag


OUT_GROUPS = ((0, 7), (7, 13), (13, 17), (17, 19))


def turn(value, shift):
    nz = value.shape[1]
    return pltpu.roll(value, shift % nz, 1) if shift % nz else value


def z_shifted(value, cz):
    return turn(value, -cz) if cz else value


def inner_kernel(
    states_ref,
    adj_ref,
    ub_ref,
    xa_ref,
    xb_ref,
    y_ref,
    ya_ref,
    yb_ref,
    out_ref,
    grad1_ref,
    grad_ref,
    pack_ref,
    f0_ref,
    f1_ref,
    ext,
    mid,
):
    nx, ny, nz = grad_ref.shape
    tiles = ny // 8
    lane = lax.broadcasted_iota(jnp.int32, (8, nz), 1)
    slot = lane // 4
    sub = lax.broadcasted_iota(jnp.int32, (8, nz), 0)
    even_x = parity("gx") == 0
    even_y = parity("gy") == 0
    base = 16

    for q in range(NSLOT):
        for x in range(nx):
            ext[q, x + 2, base : base + ny, :] = (
                adj_ref[q, x] if q < 19 else ub_ref[q - 19, x]
            )
    planes = {1: (nx + 2, nx + 3), -1: (1, 0)}
    lines = {1: (base + ny, base + ny + 1), -1: (base - 1, base - 2)}
    for sign in (1, -1):
        first, second = (xa_ref, xb_ref) if sign > 0 else (xb_ref, xa_ref)
        for names, depth, offset in ((near(0, sign), 0, 0), (far(0, sign), 1, 18)):
            for k, q in enumerate(names):
                rows = slice((k + offset) * ny, (k + offset + 1) * ny)
                ext[q, planes[sign][depth], base : base + ny, :] = jnp.where(
                    even_x, first[rows], second[rows]
                )
        block = y_rows(nx) + EDGE_ROWS
        first, second = (0, block) if sign > 0 else (block, 0)
        for names, depth, offset in ((near(1, sign), 0, 0), (far(1, sign), 1, 18)):
            line = lines[sign][depth]
            for k, q in enumerate(names):
                row = (k + offset) * nx
                got = jnp.where(
                    even_y,
                    y_ref[first + row : first + row + nx],
                    y_ref[second + row : second + row + nx],
                )
                for x in range(nx):
                    ext[q, x + 2, line : line + 1, :] = got[x : x + 1]
        for sx in (1, -1):
            xs = (ya_ref, yb_ref) if sx > 0 else (yb_ref, ya_ref)
            block = CORNER + EDGE_ROWS
            ys = (0, block) if sign > 0 else (block, 0)
            low, high = [
                jnp.where(even_x, xs[0][r : r + CORNER], xs[1][r : r + CORNER])
                for r in ys
            ]
            got = jnp.where(even_y, low, high)
            for k, (q, dx, dy) in enumerate(corner_rows(sx, sign)):
                line = lines[sign][dy]
                ext[q, planes[sx][dx], line : line + 1, :] = got[k : k + 1]

    def near_cells(q, plane, t, cy):
        if t < tiles:
            row = base + 8 * t + cy
            return ext[q, plane, row : row + 8, :]
        above = base + ny + cy
        below = base - 8 + cy
        return jnp.where(
            sub < 4, ext[q, plane, above : above + 8, :], ext[q, plane, below : below + 8, :]
        )

    def first_level(p, t, kinds):
        got = []
        for i in range(19):
            cx, cy, cz = VEL[i]
            got.append(z_shifted(near_cells(i, p + 1 + cx, t, cy), cz))
        ub = [near_cells(19 + k, p + 1, t, 0) for k in range(4)]
        out, kept = adjoint_cell(got, ub[:3], ub[3], 1.0)
        for i in kinds:
            if t < tiles:
                mid[i, p, t * 8 + 8 : t * 8 + 16, :] = out[i]
            elif VEL[i][1] > 0:
                mid[i, p, t * 8 + 8 : t * 8 + 16, :] = out[i]
            elif VEL[i][1] < 0:
                mid[i, p, 0:8, :] = out[i]
        return kept, ub[:3]

    def inside(x, carry):
        for t in range(tiles):
            kept, u = first_level(x + 1, t, range(19))
            rows = slice(t * 8, t * 8 + 8)
            f0, fs, fd, fm, _ = state_of(states_ref, (1, x, rows))
            grad1_ref[x, rows, :] = gradient_cell(kept, f0, fs, fd, fm, u)
        return carry

    lax.fori_loop(0, nx, inside, 0)
    for t in range(tiles):
        first_level(0, t, far(0, -1))
        first_level(nx + 1, t, far(0, 1))

    def rim(n, carry):
        for p in (2 * n, 2 * n + 1):
            first_level(p, tiles, far(1, -1) + far(1, 1))
        return carry

    lax.fori_loop(0, (nx + 2) // 2, rim, 0)

    def second_level(x, carry):
        for t in range(tiles):
            rows = slice(t * 8, t * 8 + 8)
            got = []
            for i in range(19):
                cx, cy, cz = VEL[i]
                low = 8 + 8 * t + cy
                value = z_shifted(mid[i, x + 1 + cx, low : low + 8, :], cz)
                got.append(value)
                pack_ref[i, rows, :] = jnp.where(
                    slot == x, pltpu.roll(value, 4 * x + 2, 1), pack_ref[i, rows, :]
                )
            f0, fs, fd, fm, u = state_of(states_ref, (0, x, rows))
            b = ub_ref[3, x, rows, :]
            out, kept = adjoint_cell(got, u, b, 1.0)
            for i in range(19):
                out_ref[i, x, rows, :] = out[i]
            grad_ref[x, rows, :] = grad1_ref[x, rows, :] + gradient_cell(
                kept, f0, fs, fd, fm, u
            )
        return carry

    lax.fori_loop(0, nx, second_level, 0)

    def tile(t, carry):
        rows = pl.ds(pl.multiple_of(t * 8, 8), 8)
        for i in range(20):
            for out_ref, level, first in ((f0_ref, 0, 0), (f1_ref, 1, 2)):
                if i == 19 and level == 1:
                    continue
                acc = jnp.zeros((8, nz), jnp.float32)
                for x in range(nx):
                    value = (
                        states_ref[level, i, x, rows, :]
                        if i < 19
                        else ub_ref[3, x, rows, :]
                    )
                    p = x + first
                    acc = jnp.where(slot == p, pltpu.roll(value, 4 * p + 2, 1), acc)
                out_ref[i, rows, :] = acc
        return carry

    lax.fori_loop(0, ny // 8, tile, 0)


def edge_kernel(
    mask_ref,
    zown_ref,
    za_ref,
    zb_ref,
    pack_ref,
    f0_ref,
    f1_ref,
    inner_ref,
    grad1_ref,
    inner_grad_ref,
    out_hbm,
    grad_hbm,
    tail_ref,
    first_ref,
    second_ref,
    zmid,
    zout,
    out_ref,
    grad_ref,
    sems,
):
    nx, ny, nz = mask_ref.shape
    tiles = ny // 8
    height = (tiles + 1) * 8
    even = parity("gz") == 0
    lane = lax.broadcasted_iota(jnp.int32, (8, nz), 1)
    even_lane = lane % 2 == 0
    low_pair = lane % 4 < 2

    last = slice(2 * height, 2 * height + 8)
    tail_ref[...] = za_ref[last] + zb_ref[last]

    def swapped(value):
        return jnp.where(even_lane, turn(value, -1), turn(value, 1))

    for t in range(tiles + 1):
        received = []
        for g in range(2):
            row = (g * (tiles + 1) + t) * 8
            va = za_ref[row : row + 8, :]
            vb = zb_ref[row : row + 8, :]
            received.append((jnp.where(even, va, vb), jnp.where(even, vb, va)))
        (high0, low0), (high1, low1) = received
        for g in range(4):
            row = (g * (tiles + 1) + t) * 8
            rows = slice(row, row + 8)
            own = zown_ref[rows]
            if g == 0:
                head, tail = own, low0
            elif g == 1:
                head, tail = high0, own
            elif g == 2:
                head = jnp.where(even_lane, own, turn(high1, 1))
                tail = jnp.where(even_lane, low1, own)
            else:
                head = jnp.where(even_lane, own, high1)
                tail = jnp.where(even_lane, turn(low1, -1), own)
            head = swapped(head)
            tail = swapped(tail)
            first_ref[rows] = jnp.where(low_pair, head, turn(tail, 2))
            second_ref[rows] = jnp.where(low_pair, turn(head, -2), tail)

    slab_grad = []
    for t in range(tiles + 1):
        got = []
        for q in range(NSLOT):
            g, k = ZSLOT[q]
            row = g * height + t * 8
            ref = second_ref if k % 2 else first_ref
            got.append(turn(ref[row : row + 8, :], -32 * (k // 2)))
        out, kept = adjoint_cell(got[:19], got[19:22], got[22], 1.0)
        for i in range(19):
            zmid[i, 8 * t + 8 : 8 * t + 16, :] = out[i]
            if t == tiles:
                zmid[i, 0:8, :] = out[i]
        if t < tiles:
            f = [f1_ref[i, 8 * t : 8 * t + 8, :] for i in range(19)]
            fs, fd = pairs_of(f)
            fm = moments(f[0], fs, fd)
            grad = gradient_cell(kept, f[0], fs, fd, fm, got[19:22])
            slab_grad.append(turn(grad, -8))

    at = lane % 4
    for t in range(tiles):
        rows = slice(8 * t, 8 * t + 8)
        got = []
        for i in range(19):
            cx, cy, cz = VEL[i]
            value = pack_ref[i, rows, :]
            edge = zmid[i, 8 + 8 * t + cy : 16 + 8 * t + cy, :]
            back = -4 * (2 + cx)
            if cz == 0:
                value = jnp.where((at == 1) | (at == 2), turn(edge, back), value)
            else:
                near_lane = 2 if cz < 0 else 0
                value = jnp.where(at == near_lane, turn(edge, back - 1), value)
                value = jnp.where(at == near_lane + 1, turn(edge, back + 1), value)
            got.append(value)
        f = [f0_ref[i, rows, :] for i in range(19)]
        fs, fd = pairs_of(f)
        fm = moments(f[0], fs, fd)
        inverse = 1.0 / fm["total"]
        u = [one * inverse for one in fm["one"]]
        out, kept = adjoint_cell(got, u, f0_ref[19, rows, :], 1.0)
        for i in range(19):
            zout[i, rows, :] = out[i]
        zout[19, rows, :] = gradient_cell(kept, f[0], fs, fd, fm, u)
        zout[20, rows, :] = slab_grad[t]

    def out_copy(k):
        part = slice(*OUT_GROUPS[k])
        return pltpu.make_async_copy(out_ref.at[part], out_hbm.at[part], sems.at[k])

    outer = (lane < 2) | (lane >= nz - 2)
    ends = (lane < 1) | (lane >= nz - 1)
    for x in range(nx):
        for t in range(tiles):
            rows = slice(8 * t, 8 * t + 8)
            level1 = jnp.where(
                ends, turn(zout[20, rows, :], -2 - 4 * x), grad1_ref[x, rows, :]
            )
            edge = turn(zout[19, rows, :], -2 - 4 * x) + level1
            grad = jnp.where(outer, edge, inner_grad_ref[x, rows, :])
            grad_ref[x, rows, :] = jnp.where(mask_ref[x, rows, :] == 0, grad, 0.0)
    grad_copy = pltpu.make_async_copy(grad_ref, grad_hbm, sems.at[len(OUT_GROUPS)])
    grad_copy.start()
    for k, group in enumerate(OUT_GROUPS):
        for i in range(*group):
            for x in range(nx):
                for t in range(tiles):
                    rows = slice(8 * t, 8 * t + 8)
                    out_ref[i, x, rows, :] = jnp.where(
                        outer,
                        turn(zout[i, rows, :], -2 - 4 * x),
                        inner_ref[i, x, rows, :],
                    )
        out_copy(k).start()
    grad_copy.wait()
    for k in range(len(OUT_GROUPS)):
        out_copy(k).wait()


def drag_kernel(whole_cells, *refs):
    total = refs[0][...]
    for ref in refs[1:-1]:
        total = total + ref[...]
    summed = jnp.sum(jnp.sum(total, axis=1, keepdims=True), axis=0, keepdims=True)
    refs[-1][...] = summed / whole_cells


def swaps(count):
    first = [(i, i ^ 1) for i in range(count)]
    second = [(i, (((i + 1) % count) ^ 1) - 1) for i in range(count)]
    second = [(i, j % count) for i, j in second]
    return first, second


VMEM = pl.BlockSpec(memory_space=pltpu.VMEM)
HBM = pl.BlockSpec(memory_space=pltpu.HBM)
PARAMS = pltpu.CompilerParams(vmem_limit_bytes=48 * 2**20)


def call(kernel, inputs, shapes, scratch=(), space=VMEM, micros=1, outs=None):
    if space is HBM:
        inputs = [pltpu.with_memory_space_constraint(x, pltpu.HBM) for x in inputs]
    return pl.pallas_call(
        kernel,
        out_shape=[jax.ShapeDtypeStruct(s, jnp.float32) for s in shapes],
        in_specs=[space] * len(inputs),
        out_specs=outs or [VMEM] * len(shapes),
        scratch_shapes=list(scratch),
        compiler_params=PARAMS,
        cost_estimate=pl.CostEstimate(
            flops=0, bytes_accessed=int(3.6e6 * micros), transcendentals=0
        ),
    )(*inputs)


def body(primal_states, adjoint_last, porosity, solid_mask):
    nx, ny, nz = porosity.shape
    gx, gy, gz = [lax.axis_size(axis) for axis in AXES]
    x_first, x_second = swaps(gx)
    y_first, y_second = swaps(gy)
    z_first, z_second = swaps(gz)
    tiles = ny // 8
    height = (tiles + 1) * 8
    f32 = jnp.float32

    def diagonal(message, x_pairs, y_pairs):
        pairs = [(a * gy + c, b * gy + d) for a, b in x_pairs for c, d in y_pairs]
        return lax.ppermute(message, ("gx", "gy"), pairs)

    rows_x = NSLOT * ny + 8
    rows_y = 2 * (y_rows(nx) + EDGE_ROWS) + 8
    rows_c = 2 * (CORNER + EDGE_ROWS) + 8
    rows_z = 2 * height + 8
    rides = (gx, gy, gz) == (4, 2, 4)
    ub, drag = call(
        state_kernel,
        (primal_states, porosity, solid_mask),
        [(4, nx, ny, nz), (8, nz)],
        [
            pltpu.VMEM((2, 19, nx, ny, nz), f32),
            pltpu.VMEM((nx, ny, nz), f32),
            pltpu.VMEM((nx, ny, nz), jnp.int32),
            pltpu.SemaphoreType.DMA((5,)),
        ],
        HBM,
    )
    cols, y, ya, yb = call(
        pack_y_kernel,
        (adjoint_last, ub, drag),
        [(4 * ny + 8, nz), (rows_y, nz), (rows_c, nz), (rows_c, nz)],
        micros=4,
    )
    xa, xb = call(
        pack_x_kernel, (adjoint_last, ub, drag), [(rows_x, nz), (rows_x, nz)]
    )
    xc = lax.ppermute(cols, "gx", x_second)
    xa = lax.ppermute(xa, "gx", x_first)
    if gy == 2:
        y = lax.ppermute(y, "gy", y_first)
        yb = diagonal(yb, x_second, y_first)
        ya = diagonal(ya, x_first, y_first)
    else:

        def both(message, block, send):
            parts = [message[:block], message[block : 2 * block], message[2 * block :]]
            return jnp.concatenate(
                [send(parts[0], y_first), send(parts[1], y_second), parts[2]]
            )

        block = y_rows(nx) + EDGE_ROWS
        y = both(y, block, lambda m, pairs: lax.ppermute(m, "gy", pairs))
        block = CORNER + EDGE_ROWS
        yb = both(yb, block, lambda m, pairs: diagonal(m, x_second, pairs))
        ya = both(ya, block, lambda m, pairs: diagonal(m, x_first, pairs))
    xb, yb = lax.optimization_barrier((xb, yb))
    xb = lax.ppermute(xb, "gx", x_second)

    zown, za, zb, drag_xy = call(
        pack_z_kernel,
        (cols, xa, xc, y, ya, yb),
        [(4 * height, nz), (rows_z, nz), (rows_z, nz), (8, nz)],
        [pltpu.VMEM((4, ny + 32, nz), f32)],
    )
    if rides:
        second = xc[4 * ny :] + yb[rows_c - 8 :]
        drag_xy = drag_xy + lax.ppermute(second, "gx", x_first)
        za = za.at[2 * height :].set(drag_xy)
        zb = zb.at[2 * height :].set(drag_xy)
    zb = lax.ppermute(zb, "gz", z_second)
    za = lax.ppermute(za, "gz", z_first)
    inner, grad1, inner_grad, pack, f0, f1 = call(
        inner_kernel,
        (primal_states, adjoint_last, ub, xa, xb, y, ya, yb),
        [
            (19, nx, ny, nz),
            (nx, ny, nz),
            (nx, ny, nz),
            (19, ny, nz),
            (20, ny, nz),
            (19, ny, nz),
        ],
        [
            pltpu.VMEM((NSLOT, nx + 4, ny + 32, nz), f32),
            pltpu.VMEM((19, nx + 2, height + 8, nz), f32),
        ],
        micros=4,
    )
    if rides:
        zhalf = lax.ppermute(drag_xy, "gz", [(i, i ^ 2) for i in range(gz)])
        drags = (drag_xy, zhalf)
    else:
        drags = (lax.psum(drag, AXES),)

    first, gradient, tails = call(
        edge_kernel,
        (solid_mask, zown, za, zb, pack, f0, f1, inner, grad1, inner_grad),
        [(19, nx, ny, nz), (nx, ny, nz), (8, nz)],
        [
            pltpu.VMEM((4 * height, nz), f32),
            pltpu.VMEM((4 * height, nz), f32),
            pltpu.VMEM((19, height + 8, nz), f32),
            pltpu.VMEM((21, ny, nz), f32),
            pltpu.VMEM((19, nx, ny, nz), f32),
            pltpu.VMEM((nx, ny, nz), f32),
            pltpu.SemaphoreType.DMA((len(OUT_GROUPS) + 1,)),
        ],
        outs=[HBM, HBM, VMEM],
    )
    if rides:
        drags += (tails,)
    whole_cells = float(nx * ny * nz * gx * gy * gz)
    (drag,) = call(functools.partial(drag_kernel, whole_cells), drags, [(1, 1)])
    return (first, gradient, drag.reshape(()))


def solution(mesh):
    return jax.shard_map(
        body,
        mesh=mesh,
        in_specs=(
            P(None, None, "gx", "gy", "gz"),
            P(None, "gx", "gy", "gz"),
            P("gx", "gy", "gz"),
            P("gx", "gy", "gz"),
        ),
        out_specs=(P(None, "gx", "gy", "gz"), P("gx", "gy", "gz"), P()),
        check_vma=False,
    )
```

```python
import functools

import jax
import jax.numpy as jnp
import numpy as np
from jax import lax
from jax.experimental import pallas as pl
from jax.experimental.pallas import tpu as pltpu
from jax.sharding import PartitionSpec as P

VEL = (
    (0, 0, 0),
    (1, 0, 0),
    (-1, 0, 0),
    (0, 1, 0),
    (0, -1, 0),
    (0, 0, 1),
    (0, 0, -1),
    (1, 1, 0),
    (-1, -1, 0),
    (1, -1, 0),
    (-1, 1, 0),
    (1, 0, 1),
    (-1, 0, -1),
    (1, 0, -1),
    (-1, 0, 1),
    (0, 1, 1),
    (0, -1, -1),
    (0, 1, -1),
    (0, -1, 1),
)
PAIRS = tuple((i, i + 1) for i in range(1, 19, 2))
AXES = ("gx", "gy", "gz")
UB = (19, 20, 21, 22)


def near(axis, sign):
    return tuple(i for i in range(19) if VEL[i][axis] * sign >= 0) + UB


def far(axis, sign):
    return tuple(i for i in range(19) if VEL[i][axis] == sign)


NSLOT = 23
CORNER = 24
EDGE_ROWS = 8


def y_rows(nx):
    return -(-NSLOT * nx // 8) * 8


ZGROUPS = (
    tuple(i for i in range(19) if VEL[i][2] == -1),
    tuple(i for i in range(19) if VEL[i][2] == 1),
    tuple(i for i in range(19) if VEL[i][2] == 0)[:8],
    tuple(i for i in range(19) if VEL[i][2] == 0)[8:] + UB,
)
ZSLOT = {q: (g, k) for g, group in enumerate(ZGROUPS) for k, q in enumerate(group)}


def pairs_of(values):
    s = [values[a] + values[b] for a, b in PAIRS]
    d = [values[a] - values[b] for a, b in PAIRS]
    return s, d


def moments(v0, s, d):
    sx, sy, sz, sp, sq, sr, ss, st, su = s
    dx, dy, dz, dp, dq, dr, ds, dt, du = d
    ex = sp + sq
    ez = sr + ss
    ey = st + su
    faces = sx + sy + sz
    edges = ex + ez + ey
    exx = ex + ez
    eyy = ex + ey
    ezz = ez + ey
    fx = (dp + dq) + (dr + ds)
    fy = (dp - dq) + (dt + du)
    fz = (dr - ds) + (dt - du)
    return dict(
        rest=v0,
        faces=faces,
        edges=edges,
        total=v0 + faces + edges,
        face1=(dx, dy, dz),
        edge1=(fx, fy, fz),
        one=(dx + fx, dy + fy, dz + fz),
        face2=(sx, sy, sz),
        edge2=(exx, eyy, ezz),
        two=(sx + exx, sy + eyy, sz + ezz),
        cross=(sp - sq, sr - ss, st - su),
    )


def adjoint_cell(g, u, b, drive):
    s, d = pairs_of(g)
    m = moments(g[0], s, d)
    total = m["total"]
    trace = m["faces"] + 2.0 * m["edges"] - (30.0 / 19.0) * total
    p0 = (-1.2 / 19.0) * total - (2.0 / 21.0) * trace
    q = [
        (0.4 / 6.0) * (two - (10.0 / 19.0) * total) + (0.8 / 21.0) * trace
        for two in m["two"]
    ]
    qsum = q[0] + q[1] + q[2]
    qab = [0.1 * c for c in m["cross"]]
    p1 = [-0.12 * one for one in m["one"]]
    h0 = (
        0.4 * m["rest"]
        + (1.2 / 18.0) * m["faces"]
        + (1.2 / 36.0) * m["edges"]
        + p0
        + (1.0 / 3.0) * qsum
    )
    h1 = [
        (1.2 / 18.0) * f + (1.2 / 36.0) * e + (1.0 / 3.0) * p
        for f, e, p in zip(m["face1"], m["edge1"], p1)
    ]
    base = (1.0 / 3.0) * p0 + (1.0 / 9.0) * qsum
    haa = [
        (1.2 / 18.0) * f + (1.2 / 36.0) * e + (2.0 / 9.0) * qa + base
        for f, e, qa in zip(m["face2"], m["edge2"], q)
    ]
    hxy, hxz, hyz = [(2.0 / 45.0) * c for c in m["cross"]]
    ux, uy, uz = u
    v = (
        haa[0] * ux + hxy * uy + hxz * uz,
        hxy * ux + haa[1] * uy + hyz * uz,
        hxz * ux + hyz * uy + haa[2] * uz,
    )
    uv = ux * v[0] + uy * v[1] + uz * v[2]
    uu = ux * ux + uy * uy + uz * uz
    uuh = 1.5 * uu * h0
    a = h0 + uuh - 4.5 * uv
    nb = 1.0 - b
    e0 = nb * (a - p0)
    nq = [nb * x for x in q]
    nxy, nxz, nyz = [nb * x for x in qab]
    o = [
        nb * (3.0 * h1[k] + 9.0 * v[k] - 3.0 * u[k] * h0 - p1[k]) for k in range(3)
    ]
    o[0] = o[0] + b * drive
    alpha = -0.2 * nb
    half_s = 0.5 * (alpha + b)
    half_d = 0.5 * (alpha - b)
    exy = e0 - nq[0] - nq[1]
    exz = e0 - nq[0] - nq[2]
    eyz = e0 - nq[1] - nq[2]
    even = (
        e0 - nq[0],
        e0 - nq[1],
        e0 - nq[2],
        exy - nxy,
        exy + nxy,
        exz - nxz,
        exz + nxz,
        eyz - nyz,
        eyz + nyz,
    )
    odd = (
        o[0],
        o[1],
        o[2],
        o[0] + o[1],
        o[0] - o[1],
        o[0] + o[2],
        o[0] - o[2],
        o[1] + o[2],
        o[1] - o[2],
    )
    out = [(alpha + b) * g[0] + e0]
    for k in range(9):
        even_k = half_s * s[k] + even[k]
        odd_k = half_d * d[k] + odd[k]
        out.append(even_k + odd_k)
        out.append(even_k - odd_k)
    kept = dict(
        s=s, d=d, g0=g[0], p0=p0, p1=p1, q=q, qab=qab, h0=h0, h1=h1, uv=uv, uuh=uuh
    )
    return out, kept


def gradient_cell(kept, f0, fs, fd, fm, u):
    rho = fm["total"]
    even = fs[0] * kept["s"][0]
    odd = fd[0] * kept["d"][0]
    for k in range(1, 9):
        even = even + fs[k] * kept["s"][k]
        odd = odd + fd[k] * kept["d"][k]
    hf = kept["p0"] * rho
    for k in range(3):
        hf = hf + kept["p1"][k] * fm["one"][k] + kept["q"][k] * fm["two"][k]
        hf = hf + kept["qab"][k] * fm["cross"][k]
    uh1 = u[0] * kept["h1"][0] + u[1] * kept["h1"][1] + u[2] * kept["h1"][2]
    hfeq = rho * (kept["h0"] - kept["uuh"] + 3.0 * uh1 + 4.5 * kept["uv"])
    pairs = 1.2 * f0 * kept["g0"] + 0.6 * even - 0.4 * odd
    return pairs + hf - hfeq + fm["one"][0]


def state_of(ref, index):
    f = [ref[(index[0], i) + index[1:]] for i in range(19)]
    s, d = pairs_of(f)
    m = moments(f[0], s, d)
    inverse = 1.0 / m["total"]
    u = [one * inverse for one in m["one"]]
    return f[0], s, d, m, u


def corner_rows(sx, sy):
    rows = []
    for dx, dy in ((0, 0), (1, 0), (0, 1), (1, 1)):
        for i in near(0, sx) if dx == 0 else far(0, sx):
            if i in (near(1, sy) if dy == 0 else far(1, sy)):
                rows.append((i, dx, dy))
    return rows


def parity(axis):
    return lax.axis_index(axis) % 2


def cell_rows(adj_ref, ub_ref, q, x, rows):
    return adj_ref[q, x, rows, :] if q < 19 else ub_ref[q - 19, x, rows, :]


def state_kernel(
    states_hbm,
    por_hbm,
    mask_hbm,
    ub_ref,
    drag_ref,
    states_ref,
    por_ref,
    mask_ref,
    sems,
):
    nx, ny, nz = por_ref.shape
    tiles = ny // 8
    copies = [
        pltpu.make_async_copy(src, dst, sems.at[k])
        for k, (src, dst) in enumerate(
            (
                (states_hbm.at[1], states_ref.at[1]),
                (por_hbm, por_ref),
                (mask_hbm, mask_ref),
                (states_hbm.at[0, 1:3], states_ref.at[0, 1:3]),
                (states_hbm.at[0, 7:15], states_ref.at[0, 7:15]),
            )
        )
    ]
    for copy in copies:
        copy.start()
    for copy in copies[:3]:
        copy.wait()

    def cells(x, carry):
        for t in range(tiles):
            rows = slice(8 * t, 8 * t + 8)
            blocking = jnp.where(mask_ref[x, rows, :] == 0, por_ref[x, rows, :], 1.0)
            f0, s, d, m, u = state_of(states_ref, (1, x, rows))
            for k in range(3):
                ub_ref[k, x, rows, :] = u[k]
            ub_ref[3, x, rows, :] = blocking
            carry = carry + blocking * m["one"][0]
        return carry

    drag = lax.fori_loop(0, nx, cells, jnp.zeros((8, nz), jnp.float32))
    for copy in copies[3:]:
        copy.wait()

    def flux_cells(x, carry):
        for t in range(tiles):
            rows = slice(8 * t, 8 * t + 8)
            flux = 0.0
            for a, b in PAIRS:
                if VEL[a][0]:
                    flux = flux + (
                        states_ref[0, a, x, rows, :] - states_ref[0, b, x, rows, :]
                    )
            carry = carry + ub_ref[3, x, rows, :] * flux
        return carry

    drag = lax.fori_loop(0, nx, flux_cells, drag)
    drag_ref[...] = drag


def pack_x_kernel(adj_ref, ub_ref, drag_ref, out_ref):
    nx, ny = adj_ref.shape[1:3]
    out_ref[NSLOT * ny :] = drag_ref[...]

    def fill(sign):
        for names, offset, x in (
            (near(0, sign), 0, 0 if sign > 0 else nx - 1),
            (far(0, sign), 18, 1 if sign > 0 else nx - 2),
        ):
            for k, q in enumerate(names):
                k += offset
                out_ref[k * ny : (k + 1) * ny] = cell_rows(
                    adj_ref, ub_ref, q, x, slice(0, ny)
                )

    pl.when(parity("gx") == 0)(functools.partial(fill, -1))
    pl.when(parity("gx") == 1)(functools.partial(fill, 1))


def edge_entries(sign):
    rows = []
    for side in (1, -1):
        rows += [(i, 0, side) for i in far(1, side) if VEL[i][0] == 0]
        rows += [(i, 1, side) for i in far(1, side) if VEL[i][0] == sign]
    return rows


def pack_partial_kernel(adj_ref, ub_ref, out_ref):
    nx, ny, nz = adj_ref.shape[1:]
    tiles = ny // 8
    sub = lax.broadcasted_iota(jnp.int32, (8, nz), 0)

    def fill(sign):
        here, inside = (0, 1) if sign > 0 else (nx - 1, nx - 2)
        names = far(0, sign)
        for t in range(tiles):
            rows = slice(8 * t, 8 * t + 8)
            got = []
            for i in range(19):
                cx, cy, cz = VEL[i]
                if cx * sign < 0:
                    got.append(jnp.zeros((8, nz), jnp.float32))
                    continue
                x = inside if cx else here
                if t == 0 and cy < 0:
                    value = pltpu.roll(adj_ref[i, x, rows, :], 1, 0)
                    value = jnp.where(sub == 0, 0.0, value)
                elif t == tiles - 1 and cy > 0:
                    value = pltpu.roll(adj_ref[i, x, rows, :], 7, 0)
                    value = jnp.where(sub == 7, 0.0, value)
                else:
                    value = adj_ref[i, x, 8 * t + cy : 8 * t + 8 + cy, :]
                got.append(z_shifted(value, cz))
            u = [ub_ref[k, here, rows, :] for k in range(3)]
            out, _ = adjoint_cell(got, u, ub_ref[3, here, rows, :], 0.0)
            for k, i in enumerate(names):
                out_ref[k * ny + 8 * t : k * ny + 8 * t + 8] = out[i]
        for k, q in enumerate(names + UB):
            k += 5
            out_ref[k * ny : (k + 1) * ny] = cell_rows(
                adj_ref, ub_ref, q, here, slice(0, ny)
            )
        for k, (i, depth, side) in enumerate(edge_entries(sign)):
            y = 0 if side > 0 else ny - 1
            row = 14 * ny + k
            out_ref[row : row + 1] = adj_ref[i, inside if depth else here, y : y + 1, :]

    pl.when(parity("gx") == 0)(functools.partial(fill, 1))
    pl.when(parity("gx") == 1)(functools.partial(fill, -1))


def column_pair(acc, value, pair, q, k, plane):
    start = 32 * (k // 2) + 4 * plane + 2 * (k % 2)
    cz = VEL[q][2] if q < 19 else 0
    return jnp.where(pair == start // 2, turn(value, start + 1 - cz), acc)


def pack_y_kernel(
    adj_ref, ub_ref, drag_ref, cols_ref, y_ref, ya_ref, yb_ref
):
    nx, ny, nz = adj_ref.shape[1:]
    pair = lax.broadcasted_iota(jnp.int32, (8, nz), 1) // 2
    for g, group in enumerate(ZGROUPS):
        for t in range(ny // 8):
            acc = jnp.zeros((8, nz), jnp.float32)
            for k, q in enumerate(group):
                for x in range(nx):
                    value = cell_rows(adj_ref, ub_ref, q, x, slice(8 * t, 8 * t + 8))
                    acc = column_pair(acc, value, pair, q, k, x + 2)
            row = g * ny + 8 * t
            cols_ref[row : row + 8] = acc
    y_block = y_rows(nx) + EDGE_ROWS
    corner_block = CORNER + EDGE_ROWS

    def fill_edges(place, sign):
        for g in range(4):
            for d in range(2):
                y = d if sign > 0 else ny - 1 - d
                line = cols_ref[g * ny + y : g * ny + y + 1]
                row = place * y_block + y_rows(nx) + 2 * g + d
                y_ref[row : row + 1] = line
                row = place * corner_block + CORNER + 2 * g + d
                ya_ref[row : row + 1] = line
                yb_ref[row : row + 1] = line

    def fill_y(place, sign):
        for names, offset, y in (
            (near(1, sign), 0, 0 if sign > 0 else ny - 1),
            (far(1, sign), 18, 1 if sign > 0 else ny - 2),
        ):
            for k, q in enumerate(names):
                for x in range(nx):
                    row = place * y_block + (k + offset) * nx + x
                    y_ref[row : row + 1] = cell_rows(
                        adj_ref, ub_ref, q, x, slice(y, y + 1)
                    )

    def fill_corner(out_ref, place, sx, sy):
        names = corner_rows(sx, sy)
        for k, (q, dx, dy) in enumerate(names):
            x = dx if sx > 0 else nx - 1 - dx
            y = dy if sy > 0 else ny - 1 - dy
            row = place * corner_block + k
            out_ref[row : row + 1] = cell_rows(adj_ref, ub_ref, q, x, slice(y, y + 1))
        row = place * corner_block + len(names)
        last = place * corner_block + CORNER
        out_ref[row:last] = jnp.zeros((last - row, nz), jnp.float32)

    drag = drag_ref[...]
    cols_ref[4 * ny :] = drag
    y_ref[2 * y_block :] = drag
    ya_ref[2 * corner_block :] = drag
    yb_ref[2 * corner_block :] = drag
    for py in (0, 1):

        @pl.when(parity("gy") == py)
        def _():
            s0 = 1 if py else -1
            fill_y(0, s0)
            fill_y(1, -s0)
            fill_edges(0, s0)
            fill_edges(1, -s0)

    for px in (0, 1):
        for py in (0, 1):

            @pl.when((parity("gx") == px) & (parity("gy") == py))
            def _():
                sa = 1 if px else -1
                s0 = 1 if py else -1
                for out_ref, sx in ((ya_ref, sa), (yb_ref, -sa)):
                    fill_corner(out_ref, 0, sx, s0)
                    fill_corner(out_ref, 1, sx, -s0)


def pack_z_kernel(
    cols_ref,
    xa_ref,
    xc_ref,
    y_ref,
    ya_ref,
    yb_ref,
    zown_ref,
    za_ref,
    zb_ref,
    drag_ref,
    ext,
):
    ny = (cols_ref.shape[0] - 8) // 4
    nz = cols_ref.shape[1]
    tiles = ny // 8
    base = 16
    even_x = parity("gx") == 0
    even_y = parity("gy") == 0
    lane = lax.broadcasted_iota(jnp.int32, (8, nz), 1)
    sub = lax.broadcasted_iota(jnp.int32, (8, nz), 0)
    plane = (lane % 32) // 4
    slot = 2 * (lane // 32) + (lane % 4) // 2

    def along_x(own, va, vb):
        low = turn(jnp.where(even_x, vb, va), -16)
        high = turn(jnp.where(even_x, va, vb), 16)
        return jnp.where(plane < 2, low, jnp.where(plane > 5, high, own))

    pair = lane // 2

    def fill_main(sign):
        halo = {}
        for names, offset, p in (
            (near(0, sign), 0, 6 if sign > 0 else 1),
            (far(0, sign), 18, 7 if sign > 0 else 0),
        ):
            for k, q in enumerate(names):
                halo.setdefault(q, []).append((k + offset, p))
        for g, group in enumerate(ZGROUPS):
            for t in range(tiles):
                rows = slice(g * ny + 8 * t, g * ny + 8 * t + 8)
                acc = jnp.where(
                    plane < 2 if sign > 0 else plane > 5,
                    turn(xc_ref[rows], -16 * sign),
                    cols_ref[rows],
                )
                for k, q in enumerate(group):
                    for at, p in halo.get(q, ()):
                        row = at * ny + 8 * t
                        acc = column_pair(acc, xa_ref[row : row + 8], pair, q, k, p)
                ext[g, base + 8 * t : base + 8 * t + 8, :] = acc

    @pl.when(parity("gx") == 0)
    def _():
        fill_main(1)

    @pl.when(parity("gx") == 1)
    def _():
        fill_main(-1)

    y_block = (y_ref.shape[0] - 8) // 2
    corner_block = CORNER + EDGE_ROWS

    def edges(ref, block, place):
        return ref[(place + 1) * block - EDGE_ROWS : (place + 1) * block]

    first, second = [
        along_x(
            edges(y_ref, y_block, place),
            edges(ya_ref, corner_block, place),
            edges(yb_ref, corner_block, place),
        )
        for place in range(2)
    ]
    high = jnp.where(even_y, first, second)
    low = jnp.where(even_y, second, first)
    for g in range(4):
        for d in range(2):
            row = 2 * g + d
            ext[g, base + ny + d : base + ny + d + 1, :] = high[row : row + 1]
            ext[g, base - 1 - d : base - d, :] = low[row : row + 1]

    packed = []
    for g, group in enumerate(ZGROUPS):
        moves = {}
        for k, q in enumerate(group):
            cx, cy, _ = VEL[q] if q < 19 else (0, 0, 0)
            moves.setdefault((cx, cy), []).append(k)
        acc = [jnp.zeros((8, nz), jnp.float32) for t in range(tiles + 1)]
        for (cx, cy), slots in moves.items():
            mask = slot == slots[0]
            for k in slots[1:]:
                mask = mask | (slot == k)
            for t in range(tiles + 1):
                if t < tiles:
                    row = base + 8 * t + cy
                    value = ext[g, row : row + 8, :]
                else:
                    above = base + ny + cy
                    below = base - 8 + cy
                    value = jnp.where(
                        sub < 4, ext[g, above : above + 8, :], ext[g, below : below + 8, :]
                    )
                acc[t] = jnp.where(mask, turn(value, -4 * cx), acc[t])
        packed.append(acc)
        for t in range(tiles + 1):
            row = (g * (tiles + 1) + t) * 8
            zown_ref[row : row + 8, :] = acc[t]
    up_first = parity("gz") == 0
    even_lane = lane % 2 == 0
    for t in range(tiles + 1):
        two, three = packed[2][t], packed[3][t]
        up = (packed[0][t], jnp.where(even_lane, two, pltpu.roll(three, 1, 1)))
        down = (packed[1][t], jnp.where(even_lane, pltpu.roll(two, nz - 1, 1), three))
        for g in range(2):
            row = (g * (tiles + 1) + t) * 8
            za_ref[row : row + 8, :] = jnp.where(up_first, up[g], down[g])
            zb_ref[row : row + 8, :] = jnp.where(up_first, down[g], up[g])
    drag = (cols_ref[4 * ny :] + y_ref[2 * y_block :]) + xa_ref[xa_ref.shape[0] - 8 :]
    drag = drag + (xc_ref[4 * ny :] + yb_ref[2 * corner_block :])
    drag_ref[...] = drag


OUT_GROUPS = ((0, 7), (7, 13), (13, 17), (17, 19))


def turn(value, shift):
    nz = value.shape[1]
    return pltpu.roll(value, shift % nz, 1) if shift % nz else value


def z_shifted(value, cz):
    return turn(value, -cz) if cz else value


def inner_kernel(
    states_ref,
    adj_ref,
    ub_ref,
    xa_ref,
    xb_ref,
    y_ref,
    ya_ref,
    yb_ref,
    out_ref,
    grad1_ref,
    grad_ref,
    pack_ref,
    f0_ref,
    f1_ref,
    ext,
    mid,
):
    nx, ny, nz = grad_ref.shape
    tiles = ny // 8
    lane = lax.broadcasted_iota(jnp.int32, (8, nz), 1)
    slot = lane // 4
    sub = lax.broadcasted_iota(jnp.int32, (8, nz), 0)
    even_x = parity("gx") == 0
    even_y = parity("gy") == 0
    base = 16

    for q in range(NSLOT):
        for x in range(nx):
            ext[q, x + 2, base : base + ny, :] = (
                adj_ref[q, x] if q < 19 else ub_ref[q - 19, x]
            )
    planes = {1: (nx + 2, nx + 3), -1: (1, 0)}
    lines = {1: (base + ny, base + ny + 1), -1: (base - 1, base - 2)}

    def fill_whole(sign):
        for names, depth, offset in ((near(0, sign), 0, 0), (far(0, sign), 1, 18)):
            for k, q in enumerate(names):
                rows = slice((k + offset) * ny, (k + offset + 1) * ny)
                ext[q, planes[sign][depth], base : base + ny, :] = xa_ref[rows]

    def fill_partial(sign):
        one, two = planes[sign]
        for k, q in enumerate(far(0, sign) + UB):
            ext[q, one, base : base + ny, :] = xb_ref[(5 + k) * ny : (6 + k) * ny]
        nothing = jnp.zeros((ny, nz), jnp.float32)
        for q in range(19):
            if VEL[q][0] == 0:
                ext[q, one, base : base + ny, :] = nothing
            elif VEL[q][0] == sign:
                ext[q, two, base : base + ny, :] = nothing
        for k, (q, depth, side) in enumerate(edge_entries(sign)):
            line = base if side > 0 else base + ny - 1
            row = 14 * ny + k
            ext[q, planes[sign][depth], line : line + 1, :] = xb_ref[row : row + 1]

    @pl.when(parity("gx") == 0)
    def _():
        fill_whole(1)
        fill_partial(-1)

    @pl.when(parity("gx") == 1)
    def _():
        fill_whole(-1)
        fill_partial(1)

    for sign in (1, -1):
        block = y_rows(nx) + EDGE_ROWS
        first, second = (0, block) if sign > 0 else (block, 0)
        for names, depth, offset in ((near(1, sign), 0, 0), (far(1, sign), 1, 18)):
            line = lines[sign][depth]
            for k, q in enumerate(names):
                row = (k + offset) * nx
                got = jnp.where(
                    even_y,
                    y_ref[first + row : first + row + nx],
                    y_ref[second + row : second + row + nx],
                )
                for x in range(nx):
                    ext[q, x + 2, line : line + 1, :] = got[x : x + 1]
        for sx in (1, -1):
            xs = (ya_ref, yb_ref) if sx > 0 else (yb_ref, ya_ref)
            block = CORNER + EDGE_ROWS
            ys = (0, block) if sign > 0 else (block, 0)
            low, high = [
                jnp.where(even_x, xs[0][r : r + CORNER], xs[1][r : r + CORNER])
                for r in ys
            ]
            got = jnp.where(even_y, low, high)
            for k, (q, dx, dy) in enumerate(corner_rows(sx, sign)):
                line = lines[sign][dy]
                ext[q, planes[sx][dx], line : line + 1, :] = got[k : k + 1]

    def near_cells(q, plane, t, cy):
        if t < tiles:
            row = base + 8 * t + cy
            return ext[q, plane, row : row + 8, :]
        above = base + ny + cy
        below = base - 8 + cy
        return jnp.where(
            sub < 4, ext[q, plane, above : above + 8, :], ext[q, plane, below : below + 8, :]
        )

    def first_level(p, t, kinds, partial=None):
        got = []
        for i in range(19):
            cx, cy, cz = VEL[i]
            got.append(z_shifted(near_cells(i, p + 1 + cx, t, cy), cz))
        ub = [near_cells(19 + k, p + 1, t, 0) for k in range(4)]
        out, kept = adjoint_cell(got, ub[:3], ub[3], 1.0)
        if partial is not None:
            for k, i in enumerate(kinds):
                row = k * ny + 8 * t
                out[i] = out[i] + jnp.where(partial, xb_ref[row : row + 8], 0.0)
        for i in kinds:
            if t < tiles:
                mid[i, p, t * 8 + 8 : t * 8 + 16, :] = out[i]
            elif VEL[i][1] > 0:
                mid[i, p, t * 8 + 8 : t * 8 + 16, :] = out[i]
            elif VEL[i][1] < 0:
                mid[i, p, 0:8, :] = out[i]
        return kept, ub[:3]

    def inside(x, carry):
        for t in range(tiles):
            kept, u = first_level(x + 1, t, range(19))
            rows = slice(t * 8, t * 8 + 8)
            f0, fs, fd, fm, _ = state_of(states_ref, (1, x, rows))
            grad1_ref[x, rows, :] = gradient_cell(kept, f0, fs, fd, fm, u)
        return carry

    lax.fori_loop(0, nx, inside, 0)
    for t in range(tiles):
        first_level(0, t, far(0, -1), even_x)
        first_level(nx + 1, t, far(0, 1), jnp.logical_not(even_x))

    def rim(n, carry):
        for p in (2 * n, 2 * n + 1):
            first_level(p, tiles, far(1, -1) + far(1, 1))
        return carry

    lax.fori_loop(0, (nx + 2) // 2, rim, 0)

    def second_level(x, carry):
        for t in range(tiles):
            rows = slice(t * 8, t * 8 + 8)
            got = []
            for i in range(19):
                cx, cy, cz = VEL[i]
                low = 8 + 8 * t + cy
                value = z_shifted(mid[i, x + 1 + cx, low : low + 8, :], cz)
                got.append(value)
                pack_ref[i, rows, :] = jnp.where(
                    slot == x, pltpu.roll(value, 4 * x + 2, 1), pack_ref[i, rows, :]
                )
            f0, fs, fd, fm, u = state_of(states_ref, (0, x, rows))
            b = ub_ref[3, x, rows, :]
            out, kept = adjoint_cell(got, u, b, 1.0)
            for i in range(19):
                out_ref[i, x, rows, :] = out[i]
            grad_ref[x, rows, :] = grad1_ref[x, rows, :] + gradient_cell(
                kept, f0, fs, fd, fm, u
            )
        return carry

    lax.fori_loop(0, nx, second_level, 0)

    def tile(t, carry):
        rows = pl.ds(pl.multiple_of(t * 8, 8), 8)
        for i in range(20):
            for out_ref, level, first in ((f0_ref, 0, 0), (f1_ref, 1, 2)):
                if i == 19 and level == 1:
                    continue
                acc = jnp.zeros((8, nz), jnp.float32)
                for x in range(nx):
                    value = (
                        states_ref[level, i, x, rows, :]
                        if i < 19
                        else ub_ref[3, x, rows, :]
                    )
                    p = x + first
                    acc = jnp.where(slot == p, pltpu.roll(value, 4 * p + 2, 1), acc)
                out_ref[i, rows, :] = acc
        return carry

    lax.fori_loop(0, ny // 8, tile, 0)


def edge_kernel(
    mask_ref,
    zown_ref,
    za_ref,
    zb_ref,
    pack_ref,
    f0_ref,
    f1_ref,
    inner_ref,
    grad1_ref,
    inner_grad_ref,
    out_hbm,
    grad_hbm,
    tail_ref,
    first_ref,
    second_ref,
    zmid,
    zout,
    out_ref,
    grad_ref,
    sems,
):
    nx, ny, nz = mask_ref.shape
    tiles = ny // 8
    height = (tiles + 1) * 8
    even = parity("gz") == 0
    lane = lax.broadcasted_iota(jnp.int32, (8, nz), 1)
    even_lane = lane % 2 == 0
    low_pair = lane % 4 < 2

    last = slice(2 * height, 2 * height + 8)
    tail_ref[...] = za_ref[last] + zb_ref[last]

    def swapped(value):
        return jnp.where(even_lane, turn(value, -1), turn(value, 1))

    for t in range(tiles + 1):
        received = []
        for g in range(2):
            row = (g * (tiles + 1) + t) * 8
            va = za_ref[row : row + 8, :]
            vb = zb_ref[row : row + 8, :]
            received.append((jnp.where(even, va, vb), jnp.where(even, vb, va)))
        (high0, low0), (high1, low1) = received
        for g in range(4):
            row = (g * (tiles + 1) + t) * 8
            rows = slice(row, row + 8)
            own = zown_ref[rows]
            if g == 0:
                head, tail = own, low0
            elif g == 1:
                head, tail = high0, own
            elif g == 2:
                head = jnp.where(even_lane, own, turn(high1, 1))
                tail = jnp.where(even_lane, low1, own)
            else:
                head = jnp.where(even_lane, own, high1)
                tail = jnp.where(even_lane, turn(low1, -1), own)
            head = swapped(head)
            tail = swapped(tail)
            first_ref[rows] = jnp.where(low_pair, head, turn(tail, 2))
            second_ref[rows] = jnp.where(low_pair, turn(head, -2), tail)

    slab_grad = []
    for t in range(tiles + 1):
        got = []
        for q in range(NSLOT):
            g, k = ZSLOT[q]
            row = g * height + t * 8
            ref = second_ref if k % 2 else first_ref
            got.append(turn(ref[row : row + 8, :], -32 * (k // 2)))
        out, kept = adjoint_cell(got[:19], got[19:22], got[22], 1.0)
        for i in range(19):
            zmid[i, 8 * t + 8 : 8 * t + 16, :] = out[i]
            if t == tiles:
                zmid[i, 0:8, :] = out[i]
        if t < tiles:
            f = [f1_ref[i, 8 * t : 8 * t + 8, :] for i in range(19)]
            fs, fd = pairs_of(f)
            fm = moments(f[0], fs, fd)
            grad = gradient_cell(kept, f[0], fs, fd, fm, got[19:22])
            slab_grad.append(turn(grad, -8))

    at = lane % 4
    for t in range(tiles):
        rows = slice(8 * t, 8 * t + 8)
        got = []
        for i in range(19):
            cx, cy, cz = VEL[i]
            value = pack_ref[i, rows, :]
            edge = zmid[i, 8 + 8 * t + cy : 16 + 8 * t + cy, :]
            back = -4 * (2 + cx)
            if cz == 0:
                value = jnp.where((at == 1) | (at == 2), turn(edge, back), value)
            else:
                near_lane = 2 if cz < 0 else 0
                value = jnp.where(at == near_lane, turn(edge, back - 1), value)
                value = jnp.where(at == near_lane + 1, turn(edge, back + 1), value)
            got.append(value)
        f = [f0_ref[i, rows, :] for i in range(19)]
        fs, fd = pairs_of(f)
        fm = moments(f[0], fs, fd)
        inverse = 1.0 / fm["total"]
        u = [one * inverse for one in fm["one"]]
        out, kept = adjoint_cell(got, u, f0_ref[19, rows, :], 1.0)
        for i in range(19):
            zout[i, rows, :] = out[i]
        zout[19, rows, :] = gradient_cell(kept, f[0], fs, fd, fm, u)
        zout[20, rows, :] = slab_grad[t]

    def out_copy(k):
        part = slice(*OUT_GROUPS[k])
        return pltpu.make_async_copy(out_ref.at[part], out_hbm.at[part], sems.at[k])

    outer = (lane < 2) | (lane >= nz - 2)
    ends = (lane < 1) | (lane >= nz - 1)
    for x in range(nx):
        for t in range(tiles):
            rows = slice(8 * t, 8 * t + 8)
            level1 = jnp.where(
                ends, turn(zout[20, rows, :], -2 - 4 * x), grad1_ref[x, rows, :]
            )
            edge = turn(zout[19, rows, :], -2 - 4 * x) + level1
            grad = jnp.where(outer, edge, inner_grad_ref[x, rows, :])
            grad_ref[x, rows, :] = jnp.where(mask_ref[x, rows, :] == 0, grad, 0.0)
    grad_copy = pltpu.make_async_copy(grad_ref, grad_hbm, sems.at[len(OUT_GROUPS)])
    grad_copy.start()
    for k, group in enumerate(OUT_GROUPS):
        for i in range(*group):
            for x in range(nx):
                for t in range(tiles):
                    rows = slice(8 * t, 8 * t + 8)
                    out_ref[i, x, rows, :] = jnp.where(
                        outer,
                        turn(zout[i, rows, :], -2 - 4 * x),
                        inner_ref[i, x, rows, :],
                    )
        out_copy(k).start()
    grad_copy.wait()
    for k in range(len(OUT_GROUPS)):
        out_copy(k).wait()


def drag_kernel(whole_cells, *refs):
    total = refs[0][...]
    for ref in refs[1:-1]:
        total = total + ref[...]
    summed = jnp.sum(jnp.sum(total, axis=1, keepdims=True), axis=0, keepdims=True)
    refs[-1][...] = summed / whole_cells


def swaps(count):
    first = [(i, i ^ 1) for i in range(count)]
    second = [(i, (((i + 1) % count) ^ 1) - 1) for i in range(count)]
    second = [(i, j % count) for i, j in second]
    return first, second


VMEM = pl.BlockSpec(memory_space=pltpu.VMEM)
HBM = pl.BlockSpec(memory_space=pltpu.HBM)
PARAMS = pltpu.CompilerParams(vmem_limit_bytes=48 * 2**20)


def call(kernel, inputs, shapes, scratch=(), space=VMEM, micros=1, outs=None):
    if space is HBM:
        inputs = [pltpu.with_memory_space_constraint(x, pltpu.HBM) for x in inputs]
    return pl.pallas_call(
        kernel,
        out_shape=[jax.ShapeDtypeStruct(s, jnp.float32) for s in shapes],
        in_specs=[space] * len(inputs),
        out_specs=outs or [VMEM] * len(shapes),
        scratch_shapes=list(scratch),
        compiler_params=PARAMS,
        cost_estimate=pl.CostEstimate(
            flops=0, bytes_accessed=int(3.6e6 * micros), transcendentals=0
        ),
    )(*inputs)


def body(primal_states, adjoint_last, porosity, solid_mask):
    nx, ny, nz = porosity.shape
    gx, gy, gz = [lax.axis_size(axis) for axis in AXES]
    x_first, x_second = swaps(gx)
    y_first, y_second = swaps(gy)
    z_first, z_second = swaps(gz)
    tiles = ny // 8
    height = (tiles + 1) * 8
    f32 = jnp.float32

    def diagonal(message, x_pairs, y_pairs):
        pairs = [(a * gy + c, b * gy + d) for a, b in x_pairs for c, d in y_pairs]
        return lax.ppermute(message, ("gx", "gy"), pairs)

    rows_x = NSLOT * ny + 8
    rows_y = 2 * (y_rows(nx) + EDGE_ROWS) + 8
    rows_c = 2 * (CORNER + EDGE_ROWS) + 8
    rows_z = 2 * height + 8
    rides = (gx, gy, gz) == (4, 2, 4)
    ub, drag = call(
        state_kernel,
        (primal_states, porosity, solid_mask),
        [(4, nx, ny, nz), (8, nz)],
        [
            pltpu.VMEM((2, 19, nx, ny, nz), f32),
            pltpu.VMEM((nx, ny, nz), f32),
            pltpu.VMEM((nx, ny, nz), jnp.int32),
            pltpu.SemaphoreType.DMA((5,)),
        ],
        HBM,
    )
    cols, y, ya, yb = call(
        pack_y_kernel,
        (adjoint_last, ub, drag),
        [(4 * ny + 8, nz), (rows_y, nz), (rows_c, nz), (rows_c, nz)],
        micros=4,
    )
    (xa,) = call(pack_x_kernel, (adjoint_last, ub, drag), [(rows_x, nz)])
    (xb,) = call(pack_partial_kernel, (adjoint_last, ub), [(14 * ny + 8, nz)])
    xc = lax.ppermute(cols, "gx", x_second)
    xa = lax.ppermute(xa, "gx", x_first)
    if gy == 2:
        y = lax.ppermute(y, "gy", y_first)
        yb = diagonal(yb, x_second, y_first)
        ya = diagonal(ya, x_first, y_first)
    else:

        def both(message, block, send):
            parts = [message[:block], message[block : 2 * block], message[2 * block :]]
            return jnp.concatenate(
                [send(parts[0], y_first), send(parts[1], y_second), parts[2]]
            )

        block = y_rows(nx) + EDGE_ROWS
        y = both(y, block, lambda m, pairs: lax.ppermute(m, "gy", pairs))
        block = CORNER + EDGE_ROWS
        yb = both(yb, block, lambda m, pairs: diagonal(m, x_second, pairs))
        ya = both(ya, block, lambda m, pairs: diagonal(m, x_first, pairs))
    xb, yb = lax.optimization_barrier((xb, yb))
    xb = lax.ppermute(xb, "gx", x_second)

    zown, za, zb, drag_xy = call(
        pack_z_kernel,
        (cols, xa, xc, y, ya, yb),
        [(4 * height, nz), (rows_z, nz), (rows_z, nz), (8, nz)],
        [pltpu.VMEM((4, ny + 32, nz), f32)],
    )
    if rides:
        second = xc[4 * ny :] + yb[rows_c - 8 :] + y[rows_y - 8 :]
        drag_xy = drag_xy + lax.ppermute(second, "gx", x_first)
        za = za.at[2 * height :].set(drag_xy)
        zb = zb.at[2 * height :].set(drag_xy)
    zb = lax.ppermute(zb, "gz", z_second)
    za = lax.ppermute(za, "gz", z_first)
    inner, grad1, inner_grad, pack, f0, f1 = call(
        inner_kernel,
        (primal_states, adjoint_last, ub, xa, xb, y, ya, yb),
        [
            (19, nx, ny, nz),
            (nx, ny, nz),
            (nx, ny, nz),
            (19, ny, nz),
            (20, ny, nz),
            (19, ny, nz),
        ],
        [
            pltpu.VMEM((NSLOT, nx + 4, ny + 32, nz), f32),
            pltpu.VMEM((19, nx + 2, height + 8, nz), f32),
        ],
        micros=4,
    )
    if rides:
        zhalf = lax.ppermute(drag_xy, "gz", [(i, i ^ 2) for i in range(gz)])
        drags = (drag_xy, zhalf)
    else:
        drags = (lax.psum(drag, AXES),)

    first, gradient, tails = call(
        edge_kernel,
        (solid_mask, zown, za, zb, pack, f0, f1, inner, grad1, inner_grad),
        [(19, nx, ny, nz), (nx, ny, nz), (8, nz)],
        [
            pltpu.VMEM((4 * height, nz), f32),
            pltpu.VMEM((4 * height, nz), f32),
            pltpu.VMEM((19, height + 8, nz), f32),
            pltpu.VMEM((21, ny, nz), f32),
            pltpu.VMEM((19, nx, ny, nz), f32),
            pltpu.VMEM((nx, ny, nz), f32),
            pltpu.SemaphoreType.DMA((len(OUT_GROUPS) + 1,)),
        ],
        outs=[HBM, HBM, VMEM],
    )
    if rides:
        drags += (tails,)
    whole_cells = float(nx * ny * nz * gx * gy * gz)
    (drag,) = call(functools.partial(drag_kernel, whole_cells), drags, [(1, 1)])
    return (first, gradient, drag.reshape(()))


def solution(mesh):
    return jax.shard_map(
        body,
        mesh=mesh,
        in_specs=(
            P(None, None, "gx", "gy", "gz"),
            P(None, "gx", "gy", "gz"),
            P("gx", "gy", "gz"),
            P("gx", "gy", "gz"),
        ),
        out_specs=(P(None, "gx", "gy", "gz"), P("gx", "gy", "gz"), P()),
        check_vma=False,
    )
```

```python
import functools

import jax
import jax.numpy as jnp
import numpy as np
from jax import lax
from jax.experimental import pallas as pl
from jax.experimental.pallas import tpu as pltpu
from jax.sharding import PartitionSpec as P

VEL = (
    (0, 0, 0),
    (1, 0, 0),
    (-1, 0, 0),
    (0, 1, 0),
    (0, -1, 0),
    (0, 0, 1),
    (0, 0, -1),
    (1, 1, 0),
    (-1, -1, 0),
    (1, -1, 0),
    (-1, 1, 0),
    (1, 0, 1),
    (-1, 0, -1),
    (1, 0, -1),
    (-1, 0, 1),
    (0, 1, 1),
    (0, -1, -1),
    (0, 1, -1),
    (0, -1, 1),
)
PAIRS = tuple((i, i + 1) for i in range(1, 19, 2))
AXES = ("gx", "gy", "gz")
UB = (19, 20, 21, 22)


def near(axis, sign):
    return tuple(i for i in range(19) if VEL[i][axis] * sign >= 0) + UB


def far(axis, sign):
    return tuple(i for i in range(19) if VEL[i][axis] == sign)


NSLOT = 23
CORNER = 24
EDGE_ROWS = 8


def y_rows(nx):
    return 14 * nx + 8


ZGROUPS = (
    tuple(i for i in range(19) if VEL[i][2] == -1),
    tuple(i for i in range(19) if VEL[i][2] == 1),
    tuple(i for i in range(19) if VEL[i][2] == 0)[:8],
    tuple(i for i in range(19) if VEL[i][2] == 0)[8:] + UB,
)
ZSLOT = {q: (g, k) for g, group in enumerate(ZGROUPS) for k, q in enumerate(group)}


def pairs_of(values):
    s = [values[a] + values[b] for a, b in PAIRS]
    d = [values[a] - values[b] for a, b in PAIRS]
    return s, d


def moments(v0, s, d):
    sx, sy, sz, sp, sq, sr, ss, st, su = s
    dx, dy, dz, dp, dq, dr, ds, dt, du = d
    ex = sp + sq
    ez = sr + ss
    ey = st + su
    faces = sx + sy + sz
    edges = ex + ez + ey
    exx = ex + ez
    eyy = ex + ey
    ezz = ez + ey
    fx = (dp + dq) + (dr + ds)
    fy = (dp - dq) + (dt + du)
    fz = (dr - ds) + (dt - du)
    return dict(
        rest=v0,
        faces=faces,
        edges=edges,
        total=v0 + faces + edges,
        face1=(dx, dy, dz),
        edge1=(fx, fy, fz),
        one=(dx + fx, dy + fy, dz + fz),
        face2=(sx, sy, sz),
        edge2=(exx, eyy, ezz),
        two=(sx + exx, sy + eyy, sz + ezz),
        cross=(sp - sq, sr - ss, st - su),
    )


def adjoint_cell(g, u, b, drive):
    s, d = pairs_of(g)
    m = moments(g[0], s, d)
    total = m["total"]
    trace = m["faces"] + 2.0 * m["edges"] - (30.0 / 19.0) * total
    p0 = (-1.2 / 19.0) * total - (2.0 / 21.0) * trace
    q = [
        (0.4 / 6.0) * (two - (10.0 / 19.0) * total) + (0.8 / 21.0) * trace
        for two in m["two"]
    ]
    qsum = q[0] + q[1] + q[2]
    qab = [0.1 * c for c in m["cross"]]
    p1 = [-0.12 * one for one in m["one"]]
    h0 = (
        0.4 * m["rest"]
        + (1.2 / 18.0) * m["faces"]
        + (1.2 / 36.0) * m["edges"]
        + p0
        + (1.0 / 3.0) * qsum
    )
    h1 = [
        (1.2 / 18.0) * f + (1.2 / 36.0) * e + (1.0 / 3.0) * p
        for f, e, p in zip(m["face1"], m["edge1"], p1)
    ]
    base = (1.0 / 3.0) * p0 + (1.0 / 9.0) * qsum
    haa = [
        (1.2 / 18.0) * f + (1.2 / 36.0) * e + (2.0 / 9.0) * qa + base
        for f, e, qa in zip(m["face2"], m["edge2"], q)
    ]
    hxy, hxz, hyz = [(2.0 / 45.0) * c for c in m["cross"]]
    ux, uy, uz = u
    v = (
        haa[0] * ux + hxy * uy + hxz * uz,
        hxy * ux + haa[1] * uy + hyz * uz,
        hxz * ux + hyz * uy + haa[2] * uz,
    )
    uv = ux * v[0] + uy * v[1] + uz * v[2]
    uu = ux * ux + uy * uy + uz * uz
    uuh = 1.5 * uu * h0
    a = h0 + uuh - 4.5 * uv
    nb = 1.0 - b
    e0 = nb * (a - p0)
    nq = [nb * x for x in q]
    nxy, nxz, nyz = [nb * x for x in qab]
    o = [
        nb * (3.0 * h1[k] + 9.0 * v[k] - 3.0 * u[k] * h0 - p1[k]) for k in range(3)
    ]
    o[0] = o[0] + b * drive
    alpha = -0.2 * nb
    half_s = 0.5 * (alpha + b)
    half_d = 0.5 * (alpha - b)
    exy = e0 - nq[0] - nq[1]
    exz = e0 - nq[0] - nq[2]
    eyz = e0 - nq[1] - nq[2]
    even = (
        e0 - nq[0],
        e0 - nq[1],
        e0 - nq[2],
        exy - nxy,
        exy + nxy,
        exz - nxz,
        exz + nxz,
        eyz - nyz,
        eyz + nyz,
    )
    odd = (
        o[0],
        o[1],
        o[2],
        o[0] + o[1],
        o[0] - o[1],
        o[0] + o[2],
        o[0] - o[2],
        o[1] + o[2],
        o[1] - o[2],
    )
    out = [(alpha + b) * g[0] + e0]
    for k in range(9):
        even_k = half_s * s[k] + even[k]
        odd_k = half_d * d[k] + odd[k]
        out.append(even_k + odd_k)
        out.append(even_k - odd_k)
    kept = dict(
        s=s, d=d, g0=g[0], p0=p0, p1=p1, q=q, qab=qab, h0=h0, h1=h1, uv=uv, uuh=uuh
    )
    return out, kept


def gradient_cell(kept, f0, fs, fd, fm, u):
    rho = fm["total"]
    even = fs[0] * kept["s"][0]
    odd = fd[0] * kept["d"][0]
    for k in range(1, 9):
        even = even + fs[k] * kept["s"][k]
        odd = odd + fd[k] * kept["d"][k]
    hf = kept["p0"] * rho
    for k in range(3):
        hf = hf + kept["p1"][k] * fm["one"][k] + kept["q"][k] * fm["two"][k]
        hf = hf + kept["qab"][k] * fm["cross"][k]
    uh1 = u[0] * kept["h1"][0] + u[1] * kept["h1"][1] + u[2] * kept["h1"][2]
    hfeq = rho * (kept["h0"] - kept["uuh"] + 3.0 * uh1 + 4.5 * kept["uv"])
    pairs = 1.2 * f0 * kept["g0"] + 0.6 * even - 0.4 * odd
    return pairs + hf - hfeq + fm["one"][0]


def state_of(ref, index):
    f = [ref[(index[0], i) + index[1:]] for i in range(19)]
    s, d = pairs_of(f)
    m = moments(f[0], s, d)
    inverse = 1.0 / m["total"]
    u = [one * inverse for one in m["one"]]
    return f[0], s, d, m, u


def corner_rows(sx, sy):
    rows = []
    for dx, dy in ((0, 0), (1, 0), (0, 1), (1, 1)):
        for i in near(0, sx) if dx == 0 else far(0, sx):
            if i in (near(1, sy) if dy == 0 else far(1, sy)):
                rows.append((i, dx, dy))
    return rows


def parity(axis):
    return lax.axis_index(axis) % 2


def cell_rows(adj_ref, ub_ref, q, x, rows):
    return adj_ref[q, x, rows, :] if q < 19 else ub_ref[q - 19, x, rows, :]


def state_kernel(
    states_hbm,
    por_hbm,
    mask_hbm,
    ub_ref,
    drag_ref,
    states_ref,
    por_ref,
    mask_ref,
    sems,
):
    nx, ny, nz = por_ref.shape
    tiles = ny // 8
    copies = [
        pltpu.make_async_copy(src, dst, sems.at[k])
        for k, (src, dst) in enumerate(
            (
                (states_hbm.at[1], states_ref.at[1]),
                (por_hbm, por_ref),
                (mask_hbm, mask_ref),
                (states_hbm.at[0, 1:3], states_ref.at[0, 1:3]),
                (states_hbm.at[0, 7:15], states_ref.at[0, 7:15]),
            )
        )
    ]
    for copy in copies:
        copy.start()
    for copy in copies[:3]:
        copy.wait()

    def cells(x, carry):
        for t in range(tiles):
            rows = slice(8 * t, 8 * t + 8)
            blocking = jnp.where(mask_ref[x, rows, :] == 0, por_ref[x, rows, :], 1.0)
            f0, s, d, m, u = state_of(states_ref, (1, x, rows))
            for k in range(3):
                ub_ref[k, x, rows, :] = u[k]
            ub_ref[3, x, rows, :] = blocking
            carry = carry + blocking * m["one"][0]
        return carry

    drag = lax.fori_loop(0, nx, cells, jnp.zeros((8, nz), jnp.float32))
    for copy in copies[3:]:
        copy.wait()

    def flux_cells(x, carry):
        for t in range(tiles):
            rows = slice(8 * t, 8 * t + 8)
            flux = 0.0
            for a, b in PAIRS:
                if VEL[a][0]:
                    flux = flux + (
                        states_ref[0, a, x, rows, :] - states_ref[0, b, x, rows, :]
                    )
            carry = carry + ub_ref[3, x, rows, :] * flux
        return carry

    drag = lax.fori_loop(0, nx, flux_cells, drag)
    drag_ref[...] = drag


def pack_x_kernel(adj_ref, ub_ref, drag_ref, out_ref):
    nx, ny = adj_ref.shape[1:3]
    out_ref[NSLOT * ny :] = drag_ref[...]

    def fill(sign):
        for names, offset, x in (
            (near(0, sign), 0, 0 if sign > 0 else nx - 1),
            (far(0, sign), 18, 1 if sign > 0 else nx - 2),
        ):
            for k, q in enumerate(names):
                k += offset
                out_ref[k * ny : (k + 1) * ny] = cell_rows(
                    adj_ref, ub_ref, q, x, slice(0, ny)
                )

    pl.when(parity("gx") == 0)(functools.partial(fill, -1))
    pl.when(parity("gx") == 1)(functools.partial(fill, 1))


def y_edge_entries(sign, nx):
    rows = []
    for side in (1, -1):
        x = 0 if side > 0 else nx - 1
        rows += [(i, 0, x) for i in far(0, side) if VEL[i][1] == 0]
        rows += [(i, 1, x) for i in far(0, side) if VEL[i][1] == sign]
    return rows


def edge_entries(sign):
    rows = []
    for side in (1, -1):
        rows += [(i, 0, side) for i in far(1, side) if VEL[i][0] == 0]
        rows += [(i, 1, side) for i in far(1, side) if VEL[i][0] == sign]
    return rows


def pack_partial_kernel(adj_ref, ub_ref, out_ref):
    nx, ny, nz = adj_ref.shape[1:]
    tiles = ny // 8
    sub = lax.broadcasted_iota(jnp.int32, (8, nz), 0)

    def fill(sign):
        here, inside = (0, 1) if sign > 0 else (nx - 1, nx - 2)
        names = far(0, sign)
        for t in range(tiles):
            rows = slice(8 * t, 8 * t + 8)
            got = []
            for i in range(19):
                cx, cy, cz = VEL[i]
                if cx * sign < 0:
                    got.append(jnp.zeros((8, nz), jnp.float32))
                    continue
                x = inside if cx else here
                if t == 0 and cy < 0:
                    value = pltpu.roll(adj_ref[i, x, rows, :], 1, 0)
                    value = jnp.where(sub == 0, 0.0, value)
                elif t == tiles - 1 and cy > 0:
                    value = pltpu.roll(adj_ref[i, x, rows, :], 7, 0)
                    value = jnp.where(sub == 7, 0.0, value)
                else:
                    value = adj_ref[i, x, 8 * t + cy : 8 * t + 8 + cy, :]
                got.append(z_shifted(value, cz))
            u = [ub_ref[k, here, rows, :] for k in range(3)]
            out, _ = adjoint_cell(got, u, ub_ref[3, here, rows, :], 0.0)
            for k, i in enumerate(names):
                out_ref[k * ny + 8 * t : k * ny + 8 * t + 8] = out[i]
        for k, q in enumerate(names + UB):
            k += 5
            out_ref[k * ny : (k + 1) * ny] = cell_rows(
                adj_ref, ub_ref, q, here, slice(0, ny)
            )
        for k, (i, depth, side) in enumerate(edge_entries(sign)):
            y = 0 if side > 0 else ny - 1
            row = 14 * ny + k
            out_ref[row : row + 1] = adj_ref[i, inside if depth else here, y : y + 1, :]

    pl.when(parity("gx") == 0)(functools.partial(fill, 1))
    pl.when(parity("gx") == 1)(functools.partial(fill, -1))


def column_pair(acc, value, pair, q, k, plane):
    start = 32 * (k // 2) + 4 * plane + 2 * (k % 2)
    cz = VEL[q][2] if q < 19 else 0
    return jnp.where(pair == start // 2, turn(value, start + 1 - cz), acc)


def pack_y_kernel(
    adj_ref, ub_ref, drag_ref, cols_ref, y_ref, ya_ref, yb_ref, read_ref
):
    nx, ny, nz = adj_ref.shape[1:]
    pair = lax.broadcasted_iota(jnp.int32, (8, nz), 1) // 2
    for g, group in enumerate(ZGROUPS):
        for t in range(ny // 8):
            acc = jnp.zeros((8, nz), jnp.float32)
            for k, q in enumerate(group):
                for x in range(nx):
                    value = cell_rows(adj_ref, ub_ref, q, x, slice(8 * t, 8 * t + 8))
                    acc = column_pair(acc, value, pair, q, k, x + 2)
            row = g * ny + 8 * t
            cols_ref[row : row + 8] = acc
    y_block = y_rows(nx) + EDGE_ROWS
    corner_block = CORNER + EDGE_ROWS

    def fill_edges(place, sign):
        for g in range(4):
            for d in range(2):
                y = d if sign > 0 else ny - 1 - d
                line = cols_ref[g * ny + y : g * ny + y + 1]
                row = place * y_block + y_rows(nx) + 2 * g + d
                y_ref[row : row + 1] = line
                row = place * corner_block + CORNER + 2 * g + d
                ya_ref[row : row + 1] = line
                yb_ref[row : row + 1] = line

    faces = ((1, 0, 1), (-1, ny - 1, ny - 2))
    for i in range(19):
        cx, cy, _ = VEL[i]
        read_ref[i] = jnp.zeros((2 * nx, nz), jnp.float32)
        for n, (sign, here, inside) in enumerate(faces):
            for x in range(max(0, -cx), min(nx, nx - cx)):
                if cy * sign >= 0:
                    y = inside if cy else here
                    read_ref[i, n * nx + x : n * nx + x + 1, :] = adj_ref[
                        i, x + cx, y : y + 1, :
                    ]
    for k in range(4):
        for n, (sign, here, inside) in enumerate(faces):
            for x in range(nx):
                read_ref[19 + k, n * nx + x : n * nx + x + 1, :] = ub_ref[
                    k, x, here : here + 1, :
                ]
    got = [z_shifted(read_ref[i], VEL[i][2]) for i in range(19)]
    sums, _ = adjoint_cell(
        got, [read_ref[19 + k] for k in range(3)], read_ref[22], 0.0
    )

    def fill_y(place, sign):
        n = 0 if sign > 0 else 1
        _, here, inside = faces[n]
        first = place * y_block
        for k, i in enumerate(far(1, sign)):
            row = first + k * nx
            y_ref[row : row + nx] = sums[i][n * nx : (n + 1) * nx]
        for k, q in enumerate(far(1, sign) + UB):
            for x in range(nx):
                row = first + (5 + k) * nx + x
                y_ref[row : row + 1] = cell_rows(
                    adj_ref, ub_ref, q, x, slice(here, here + 1)
                )
        for k, (i, depth, x) in enumerate(y_edge_entries(sign, nx)):
            y = inside if depth else here
            row = first + 14 * nx + k
            y_ref[row : row + 1] = adj_ref[i, x, y : y + 1, :]

    def fill_corner(out_ref, place, sx, sy):
        names = corner_rows(sx, sy)
        for k, (q, dx, dy) in enumerate(names):
            x = dx if sx > 0 else nx - 1 - dx
            y = dy if sy > 0 else ny - 1 - dy
            row = place * corner_block + k
            out_ref[row : row + 1] = cell_rows(adj_ref, ub_ref, q, x, slice(y, y + 1))
        row = place * corner_block + len(names)
        last = place * corner_block + CORNER
        out_ref[row:last] = jnp.zeros((last - row, nz), jnp.float32)

    drag = drag_ref[...]
    cols_ref[4 * ny :] = drag
    y_ref[2 * y_block :] = drag
    ya_ref[2 * corner_block :] = drag
    yb_ref[2 * corner_block :] = drag
    for py in (0, 1):

        @pl.when(parity("gy") == py)
        def _():
            s0 = 1 if py else -1
            fill_y(0, s0)
            fill_y(1, -s0)
            fill_edges(0, s0)
            fill_edges(1, -s0)

    for px in (0, 1):
        for py in (0, 1):

            @pl.when((parity("gx") == px) & (parity("gy") == py))
            def _():
                sa = 1 if px else -1
                s0 = 1 if py else -1
                for out_ref, sx in ((ya_ref, sa), (yb_ref, -sa)):
                    fill_corner(out_ref, 0, sx, s0)
                    fill_corner(out_ref, 1, sx, -s0)


def pack_z_kernel(
    cols_ref,
    xa_ref,
    xc_ref,
    y_ref,
    ya_ref,
    yb_ref,
    zown_ref,
    za_ref,
    zb_ref,
    drag_ref,
    ext,
):
    ny = (cols_ref.shape[0] - 8) // 4
    nz = cols_ref.shape[1]
    tiles = ny // 8
    base = 16
    even_x = parity("gx") == 0
    even_y = parity("gy") == 0
    lane = lax.broadcasted_iota(jnp.int32, (8, nz), 1)
    sub = lax.broadcasted_iota(jnp.int32, (8, nz), 0)
    plane = (lane % 32) // 4
    slot = 2 * (lane // 32) + (lane % 4) // 2

    def along_x(own, va, vb):
        low = turn(jnp.where(even_x, vb, va), -16)
        high = turn(jnp.where(even_x, va, vb), 16)
        return jnp.where(plane < 2, low, jnp.where(plane > 5, high, own))

    pair = lane // 2

    def fill_main(sign):
        halo = {}
        for names, offset, p in (
            (near(0, sign), 0, 6 if sign > 0 else 1),
            (far(0, sign), 18, 7 if sign > 0 else 0),
        ):
            for k, q in enumerate(names):
                halo.setdefault(q, []).append((k + offset, p))
        for g, group in enumerate(ZGROUPS):
            for t in range(tiles):
                rows = slice(g * ny + 8 * t, g * ny + 8 * t + 8)
                acc = jnp.where(
                    plane < 2 if sign > 0 else plane > 5,
                    turn(xc_ref[rows], -16 * sign),
                    cols_ref[rows],
                )
                for k, q in enumerate(group):
                    for at, p in halo.get(q, ()):
                        row = at * ny + 8 * t
                        acc = column_pair(acc, xa_ref[row : row + 8], pair, q, k, p)
                ext[g, base + 8 * t : base + 8 * t + 8, :] = acc

    @pl.when(parity("gx") == 0)
    def _():
        fill_main(1)

    @pl.when(parity("gx") == 1)
    def _():
        fill_main(-1)

    y_block = (y_ref.shape[0] - 8) // 2
    corner_block = CORNER + EDGE_ROWS

    def edges(ref, block, place):
        return ref[(place + 1) * block - EDGE_ROWS : (place + 1) * block]

    first, second = [
        along_x(
            edges(y_ref, y_block, place),
            edges(ya_ref, corner_block, place),
            edges(yb_ref, corner_block, place),
        )
        for place in range(2)
    ]
    high = jnp.where(even_y, first, second)
    low = jnp.where(even_y, second, first)
    for g in range(4):
        for d in range(2):
            row = 2 * g + d
            ext[g, base + ny + d : base + ny + d + 1, :] = high[row : row + 1]
            ext[g, base - 1 - d : base - d, :] = low[row : row + 1]

    packed = []
    for g, group in enumerate(ZGROUPS):
        moves = {}
        for k, q in enumerate(group):
            cx, cy, _ = VEL[q] if q < 19 else (0, 0, 0)
            moves.setdefault((cx, cy), []).append(k)
        acc = [jnp.zeros((8, nz), jnp.float32) for t in range(tiles + 1)]
        for (cx, cy), slots in moves.items():
            mask = slot == slots[0]
            for k in slots[1:]:
                mask = mask | (slot == k)
            for t in range(tiles + 1):
                if t < tiles:
                    row = base + 8 * t + cy
                    value = ext[g, row : row + 8, :]
                else:
                    above = base + ny + cy
                    below = base - 8 + cy
                    value = jnp.where(
                        sub < 4, ext[g, above : above + 8, :], ext[g, below : below + 8, :]
                    )
                acc[t] = jnp.where(mask, turn(value, -4 * cx), acc[t])
        packed.append(acc)
        for t in range(tiles + 1):
            row = (g * (tiles + 1) + t) * 8
            zown_ref[row : row + 8, :] = acc[t]
    up_first = parity("gz") == 0
    even_lane = lane % 2 == 0
    for t in range(tiles + 1):
        two, three = packed[2][t], packed[3][t]
        up = (packed[0][t], jnp.where(even_lane, two, pltpu.roll(three, 1, 1)))
        down = (packed[1][t], jnp.where(even_lane, pltpu.roll(two, nz - 1, 1), three))
        for g in range(2):
            row = (g * (tiles + 1) + t) * 8
            za_ref[row : row + 8, :] = jnp.where(up_first, up[g], down[g])
            zb_ref[row : row + 8, :] = jnp.where(up_first, down[g], up[g])
    drag = (cols_ref[4 * ny :] + y_ref[2 * y_block :]) + xa_ref[xa_ref.shape[0] - 8 :]
    drag = drag + (xc_ref[4 * ny :] + yb_ref[2 * corner_block :])
    drag_ref[...] = drag


def turn(value, shift):
    nz = value.shape[1]
    return pltpu.roll(value, shift % nz, 1) if shift % nz else value


def z_shifted(value, cz):
    return turn(value, -cz) if cz else value


def inner_kernel(
    states_ref,
    adj_ref,
    ub_ref,
    xa_ref,
    xb_ref,
    y_ref,
    ya_ref,
    yb_ref,
    out_ref,
    grad1_ref,
    grad_ref,
    pack_ref,
    f0_ref,
    f1_ref,
    ext,
    mid,
):
    nx, ny, nz = grad_ref.shape
    tiles = ny // 8
    lane = lax.broadcasted_iota(jnp.int32, (8, nz), 1)
    slot = lane // 4
    sub = lax.broadcasted_iota(jnp.int32, (8, nz), 0)
    even_x = parity("gx") == 0
    even_y = parity("gy") == 0
    base = 16

    for q in range(NSLOT):
        for x in range(nx):
            ext[q, x + 2, base : base + ny, :] = (
                adj_ref[q, x] if q < 19 else ub_ref[q - 19, x]
            )
    planes = {1: (nx + 2, nx + 3), -1: (1, 0)}
    lines = {1: (base + ny, base + ny + 1), -1: (base - 1, base - 2)}

    def fill_whole(sign):
        for names, depth, offset in ((near(0, sign), 0, 0), (far(0, sign), 1, 18)):
            for k, q in enumerate(names):
                rows = slice((k + offset) * ny, (k + offset + 1) * ny)
                ext[q, planes[sign][depth], base : base + ny, :] = xa_ref[rows]

    def fill_partial(sign):
        one, two = planes[sign]
        for k, q in enumerate(far(0, sign) + UB):
            ext[q, one, base : base + ny, :] = xb_ref[(5 + k) * ny : (6 + k) * ny]
        nothing = jnp.zeros((ny, nz), jnp.float32)
        for q in range(19):
            if VEL[q][0] == 0:
                ext[q, one, base : base + ny, :] = nothing
            elif VEL[q][0] == sign:
                ext[q, two, base : base + ny, :] = nothing
        for k, (q, depth, side) in enumerate(edge_entries(sign)):
            line = base if side > 0 else base + ny - 1
            row = 14 * ny + k
            ext[q, planes[sign][depth], line : line + 1, :] = xb_ref[row : row + 1]

    @pl.when(parity("gx") == 0)
    def _():
        fill_whole(1)
        fill_partial(-1)

    @pl.when(parity("gx") == 1)
    def _():
        fill_whole(-1)
        fill_partial(1)

    sums = {}
    for sign in (1, -1):
        block = y_rows(nx) + EDGE_ROWS
        first, second = (0, block) if sign > 0 else (block, 0)
        one, two = lines[sign]
        nothing = jnp.zeros((1, nz), jnp.float32)
        for q in range(19):
            for x in range(nx):
                if VEL[q][1] == 0:
                    ext[q, x + 2, one : one + 1, :] = nothing
                elif VEL[q][1] == sign:
                    ext[q, x + 2, two : two + 1, :] = nothing
        got = jnp.where(
            even_y,
            y_ref[first : first + y_rows(nx)],
            y_ref[second : second + y_rows(nx)],
        )
        sums[sign] = got
        for k, q in enumerate(far(1, sign) + UB):
            for x in range(nx):
                row = (5 + k) * nx + x
                ext[q, x + 2, one : one + 1, :] = got[row : row + 1]
        for k, (q, depth, x) in enumerate(y_edge_entries(sign, nx)):
            line = lines[sign][depth]
            row = 14 * nx + k
            ext[q, x + 2, line : line + 1, :] = got[row : row + 1]
        for sx in (1, -1):
            xs = (ya_ref, yb_ref) if sx > 0 else (yb_ref, ya_ref)
            block = CORNER + EDGE_ROWS
            ys = (0, block) if sign > 0 else (block, 0)
            low, high = [
                jnp.where(even_x, xs[0][r : r + CORNER], xs[1][r : r + CORNER])
                for r in ys
            ]
            got = jnp.where(even_y, low, high)
            for k, (q, dx, dy) in enumerate(corner_rows(sx, sign)):
                line = lines[sign][dy]
                ext[q, planes[sx][dx], line : line + 1, :] = got[k : k + 1]

    def near_cells(q, plane, t, cy):
        if t < tiles:
            row = base + 8 * t + cy
            return ext[q, plane, row : row + 8, :]
        above = base + ny + cy
        below = base - 8 + cy
        return jnp.where(
            sub < 4, ext[q, plane, above : above + 8, :], ext[q, plane, below : below + 8, :]
        )

    def first_level(p, t, kinds, partial=None):
        got = []
        for i in range(19):
            cx, cy, cz = VEL[i]
            got.append(z_shifted(near_cells(i, p + 1 + cx, t, cy), cz))
        ub = [near_cells(19 + k, p + 1, t, 0) for k in range(4)]
        out, kept = adjoint_cell(got, ub[:3], ub[3], 1.0)
        if t == tiles and 1 <= p <= nx:
            for sign, row in ((1, 0), (-1, 7)):
                for k, i in enumerate(far(1, sign)):
                    line = k * nx + p - 1
                    term = sums[sign][line : line + 1]
                    out[i] = out[i] + jnp.where(sub == row, term, 0.0)
        if partial is not None:
            for k, i in enumerate(kinds):
                row = k * ny + 8 * t
                out[i] = out[i] + jnp.where(partial, xb_ref[row : row + 8], 0.0)
        for i in kinds:
            if t < tiles:
                mid[i, p, t * 8 + 8 : t * 8 + 16, :] = out[i]
            elif VEL[i][1] > 0:
                mid[i, p, t * 8 + 8 : t * 8 + 16, :] = out[i]
            elif VEL[i][1] < 0:
                mid[i, p, 0:8, :] = out[i]
        return kept, ub[:3]

    def inside(x, carry):
        for t in range(tiles):
            kept, u = first_level(x + 1, t, range(19))
            rows = slice(t * 8, t * 8 + 8)
            f0, fs, fd, fm, _ = state_of(states_ref, (1, x, rows))
            grad1_ref[x, rows, :] = gradient_cell(kept, f0, fs, fd, fm, u)
        return carry

    lax.fori_loop(0, nx, inside, 0)
    for t in range(tiles):
        first_level(0, t, far(0, -1), even_x)
        first_level(nx + 1, t, far(0, 1), jnp.logical_not(even_x))

    for p in range(nx + 2):
        first_level(p, tiles, far(1, -1) + far(1, 1))

    def second_level(x, carry):
        for t in range(tiles):
            rows = slice(t * 8, t * 8 + 8)
            got = []
            for i in range(19):
                cx, cy, cz = VEL[i]
                low = 8 + 8 * t + cy
                value = z_shifted(mid[i, x + 1 + cx, low : low + 8, :], cz)
                got.append(value)
                pack_ref[i, rows, :] = jnp.where(
                    slot == x, pltpu.roll(value, 4 * x + 2, 1), pack_ref[i, rows, :]
                )
            f0, fs, fd, fm, u = state_of(states_ref, (0, x, rows))
            b = ub_ref[3, x, rows, :]
            out, kept = adjoint_cell(got, u, b, 1.0)
            for i in range(19):
                out_ref[i, x, rows, :] = out[i]
            grad_ref[x, rows, :] = grad1_ref[x, rows, :] + gradient_cell(
                kept, f0, fs, fd, fm, u
            )
        return carry

    lax.fori_loop(0, nx, second_level, 0)

    def tile(t, carry):
        rows = pl.ds(pl.multiple_of(t * 8, 8), 8)
        for i in range(20):
            for out_ref, level, first in ((f0_ref, 0, 0), (f1_ref, 1, 2)):
                if i == 19 and level == 1:
                    continue
                acc = jnp.zeros((8, nz), jnp.float32)
                for x in range(nx):
                    value = (
                        states_ref[level, i, x, rows, :]
                        if i < 19
                        else ub_ref[3, x, rows, :]
                    )
                    p = x + first
                    acc = jnp.where(slot == p, pltpu.roll(value, 4 * p + 2, 1), acc)
                out_ref[i, rows, :] = acc
        return carry

    lax.fori_loop(0, ny // 8, tile, 0)


def edge_kernel(
    mask_ref,
    zown_ref,
    za_ref,
    zb_ref,
    pack_ref,
    f0_ref,
    f1_ref,
    inner_ref,
    grad1_ref,
    inner_grad_ref,
    out_ref,
    grad_ref,
    tail_ref,
    first_ref,
    second_ref,
    zmid,
    zout,
):
    nx, ny, nz = mask_ref.shape
    tiles = ny // 8
    height = (tiles + 1) * 8
    even = parity("gz") == 0
    lane = lax.broadcasted_iota(jnp.int32, (8, nz), 1)
    even_lane = lane % 2 == 0
    low_pair = lane % 4 < 2

    last = slice(2 * height, 2 * height + 8)
    tail_ref[...] = za_ref[last] + zb_ref[last]

    def swapped(value):
        return jnp.where(even_lane, turn(value, -1), turn(value, 1))

    for t in range(tiles + 1):
        received = []
        for g in range(2):
            row = (g * (tiles + 1) + t) * 8
            va = za_ref[row : row + 8, :]
            vb = zb_ref[row : row + 8, :]
            received.append((jnp.where(even, va, vb), jnp.where(even, vb, va)))
        (high0, low0), (high1, low1) = received
        for g in range(4):
            row = (g * (tiles + 1) + t) * 8
            rows = slice(row, row + 8)
            own = zown_ref[rows]
            if g == 0:
                head, tail = own, low0
            elif g == 1:
                head, tail = high0, own
            elif g == 2:
                head = jnp.where(even_lane, own, turn(high1, 1))
                tail = jnp.where(even_lane, low1, own)
            else:
                head = jnp.where(even_lane, own, high1)
                tail = jnp.where(even_lane, turn(low1, -1), own)
            head = swapped(head)
            tail = swapped(tail)
            first_ref[rows] = jnp.where(low_pair, head, turn(tail, 2))
            second_ref[rows] = jnp.where(low_pair, turn(head, -2), tail)

    slab_grad = []
    for t in range(tiles + 1):
        got = []
        for q in range(NSLOT):
            g, k = ZSLOT[q]
            row = g * height + t * 8
            ref = second_ref if k % 2 else first_ref
            got.append(turn(ref[row : row + 8, :], -32 * (k // 2)))
        out, kept = adjoint_cell(got[:19], got[19:22], got[22], 1.0)
        for i in range(19):
            zmid[i, 8 * t + 8 : 8 * t + 16, :] = out[i]
            if t == tiles:
                zmid[i, 0:8, :] = out[i]
        if t < tiles:
            f = [f1_ref[i, 8 * t : 8 * t + 8, :] for i in range(19)]
            fs, fd = pairs_of(f)
            fm = moments(f[0], fs, fd)
            grad = gradient_cell(kept, f[0], fs, fd, fm, got[19:22])
            slab_grad.append(turn(grad, -8))

    at = lane % 4
    for t in range(tiles):
        rows = slice(8 * t, 8 * t + 8)
        got = []
        for i in range(19):
            cx, cy, cz = VEL[i]
            value = pack_ref[i, rows, :]
            edge = zmid[i, 8 + 8 * t + cy : 16 + 8 * t + cy, :]
            back = -4 * (2 + cx)
            if cz == 0:
                value = jnp.where((at == 1) | (at == 2), turn(edge, back), value)
            else:
                near_lane = 2 if cz < 0 else 0
                value = jnp.where(at == near_lane, turn(edge, back - 1), value)
                value = jnp.where(at == near_lane + 1, turn(edge, back + 1), value)
            got.append(value)
        f = [f0_ref[i, rows, :] for i in range(19)]
        fs, fd = pairs_of(f)
        fm = moments(f[0], fs, fd)
        inverse = 1.0 / fm["total"]
        u = [one * inverse for one in fm["one"]]
        out, kept = adjoint_cell(got, u, f0_ref[19, rows, :], 1.0)
        for i in range(19):
            zout[i, rows, :] = out[i]
        zout[19, rows, :] = gradient_cell(kept, f[0], fs, fd, fm, u)
        zout[20, rows, :] = slab_grad[t]

    outer = (lane < 2) | (lane >= nz - 2)
    ends = (lane < 1) | (lane >= nz - 1)
    for x in range(nx):
        for t in range(tiles):
            rows = slice(8 * t, 8 * t + 8)
            level1 = jnp.where(
                ends, turn(zout[20, rows, :], -2 - 4 * x), grad1_ref[x, rows, :]
            )
            edge = turn(zout[19, rows, :], -2 - 4 * x) + level1
            grad = jnp.where(outer, edge, inner_grad_ref[x, rows, :])
            grad_ref[x, rows, :] = jnp.where(mask_ref[x, rows, :] == 0, grad, 0.0)
    for i in range(19):
        for x in range(nx):
            for t in range(tiles):
                rows = slice(8 * t, 8 * t + 8)
                out_ref[i, x, rows, :] = jnp.where(
                    outer, turn(zout[i, rows, :], -2 - 4 * x), inner_ref[i, x, rows, :]
                )


def finish_kernel(whole_cells, out_ref, grad_ref, *refs):
    tiles, (out_hbm, grad_hbm, drag_hbm, drag_ref, sems) = refs[:-5], refs[-5:]
    copies = [
        pltpu.make_async_copy(out_ref, out_hbm, sems.at[0]),
        pltpu.make_async_copy(grad_ref, grad_hbm, sems.at[1]),
        pltpu.make_async_copy(drag_ref, drag_hbm, sems.at[2]),
    ]
    for copy in copies[:2]:
        copy.start()
    total = tiles[0][...]
    for ref in tiles[1:]:
        total = total + ref[...]
    summed = jnp.sum(jnp.sum(total, axis=1, keepdims=True), axis=0, keepdims=True)
    drag_ref[...] = summed / whole_cells
    copies[2].start()
    for copy in copies:
        copy.wait()


def swaps(count):
    first = [(i, i ^ 1) for i in range(count)]
    second = [(i, (((i + 1) % count) ^ 1) - 1) for i in range(count)]
    second = [(i, j % count) for i, j in second]
    return first, second


VMEM = pl.BlockSpec(memory_space=pltpu.VMEM)
HBM = pl.BlockSpec(memory_space=pltpu.HBM)
PARAMS = pltpu.CompilerParams(vmem_limit_bytes=48 * 2**20)


def call(kernel, inputs, shapes, scratch=(), space=VMEM, micros=0.05, outs=None):
    if space is HBM:
        inputs = [pltpu.with_memory_space_constraint(x, pltpu.HBM) for x in inputs]
    return pl.pallas_call(
        kernel,
        out_shape=[jax.ShapeDtypeStruct(s, jnp.float32) for s in shapes],
        in_specs=[space] * len(inputs),
        out_specs=outs or [VMEM] * len(shapes),
        scratch_shapes=list(scratch),
        compiler_params=PARAMS,
        cost_estimate=pl.CostEstimate(
            flops=0, bytes_accessed=int(3.6e6 * micros), transcendentals=0
        ),
    )(*inputs)


def body(primal_states, adjoint_last, porosity, solid_mask):
    nx, ny, nz = porosity.shape
    gx, gy, gz = [lax.axis_size(axis) for axis in AXES]
    x_first, x_second = swaps(gx)
    y_first, y_second = swaps(gy)
    z_first, z_second = swaps(gz)
    tiles = ny // 8
    height = (tiles + 1) * 8
    f32 = jnp.float32

    def diagonal(message, x_pairs, y_pairs):
        pairs = [(a * gy + c, b * gy + d) for a, b in x_pairs for c, d in y_pairs]
        return lax.ppermute(message, ("gx", "gy"), pairs)

    rows_x = NSLOT * ny + 8
    rows_y = 2 * (y_rows(nx) + EDGE_ROWS) + 8
    rows_c = 2 * (CORNER + EDGE_ROWS) + 8
    rows_z = 2 * height + 8
    rides = (gx, gy, gz) == (4, 2, 4)
    ub, drag = call(
        state_kernel,
        (primal_states, porosity, solid_mask),
        [(4, nx, ny, nz), (8, nz)],
        [
            pltpu.VMEM((2, 19, nx, ny, nz), f32),
            pltpu.VMEM((nx, ny, nz), f32),
            pltpu.VMEM((nx, ny, nz), jnp.int32),
            pltpu.SemaphoreType.DMA((5,)),
        ],
        HBM,
    )
    cols, y, ya, yb = call(
        pack_y_kernel,
        (adjoint_last, ub, drag),
        [(4 * ny + 8, nz), (rows_y, nz), (rows_c, nz), (rows_c, nz)],
        [pltpu.VMEM((NSLOT, 2 * nx, nz), f32)],
        micros=4,
    )
    (xa,) = call(pack_x_kernel, (adjoint_last, ub, drag), [(rows_x, nz)])
    (xb,) = call(pack_partial_kernel, (adjoint_last, ub), [(14 * ny + 8, nz)])
    xc = lax.ppermute(cols, "gx", x_second)
    xa = lax.ppermute(xa, "gx", x_first)
    if gy == 2:
        y = lax.ppermute(y, "gy", y_first)
        yb = diagonal(yb, x_second, y_first)
        ya = diagonal(ya, x_first, y_first)
    else:

        def both(message, block, send):
            parts = [message[:block], message[block : 2 * block], message[2 * block :]]
            return jnp.concatenate(
                [send(parts[0], y_first), send(parts[1], y_second), parts[2]]
            )

        block = y_rows(nx) + EDGE_ROWS
        y = both(y, block, lambda m, pairs: lax.ppermute(m, "gy", pairs))
        block = CORNER + EDGE_ROWS
        yb = both(yb, block, lambda m, pairs: diagonal(m, x_second, pairs))
        ya = both(ya, block, lambda m, pairs: diagonal(m, x_first, pairs))
    xb, y = lax.optimization_barrier((xb, y))
    xb = lax.ppermute(xb, "gx", x_second)

    zown, za, zb, drag_xy = call(
        pack_z_kernel,
        (cols, xa, xc, y, ya, yb),
        [(4 * height, nz), (rows_z, nz), (rows_z, nz), (8, nz)],
        [pltpu.VMEM((4, ny + 32, nz), f32)],
    )
    if rides:
        second = xc[4 * ny :] + yb[rows_c - 8 :] + y[rows_y - 8 :]
        drag_xy = drag_xy + lax.ppermute(second, "gx", x_first)
        za = za.at[2 * height :].set(drag_xy)
        zb = zb.at[2 * height :].set(drag_xy)
    zb = lax.ppermute(zb, "gz", z_second)
    za = lax.ppermute(za, "gz", z_first)
    inner, grad1, inner_grad, pack, f0, f1 = call(
        inner_kernel,
        (primal_states, adjoint_last, ub, xa, xb, y, ya, yb),
        [
            (19, nx, ny, nz),
            (nx, ny, nz),
            (nx, ny, nz),
            (19, ny, nz),
            (20, ny, nz),
            (19, ny, nz),
        ],
        [
            pltpu.VMEM((NSLOT, nx + 4, ny + 32, nz), f32),
            pltpu.VMEM((19, nx + 2, height + 8, nz), f32),
        ],
        micros=4,
    )
    if rides:
        zhalf = lax.ppermute(drag_xy, "gz", [(i, i ^ 2) for i in range(gz)])
        drags = (drag_xy, zhalf)
    else:
        drags = (lax.psum(drag, AXES),)

    first, gradient, tails = call(
        edge_kernel,
        (solid_mask, zown, za, zb, pack, f0, f1, inner, grad1, inner_grad),
        [(19, nx, ny, nz), (nx, ny, nz), (8, nz)],
        [
            pltpu.VMEM((4 * height, nz), f32),
            pltpu.VMEM((4 * height, nz), f32),
            pltpu.VMEM((19, height + 8, nz), f32),
            pltpu.VMEM((21, ny, nz), f32),
        ],
    )
    if rides:
        drags += (tails,)
    whole_cells = float(nx * ny * nz * gx * gy * gz)
    first, gradient, drag = call(
        functools.partial(finish_kernel, whole_cells),
        (first, gradient) + drags,
        [(19, nx, ny, nz), (nx, ny, nz), (1, 1)],
        [pltpu.VMEM((1, 1), f32), pltpu.SemaphoreType.DMA((3,))],
        outs=[HBM, HBM, HBM],
    )
    return (first, gradient, drag.reshape(()))


def solution(mesh):
    return jax.shard_map(
        body,
        mesh=mesh,
        in_specs=(
            P(None, None, "gx", "gy", "gz"),
            P(None, "gx", "gy", "gz"),
            P("gx", "gy", "gz"),
            P("gx", "gy", "gz"),
        ),
        out_specs=(P(None, "gx", "gy", "gz"), P("gx", "gy", "gz"), P()),
        check_vma=False,
    )
```

```python
import functools

import jax
import jax.numpy as jnp
import numpy as np
from jax import lax
from jax.experimental import pallas as pl
from jax.experimental.pallas import tpu as pltpu
from jax.sharding import PartitionSpec as P

VEL = (
    (0, 0, 0),
    (1, 0, 0),
    (-1, 0, 0),
    (0, 1, 0),
    (0, -1, 0),
    (0, 0, 1),
    (0, 0, -1),
    (1, 1, 0),
    (-1, -1, 0),
    (1, -1, 0),
    (-1, 1, 0),
    (1, 0, 1),
    (-1, 0, -1),
    (1, 0, -1),
    (-1, 0, 1),
    (0, 1, 1),
    (0, -1, -1),
    (0, 1, -1),
    (0, -1, 1),
)
PAIRS = tuple((i, i + 1) for i in range(1, 19, 2))
AXES = ("gx", "gy", "gz")
UB = (19, 20, 21, 22)


def near(axis, sign):
    return tuple(i for i in range(19) if VEL[i][axis] * sign >= 0) + UB


def far(axis, sign):
    return tuple(i for i in range(19) if VEL[i][axis] == sign)


NSLOT = 23
CORNER = 24
EDGE_ROWS = 8


def y_rows(nx):
    return 14 * nx + 8


ZGROUPS = (
    tuple(i for i in range(19) if VEL[i][2] == -1),
    tuple(i for i in range(19) if VEL[i][2] == 1),
    tuple(i for i in range(19) if VEL[i][2] == 0)[:8],
    tuple(i for i in range(19) if VEL[i][2] == 0)[8:] + UB,
)
ZSLOT = {q: (g, k) for g, group in enumerate(ZGROUPS) for k, q in enumerate(group)}


def pairs_of(values):
    s = [values[a] + values[b] for a, b in PAIRS]
    d = [values[a] - values[b] for a, b in PAIRS]
    return s, d


def moments(v0, s, d):
    sx, sy, sz, sp, sq, sr, ss, st, su = s
    dx, dy, dz, dp, dq, dr, ds, dt, du = d
    ex = sp + sq
    ez = sr + ss
    ey = st + su
    faces = sx + sy + sz
    edges = ex + ez + ey
    exx = ex + ez
    eyy = ex + ey
    ezz = ez + ey
    fx = (dp + dq) + (dr + ds)
    fy = (dp - dq) + (dt + du)
    fz = (dr - ds) + (dt - du)
    return dict(
        rest=v0,
        faces=faces,
        edges=edges,
        total=v0 + faces + edges,
        face1=(dx, dy, dz),
        edge1=(fx, fy, fz),
        one=(dx + fx, dy + fy, dz + fz),
        face2=(sx, sy, sz),
        edge2=(exx, eyy, ezz),
        two=(sx + exx, sy + eyy, sz + ezz),
        cross=(sp - sq, sr - ss, st - su),
    )


def adjoint_cell(g, u, b, drive):
    s, d = pairs_of(g)
    m = moments(g[0], s, d)
    total = m["total"]
    trace = m["faces"] + 2.0 * m["edges"] - (30.0 / 19.0) * total
    p0 = (-1.2 / 19.0) * total - (2.0 / 21.0) * trace
    q = [
        (0.4 / 6.0) * (two - (10.0 / 19.0) * total) + (0.8 / 21.0) * trace
        for two in m["two"]
    ]
    qsum = q[0] + q[1] + q[2]
    qab = [0.1 * c for c in m["cross"]]
    p1 = [-0.12 * one for one in m["one"]]
    h0 = (
        0.4 * m["rest"]
        + (1.2 / 18.0) * m["faces"]
        + (1.2 / 36.0) * m["edges"]
        + p0
        + (1.0 / 3.0) * qsum
    )
    h1 = [
        (1.2 / 18.0) * f + (1.2 / 36.0) * e + (1.0 / 3.0) * p
        for f, e, p in zip(m["face1"], m["edge1"], p1)
    ]
    base = (1.0 / 3.0) * p0 + (1.0 / 9.0) * qsum
    haa = [
        (1.2 / 18.0) * f + (1.2 / 36.0) * e + (2.0 / 9.0) * qa + base
        for f, e, qa in zip(m["face2"], m["edge2"], q)
    ]
    hxy, hxz, hyz = [(2.0 / 45.0) * c for c in m["cross"]]
    ux, uy, uz = u
    v = (
        haa[0] * ux + hxy * uy + hxz * uz,
        hxy * ux + haa[1] * uy + hyz * uz,
        hxz * ux + hyz * uy + haa[2] * uz,
    )
    uv = ux * v[0] + uy * v[1] + uz * v[2]
    uu = ux * ux + uy * uy + uz * uz
    uuh = 1.5 * uu * h0
    a = h0 + uuh - 4.5 * uv
    nb = 1.0 - b
    e0 = nb * (a - p0)
    nq = [nb * x for x in q]
    nxy, nxz, nyz = [nb * x for x in qab]
    o = [
        nb * (3.0 * h1[k] + 9.0 * v[k] - 3.0 * u[k] * h0 - p1[k]) for k in range(3)
    ]
    o[0] = o[0] + b * drive
    alpha = -0.2 * nb
    half_s = 0.5 * (alpha + b)
    half_d = 0.5 * (alpha - b)
    exy = e0 - nq[0] - nq[1]
    exz = e0 - nq[0] - nq[2]
    eyz = e0 - nq[1] - nq[2]
    even = (
        e0 - nq[0],
        e0 - nq[1],
        e0 - nq[2],
        exy - nxy,
        exy + nxy,
        exz - nxz,
        exz + nxz,
        eyz - nyz,
        eyz + nyz,
    )
    odd = (
        o[0],
        o[1],
        o[2],
        o[0] + o[1],
        o[0] - o[1],
        o[0] + o[2],
        o[0] - o[2],
        o[1] + o[2],
        o[1] - o[2],
    )
    out = [(alpha + b) * g[0] + e0]
    for k in range(9):
        even_k = half_s * s[k] + even[k]
        odd_k = half_d * d[k] + odd[k]
        out.append(even_k + odd_k)
        out.append(even_k - odd_k)
    kept = dict(
        s=s, d=d, g0=g[0], p0=p0, p1=p1, q=q, qab=qab, h0=h0, h1=h1, uv=uv, uuh=uuh
    )
    return out, kept


def gradient_cell(kept, f0, fs, fd, fm, u):
    rho = fm["total"]
    even = fs[0] * kept["s"][0]
    odd = fd[0] * kept["d"][0]
    for k in range(1, 9):
        even = even + fs[k] * kept["s"][k]
        odd = odd + fd[k] * kept["d"][k]
    hf = kept["p0"] * rho
    for k in range(3):
        hf = hf + kept["p1"][k] * fm["one"][k] + kept["q"][k] * fm["two"][k]
        hf = hf + kept["qab"][k] * fm["cross"][k]
    uh1 = u[0] * kept["h1"][0] + u[1] * kept["h1"][1] + u[2] * kept["h1"][2]
    hfeq = rho * (kept["h0"] - kept["uuh"] + 3.0 * uh1 + 4.5 * kept["uv"])
    pairs = 1.2 * f0 * kept["g0"] + 0.6 * even - 0.4 * odd
    return pairs + hf - hfeq + fm["one"][0]


def state_of(ref, index):
    f = [ref[(index[0], i) + index[1:]] for i in range(19)]
    s, d = pairs_of(f)
    m = moments(f[0], s, d)
    inverse = 1.0 / m["total"]
    u = [one * inverse for one in m["one"]]
    return f[0], s, d, m, u


def corner_rows(sx, sy):
    rows = []
    for dx, dy in ((0, 0), (1, 0), (0, 1), (1, 1)):
        for i in near(0, sx) if dx == 0 else far(0, sx):
            if i in (near(1, sy) if dy == 0 else far(1, sy)):
                rows.append((i, dx, dy))
    return rows


def parity(axis):
    return lax.axis_index(axis) % 2


def cell_rows(adj_ref, ub_ref, q, x, rows):
    return adj_ref[q, x, rows, :] if q < 19 else ub_ref[q - 19, x, rows, :]


def state_kernel(
    states_hbm,
    por_hbm,
    mask_hbm,
    ub_ref,
    drag_ref,
    states_ref,
    por_ref,
    mask_ref,
    sems,
):
    nx, ny, nz = por_ref.shape
    tiles = ny // 8
    copies = [
        pltpu.make_async_copy(src, dst, sems.at[k])
        for k, (src, dst) in enumerate(
            (
                (states_hbm.at[1], states_ref.at[1]),
                (por_hbm, por_ref),
                (mask_hbm, mask_ref),
                (states_hbm.at[0, 1:3], states_ref.at[0, 1:3]),
                (states_hbm.at[0, 7:15], states_ref.at[0, 7:15]),
            )
        )
    ]
    for copy in copies:
        copy.start()
    for copy in copies[:3]:
        copy.wait()

    def cells(x, carry):
        for t in range(tiles):
            rows = slice(8 * t, 8 * t + 8)
            blocking = jnp.where(mask_ref[x, rows, :] == 0, por_ref[x, rows, :], 1.0)
            f0, s, d, m, u = state_of(states_ref, (1, x, rows))
            for k in range(3):
                ub_ref[k, x, rows, :] = u[k]
            ub_ref[3, x, rows, :] = blocking
            carry = carry + blocking * m["one"][0]
        return carry

    drag = lax.fori_loop(0, nx, cells, jnp.zeros((8, nz), jnp.float32))
    for copy in copies[3:]:
        copy.wait()

    def flux_cells(x, carry):
        for t in range(tiles):
            rows = slice(8 * t, 8 * t + 8)
            flux = 0.0
            for a, b in PAIRS:
                if VEL[a][0]:
                    flux = flux + (
                        states_ref[0, a, x, rows, :] - states_ref[0, b, x, rows, :]
                    )
            carry = carry + ub_ref[3, x, rows, :] * flux
        return carry

    drag = lax.fori_loop(0, nx, flux_cells, drag)
    drag_ref[...] = drag


def pack_x_kernel(adj_ref, ub_ref, drag_ref, out_ref):
    nx, ny = adj_ref.shape[1:3]
    out_ref[NSLOT * ny :] = drag_ref[...]

    def fill(sign):
        for names, offset, x in (
            (near(0, sign), 0, 0 if sign > 0 else nx - 1),
            (far(0, sign), 18, 1 if sign > 0 else nx - 2),
        ):
            for k, q in enumerate(names):
                k += offset
                out_ref[k * ny : (k + 1) * ny] = cell_rows(
                    adj_ref, ub_ref, q, x, slice(0, ny)
                )

    pl.when(parity("gx") == 0)(functools.partial(fill, -1))
    pl.when(parity("gx") == 1)(functools.partial(fill, 1))


def y_edge_entries(sign, nx):
    rows = []
    for side in (1, -1):
        x = 0 if side > 0 else nx - 1
        rows += [(i, 0, x) for i in far(0, side) if VEL[i][1] == 0]
        rows += [(i, 1, x) for i in far(0, side) if VEL[i][1] == sign]
    return rows


def edge_entries(sign):
    rows = []
    for side in (1, -1):
        rows += [(i, 0, side) for i in far(1, side) if VEL[i][0] == 0]
        rows += [(i, 1, side) for i in far(1, side) if VEL[i][0] == sign]
    return rows


def pack_partial_kernel(adj_ref, ub_ref, out_ref):
    nx, ny, nz = adj_ref.shape[1:]
    tiles = ny // 8
    sub = lax.broadcasted_iota(jnp.int32, (8, nz), 0)

    def fill(sign):
        here, inside = (0, 1) if sign > 0 else (nx - 1, nx - 2)
        names = far(0, sign)
        for t in range(tiles):
            rows = slice(8 * t, 8 * t + 8)
            got = []
            for i in range(19):
                cx, cy, cz = VEL[i]
                if cx * sign < 0:
                    got.append(jnp.zeros((8, nz), jnp.float32))
                    continue
                x = inside if cx else here
                if t == 0 and cy < 0:
                    value = pltpu.roll(adj_ref[i, x, rows, :], 1, 0)
                    value = jnp.where(sub == 0, 0.0, value)
                elif t == tiles - 1 and cy > 0:
                    value = pltpu.roll(adj_ref[i, x, rows, :], 7, 0)
                    value = jnp.where(sub == 7, 0.0, value)
                else:
                    value = adj_ref[i, x, 8 * t + cy : 8 * t + 8 + cy, :]
                got.append(z_shifted(value, cz))
            u = [ub_ref[k, here, rows, :] for k in range(3)]
            out, _ = adjoint_cell(got, u, ub_ref[3, here, rows, :], 0.0)
            for k, i in enumerate(names):
                out_ref[k * ny + 8 * t : k * ny + 8 * t + 8] = out[i]
        for k, q in enumerate(names + UB):
            k += 5
            out_ref[k * ny : (k + 1) * ny] = cell_rows(
                adj_ref, ub_ref, q, here, slice(0, ny)
            )
        for k, (i, depth, side) in enumerate(edge_entries(sign)):
            y = 0 if side > 0 else ny - 1
            row = 14 * ny + k
            out_ref[row : row + 1] = adj_ref[i, inside if depth else here, y : y + 1, :]

    pl.when(parity("gx") == 0)(functools.partial(fill, 1))
    pl.when(parity("gx") == 1)(functools.partial(fill, -1))


def column_pair(acc, value, pair, q, k, plane):
    start = 32 * (k // 2) + 4 * plane + 2 * (k % 2)
    cz = VEL[q][2] if q < 19 else 0
    return jnp.where(pair == start // 2, turn(value, start + 1 - cz), acc)


def pack_y_kernel(
    adj_ref, ub_ref, drag_ref, cols_ref, y_ref, ya_ref, yb_ref, read_ref
):
    nx, ny, nz = adj_ref.shape[1:]
    pair = lax.broadcasted_iota(jnp.int32, (8, nz), 1) // 2
    for g, group in enumerate(ZGROUPS):
        for t in range(ny // 8):
            acc = jnp.zeros((8, nz), jnp.float32)
            for k, q in enumerate(group):
                for x in range(nx):
                    value = cell_rows(adj_ref, ub_ref, q, x, slice(8 * t, 8 * t + 8))
                    acc = column_pair(acc, value, pair, q, k, x + 2)
            row = g * ny + 8 * t
            cols_ref[row : row + 8] = acc
    y_block = y_rows(nx) + EDGE_ROWS
    corner_block = CORNER + EDGE_ROWS

    def fill_edges(place, sign):
        for g in range(4):
            for d in range(2):
                y = d if sign > 0 else ny - 1 - d
                line = cols_ref[g * ny + y : g * ny + y + 1]
                row = place * y_block + y_rows(nx) + 2 * g + d
                y_ref[row : row + 1] = line
                row = place * corner_block + CORNER + 2 * g + d
                ya_ref[row : row + 1] = line
                yb_ref[row : row + 1] = line

    faces = ((1, 0, 1), (-1, ny - 1, ny - 2))
    for i in range(19):
        cx, cy, _ = VEL[i]
        read_ref[i] = jnp.zeros((2 * nx, nz), jnp.float32)
        for n, (sign, here, inside) in enumerate(faces):
            for x in range(max(0, -cx), min(nx, nx - cx)):
                if cy * sign >= 0:
                    y = inside if cy else here
                    read_ref[i, n * nx + x : n * nx + x + 1, :] = adj_ref[
                        i, x + cx, y : y + 1, :
                    ]
    for k in range(4):
        for n, (sign, here, inside) in enumerate(faces):
            for x in range(nx):
                read_ref[19 + k, n * nx + x : n * nx + x + 1, :] = ub_ref[
                    k, x, here : here + 1, :
                ]
    got = [z_shifted(read_ref[i], VEL[i][2]) for i in range(19)]
    sums, _ = adjoint_cell(
        got, [read_ref[19 + k] for k in range(3)], read_ref[22], 0.0
    )

    def fill_y(place, sign):
        n = 0 if sign > 0 else 1
        _, here, inside = faces[n]
        first = place * y_block
        for k, i in enumerate(far(1, sign)):
            row = first + k * nx
            y_ref[row : row + nx] = sums[i][n * nx : (n + 1) * nx]
        for k, q in enumerate(far(1, sign) + UB):
            for x in range(nx):
                row = first + (5 + k) * nx + x
                y_ref[row : row + 1] = cell_rows(
                    adj_ref, ub_ref, q, x, slice(here, here + 1)
                )
        for k, (i, depth, x) in enumerate(y_edge_entries(sign, nx)):
            y = inside if depth else here
            row = first + 14 * nx + k
            y_ref[row : row + 1] = adj_ref[i, x, y : y + 1, :]

    def fill_corner(out_ref, place, sx, sy):
        names = corner_rows(sx, sy)
        for k, (q, dx, dy) in enumerate(names):
            x = dx if sx > 0 else nx - 1 - dx
            y = dy if sy > 0 else ny - 1 - dy
            row = place * corner_block + k
            out_ref[row : row + 1] = cell_rows(adj_ref, ub_ref, q, x, slice(y, y + 1))
        row = place * corner_block + len(names)
        last = place * corner_block + CORNER
        out_ref[row:last] = jnp.zeros((last - row, nz), jnp.float32)

    drag = drag_ref[...]
    cols_ref[4 * ny :] = drag
    y_ref[2 * y_block :] = drag
    ya_ref[2 * corner_block :] = drag
    yb_ref[2 * corner_block :] = drag
    for py in (0, 1):

        @pl.when(parity("gy") == py)
        def _():
            s0 = 1 if py else -1
            fill_y(0, s0)
            fill_y(1, -s0)
            fill_edges(0, s0)
            fill_edges(1, -s0)

    for px in (0, 1):
        for py in (0, 1):

            @pl.when((parity("gx") == px) & (parity("gy") == py))
            def _():
                sa = 1 if px else -1
                s0 = 1 if py else -1
                for out_ref, sx in ((ya_ref, sa), (yb_ref, -sa)):
                    fill_corner(out_ref, 0, sx, s0)
                    fill_corner(out_ref, 1, sx, -s0)


def pack_z_kernel(
    cols_ref,
    xa_ref,
    xc_ref,
    y_ref,
    ya_ref,
    yb_ref,
    zown_ref,
    za_ref,
    zb_ref,
    drag_ref,
    ext,
):
    ny = (cols_ref.shape[0] - 8) // 4
    nz = cols_ref.shape[1]
    tiles = ny // 8
    base = 16
    even_x = parity("gx") == 0
    even_y = parity("gy") == 0
    lane = lax.broadcasted_iota(jnp.int32, (8, nz), 1)
    sub = lax.broadcasted_iota(jnp.int32, (8, nz), 0)
    plane = (lane % 32) // 4
    slot = 2 * (lane // 32) + (lane % 4) // 2

    def along_x(own, va, vb):
        low = turn(jnp.where(even_x, vb, va), -16)
        high = turn(jnp.where(even_x, va, vb), 16)
        return jnp.where(plane < 2, low, jnp.where(plane > 5, high, own))

    pair = lane // 2

    def fill_main(sign):
        halo = {}
        for names, offset, p in (
            (near(0, sign), 0, 6 if sign > 0 else 1),
            (far(0, sign), 18, 7 if sign > 0 else 0),
        ):
            for k, q in enumerate(names):
                halo.setdefault(q, []).append((k + offset, p))
        for g, group in enumerate(ZGROUPS):
            for t in range(tiles):
                rows = slice(g * ny + 8 * t, g * ny + 8 * t + 8)
                acc = jnp.where(
                    plane < 2 if sign > 0 else plane > 5,
                    turn(xc_ref[rows], -16 * sign),
                    cols_ref[rows],
                )
                for k, q in enumerate(group):
                    for at, p in halo.get(q, ()):
                        row = at * ny + 8 * t
                        acc = column_pair(acc, xa_ref[row : row + 8], pair, q, k, p)
                ext[g, base + 8 * t : base + 8 * t + 8, :] = acc

    @pl.when(parity("gx") == 0)
    def _():
        fill_main(1)

    @pl.when(parity("gx") == 1)
    def _():
        fill_main(-1)

    y_block = (y_ref.shape[0] - 8) // 2
    corner_block = CORNER + EDGE_ROWS

    def edges(ref, block, place):
        return ref[(place + 1) * block - EDGE_ROWS : (place + 1) * block]

    first, second = [
        along_x(
            edges(y_ref, y_block, place),
            edges(ya_ref, corner_block, place),
            edges(yb_ref, corner_block, place),
        )
        for place in range(2)
    ]
    high = jnp.where(even_y, first, second)
    low = jnp.where(even_y, second, first)
    for g in range(4):
        for d in range(2):
            row = 2 * g + d
            ext[g, base + ny + d : base + ny + d + 1, :] = high[row : row + 1]
            ext[g, base - 1 - d : base - d, :] = low[row : row + 1]

    packed = []
    for g, group in enumerate(ZGROUPS):
        moves = {}
        for k, q in enumerate(group):
            cx, cy, _ = VEL[q] if q < 19 else (0, 0, 0)
            moves.setdefault((cx, cy), []).append(k)
        acc = [jnp.zeros((8, nz), jnp.float32) for t in range(tiles + 1)]
        for (cx, cy), slots in moves.items():
            mask = slot == slots[0]
            for k in slots[1:]:
                mask = mask | (slot == k)
            for t in range(tiles + 1):
                if t < tiles:
                    row = base + 8 * t + cy
                    value = ext[g, row : row + 8, :]
                else:
                    above = base + ny + cy
                    below = base - 8 + cy
                    value = jnp.where(
                        sub < 4, ext[g, above : above + 8, :], ext[g, below : below + 8, :]
                    )
                acc[t] = jnp.where(mask, turn(value, -4 * cx), acc[t])
        packed.append(acc)
        for t in range(tiles + 1):
            row = (g * (tiles + 1) + t) * 8
            zown_ref[row : row + 8, :] = acc[t]
    up_first = parity("gz") == 0
    even_lane = lane % 2 == 0
    for t in range(tiles + 1):
        two, three = packed[2][t], packed[3][t]
        up = (packed[0][t], jnp.where(even_lane, two, pltpu.roll(three, 1, 1)))
        down = (packed[1][t], jnp.where(even_lane, pltpu.roll(two, nz - 1, 1), three))
        if t == tiles:
            up, down = [
                (
                    jnp.where(
                        (sub == 0) | (sub == 7),
                        side[0],
                        jnp.where(
                            sub < 4, pltpu.roll(side[1], 1, 0), pltpu.roll(side[1], 7, 0)
                        ),
                    ),
                )
                for side in (up, down)
            ]
        for g in range(len(up)):
            row = (g * tiles + t) * 8 if t < tiles else 2 * tiles * 8
            za_ref[row : row + 8, :] = jnp.where(up_first, up[g], down[g])
            zb_ref[row : row + 8, :] = jnp.where(up_first, down[g], up[g])
    drag = cols_ref[4 * ny :] + y_ref[2 * y_block :]
    for x_ref, c_ref in ((xa_ref, ya_ref), (xc_ref, yb_ref)):
        drag = drag + (x_ref[x_ref.shape[0] - 8 :] + c_ref[2 * corner_block :])
    drag_ref[...] = drag


def turn(value, shift):
    nz = value.shape[1]
    return pltpu.roll(value, shift % nz, 1) if shift % nz else value


def z_shifted(value, cz):
    return turn(value, -cz) if cz else value


def inner_kernel(
    states_ref,
    adj_ref,
    ub_ref,
    xa_ref,
    xb_ref,
    y_ref,
    ya_ref,
    yb_ref,
    out_ref,
    grad1_ref,
    grad_ref,
    pack_ref,
    f0_ref,
    f1_ref,
    ext,
    mid,
):
    nx, ny, nz = grad_ref.shape
    tiles = ny // 8
    lane = lax.broadcasted_iota(jnp.int32, (8, nz), 1)
    slot = lane // 4
    sub = lax.broadcasted_iota(jnp.int32, (8, nz), 0)
    even_x = parity("gx") == 0
    even_y = parity("gy") == 0
    base = 16

    for q in range(NSLOT):
        for x in range(nx):
            ext[q, x + 2, base : base + ny, :] = (
                adj_ref[q, x] if q < 19 else ub_ref[q - 19, x]
            )
    planes = {1: (nx + 2, nx + 3), -1: (1, 0)}
    lines = {1: (base + ny, base + ny + 1), -1: (base - 1, base - 2)}

    def fill_whole(sign):
        for names, depth, offset in ((near(0, sign), 0, 0), (far(0, sign), 1, 18)):
            for k, q in enumerate(names):
                rows = slice((k + offset) * ny, (k + offset + 1) * ny)
                ext[q, planes[sign][depth], base : base + ny, :] = xa_ref[rows]

    def fill_partial(sign):
        one, two = planes[sign]
        for k, q in enumerate(far(0, sign) + UB):
            ext[q, one, base : base + ny, :] = xb_ref[(5 + k) * ny : (6 + k) * ny]
        nothing = jnp.zeros((ny, nz), jnp.float32)
        for q in range(19):
            if VEL[q][0] == 0:
                ext[q, one, base : base + ny, :] = nothing
            elif VEL[q][0] == sign:
                ext[q, two, base : base + ny, :] = nothing
        for k, (q, depth, side) in enumerate(edge_entries(sign)):
            line = base if side > 0 else base + ny - 1
            row = 14 * ny + k
            ext[q, planes[sign][depth], line : line + 1, :] = xb_ref[row : row + 1]

    @pl.when(parity("gx") == 0)
    def _():
        fill_whole(1)
        fill_partial(-1)

    @pl.when(parity("gx") == 1)
    def _():
        fill_whole(-1)
        fill_partial(1)

    sums = {}
    for sign in (1, -1):
        block = y_rows(nx) + EDGE_ROWS
        first, second = (0, block) if sign > 0 else (block, 0)
        one, two = lines[sign]
        nothing = jnp.zeros((1, nz), jnp.float32)
        for q in range(19):
            for x in range(nx):
                if VEL[q][1] == 0:
                    ext[q, x + 2, one : one + 1, :] = nothing
                elif VEL[q][1] == sign:
                    ext[q, x + 2, two : two + 1, :] = nothing
        got = jnp.where(
            even_y,
            y_ref[first : first + y_rows(nx)],
            y_ref[second : second + y_rows(nx)],
        )
        sums[sign] = got
        for k, q in enumerate(far(1, sign) + UB):
            for x in range(nx):
                row = (5 + k) * nx + x
                ext[q, x + 2, one : one + 1, :] = got[row : row + 1]
        for k, (q, depth, x) in enumerate(y_edge_entries(sign, nx)):
            line = lines[sign][depth]
            row = 14 * nx + k
            ext[q, x + 2, line : line + 1, :] = got[row : row + 1]
        for sx in (1, -1):
            xs = (ya_ref, yb_ref) if sx > 0 else (yb_ref, ya_ref)
            block = CORNER + EDGE_ROWS
            ys = (0, block) if sign > 0 else (block, 0)
            low, high = [
                jnp.where(even_x, xs[0][r : r + CORNER], xs[1][r : r + CORNER])
                for r in ys
            ]
            got = jnp.where(even_y, low, high)
            for k, (q, dx, dy) in enumerate(corner_rows(sx, sign)):
                line = lines[sign][dy]
                ext[q, planes[sx][dx], line : line + 1, :] = got[k : k + 1]

    def near_cells(q, plane, t, cy):
        if t < tiles:
            row = base + 8 * t + cy
            return ext[q, plane, row : row + 8, :]
        above = base + ny + cy
        below = base - 8 + cy
        return jnp.where(
            sub < 4, ext[q, plane, above : above + 8, :], ext[q, plane, below : below + 8, :]
        )

    def first_level(p, t, kinds, partial=None):
        got = []
        for i in range(19):
            cx, cy, cz = VEL[i]
            got.append(z_shifted(near_cells(i, p + 1 + cx, t, cy), cz))
        ub = [near_cells(19 + k, p + 1, t, 0) for k in range(4)]
        out, kept = adjoint_cell(got, ub[:3], ub[3], 1.0)
        if t == tiles and 1 <= p <= nx:
            for sign, row in ((1, 0), (-1, 7)):
                for k, i in enumerate(far(1, sign)):
                    line = k * nx + p - 1
                    term = sums[sign][line : line + 1]
                    out[i] = out[i] + jnp.where(sub == row, term, 0.0)
        if partial is not None:
            for k, i in enumerate(kinds):
                row = k * ny + 8 * t
                out[i] = out[i] + jnp.where(partial, xb_ref[row : row + 8], 0.0)
        for i in kinds:
            if t < tiles:
                mid[i, p, t * 8 + 8 : t * 8 + 16, :] = out[i]
            elif VEL[i][1] > 0:
                mid[i, p, t * 8 + 8 : t * 8 + 16, :] = out[i]
            elif VEL[i][1] < 0:
                mid[i, p, 0:8, :] = out[i]
        return kept, ub[:3]

    def inside(x, carry):
        for t in range(tiles):
            kept, u = first_level(x + 1, t, range(19))
            rows = slice(t * 8, t * 8 + 8)
            f0, fs, fd, fm, _ = state_of(states_ref, (1, x, rows))
            grad1_ref[x, rows, :] = gradient_cell(kept, f0, fs, fd, fm, u)
        return carry

    lax.fori_loop(0, nx, inside, 0)
    for t in range(tiles):
        first_level(0, t, far(0, -1), even_x)
        first_level(nx + 1, t, far(0, 1), jnp.logical_not(even_x))

    for p in range(nx + 2):
        first_level(p, tiles, far(1, -1) + far(1, 1))

    def second_level(x, carry):
        for t in range(tiles):
            rows = slice(t * 8, t * 8 + 8)
            got = []
            for i in range(19):
                cx, cy, cz = VEL[i]
                low = 8 + 8 * t + cy
                value = z_shifted(mid[i, x + 1 + cx, low : low + 8, :], cz)
                got.append(value)
                pack_ref[i, rows, :] = jnp.where(
                    slot == x, pltpu.roll(value, 4 * x + 2, 1), pack_ref[i, rows, :]
                )
            f0, fs, fd, fm, u = state_of(states_ref, (0, x, rows))
            b = ub_ref[3, x, rows, :]
            out, kept = adjoint_cell(got, u, b, 1.0)
            for i in range(19):
                out_ref[i, x, rows, :] = out[i]
            grad_ref[x, rows, :] = grad1_ref[x, rows, :] + gradient_cell(
                kept, f0, fs, fd, fm, u
            )
        return carry

    lax.fori_loop(0, nx, second_level, 0)

    def tile(t, carry):
        rows = pl.ds(pl.multiple_of(t * 8, 8), 8)
        for i in range(20):
            for out_ref, level, first in ((f0_ref, 0, 0), (f1_ref, 1, 2)):
                if i == 19 and level == 1:
                    continue
                acc = jnp.zeros((8, nz), jnp.float32)
                for x in range(nx):
                    value = (
                        states_ref[level, i, x, rows, :]
                        if i < 19
                        else ub_ref[3, x, rows, :]
                    )
                    p = x + first
                    acc = jnp.where(slot == p, pltpu.roll(value, 4 * p + 2, 1), acc)
                out_ref[i, rows, :] = acc
        return carry

    lax.fori_loop(0, ny // 8, tile, 0)


def edge_kernel(
    mask_ref,
    zown_ref,
    za_ref,
    zb_ref,
    pack_ref,
    f0_ref,
    f1_ref,
    inner_ref,
    grad1_ref,
    inner_grad_ref,
    out_ref,
    grad_ref,
    tail_ref,
    first_ref,
    second_ref,
    zmid,
    zout,
):
    nx, ny, nz = mask_ref.shape
    tiles = ny // 8
    height = (tiles + 1) * 8
    even = parity("gz") == 0
    lane = lax.broadcasted_iota(jnp.int32, (8, nz), 1)
    sub = lax.broadcasted_iota(jnp.int32, (8, nz), 0)
    even_lane = lane % 2 == 0
    low_pair = lane % 4 < 2

    last = slice(2 * ny + 3, 2 * ny + 4)
    tail_ref[...] = za_ref[last] + zb_ref[last]

    def swapped(value):
        return jnp.where(even_lane, turn(value, -1), turn(value, 1))

    for t in range(tiles + 1):
        received = []
        for g in range(2):
            row = (g * tiles + t) * 8 if t < tiles else 2 * ny
            va = za_ref[row : row + 8, :]
            vb = zb_ref[row : row + 8, :]
            if t == tiles and g:
                va, vb = [
                    jnp.where(sub < 4, pltpu.roll(v, 7, 0), pltpu.roll(v, 1, 0))
                    for v in (va, vb)
                ]
            received.append((jnp.where(even, va, vb), jnp.where(even, vb, va)))
        (high0, low0), (high1, low1) = received
        for g in range(4):
            row = (g * (tiles + 1) + t) * 8
            rows = slice(row, row + 8)
            own = zown_ref[rows]
            if g == 0:
                head, tail = own, low0
            elif g == 1:
                head, tail = high0, own
            elif g == 2:
                head = jnp.where(even_lane, own, turn(high1, 1))
                tail = jnp.where(even_lane, low1, own)
            else:
                head = jnp.where(even_lane, own, high1)
                tail = jnp.where(even_lane, turn(low1, -1), own)
            head = swapped(head)
            tail = swapped(tail)
            first_ref[rows] = jnp.where(low_pair, head, turn(tail, 2))
            second_ref[rows] = jnp.where(low_pair, turn(head, -2), tail)

    slab_grad = []
    for t in range(tiles + 1):
        got = []
        for q in range(NSLOT):
            g, k = ZSLOT[q]
            row = g * height + t * 8
            ref = second_ref if k % 2 else first_ref
            got.append(turn(ref[row : row + 8, :], -32 * (k // 2)))
        out, kept = adjoint_cell(got[:19], got[19:22], got[22], 1.0)
        for i in range(19):
            zmid[i, 8 * t + 8 : 8 * t + 16, :] = out[i]
            if t == tiles:
                zmid[i, 0:8, :] = out[i]
        if t < tiles:
            f = [f1_ref[i, 8 * t : 8 * t + 8, :] for i in range(19)]
            fs, fd = pairs_of(f)
            fm = moments(f[0], fs, fd)
            grad = gradient_cell(kept, f[0], fs, fd, fm, got[19:22])
            slab_grad.append(turn(grad, -8))

    at = lane % 4
    for t in range(tiles):
        rows = slice(8 * t, 8 * t + 8)
        got = []
        for i in range(19):
            cx, cy, cz = VEL[i]
            value = pack_ref[i, rows, :]
            edge = zmid[i, 8 + 8 * t + cy : 16 + 8 * t + cy, :]
            back = -4 * (2 + cx)
            if cz == 0:
                value = jnp.where((at == 1) | (at == 2), turn(edge, back), value)
            else:
                near_lane = 2 if cz < 0 else 0
                value = jnp.where(at == near_lane, turn(edge, back - 1), value)
                value = jnp.where(at == near_lane + 1, turn(edge, back + 1), value)
            got.append(value)
        f = [f0_ref[i, rows, :] for i in range(19)]
        fs, fd = pairs_of(f)
        fm = moments(f[0], fs, fd)
        inverse = 1.0 / fm["total"]
        u = [one * inverse for one in fm["one"]]
        out, kept = adjoint_cell(got, u, f0_ref[19, rows, :], 1.0)
        for i in range(19):
            zout[i, rows, :] = out[i]
        zout[19, rows, :] = gradient_cell(kept, f[0], fs, fd, fm, u)
        zout[20, rows, :] = slab_grad[t]

    outer = (lane < 2) | (lane >= nz - 2)
    ends = (lane < 1) | (lane >= nz - 1)
    for x in range(nx):
        for t in range(tiles):
            rows = slice(8 * t, 8 * t + 8)
            level1 = jnp.where(
                ends, turn(zout[20, rows, :], -2 - 4 * x), grad1_ref[x, rows, :]
            )
            edge = turn(zout[19, rows, :], -2 - 4 * x) + level1
            grad = jnp.where(outer, edge, inner_grad_ref[x, rows, :])
            grad_ref[x, rows, :] = jnp.where(mask_ref[x, rows, :] == 0, grad, 0.0)
    for i in range(19):
        for x in range(nx):
            for t in range(tiles):
                rows = slice(8 * t, 8 * t + 8)
                out_ref[i, x, rows, :] = jnp.where(
                    outer, turn(zout[i, rows, :], -2 - 4 * x), inner_ref[i, x, rows, :]
                )


def finish_kernel(whole_cells, out_ref, grad_ref, *refs):
    tiles, (out_hbm, grad_hbm, drag_hbm, drag_ref, sems) = refs[:-5], refs[-5:]
    copies = [
        pltpu.make_async_copy(out_ref, out_hbm, sems.at[0]),
        pltpu.make_async_copy(grad_ref, grad_hbm, sems.at[1]),
        pltpu.make_async_copy(drag_ref, drag_hbm, sems.at[2]),
    ]
    for copy in copies[:2]:
        copy.start()
    total = 0.0
    for ref in tiles:
        total = total + jnp.sum(ref[...], axis=0, keepdims=True)
    drag_ref[...] = jnp.sum(total, axis=1, keepdims=True) / whole_cells
    copies[2].start()
    for copy in copies:
        copy.wait()


def swaps(count):
    first = [(i, i ^ 1) for i in range(count)]
    second = [(i, (((i + 1) % count) ^ 1) - 1) for i in range(count)]
    second = [(i, j % count) for i, j in second]
    return first, second


VMEM = pl.BlockSpec(memory_space=pltpu.VMEM)
HBM = pl.BlockSpec(memory_space=pltpu.HBM)
PARAMS = pltpu.CompilerParams(vmem_limit_bytes=48 * 2**20)


def call(kernel, inputs, shapes, scratch=(), space=VMEM, micros=0.05, outs=None):
    if space is HBM:
        inputs = [pltpu.with_memory_space_constraint(x, pltpu.HBM) for x in inputs]
    return pl.pallas_call(
        kernel,
        out_shape=[jax.ShapeDtypeStruct(s, jnp.float32) for s in shapes],
        in_specs=[space] * len(inputs),
        out_specs=outs or [VMEM] * len(shapes),
        scratch_shapes=list(scratch),
        compiler_params=PARAMS,
        cost_estimate=pl.CostEstimate(
            flops=0, bytes_accessed=int(3.6e6 * micros), transcendentals=0
        ),
    )(*inputs)


def body(primal_states, adjoint_last, porosity, solid_mask):
    nx, ny, nz = porosity.shape
    gx, gy, gz = [lax.axis_size(axis) for axis in AXES]
    x_first, x_second = swaps(gx)
    y_first, y_second = swaps(gy)
    z_first, z_second = swaps(gz)
    tiles = ny // 8
    height = (tiles + 1) * 8
    f32 = jnp.float32

    def diagonal(message, x_pairs, y_pairs):
        pairs = [(a * gy + c, b * gy + d) for a, b in x_pairs for c, d in y_pairs]
        return lax.ppermute(message, ("gx", "gy"), pairs)

    rows_x = NSLOT * ny + 8
    rows_y = 2 * (y_rows(nx) + EDGE_ROWS) + 8
    rows_c = 2 * (CORNER + EDGE_ROWS) + 8
    rows_z = 2 * ny + 8
    rides = (gx, gy, gz) == (4, 2, 4)
    ub, drag = call(
        state_kernel,
        (primal_states, porosity, solid_mask),
        [(4, nx, ny, nz), (8, nz)],
        [
            pltpu.VMEM((2, 19, nx, ny, nz), f32),
            pltpu.VMEM((nx, ny, nz), f32),
            pltpu.VMEM((nx, ny, nz), jnp.int32),
            pltpu.SemaphoreType.DMA((5,)),
        ],
        HBM,
    )
    cols, y, ya, yb = call(
        pack_y_kernel,
        (adjoint_last, ub, drag),
        [(4 * ny + 8, nz), (rows_y, nz), (rows_c, nz), (rows_c, nz)],
        [pltpu.VMEM((NSLOT, 2 * nx, nz), f32)],
        micros=4,
    )
    (xa,) = call(pack_x_kernel, (adjoint_last, ub, drag), [(rows_x, nz)])
    (xb,) = call(pack_partial_kernel, (adjoint_last, ub), [(14 * ny + 8, nz)])
    xc = lax.ppermute(cols, "gx", x_second)
    xa = lax.ppermute(xa, "gx", x_first)
    if gy == 2:
        y = lax.ppermute(y, "gy", y_first)
        yb = diagonal(yb, x_second, y_first)
        ya = diagonal(ya, x_first, y_first)
    else:

        def both(message, block, send):
            parts = [message[:block], message[block : 2 * block], message[2 * block :]]
            return jnp.concatenate(
                [send(parts[0], y_first), send(parts[1], y_second), parts[2]]
            )

        block = y_rows(nx) + EDGE_ROWS
        y = both(y, block, lambda m, pairs: lax.ppermute(m, "gy", pairs))
        block = CORNER + EDGE_ROWS
        yb = both(yb, block, lambda m, pairs: diagonal(m, x_second, pairs))
        ya = both(ya, block, lambda m, pairs: diagonal(m, x_first, pairs))
    xb, yb = lax.optimization_barrier((xb, yb))
    xb = lax.ppermute(xb, "gx", x_second)

    zown, za, zb, drag_xy = call(
        pack_z_kernel,
        (cols, xa, xc, y, ya, yb),
        [(4 * height, nz), (rows_z, nz), (rows_z, nz), (8, nz)],
        [pltpu.VMEM((4, ny + 32, nz), f32)],
    )
    if rides:
        second = xc[4 * ny :] + yb[rows_c - 8 :]
        drag_xy = drag_xy + lax.ppermute(second, "gx", x_first)
        drag_xy = jnp.sum(drag_xy, axis=0, keepdims=True)
        za = za.at[2 * ny + 3 : 2 * ny + 4].set(drag_xy)
        zb = zb.at[2 * ny + 3 : 2 * ny + 4].set(drag_xy)
    zb = lax.ppermute(zb, "gz", z_second)
    za = lax.ppermute(za, "gz", z_first)
    inner, grad1, inner_grad, pack, f0, f1 = call(
        inner_kernel,
        (primal_states, adjoint_last, ub, xa, xb, y, ya, yb),
        [
            (19, nx, ny, nz),
            (nx, ny, nz),
            (nx, ny, nz),
            (19, ny, nz),
            (20, ny, nz),
            (19, ny, nz),
        ],
        [
            pltpu.VMEM((NSLOT, nx + 4, ny + 32, nz), f32),
            pltpu.VMEM((19, nx + 2, height + 8, nz), f32),
        ],
        micros=4,
    )
    if rides:
        zhalf = lax.ppermute(drag_xy, "gz", [(i, i ^ 2) for i in range(gz)])
        drags = (drag_xy, zhalf)
    else:
        drags = (lax.psum(drag, AXES),)

    first, gradient, tails = call(
        edge_kernel,
        (solid_mask, zown, za, zb, pack, f0, f1, inner, grad1, inner_grad),
        [(19, nx, ny, nz), (nx, ny, nz), (1, nz)],
        [
            pltpu.VMEM((4 * height, nz), f32),
            pltpu.VMEM((4 * height, nz), f32),
            pltpu.VMEM((19, height + 8, nz), f32),
            pltpu.VMEM((21, ny, nz), f32),
        ],
    )
    if rides:
        drags += (tails,)
    whole_cells = float(nx * ny * nz * gx * gy * gz)
    first, gradient, drag = call(
        functools.partial(finish_kernel, whole_cells),
        (first, gradient) + drags,
        [(19, nx, ny, nz), (nx, ny, nz), (1, 1)],
        [pltpu.VMEM((1, 1), f32), pltpu.SemaphoreType.DMA((3,))],
        outs=[HBM, HBM, HBM],
    )
    return (first, gradient, drag.reshape(()))


def solution(mesh):
    return jax.shard_map(
        body,
        mesh=mesh,
        in_specs=(
            P(None, None, "gx", "gy", "gz"),
            P(None, "gx", "gy", "gz"),
            P("gx", "gy", "gz"),
            P("gx", "gy", "gz"),
        ),
        out_specs=(P(None, "gx", "gy", "gz"), P("gx", "gy", "gz"), P()),
        check_vma=False,
    )
```

```python
import functools

import jax
import jax.numpy as jnp
import numpy as np
from jax import lax
from jax.experimental import pallas as pl
from jax.experimental.pallas import tpu as pltpu
from jax.sharding import PartitionSpec as P

VEL = (
    (0, 0, 0),
    (1, 0, 0),
    (-1, 0, 0),
    (0, 1, 0),
    (0, -1, 0),
    (0, 0, 1),
    (0, 0, -1),
    (1, 1, 0),
    (-1, -1, 0),
    (1, -1, 0),
    (-1, 1, 0),
    (1, 0, 1),
    (-1, 0, -1),
    (1, 0, -1),
    (-1, 0, 1),
    (0, 1, 1),
    (0, -1, -1),
    (0, 1, -1),
    (0, -1, 1),
)
PAIRS = tuple((i, i + 1) for i in range(1, 19, 2))
AXES = ("gx", "gy", "gz")
UB = (19, 20, 21, 22)


def near(axis, sign):
    return tuple(i for i in range(19) if VEL[i][axis] * sign >= 0) + UB


def far(axis, sign):
    return tuple(i for i in range(19) if VEL[i][axis] == sign)


NSLOT = 23
CORNER = 16
DRAG_ROW = 14
EDGE_ROWS = 8


def y_rows(nx):
    return 14 * nx + 8


ZGROUPS = (
    tuple(i for i in range(19) if VEL[i][2] == -1),
    tuple(i for i in range(19) if VEL[i][2] == 1),
    tuple(i for i in range(19) if VEL[i][2] == 0)[:8],
    tuple(i for i in range(19) if VEL[i][2] == 0)[8:] + UB,
)
ZSLOT = {q: (g, k) for g, group in enumerate(ZGROUPS) for k, q in enumerate(group)}


def pairs_of(values):
    s = [values[a] + values[b] for a, b in PAIRS]
    d = [values[a] - values[b] for a, b in PAIRS]
    return s, d


def moments(v0, s, d):
    sx, sy, sz, sp, sq, sr, ss, st, su = s
    dx, dy, dz, dp, dq, dr, ds, dt, du = d
    ex = sp + sq
    ez = sr + ss
    ey = st + su
    faces = sx + sy + sz
    edges = ex + ez + ey
    exx = ex + ez
    eyy = ex + ey
    ezz = ez + ey
    fx = (dp + dq) + (dr + ds)
    fy = (dp - dq) + (dt + du)
    fz = (dr - ds) + (dt - du)
    return dict(
        rest=v0,
        faces=faces,
        edges=edges,
        total=v0 + faces + edges,
        face1=(dx, dy, dz),
        edge1=(fx, fy, fz),
        one=(dx + fx, dy + fy, dz + fz),
        face2=(sx, sy, sz),
        edge2=(exx, eyy, ezz),
        two=(sx + exx, sy + eyy, sz + ezz),
        cross=(sp - sq, sr - ss, st - su),
    )


def adjoint_cell(g, u, b, drive):
    s, d = pairs_of(g)
    m = moments(g[0], s, d)
    total = m["total"]
    trace = m["faces"] + 2.0 * m["edges"] - (30.0 / 19.0) * total
    p0 = (-1.2 / 19.0) * total - (2.0 / 21.0) * trace
    q = [
        (0.4 / 6.0) * (two - (10.0 / 19.0) * total) + (0.8 / 21.0) * trace
        for two in m["two"]
    ]
    qsum = q[0] + q[1] + q[2]
    qab = [0.1 * c for c in m["cross"]]
    p1 = [-0.12 * one for one in m["one"]]
    h0 = (
        0.4 * m["rest"]
        + (1.2 / 18.0) * m["faces"]
        + (1.2 / 36.0) * m["edges"]
        + p0
        + (1.0 / 3.0) * qsum
    )
    h1 = [
        (1.2 / 18.0) * f + (1.2 / 36.0) * e + (1.0 / 3.0) * p
        for f, e, p in zip(m["face1"], m["edge1"], p1)
    ]
    base = (1.0 / 3.0) * p0 + (1.0 / 9.0) * qsum
    haa = [
        (1.2 / 18.0) * f + (1.2 / 36.0) * e + (2.0 / 9.0) * qa + base
        for f, e, qa in zip(m["face2"], m["edge2"], q)
    ]
    hxy, hxz, hyz = [(2.0 / 45.0) * c for c in m["cross"]]
    ux, uy, uz = u
    v = (
        haa[0] * ux + hxy * uy + hxz * uz,
        hxy * ux + haa[1] * uy + hyz * uz,
        hxz * ux + hyz * uy + haa[2] * uz,
    )
    uv = ux * v[0] + uy * v[1] + uz * v[2]
    uu = ux * ux + uy * uy + uz * uz
    uuh = 1.5 * uu * h0
    a = h0 + uuh - 4.5 * uv
    nb = 1.0 - b
    e0 = nb * (a - p0)
    nq = [nb * x for x in q]
    nxy, nxz, nyz = [nb * x for x in qab]
    o = [
        nb * (3.0 * h1[k] + 9.0 * v[k] - 3.0 * u[k] * h0 - p1[k]) for k in range(3)
    ]
    o[0] = o[0] + b * drive
    alpha = -0.2 * nb
    half_s = 0.5 * (alpha + b)
    half_d = 0.5 * (alpha - b)
    exy = e0 - nq[0] - nq[1]
    exz = e0 - nq[0] - nq[2]
    eyz = e0 - nq[1] - nq[2]
    even = (
        e0 - nq[0],
        e0 - nq[1],
        e0 - nq[2],
        exy - nxy,
        exy + nxy,
        exz - nxz,
        exz + nxz,
        eyz - nyz,
        eyz + nyz,
    )
    odd = (
        o[0],
        o[1],
        o[2],
        o[0] + o[1],
        o[0] - o[1],
        o[0] + o[2],
        o[0] - o[2],
        o[1] + o[2],
        o[1] - o[2],
    )
    out = [(alpha + b) * g[0] + e0]
    for k in range(9):
        even_k = half_s * s[k] + even[k]
        odd_k = half_d * d[k] + odd[k]
        out.append(even_k + odd_k)
        out.append(even_k - odd_k)
    kept = dict(
        s=s, d=d, g0=g[0], p0=p0, p1=p1, q=q, qab=qab, h0=h0, h1=h1, uv=uv, uuh=uuh
    )
    return out, kept


def gradient_cell(kept, f0, fs, fd, fm, u):
    rho = fm["total"]
    even = fs[0] * kept["s"][0]
    odd = fd[0] * kept["d"][0]
    for k in range(1, 9):
        even = even + fs[k] * kept["s"][k]
        odd = odd + fd[k] * kept["d"][k]
    hf = kept["p0"] * rho
    for k in range(3):
        hf = hf + kept["p1"][k] * fm["one"][k] + kept["q"][k] * fm["two"][k]
        hf = hf + kept["qab"][k] * fm["cross"][k]
    uh1 = u[0] * kept["h1"][0] + u[1] * kept["h1"][1] + u[2] * kept["h1"][2]
    hfeq = rho * (kept["h0"] - kept["uuh"] + 3.0 * uh1 + 4.5 * kept["uv"])
    pairs = 1.2 * f0 * kept["g0"] + 0.6 * even - 0.4 * odd
    return pairs + hf - hfeq + fm["one"][0]


def state_of(ref, index):
    f = [ref[(index[0], i) + index[1:]] for i in range(19)]
    s, d = pairs_of(f)
    m = moments(f[0], s, d)
    inverse = 1.0 / m["total"]
    u = [one * inverse for one in m["one"]]
    return f[0], s, d, m, u


def corner_rows(sx, sy):
    both = [i for i in far(0, sx) if VEL[i][1] == sy]
    along_y = [i for i in far(1, sy) if VEL[i][0] == 0]
    along_x = [i for i in far(0, sx) if VEL[i][1] == 0]
    rows = [(i, 0, 0) for i in both + along_y + along_x]
    return rows + [(i, 1, 0) for i in both] + [(i, 0, 1) for i in both]


def corner_zeros(sx, sy):
    rows = [(i, 0, 0) for i in range(19) if VEL[i][0] == 0 and VEL[i][1] == 0]
    rows += [(i, 1, 0) for i in far(0, sx) if VEL[i][1] == 0]
    rows += [(i, 0, 1) for i in far(1, sy) if VEL[i][0] == 0]
    return rows + [(i, 1, 1) for i in far(0, sx) if VEL[i][1] == sy]


CORNERS = ((1, 1), (1, -1), (-1, 1), (-1, -1))


def parity(axis):
    return lax.axis_index(axis) % 2


def cell_rows(adj_ref, ub_ref, q, x, rows):
    return adj_ref[q, x, rows, :] if q < 19 else ub_ref[q - 19, x, rows, :]


def state_kernel(
    states_hbm,
    por_hbm,
    mask_hbm,
    ub_ref,
    drag_ref,
    states_ref,
    por_ref,
    mask_ref,
    sems,
):
    nx, ny, nz = por_ref.shape
    tiles = ny // 8
    copies = [
        pltpu.make_async_copy(src, dst, sems.at[k])
        for k, (src, dst) in enumerate(
            (
                (states_hbm.at[1], states_ref.at[1]),
                (por_hbm, por_ref),
                (mask_hbm, mask_ref),
                (states_hbm.at[0, 1:3], states_ref.at[0, 1:3]),
                (states_hbm.at[0, 7:15], states_ref.at[0, 7:15]),
            )
        )
    ]
    for copy in copies:
        copy.start()
    for copy in copies[:3]:
        copy.wait()

    def cells(x, carry):
        for t in range(tiles):
            rows = slice(8 * t, 8 * t + 8)
            blocking = jnp.where(mask_ref[x, rows, :] == 0, por_ref[x, rows, :], 1.0)
            f0, s, d, m, u = state_of(states_ref, (1, x, rows))
            for k in range(3):
                ub_ref[k, x, rows, :] = u[k]
            ub_ref[3, x, rows, :] = blocking
            carry = carry + blocking * m["one"][0]
        return carry

    drag = lax.fori_loop(0, nx, cells, jnp.zeros((8, nz), jnp.float32))
    for copy in copies[3:]:
        copy.wait()

    def flux_cells(x, carry):
        for t in range(tiles):
            rows = slice(8 * t, 8 * t + 8)
            flux = 0.0
            for a, b in PAIRS:
                if VEL[a][0]:
                    flux = flux + (
                        states_ref[0, a, x, rows, :] - states_ref[0, b, x, rows, :]
                    )
            carry = carry + ub_ref[3, x, rows, :] * flux
        return carry

    drag = lax.fori_loop(0, nx, flux_cells, drag)
    drag_ref[...] = drag


def pack_x_kernel(adj_ref, ub_ref, drag_ref, out_ref):
    nx, ny = adj_ref.shape[1:3]
    out_ref[NSLOT * ny :] = drag_ref[...]

    def fill(sign):
        for names, offset, x in (
            (near(0, sign), 0, 0 if sign > 0 else nx - 1),
            (far(0, sign), 18, 1 if sign > 0 else nx - 2),
        ):
            for k, q in enumerate(names):
                k += offset
                out_ref[k * ny : (k + 1) * ny] = cell_rows(
                    adj_ref, ub_ref, q, x, slice(0, ny)
                )

    pl.when(parity("gx") == 0)(functools.partial(fill, -1))
    pl.when(parity("gx") == 1)(functools.partial(fill, 1))


def y_edge_entries(sign, nx):
    rows = []
    for side in (1, -1):
        x = 0 if side > 0 else nx - 1
        rows += [(i, 0, x) for i in far(0, side) if VEL[i][1] == 0]
        rows += [(i, 1, x) for i in far(0, side) if VEL[i][1] == sign]
    return rows


def edge_entries(sign):
    rows = []
    for side in (1, -1):
        rows += [(i, 0, side) for i in far(1, side) if VEL[i][0] == 0]
        rows += [(i, 1, side) for i in far(1, side) if VEL[i][0] == sign]
    return rows


def pack_partial_kernel(adj_ref, ub_ref, out_ref):
    nx, ny, nz = adj_ref.shape[1:]
    tiles = ny // 8
    sub = lax.broadcasted_iota(jnp.int32, (8, nz), 0)

    def fill(sign):
        here, inside = (0, 1) if sign > 0 else (nx - 1, nx - 2)
        names = far(0, sign)
        for t in range(tiles):
            rows = slice(8 * t, 8 * t + 8)
            got = []
            for i in range(19):
                cx, cy, cz = VEL[i]
                if cx * sign < 0:
                    got.append(jnp.zeros((8, nz), jnp.float32))
                    continue
                x = inside if cx else here
                if t == 0 and cy < 0:
                    value = pltpu.roll(adj_ref[i, x, rows, :], 1, 0)
                    value = jnp.where(sub == 0, 0.0, value)
                elif t == tiles - 1 and cy > 0:
                    value = pltpu.roll(adj_ref[i, x, rows, :], 7, 0)
                    value = jnp.where(sub == 7, 0.0, value)
                else:
                    value = adj_ref[i, x, 8 * t + cy : 8 * t + 8 + cy, :]
                got.append(z_shifted(value, cz))
            u = [ub_ref[k, here, rows, :] for k in range(3)]
            out, _ = adjoint_cell(got, u, ub_ref[3, here, rows, :], 0.0)
            for k, i in enumerate(names):
                out_ref[k * ny + 8 * t : k * ny + 8 * t + 8] = out[i]
        for k, q in enumerate(names + UB):
            k += 5
            out_ref[k * ny : (k + 1) * ny] = cell_rows(
                adj_ref, ub_ref, q, here, slice(0, ny)
            )
        for k, (i, depth, side) in enumerate(edge_entries(sign)):
            y = 0 if side > 0 else ny - 1
            row = 14 * ny + k
            out_ref[row : row + 1] = adj_ref[i, inside if depth else here, y : y + 1, :]

    pl.when(parity("gx") == 0)(functools.partial(fill, 1))
    pl.when(parity("gx") == 1)(functools.partial(fill, -1))


def column_pair(acc, value, pair, q, k, plane):
    start = 32 * (k // 2) + 4 * plane + 2 * (k % 2)
    cz = VEL[q][2] if q < 19 else 0
    return jnp.where(pair == start // 2, turn(value, start + 1 - cz), acc)


def pack_y_kernel(
    adj_ref, ub_ref, drag_ref, cols_ref, y_ref, ya_ref, yb_ref, read_ref
):
    nx, ny, nz = adj_ref.shape[1:]
    pair = lax.broadcasted_iota(jnp.int32, (8, nz), 1) // 2
    for g, group in enumerate(ZGROUPS):
        for t in range(ny // 8):
            acc = jnp.zeros((8, nz), jnp.float32)
            for k, q in enumerate(group):
                for x in range(nx):
                    value = cell_rows(adj_ref, ub_ref, q, x, slice(8 * t, 8 * t + 8))
                    acc = column_pair(acc, value, pair, q, k, x + 2)
            row = g * ny + 8 * t
            cols_ref[row : row + 8] = acc
    y_block = y_rows(nx) + EDGE_ROWS
    corner_block = CORNER + EDGE_ROWS

    def fill_edges(place, sign):
        for g in range(4):
            for d in range(2):
                y = d if sign > 0 else ny - 1 - d
                line = cols_ref[g * ny + y : g * ny + y + 1]
                row = place * y_block + y_rows(nx) + 2 * g + d
                y_ref[row : row + 1] = line
                row = place * corner_block + CORNER + 2 * g + d
                ya_ref[row : row + 1] = line
                yb_ref[row : row + 1] = line

    faces = ((1, 0, 1), (-1, ny - 1, ny - 2))
    for i in range(19):
        cx, cy, _ = VEL[i]
        read_ref[i] = jnp.zeros((2 * nx, nz), jnp.float32)
        for n, (sign, here, inside) in enumerate(faces):
            for x in range(max(0, -cx), min(nx, nx - cx)):
                if cy * sign >= 0:
                    y = inside if cy else here
                    read_ref[i, n * nx + x : n * nx + x + 1, :] = adj_ref[
                        i, x + cx, y : y + 1, :
                    ]
    for k in range(4):
        for n, (sign, here, inside) in enumerate(faces):
            for x in range(nx):
                read_ref[19 + k, n * nx + x : n * nx + x + 1, :] = ub_ref[
                    k, x, here : here + 1, :
                ]
    got = [z_shifted(read_ref[i], VEL[i][2]) for i in range(19)]
    sums, _ = adjoint_cell(
        got, [read_ref[19 + k] for k in range(3)], read_ref[22], 0.0
    )

    def fill_y(place, sign):
        n = 0 if sign > 0 else 1
        _, here, inside = faces[n]
        first = place * y_block
        for k, i in enumerate(far(1, sign)):
            row = first + k * nx
            y_ref[row : row + nx] = sums[i][n * nx : (n + 1) * nx]
        for k, q in enumerate(far(1, sign) + UB):
            for x in range(nx):
                row = first + (5 + k) * nx + x
                y_ref[row : row + 1] = cell_rows(
                    adj_ref, ub_ref, q, x, slice(here, here + 1)
                )
        for k, (i, depth, x) in enumerate(y_edge_entries(sign, nx)):
            y = inside if depth else here
            row = first + 14 * nx + k
            y_ref[row : row + 1] = adj_ref[i, x, y : y + 1, :]

    for i in range(19):
        read_ref[i] = jnp.zeros((2 * nx, nz), jnp.float32)
    for n, (sx, sy) in enumerate(CORNERS):
        xs = (0, 1) if sx > 0 else (nx - 1, nx - 2)
        ys = (0, 1) if sy > 0 else (ny - 1, ny - 2)
        for i, dx, dy in corner_zeros(sx, sy):
            read_ref[i, n : n + 1, :] = adj_ref[i, xs[dx], ys[dy] : ys[dy] + 1, :]
        for k in range(4):
            read_ref[19 + k, n : n + 1, :] = ub_ref[k, xs[0], ys[0] : ys[0] + 1, :]
    got = [z_shifted(read_ref[i], VEL[i][2]) for i in range(19)]
    corner_sums, _ = adjoint_cell(
        got, [read_ref[19 + k] for k in range(3)], read_ref[22], 0.0
    )
    line = jnp.sum(drag_ref[...], axis=0, keepdims=True)

    def fill_corner(out_ref, place, sx, sy):
        xs = (0, 1) if sx > 0 else (nx - 1, nx - 2)
        ys = (0, 1) if sy > 0 else (ny - 1, ny - 2)
        n = CORNERS.index((sx, sy))
        first = place * corner_block
        rows = corner_rows(sx, sy)
        out_ref[first : first + 1] = corner_sums[rows[0][0]][n : n + 1]
        for k in range(4):
            out_ref[first + 1 + k : first + 2 + k] = ub_ref[
                k, xs[0], ys[0] : ys[0] + 1, :
            ]
        for k, (i, dx, dy) in enumerate(rows):
            row = first + 5 + k
            out_ref[row : row + 1] = adj_ref[i, xs[dx], ys[dy] : ys[dy] + 1, :]
        out_ref[first + DRAG_ROW : first + DRAG_ROW + 1] = line
        out_ref[first + DRAG_ROW + 1 : first + CORNER] = jnp.zeros((1, nz), jnp.float32)

    drag = drag_ref[...]
    cols_ref[4 * ny :] = drag
    y_ref[2 * y_block :] = drag
    for py in (0, 1):

        @pl.when(parity("gy") == py)
        def _():
            s0 = 1 if py else -1
            fill_y(0, s0)
            fill_y(1, -s0)
            fill_edges(0, s0)
            fill_edges(1, -s0)

    for px in (0, 1):
        for py in (0, 1):

            @pl.when((parity("gx") == px) & (parity("gy") == py))
            def _():
                sa = 1 if px else -1
                s0 = 1 if py else -1
                for out_ref, sx in ((ya_ref, sa), (yb_ref, -sa)):
                    fill_corner(out_ref, 0, sx, s0)
                    fill_corner(out_ref, 1, sx, -s0)


def pack_z_kernel(
    cols_ref,
    xa_ref,
    xc_ref,
    y_ref,
    ya_ref,
    yb_ref,
    zown_ref,
    za_ref,
    zb_ref,
    drag_ref,
    ext,
):
    ny = (cols_ref.shape[0] - 8) // 4
    nz = cols_ref.shape[1]
    tiles = ny // 8
    base = 16
    even_x = parity("gx") == 0
    even_y = parity("gy") == 0
    lane = lax.broadcasted_iota(jnp.int32, (8, nz), 1)
    sub = lax.broadcasted_iota(jnp.int32, (8, nz), 0)
    plane = (lane % 32) // 4
    slot = 2 * (lane // 32) + (lane % 4) // 2

    def along_x(own, va, vb):
        low = turn(jnp.where(even_x, vb, va), -16)
        high = turn(jnp.where(even_x, va, vb), 16)
        return jnp.where(plane < 2, low, jnp.where(plane > 5, high, own))

    pair = lane // 2

    def fill_main(sign):
        halo = {}
        for names, offset, p in (
            (near(0, sign), 0, 6 if sign > 0 else 1),
            (far(0, sign), 18, 7 if sign > 0 else 0),
        ):
            for k, q in enumerate(names):
                halo.setdefault(q, []).append((k + offset, p))
        for g, group in enumerate(ZGROUPS):
            for t in range(tiles):
                rows = slice(g * ny + 8 * t, g * ny + 8 * t + 8)
                acc = jnp.where(
                    plane < 2 if sign > 0 else plane > 5,
                    turn(xc_ref[rows], -16 * sign),
                    cols_ref[rows],
                )
                for k, q in enumerate(group):
                    for at, p in halo.get(q, ()):
                        row = at * ny + 8 * t
                        acc = column_pair(acc, xa_ref[row : row + 8], pair, q, k, p)
                ext[g, base + 8 * t : base + 8 * t + 8, :] = acc

    @pl.when(parity("gx") == 0)
    def _():
        fill_main(1)

    @pl.when(parity("gx") == 1)
    def _():
        fill_main(-1)

    y_block = (y_ref.shape[0] - 8) // 2
    corner_block = CORNER + EDGE_ROWS

    def edges(ref, block, place):
        return ref[(place + 1) * block - EDGE_ROWS : (place + 1) * block]

    first, second = [
        along_x(
            edges(y_ref, y_block, place),
            edges(ya_ref, corner_block, place),
            edges(yb_ref, corner_block, place),
        )
        for place in range(2)
    ]
    high = jnp.where(even_y, first, second)
    low = jnp.where(even_y, second, first)
    for g in range(4):
        for d in range(2):
            row = 2 * g + d
            ext[g, base + ny + d : base + ny + d + 1, :] = high[row : row + 1]
            ext[g, base - 1 - d : base - d, :] = low[row : row + 1]

    packed = []
    for g, group in enumerate(ZGROUPS):
        moves = {}
        for k, q in enumerate(group):
            cx, cy, _ = VEL[q] if q < 19 else (0, 0, 0)
            moves.setdefault((cx, cy), []).append(k)
        acc = [jnp.zeros((8, nz), jnp.float32) for t in range(tiles + 1)]
        for (cx, cy), slots in moves.items():
            mask = slot == slots[0]
            for k in slots[1:]:
                mask = mask | (slot == k)
            for t in range(tiles + 1):
                if t < tiles:
                    row = base + 8 * t + cy
                    value = ext[g, row : row + 8, :]
                else:
                    above = base + ny + cy
                    below = base - 8 + cy
                    value = jnp.where(
                        sub < 4, ext[g, above : above + 8, :], ext[g, below : below + 8, :]
                    )
                acc[t] = jnp.where(mask, turn(value, -4 * cx), acc[t])
        packed.append(acc)
        for t in range(tiles + 1):
            row = (g * (tiles + 1) + t) * 8
            zown_ref[row : row + 8, :] = acc[t]
    up_first = parity("gz") == 0
    even_lane = lane % 2 == 0
    for t in range(tiles + 1):
        two, three = packed[2][t], packed[3][t]
        up = (packed[0][t], jnp.where(even_lane, two, pltpu.roll(three, 1, 1)))
        down = (packed[1][t], jnp.where(even_lane, pltpu.roll(two, nz - 1, 1), three))
        if t == tiles:
            up, down = [
                (
                    jnp.where(
                        (sub == 0) | (sub == 7),
                        side[0],
                        jnp.where(
                            sub < 4, pltpu.roll(side[1], 1, 0), pltpu.roll(side[1], 7, 0)
                        ),
                    ),
                )
                for side in (up, down)
            ]
        for g in range(len(up)):
            row = (g * tiles + t) * 8 if t < tiles else 2 * tiles * 8
            za_ref[row : row + 8, :] = jnp.where(up_first, up[g], down[g])
            zb_ref[row : row + 8, :] = jnp.where(up_first, down[g], up[g])
    drag = (cols_ref[4 * ny :] + y_ref[2 * y_block :]) + (
        xa_ref[xa_ref.shape[0] - 8 :] + xc_ref[4 * ny :]
    )
    row = slice(DRAG_ROW, DRAG_ROW + 1)
    drag_ref[...] = jnp.sum(drag, axis=0, keepdims=True) + (ya_ref[row] + yb_ref[row])


OUT_GROUPS = ((0, 5), (5, 10), (10, 15), (15, 19))


def turn(value, shift):
    nz = value.shape[1]
    return pltpu.roll(value, shift % nz, 1) if shift % nz else value


def z_shifted(value, cz):
    return turn(value, -cz) if cz else value


def inner_kernel(
    states_ref,
    adj_ref,
    ub_ref,
    xa_ref,
    xb_ref,
    y_ref,
    ya_ref,
    yb_ref,
    out_ref,
    grad1_ref,
    grad_ref,
    pack_ref,
    f0_ref,
    f1_ref,
    ext,
    mid,
):
    nx, ny, nz = grad_ref.shape
    tiles = ny // 8
    lane = lax.broadcasted_iota(jnp.int32, (8, nz), 1)
    slot = lane // 4
    sub = lax.broadcasted_iota(jnp.int32, (8, nz), 0)
    even_x = parity("gx") == 0
    even_y = parity("gy") == 0
    base = 16

    for q in range(NSLOT):
        for x in range(nx):
            ext[q, x + 2, base : base + ny, :] = (
                adj_ref[q, x] if q < 19 else ub_ref[q - 19, x]
            )
    planes = {1: (nx + 2, nx + 3), -1: (1, 0)}
    lines = {1: (base + ny, base + ny + 1), -1: (base - 1, base - 2)}

    def fill_whole(sign):
        for names, depth, offset in ((near(0, sign), 0, 0), (far(0, sign), 1, 18)):
            for k, q in enumerate(names):
                rows = slice((k + offset) * ny, (k + offset + 1) * ny)
                ext[q, planes[sign][depth], base : base + ny, :] = xa_ref[rows]

    def fill_partial(sign):
        one, two = planes[sign]
        for k, q in enumerate(far(0, sign) + UB):
            ext[q, one, base : base + ny, :] = xb_ref[(5 + k) * ny : (6 + k) * ny]
        nothing = jnp.zeros((ny, nz), jnp.float32)
        for q in range(19):
            if VEL[q][0] == 0:
                ext[q, one, base : base + ny, :] = nothing
            elif VEL[q][0] == sign:
                ext[q, two, base : base + ny, :] = nothing
        for k, (q, depth, side) in enumerate(edge_entries(sign)):
            line = base if side > 0 else base + ny - 1
            row = 14 * ny + k
            ext[q, planes[sign][depth], line : line + 1, :] = xb_ref[row : row + 1]

    @pl.when(parity("gx") == 0)
    def _():
        fill_whole(1)
        fill_partial(-1)

    @pl.when(parity("gx") == 1)
    def _():
        fill_whole(-1)
        fill_partial(1)

    sums = {}
    corner_sums = {}
    for sign in (1, -1):
        block = y_rows(nx) + EDGE_ROWS
        first, second = (0, block) if sign > 0 else (block, 0)
        one, two = lines[sign]
        nothing = jnp.zeros((1, nz), jnp.float32)
        for q in range(19):
            for x in range(nx):
                if VEL[q][1] == 0:
                    ext[q, x + 2, one : one + 1, :] = nothing
                elif VEL[q][1] == sign:
                    ext[q, x + 2, two : two + 1, :] = nothing
        got = jnp.where(
            even_y,
            y_ref[first : first + y_rows(nx)],
            y_ref[second : second + y_rows(nx)],
        )
        sums[sign] = got
        for k, q in enumerate(far(1, sign) + UB):
            for x in range(nx):
                row = (5 + k) * nx + x
                ext[q, x + 2, one : one + 1, :] = got[row : row + 1]
        for k, (q, depth, x) in enumerate(y_edge_entries(sign, nx)):
            line = lines[sign][depth]
            row = 14 * nx + k
            ext[q, x + 2, line : line + 1, :] = got[row : row + 1]
        for sx in (1, -1):
            xs = (ya_ref, yb_ref) if sx > 0 else (yb_ref, ya_ref)
            block = CORNER + EDGE_ROWS
            ys = (0, block) if sign > 0 else (block, 0)
            low, high = [
                jnp.where(even_x, xs[0][r : r + CORNER], xs[1][r : r + CORNER])
                for r in ys
            ]
            got = jnp.where(even_y, low, high)
            corner_sums[sx, sign] = got[0:1]
            for k in range(4):
                line = lines[sign][0]
                ext[19 + k, planes[sx][0], line : line + 1, :] = got[1 + k : 2 + k]
            for q, dx, dy in corner_zeros(sx, sign):
                line = lines[sign][dy]
                ext[q, planes[sx][dx], line : line + 1, :] = nothing
            for k, (q, dx, dy) in enumerate(corner_rows(sx, sign)):
                line = lines[sign][dy]
                ext[q, planes[sx][dx], line : line + 1, :] = got[5 + k : 6 + k]

    def near_cells(q, plane, t, cy):
        if t < tiles:
            row = base + 8 * t + cy
            return ext[q, plane, row : row + 8, :]
        above = base + ny + cy
        below = base - 8 + cy
        return jnp.where(
            sub < 4, ext[q, plane, above : above + 8, :], ext[q, plane, below : below + 8, :]
        )

    def first_level(p, t, kinds, partial=None):
        got = []
        for i in range(19):
            cx, cy, cz = VEL[i]
            got.append(z_shifted(near_cells(i, p + 1 + cx, t, cy), cz))
        ub = [near_cells(19 + k, p + 1, t, 0) for k in range(4)]
        out, kept = adjoint_cell(got, ub[:3], ub[3], 1.0)
        if t == tiles and 1 <= p <= nx:
            for sign, row in ((1, 0), (-1, 7)):
                for k, i in enumerate(far(1, sign)):
                    line = k * nx + p - 1
                    term = sums[sign][line : line + 1]
                    out[i] = out[i] + jnp.where(sub == row, term, 0.0)
        elif t == tiles:
            sx = -1 if p == 0 else 1
            for sign, row in ((1, 0), (-1, 7)):
                i = corner_rows(sx, sign)[0][0]
                out[i] = out[i] + jnp.where(sub == row, corner_sums[sx, sign], 0.0)
        if partial is not None:
            for k, i in enumerate(kinds):
                row = k * ny + 8 * t
                out[i] = out[i] + jnp.where(partial, xb_ref[row : row + 8], 0.0)
        for i in kinds:
            if t < tiles:
                mid[i, p, t * 8 + 8 : t * 8 + 16, :] = out[i]
            elif VEL[i][1] > 0:
                mid[i, p, t * 8 + 8 : t * 8 + 16, :] = out[i]
            elif VEL[i][1] < 0:
                mid[i, p, 0:8, :] = out[i]
        return kept, ub[:3]

    def inside(x, carry):
        for t in range(tiles):
            kept, u = first_level(x + 1, t, range(19))
            rows = slice(t * 8, t * 8 + 8)
            f0, fs, fd, fm, _ = state_of(states_ref, (1, x, rows))
            grad1_ref[x, rows, :] = gradient_cell(kept, f0, fs, fd, fm, u)
        return carry

    lax.fori_loop(0, nx, inside, 0)
    for t in range(tiles):
        first_level(0, t, far(0, -1), even_x)
        first_level(nx + 1, t, far(0, 1), jnp.logical_not(even_x))

    for p in range(nx + 2):
        first_level(p, tiles, far(1, -1) + far(1, 1))

    def second_level(x, carry):
        for t in range(tiles):
            rows = slice(t * 8, t * 8 + 8)
            got = []
            for i in range(19):
                cx, cy, cz = VEL[i]
                low = 8 + 8 * t + cy
                value = z_shifted(mid[i, x + 1 + cx, low : low + 8, :], cz)
                got.append(value)
                pack_ref[i, rows, :] = jnp.where(
                    slot == x, pltpu.roll(value, 4 * x + 2, 1), pack_ref[i, rows, :]
                )
            f0, fs, fd, fm, u = state_of(states_ref, (0, x, rows))
            b = ub_ref[3, x, rows, :]
            out, kept = adjoint_cell(got, u, b, 1.0)
            for i in range(19):
                out_ref[i, x, rows, :] = out[i]
            grad_ref[x, rows, :] = grad1_ref[x, rows, :] + gradient_cell(
                kept, f0, fs, fd, fm, u
            )
        return carry

    lax.fori_loop(0, nx, second_level, 0)

    def tile(t, carry):
        rows = pl.ds(pl.multiple_of(t * 8, 8), 8)
        for i in range(20):
            for out_ref, level, first in ((f0_ref, 0, 0), (f1_ref, 1, 2)):
                if i == 19 and level == 1:
                    continue
                acc = jnp.zeros((8, nz), jnp.float32)
                for x in range(nx):
                    value = (
                        states_ref[level, i, x, rows, :]
                        if i < 19
                        else ub_ref[3, x, rows, :]
                    )
                    p = x + first
                    acc = jnp.where(slot == p, pltpu.roll(value, 4 * p + 2, 1), acc)
                out_ref[i, rows, :] = acc
        return carry

    lax.fori_loop(0, ny // 8, tile, 0)


def edge_kernel(
    zown_ref,
    za_ref,
    zb_ref,
    pack_ref,
    f0_ref,
    f1_ref,
    zout,
    tail_ref,
    zmid,
):
    ny, nz = pack_ref.shape[1:]
    tiles = ny // 8
    height = (tiles + 1) * 8
    even = parity("gz") == 0
    lane = lax.broadcasted_iota(jnp.int32, (8, nz), 1)
    sub = lax.broadcasted_iota(jnp.int32, (8, nz), 0)
    even_lane = lane % 2 == 0
    low_pair = lane % 4 < 2

    last = slice(2 * ny + 3, 2 * ny + 4)
    tail_ref[...] = za_ref[last] + zb_ref[last]

    def swapped(value):
        return jnp.where(even_lane, turn(value, -1), turn(value, 1))

    slab_grad = []
    for t in range(tiles + 1):
        received = []
        for g in range(2):
            row = (g * tiles + t) * 8 if t < tiles else 2 * ny
            va = za_ref[row : row + 8, :]
            vb = zb_ref[row : row + 8, :]
            if t == tiles and g:
                va, vb = [
                    jnp.where(sub < 4, pltpu.roll(v, 7, 0), pltpu.roll(v, 1, 0))
                    for v in (va, vb)
                ]
            received.append((jnp.where(even, va, vb), jnp.where(even, vb, va)))
        (high0, low0), (high1, low1) = received
        pairs = []
        for g in range(4):
            row = (g * (tiles + 1) + t) * 8
            own = zown_ref[row : row + 8]
            if g == 0:
                head, tail = own, low0
            elif g == 1:
                head, tail = high0, own
            elif g == 2:
                head = jnp.where(even_lane, own, turn(high1, 1))
                tail = jnp.where(even_lane, low1, own)
            else:
                head = jnp.where(even_lane, own, high1)
                tail = jnp.where(even_lane, turn(low1, -1), own)
            head = swapped(head)
            tail = swapped(tail)
            pairs.append(
                (
                    jnp.where(low_pair, head, turn(tail, 2)),
                    jnp.where(low_pair, turn(head, -2), tail),
                )
            )
        got = []
        for q in range(NSLOT):
            g, k = ZSLOT[q]
            got.append(turn(pairs[g][k % 2], -32 * (k // 2)))
        out, kept = adjoint_cell(got[:19], got[19:22], got[22], 1.0)
        for i in range(19):
            if t < tiles or VEL[i][1] > 0:
                zmid[i, 8 * t + 8 : 8 * t + 16, :] = out[i]
            elif VEL[i][1] < 0:
                zmid[i, 0:8, :] = out[i]
        if t < tiles:
            f = [f1_ref[i, 8 * t : 8 * t + 8, :] for i in range(19)]
            fs, fd = pairs_of(f)
            fm = moments(f[0], fs, fd)
            grad = gradient_cell(kept, f[0], fs, fd, fm, got[19:22])
            slab_grad.append(turn(grad, -8))

    at = lane % 4
    for t in range(tiles):
        rows = slice(8 * t, 8 * t + 8)
        got = []
        for i in range(19):
            cx, cy, cz = VEL[i]
            value = pack_ref[i, rows, :]
            edge = zmid[i, 8 + 8 * t + cy : 16 + 8 * t + cy, :]
            back = -4 * (2 + cx)
            if cz == 0:
                value = jnp.where((at == 1) | (at == 2), turn(edge, back), value)
            else:
                near_lane = 2 if cz < 0 else 0
                value = jnp.where(at == near_lane, turn(edge, back - 1), value)
                value = jnp.where(at == near_lane + 1, turn(edge, back + 1), value)
            got.append(value)
        f = [f0_ref[i, rows, :] for i in range(19)]
        fs, fd = pairs_of(f)
        fm = moments(f[0], fs, fd)
        inverse = 1.0 / fm["total"]
        u = [one * inverse for one in fm["one"]]
        out, kept = adjoint_cell(got, u, f0_ref[19, rows, :], 1.0)
        for i in range(19):
            zout[i, rows, :] = out[i]
        zout[19, rows, :] = gradient_cell(kept, f[0], fs, fd, fm, u)
        zout[20, rows, :] = slab_grad[t]


def finish_kernel(whole_cells, mask_ref, zout, inner_ref, grad1_ref, inner_grad_ref, *refs):
    tiles_of_drag, (out_hbm, grad_hbm, drag_hbm, out_ref, grad_ref, drag_ref, sems) = (
        refs[:-7],
        refs[-7:],
    )
    nx, ny, nz = mask_ref.shape
    tiles = ny // 8
    lane = lax.broadcasted_iota(jnp.int32, (8, nz), 1)
    outer = (lane < 2) | (lane >= nz - 2)
    ends = (lane < 1) | (lane >= nz - 1)
    copies = []

    def send(src, dst):
        copy = pltpu.make_async_copy(src, dst, sems.at[len(copies)])
        copy.start()
        copies.append(copy)

    for low, high in OUT_GROUPS:
        for i in range(low, high):
            for x in range(nx):
                for t in range(tiles):
                    rows = slice(8 * t, 8 * t + 8)
                    out_ref[i, x, rows, :] = jnp.where(
                        outer,
                        turn(zout[i, rows, :], -2 - 4 * x),
                        inner_ref[i, x, rows, :],
                    )
        send(out_ref.at[low:high], out_hbm.at[low:high])
    for x in range(nx):
        for t in range(tiles):
            rows = slice(8 * t, 8 * t + 8)
            level1 = jnp.where(
                ends, turn(zout[20, rows, :], -2 - 4 * x), grad1_ref[x, rows, :]
            )
            edge = turn(zout[19, rows, :], -2 - 4 * x) + level1
            grad = jnp.where(outer, edge, inner_grad_ref[x, rows, :])
            grad_ref[x, rows, :] = jnp.where(mask_ref[x, rows, :] == 0, grad, 0.0)
    send(grad_ref, grad_hbm)
    total = 0.0
    for ref in tiles_of_drag:
        total = total + jnp.sum(ref[...], axis=0, keepdims=True)
    drag_ref[...] = jnp.sum(total, axis=1, keepdims=True) / whole_cells
    send(drag_ref, drag_hbm)
    for copy in copies:
        copy.wait()


def swaps(count):
    first = [(i, i ^ 1) for i in range(count)]
    second = [(i, (((i + 1) % count) ^ 1) - 1) for i in range(count)]
    second = [(i, j % count) for i, j in second]
    return first, second


VMEM = pl.BlockSpec(memory_space=pltpu.VMEM)
HBM = pl.BlockSpec(memory_space=pltpu.HBM)
PARAMS = pltpu.CompilerParams(vmem_limit_bytes=48 * 2**20)


def call(kernel, inputs, shapes, scratch=(), space=VMEM, micros=0.05, outs=None):
    if space is HBM:
        inputs = [pltpu.with_memory_space_constraint(x, pltpu.HBM) for x in inputs]
    return pl.pallas_call(
        kernel,
        out_shape=[jax.ShapeDtypeStruct(s, jnp.float32) for s in shapes],
        in_specs=[space] * len(inputs),
        out_specs=outs or [VMEM] * len(shapes),
        scratch_shapes=list(scratch),
        compiler_params=PARAMS,
        cost_estimate=pl.CostEstimate(
            flops=0, bytes_accessed=int(3.6e6 * micros), transcendentals=0
        ),
    )(*inputs)


def body(primal_states, adjoint_last, porosity, solid_mask):
    nx, ny, nz = porosity.shape
    gx, gy, gz = [lax.axis_size(axis) for axis in AXES]
    x_first, x_second = swaps(gx)
    y_first, y_second = swaps(gy)
    z_first, z_second = swaps(gz)
    tiles = ny // 8
    height = (tiles + 1) * 8
    f32 = jnp.float32

    def diagonal(message, x_pairs, y_pairs):
        pairs = [(a * gy + c, b * gy + d) for a, b in x_pairs for c, d in y_pairs]
        return lax.ppermute(message, ("gx", "gy"), pairs)

    rows_x = NSLOT * ny + 8
    rows_y = 2 * (y_rows(nx) + EDGE_ROWS) + 8
    rows_c = 2 * (CORNER + EDGE_ROWS)
    rows_z = 2 * ny + 8
    rides = (gx, gy, gz) == (4, 2, 4)
    ub, drag = call(
        state_kernel,
        (primal_states, porosity, solid_mask),
        [(4, nx, ny, nz), (8, nz)],
        [
            pltpu.VMEM((2, 19, nx, ny, nz), f32),
            pltpu.VMEM((nx, ny, nz), f32),
            pltpu.VMEM((nx, ny, nz), jnp.int32),
            pltpu.SemaphoreType.DMA((5,)),
        ],
        HBM,
    )
    cols, y, ya, yb = call(
        pack_y_kernel,
        (adjoint_last, ub, drag),
        [(4 * ny + 8, nz), (rows_y, nz), (rows_c, nz), (rows_c, nz)],
        [pltpu.VMEM((NSLOT, 2 * nx, nz), f32)],
        micros=4,
    )
    (xa,) = call(pack_x_kernel, (adjoint_last, ub, drag), [(rows_x, nz)])
    (xb,) = call(pack_partial_kernel, (adjoint_last, ub), [(14 * ny + 8, nz)])
    xc = lax.ppermute(cols, "gx", x_second)
    xa = lax.ppermute(xa, "gx", x_first)
    if gy == 2:
        y = lax.ppermute(y, "gy", y_first)
        yb = diagonal(yb, x_second, y_first)
        ya = diagonal(ya, x_first, y_first)
    else:

        def both(message, block, send):
            parts = [message[:block], message[block : 2 * block], message[2 * block :]]
            return jnp.concatenate(
                [send(parts[0], y_first), send(parts[1], y_second), parts[2]]
            )

        block = y_rows(nx) + EDGE_ROWS
        y = both(y, block, lambda m, pairs: lax.ppermute(m, "gy", pairs))
        block = CORNER + EDGE_ROWS
        yb = both(yb, block, lambda m, pairs: diagonal(m, x_second, pairs))
        ya = both(ya, block, lambda m, pairs: diagonal(m, x_first, pairs))
    xb, xc = lax.optimization_barrier((xb, xc))
    xb = lax.ppermute(xb, "gx", x_second)

    zown, za, zb, drag_xy = call(
        pack_z_kernel,
        (cols, xa, xc, y, ya, yb),
        [(4 * height, nz), (rows_z, nz), (rows_z, nz), (1, nz)],
        [pltpu.VMEM((4, ny + 32, nz), f32)],
    )
    if rides:
        second = jnp.sum(xc[4 * ny :], axis=0, keepdims=True)
        second = second + yb[DRAG_ROW : DRAG_ROW + 1]
        drag_xy = drag_xy + lax.ppermute(second, "gx", x_first)
        za = za.at[2 * ny + 3 : 2 * ny + 4].set(drag_xy)
        zb = zb.at[2 * ny + 3 : 2 * ny + 4].set(drag_xy)
    zb = lax.ppermute(zb, "gz", z_second)
    za = lax.ppermute(za, "gz", z_first)
    inner, grad1, inner_grad, pack, f0, f1 = call(
        inner_kernel,
        (primal_states, adjoint_last, ub, xa, xb, y, ya, yb),
        [
            (19, nx, ny, nz),
            (nx, ny, nz),
            (nx, ny, nz),
            (19, ny, nz),
            (20, ny, nz),
            (19, ny, nz),
        ],
        [
            pltpu.VMEM((NSLOT, nx + 4, ny + 32, nz), f32),
            pltpu.VMEM((19, nx + 2, height + 8, nz), f32),
        ],
        micros=4,
    )
    if rides:
        zhalf = lax.ppermute(drag_xy, "gz", [(i, i ^ 2) for i in range(gz)])
        drags = (drag_xy, zhalf)
    else:
        drags = (lax.psum(drag, AXES),)

    zout, tails = call(
        edge_kernel,
        (zown, za, zb, pack, f0, f1),
        [(21, ny, nz), (1, nz)],
        [pltpu.VMEM((19, height + 8, nz), f32)],
    )
    if rides:
        drags += (tails,)
    whole_cells = float(nx * ny * nz * gx * gy * gz)
    first, gradient, drag = call(
        functools.partial(finish_kernel, whole_cells),
        (solid_mask, zout, inner, grad1, inner_grad) + drags,
        [(19, nx, ny, nz), (nx, ny, nz), (1, 1)],
        [
            pltpu.VMEM((19, nx, ny, nz), f32),
            pltpu.VMEM((nx, ny, nz), f32),
            pltpu.VMEM((1, 1), f32),
            pltpu.SemaphoreType.DMA((len(OUT_GROUPS) + 2,)),
        ],
        outs=[HBM, HBM, HBM],
    )
    return (first, gradient, drag.reshape(()))


def solution(mesh):
    return jax.shard_map(
        body,
        mesh=mesh,
        in_specs=(
            P(None, None, "gx", "gy", "gz"),
            P(None, "gx", "gy", "gz"),
            P("gx", "gy", "gz"),
            P("gx", "gy", "gz"),
        ),
        out_specs=(P(None, "gx", "gy", "gz"), P("gx", "gy", "gz"), P()),
        check_vma=False,
    )
```

```python
import functools

import jax
import jax.numpy as jnp
import numpy as np
from jax import lax
from jax.experimental import pallas as pl
from jax.experimental.pallas import tpu as pltpu
from jax.sharding import PartitionSpec as P

VEL = (
    (0, 0, 0),
    (1, 0, 0),
    (-1, 0, 0),
    (0, 1, 0),
    (0, -1, 0),
    (0, 0, 1),
    (0, 0, -1),
    (1, 1, 0),
    (-1, -1, 0),
    (1, -1, 0),
    (-1, 1, 0),
    (1, 0, 1),
    (-1, 0, -1),
    (1, 0, -1),
    (-1, 0, 1),
    (0, 1, 1),
    (0, -1, -1),
    (0, 1, -1),
    (0, -1, 1),
)
PAIRS = tuple((i, i + 1) for i in range(1, 19, 2))
AXES = ("gx", "gy", "gz")
UB = (19, 20, 21, 22)


def near(axis, sign):
    return tuple(i for i in range(19) if VEL[i][axis] * sign >= 0) + UB


def far(axis, sign):
    return tuple(i for i in range(19) if VEL[i][axis] == sign)


NSLOT = 23
CORNER = 16
DRAG_ROW = 14
EDGE_ROWS = 8


def y_rows(nx):
    return 14 * nx + 8


ZGROUPS = (
    tuple(i for i in range(19) if VEL[i][2] == -1),
    tuple(i for i in range(19) if VEL[i][2] == 1),
    tuple(i for i in range(19) if VEL[i][2] == 0)[:8],
    tuple(i for i in range(19) if VEL[i][2] == 0)[8:] + UB,
)
ZSLOT = {q: (g, k) for g, group in enumerate(ZGROUPS) for k, q in enumerate(group)}


def pairs_of(values):
    s = [values[a] + values[b] for a, b in PAIRS]
    d = [values[a] - values[b] for a, b in PAIRS]
    return s, d


def moments(v0, s, d):
    sx, sy, sz, sp, sq, sr, ss, st, su = s
    dx, dy, dz, dp, dq, dr, ds, dt, du = d
    ex = sp + sq
    ez = sr + ss
    ey = st + su
    faces = sx + sy + sz
    edges = ex + ez + ey
    exx = ex + ez
    eyy = ex + ey
    ezz = ez + ey
    fx = (dp + dq) + (dr + ds)
    fy = (dp - dq) + (dt + du)
    fz = (dr - ds) + (dt - du)
    return dict(
        rest=v0,
        faces=faces,
        edges=edges,
        total=v0 + faces + edges,
        face1=(dx, dy, dz),
        edge1=(fx, fy, fz),
        one=(dx + fx, dy + fy, dz + fz),
        face2=(sx, sy, sz),
        edge2=(exx, eyy, ezz),
        two=(sx + exx, sy + eyy, sz + ezz),
        cross=(sp - sq, sr - ss, st - su),
    )


def adjoint_cell(g, u, b, drive):
    s, d = pairs_of(g)
    m = moments(g[0], s, d)
    total = m["total"]
    trace = m["faces"] + 2.0 * m["edges"] - (30.0 / 19.0) * total
    p0 = (-1.2 / 19.0) * total - (2.0 / 21.0) * trace
    q = [
        (0.4 / 6.0) * (two - (10.0 / 19.0) * total) + (0.8 / 21.0) * trace
        for two in m["two"]
    ]
    qsum = q[0] + q[1] + q[2]
    qab = [0.1 * c for c in m["cross"]]
    p1 = [-0.12 * one for one in m["one"]]
    h0 = (
        0.4 * m["rest"]
        + (1.2 / 18.0) * m["faces"]
        + (1.2 / 36.0) * m["edges"]
        + p0
        + (1.0 / 3.0) * qsum
    )
    h1 = [
        (1.2 / 18.0) * f + (1.2 / 36.0) * e + (1.0 / 3.0) * p
        for f, e, p in zip(m["face1"], m["edge1"], p1)
    ]
    base = (1.0 / 3.0) * p0 + (1.0 / 9.0) * qsum
    haa = [
        (1.2 / 18.0) * f + (1.2 / 36.0) * e + (2.0 / 9.0) * qa + base
        for f, e, qa in zip(m["face2"], m["edge2"], q)
    ]
    hxy, hxz, hyz = [(2.0 / 45.0) * c for c in m["cross"]]
    ux, uy, uz = u
    v = (
        haa[0] * ux + hxy * uy + hxz * uz,
        hxy * ux + haa[1] * uy + hyz * uz,
        hxz * ux + hyz * uy + haa[2] * uz,
    )
    uv = ux * v[0] + uy * v[1] + uz * v[2]
    uu = ux * ux + uy * uy + uz * uz
    uuh = 1.5 * uu * h0
    a = h0 + uuh - 4.5 * uv
    nb = 1.0 - b
    e0 = nb * (a - p0)
    nq = [nb * x for x in q]
    nxy, nxz, nyz = [nb * x for x in qab]
    o = [
        nb * (3.0 * h1[k] + 9.0 * v[k] - 3.0 * u[k] * h0 - p1[k]) for k in range(3)
    ]
    o[0] = o[0] + b * drive
    alpha = -0.2 * nb
    half_s = 0.5 * (alpha + b)
    half_d = 0.5 * (alpha - b)
    exy = e0 - nq[0] - nq[1]
    exz = e0 - nq[0] - nq[2]
    eyz = e0 - nq[1] - nq[2]
    even = (
        e0 - nq[0],
        e0 - nq[1],
        e0 - nq[2],
        exy - nxy,
        exy + nxy,
        exz - nxz,
        exz + nxz,
        eyz - nyz,
        eyz + nyz,
    )
    odd = (
        o[0],
        o[1],
        o[2],
        o[0] + o[1],
        o[0] - o[1],
        o[0] + o[2],
        o[0] - o[2],
        o[1] + o[2],
        o[1] - o[2],
    )
    out = [(alpha + b) * g[0] + e0]
    for k in range(9):
        even_k = half_s * s[k] + even[k]
        odd_k = half_d * d[k] + odd[k]
        out.append(even_k + odd_k)
        out.append(even_k - odd_k)
    kept = dict(
        s=s, d=d, g0=g[0], p0=p0, p1=p1, q=q, qab=qab, h0=h0, h1=h1, uv=uv, uuh=uuh
    )
    return out, kept


def gradient_cell(kept, f0, fs, fd, fm, u):
    rho = fm["total"]
    even = fs[0] * kept["s"][0]
    odd = fd[0] * kept["d"][0]
    for k in range(1, 9):
        even = even + fs[k] * kept["s"][k]
        odd = odd + fd[k] * kept["d"][k]
    hf = kept["p0"] * rho
    for k in range(3):
        hf = hf + kept["p1"][k] * fm["one"][k] + kept["q"][k] * fm["two"][k]
        hf = hf + kept["qab"][k] * fm["cross"][k]
    uh1 = u[0] * kept["h1"][0] + u[1] * kept["h1"][1] + u[2] * kept["h1"][2]
    hfeq = rho * (kept["h0"] - kept["uuh"] + 3.0 * uh1 + 4.5 * kept["uv"])
    pairs = 1.2 * f0 * kept["g0"] + 0.6 * even - 0.4 * odd
    return pairs + hf - hfeq + fm["one"][0]


def state_of(ref, index):
    f = [ref[(index[0], i) + index[1:]] for i in range(19)]
    s, d = pairs_of(f)
    m = moments(f[0], s, d)
    inverse = 1.0 / m["total"]
    u = [one * inverse for one in m["one"]]
    return f[0], s, d, m, u


def corner_rows(sx, sy):
    both = [i for i in far(0, sx) if VEL[i][1] == sy]
    along_y = [i for i in far(1, sy) if VEL[i][0] == 0]
    along_x = [i for i in far(0, sx) if VEL[i][1] == 0]
    rows = [(i, 0, 0) for i in both + along_y + along_x]
    return rows + [(i, 1, 0) for i in both] + [(i, 0, 1) for i in both]


def corner_zeros(sx, sy):
    rows = [(i, 0, 0) for i in range(19) if VEL[i][0] == 0 and VEL[i][1] == 0]
    rows += [(i, 1, 0) for i in far(0, sx) if VEL[i][1] == 0]
    rows += [(i, 0, 1) for i in far(1, sy) if VEL[i][0] == 0]
    return rows + [(i, 1, 1) for i in far(0, sx) if VEL[i][1] == sy]


CORNERS = ((1, 1), (1, -1), (-1, 1), (-1, -1))


def parity(axis):
    return lax.axis_index(axis) % 2


def cell_rows(adj_ref, ub_ref, q, x, rows):
    return adj_ref[q, x, rows, :] if q < 19 else ub_ref[q - 19, x, rows, :]


def state_kernel(
    states_hbm,
    por_hbm,
    mask_hbm,
    ub_ref,
    drag_ref,
    states_ref,
    por_ref,
    mask_ref,
    sems,
):
    nx, ny, nz = por_ref.shape
    tiles = ny // 8
    copies = [
        pltpu.make_async_copy(src, dst, sems.at[k])
        for k, (src, dst) in enumerate(
            (
                (states_hbm.at[1], states_ref.at[1]),
                (por_hbm, por_ref),
                (mask_hbm, mask_ref),
                (states_hbm.at[0, 1:3], states_ref.at[0, 1:3]),
                (states_hbm.at[0, 7:15], states_ref.at[0, 7:15]),
            )
        )
    ]
    for copy in copies:
        copy.start()
    for copy in copies[:3]:
        copy.wait()

    def cells(x, carry):
        for t in range(tiles):
            rows = slice(8 * t, 8 * t + 8)
            blocking = jnp.where(mask_ref[x, rows, :] == 0, por_ref[x, rows, :], 1.0)
            f0, s, d, m, u = state_of(states_ref, (1, x, rows))
            for k in range(3):
                ub_ref[k, x, rows, :] = u[k]
            ub_ref[3, x, rows, :] = blocking
            carry = carry + blocking * m["one"][0]
        return carry

    drag = lax.fori_loop(0, nx, cells, jnp.zeros((8, nz), jnp.float32))
    for copy in copies[3:]:
        copy.wait()

    def flux_cells(x, carry):
        for t in range(tiles):
            rows = slice(8 * t, 8 * t + 8)
            flux = 0.0
            for a, b in PAIRS:
                if VEL[a][0]:
                    flux = flux + (
                        states_ref[0, a, x, rows, :] - states_ref[0, b, x, rows, :]
                    )
            carry = carry + ub_ref[3, x, rows, :] * flux
        return carry

    drag = lax.fori_loop(0, nx, flux_cells, drag)
    drag_ref[...] = drag


def pack_x_kernel(adj_ref, ub_ref, drag_ref, out_ref):
    nx, ny = adj_ref.shape[1:3]
    out_ref[NSLOT * ny :] = drag_ref[...]

    def fill(sign):
        for names, offset, x in (
            (near(0, sign), 0, 0 if sign > 0 else nx - 1),
            (far(0, sign), 18, 1 if sign > 0 else nx - 2),
        ):
            for k, q in enumerate(names):
                k += offset
                out_ref[k * ny : (k + 1) * ny] = cell_rows(
                    adj_ref, ub_ref, q, x, slice(0, ny)
                )

    pl.when(parity("gx") == 0)(functools.partial(fill, -1))
    pl.when(parity("gx") == 1)(functools.partial(fill, 1))


def y_edge_entries(sign, nx):
    rows = []
    for side in (1, -1):
        x = 0 if side > 0 else nx - 1
        rows += [(i, 0, x) for i in far(0, side) if VEL[i][1] == 0]
        rows += [(i, 1, x) for i in far(0, side) if VEL[i][1] == sign]
    return rows


def edge_entries(sign):
    rows = []
    for side in (1, -1):
        rows += [(i, 0, side) for i in far(1, side) if VEL[i][0] == 0]
        rows += [(i, 1, side) for i in far(1, side) if VEL[i][0] == sign]
    return rows


def pack_partial_kernel(adj_ref, ub_ref, out_ref):
    nx, ny, nz = adj_ref.shape[1:]
    tiles = ny // 8
    sub = lax.broadcasted_iota(jnp.int32, (8, nz), 0)

    def fill(sign):
        here, inside = (0, 1) if sign > 0 else (nx - 1, nx - 2)
        names = far(0, sign)
        for t in range(tiles):
            rows = slice(8 * t, 8 * t + 8)
            got = []
            for i in range(19):
                cx, cy, cz = VEL[i]
                if cx * sign < 0:
                    got.append(jnp.zeros((8, nz), jnp.float32))
                    continue
                x = inside if cx else here
                if t == 0 and cy < 0:
                    value = pltpu.roll(adj_ref[i, x, rows, :], 1, 0)
                    value = jnp.where(sub == 0, 0.0, value)
                elif t == tiles - 1 and cy > 0:
                    value = pltpu.roll(adj_ref[i, x, rows, :], 7, 0)
                    value = jnp.where(sub == 7, 0.0, value)
                else:
                    value = adj_ref[i, x, 8 * t + cy : 8 * t + 8 + cy, :]
                got.append(z_shifted(value, cz))
            u = [ub_ref[k, here, rows, :] for k in range(3)]
            out, _ = adjoint_cell(got, u, ub_ref[3, here, rows, :], 0.0)
            for k, i in enumerate(names):
                out_ref[k * ny + 8 * t : k * ny + 8 * t + 8] = out[i]
        for k, q in enumerate(names + UB):
            k += 5
            out_ref[k * ny : (k + 1) * ny] = cell_rows(
                adj_ref, ub_ref, q, here, slice(0, ny)
            )
        for k, (i, depth, side) in enumerate(edge_entries(sign)):
            y = 0 if side > 0 else ny - 1
            row = 14 * ny + k
            out_ref[row : row + 1] = adj_ref[i, inside if depth else here, y : y + 1, :]

    pl.when(parity("gx") == 0)(functools.partial(fill, 1))
    pl.when(parity("gx") == 1)(functools.partial(fill, -1))


def column_pair(acc, value, pair, q, k, plane):
    start = 32 * (k // 2) + 4 * plane + 2 * (k % 2)
    cz = VEL[q][2] if q < 19 else 0
    return jnp.where(pair == start // 2, turn(value, start + 1 - cz), acc)


def pack_y_kernel(
    adj_ref, ub_ref, drag_ref, cols_ref, y_ref, ya_ref, yb_ref, read_ref
):
    nx, ny, nz = adj_ref.shape[1:]
    pair = lax.broadcasted_iota(jnp.int32, (8, nz), 1) // 2
    for g, group in enumerate(ZGROUPS):
        for t in range(ny // 8):
            acc = jnp.zeros((8, nz), jnp.float32)
            for k, q in enumerate(group):
                for x in range(nx):
                    value = cell_rows(adj_ref, ub_ref, q, x, slice(8 * t, 8 * t + 8))
                    acc = column_pair(acc, value, pair, q, k, x + 2)
            row = g * ny + 8 * t
            cols_ref[row : row + 8] = acc
    y_block = y_rows(nx) + EDGE_ROWS
    corner_block = CORNER + EDGE_ROWS

    def fill_edges(place, sign):
        for g in range(4):
            for d in range(2):
                y = d if sign > 0 else ny - 1 - d
                line = cols_ref[g * ny + y : g * ny + y + 1]
                row = place * y_block + y_rows(nx) + 2 * g + d
                y_ref[row : row + 1] = line
                row = place * corner_block + CORNER + 2 * g + d
                ya_ref[row : row + 1] = line
                yb_ref[row : row + 1] = line

    faces = ((1, 0, 1), (-1, ny - 1, ny - 2))
    for i in range(19):
        cx, cy, _ = VEL[i]
        read_ref[i] = jnp.zeros((2 * nx, nz), jnp.float32)
        for n, (sign, here, inside) in enumerate(faces):
            for x in range(max(0, -cx), min(nx, nx - cx)):
                if cy * sign >= 0:
                    y = inside if cy else here
                    read_ref[i, n * nx + x : n * nx + x + 1, :] = adj_ref[
                        i, x + cx, y : y + 1, :
                    ]
    for k in range(4):
        for n, (sign, here, inside) in enumerate(faces):
            for x in range(nx):
                read_ref[19 + k, n * nx + x : n * nx + x + 1, :] = ub_ref[
                    k, x, here : here + 1, :
                ]
    got = [z_shifted(read_ref[i], VEL[i][2]) for i in range(19)]
    sums, _ = adjoint_cell(
        got, [read_ref[19 + k] for k in range(3)], read_ref[22], 0.0
    )

    def fill_y(place, sign):
        n = 0 if sign > 0 else 1
        _, here, inside = faces[n]
        first = place * y_block
        for k, i in enumerate(far(1, sign)):
            row = first + k * nx
            y_ref[row : row + nx] = sums[i][n * nx : (n + 1) * nx]
        for k, q in enumerate(far(1, sign) + UB):
            for x in range(nx):
                row = first + (5 + k) * nx + x
                y_ref[row : row + 1] = cell_rows(
                    adj_ref, ub_ref, q, x, slice(here, here + 1)
                )
        for k, (i, depth, x) in enumerate(y_edge_entries(sign, nx)):
            y = inside if depth else here
            row = first + 14 * nx + k
            y_ref[row : row + 1] = adj_ref[i, x, y : y + 1, :]

    for i in range(19):
        read_ref[i] = jnp.zeros((2 * nx, nz), jnp.float32)
    for n, (sx, sy) in enumerate(CORNERS):
        xs = (0, 1) if sx > 0 else (nx - 1, nx - 2)
        ys = (0, 1) if sy > 0 else (ny - 1, ny - 2)
        for i, dx, dy in corner_zeros(sx, sy):
            read_ref[i, n : n + 1, :] = adj_ref[i, xs[dx], ys[dy] : ys[dy] + 1, :]
        for k in range(4):
            read_ref[19 + k, n : n + 1, :] = ub_ref[k, xs[0], ys[0] : ys[0] + 1, :]
    got = [z_shifted(read_ref[i], VEL[i][2]) for i in range(19)]
    corner_sums, _ = adjoint_cell(
        got, [read_ref[19 + k] for k in range(3)], read_ref[22], 0.0
    )
    line = jnp.sum(drag_ref[...], axis=0, keepdims=True)

    def fill_corner(out_ref, place, sx, sy):
        xs = (0, 1) if sx > 0 else (nx - 1, nx - 2)
        ys = (0, 1) if sy > 0 else (ny - 1, ny - 2)
        n = CORNERS.index((sx, sy))
        first = place * corner_block
        rows = corner_rows(sx, sy)
        out_ref[first : first + 1] = corner_sums[rows[0][0]][n : n + 1]
        for k in range(4):
            out_ref[first + 1 + k : first + 2 + k] = ub_ref[
                k, xs[0], ys[0] : ys[0] + 1, :
            ]
        for k, (i, dx, dy) in enumerate(rows):
            row = first + 5 + k
            out_ref[row : row + 1] = adj_ref[i, xs[dx], ys[dy] : ys[dy] + 1, :]
        out_ref[first + DRAG_ROW : first + DRAG_ROW + 1] = line
        out_ref[first + DRAG_ROW + 1 : first + CORNER] = jnp.zeros((1, nz), jnp.float32)

    drag = drag_ref[...]
    cols_ref[4 * ny :] = drag
    y_ref[2 * y_block :] = drag
    for py in (0, 1):

        @pl.when(parity("gy") == py)
        def _():
            s0 = 1 if py else -1
            fill_y(0, s0)
            fill_y(1, -s0)
            fill_edges(0, s0)
            fill_edges(1, -s0)

    for px in (0, 1):
        for py in (0, 1):

            @pl.when((parity("gx") == px) & (parity("gy") == py))
            def _():
                sa = 1 if px else -1
                s0 = 1 if py else -1
                for out_ref, sx in ((ya_ref, sa), (yb_ref, -sa)):
                    fill_corner(out_ref, 0, sx, s0)
                    fill_corner(out_ref, 1, sx, -s0)


def pack_columns_kernel(cols_ref, xa_ref, xc_ref, out_ref):
    ny = (cols_ref.shape[0] - 8) // 4
    nz = cols_ref.shape[1]
    tiles = ny // 8
    lane = lax.broadcasted_iota(jnp.int32, (8, nz), 1)
    plane = (lane % 32) // 4
    pair = lane // 2

    def fill_main(sign):
        halo = {}
        for names, offset, p in (
            (near(0, sign), 0, 6 if sign > 0 else 1),
            (far(0, sign), 18, 7 if sign > 0 else 0),
        ):
            for k, q in enumerate(names):
                halo.setdefault(q, []).append((k + offset, p))
        for g, group in enumerate(ZGROUPS):
            for t in range(tiles):
                rows = slice(g * ny + 8 * t, g * ny + 8 * t + 8)
                acc = jnp.where(
                    plane < 2 if sign > 0 else plane > 5,
                    turn(xc_ref[rows], -16 * sign),
                    cols_ref[rows],
                )
                for k, q in enumerate(group):
                    for at, p in halo.get(q, ()):
                        row = at * ny + 8 * t
                        acc = column_pair(acc, xa_ref[row : row + 8], pair, q, k, p)
                    out_ref[rows] = acc

    @pl.when(parity("gx") == 0)
    def _():
        fill_main(1)

    @pl.when(parity("gx") == 1)
    def _():
        fill_main(-1)


def pack_z_kernel(
    main_ref,
    cols_ref,
    xa_ref,
    xc_ref,
    y_ref,
    ya_ref,
    yb_ref,
    zown_ref,
    za_ref,
    zb_ref,
    drag_ref,
    ext,
):
    ny = (cols_ref.shape[0] - 8) // 4
    nz = cols_ref.shape[1]
    tiles = ny // 8
    base = 16
    even_x = parity("gx") == 0
    even_y = parity("gy") == 0
    lane = lax.broadcasted_iota(jnp.int32, (8, nz), 1)
    sub = lax.broadcasted_iota(jnp.int32, (8, nz), 0)
    plane = (lane % 32) // 4
    slot = 2 * (lane // 32) + (lane % 4) // 2

    def along_x(own, va, vb):
        low = turn(jnp.where(even_x, vb, va), -16)
        high = turn(jnp.where(even_x, va, vb), 16)
        return jnp.where(plane < 2, low, jnp.where(plane > 5, high, own))

    for g in range(4):
        for t in range(tiles):
            row = g * ny + 8 * t
            ext[g, base + 8 * t : base + 8 * t + 8, :] = main_ref[row : row + 8]

    y_block = (y_ref.shape[0] - 8) // 2
    corner_block = CORNER + EDGE_ROWS

    def edges(ref, block, place):
        return ref[(place + 1) * block - EDGE_ROWS : (place + 1) * block]

    first, second = [
        along_x(
            edges(y_ref, y_block, place),
            edges(ya_ref, corner_block, place),
            edges(yb_ref, corner_block, place),
        )
        for place in range(2)
    ]
    high = jnp.where(even_y, first, second)
    low = jnp.where(even_y, second, first)
    for g in range(4):
        for d in range(2):
            row = 2 * g + d
            ext[g, base + ny + d : base + ny + d + 1, :] = high[row : row + 1]
            ext[g, base - 1 - d : base - d, :] = low[row : row + 1]

    packed = []
    for g, group in enumerate(ZGROUPS):
        moves = {}
        for k, q in enumerate(group):
            cx, cy, _ = VEL[q] if q < 19 else (0, 0, 0)
            moves.setdefault((cx, cy), []).append(k)
        acc = [jnp.zeros((8, nz), jnp.float32) for t in range(tiles + 1)]
        for (cx, cy), slots in moves.items():
            mask = slot == slots[0]
            for k in slots[1:]:
                mask = mask | (slot == k)
            for t in range(tiles + 1):
                if t < tiles:
                    row = base + 8 * t + cy
                    value = ext[g, row : row + 8, :]
                else:
                    above = base + ny + cy
                    below = base - 8 + cy
                    value = jnp.where(
                        sub < 4, ext[g, above : above + 8, :], ext[g, below : below + 8, :]
                    )
                acc[t] = jnp.where(mask, turn(value, -4 * cx), acc[t])
        packed.append(acc)
        for t in range(tiles + 1):
            row = (g * (tiles + 1) + t) * 8
            zown_ref[row : row + 8, :] = acc[t]
    up_first = parity("gz") == 0
    even_lane = lane % 2 == 0
    for t in range(tiles + 1):
        two, three = packed[2][t], packed[3][t]
        up = (packed[0][t], jnp.where(even_lane, two, pltpu.roll(three, 1, 1)))
        down = (packed[1][t], jnp.where(even_lane, pltpu.roll(two, nz - 1, 1), three))
        if t == tiles:
            up, down = [
                (
                    jnp.where(
                        (sub == 0) | (sub == 7),
                        side[0],
                        jnp.where(
                            sub < 4, pltpu.roll(side[1], 1, 0), pltpu.roll(side[1], 7, 0)
                        ),
                    ),
                )
                for side in (up, down)
            ]
        for g in range(len(up)):
            row = (g * tiles + t) * 8 if t < tiles else 2 * tiles * 8
            za_ref[row : row + 8, :] = jnp.where(up_first, up[g], down[g])
            zb_ref[row : row + 8, :] = jnp.where(up_first, down[g], up[g])
    drag = (cols_ref[4 * ny :] + y_ref[2 * y_block :]) + (
        xa_ref[xa_ref.shape[0] - 8 :] + xc_ref[4 * ny :]
    )
    row = slice(DRAG_ROW, DRAG_ROW + 1)
    drag_ref[...] = jnp.sum(drag, axis=0, keepdims=True) + (ya_ref[row] + yb_ref[row])


OUT_GROUPS = ((0, 5), (5, 10), (10, 15), (15, 19))


def turn(value, shift):
    nz = value.shape[1]
    return pltpu.roll(value, shift % nz, 1) if shift % nz else value


def z_shifted(value, cz):
    return turn(value, -cz) if cz else value


def inner_kernel(
    states_ref,
    adj_ref,
    ub_ref,
    xa_ref,
    xb_ref,
    y_ref,
    ya_ref,
    yb_ref,
    out_ref,
    grad1_ref,
    grad_ref,
    pack_ref,
    f0_ref,
    f1_ref,
    ext,
    mid,
):
    nx, ny, nz = grad_ref.shape
    tiles = ny // 8
    lane = lax.broadcasted_iota(jnp.int32, (8, nz), 1)
    slot = lane // 4
    sub = lax.broadcasted_iota(jnp.int32, (8, nz), 0)
    even_x = parity("gx") == 0
    even_y = parity("gy") == 0
    base = 16

    for q in range(NSLOT):
        for x in range(nx):
            ext[q, x + 2, base : base + ny, :] = (
                adj_ref[q, x] if q < 19 else ub_ref[q - 19, x]
            )
    planes = {1: (nx + 2, nx + 3), -1: (1, 0)}
    lines = {1: (base + ny, base + ny + 1), -1: (base - 1, base - 2)}

    def fill_whole(sign):
        for names, depth, offset in ((near(0, sign), 0, 0), (far(0, sign), 1, 18)):
            for k, q in enumerate(names):
                rows = slice((k + offset) * ny, (k + offset + 1) * ny)
                ext[q, planes[sign][depth], base : base + ny, :] = xa_ref[rows]

    def fill_partial(sign):
        one, two = planes[sign]
        for k, q in enumerate(far(0, sign) + UB):
            ext[q, one, base : base + ny, :] = xb_ref[(5 + k) * ny : (6 + k) * ny]
        nothing = jnp.zeros((ny, nz), jnp.float32)
        for q in range(19):
            if VEL[q][0] == 0:
                ext[q, one, base : base + ny, :] = nothing
            elif VEL[q][0] == sign:
                ext[q, two, base : base + ny, :] = nothing
        for k, (q, depth, side) in enumerate(edge_entries(sign)):
            line = base if side > 0 else base + ny - 1
            row = 14 * ny + k
            ext[q, planes[sign][depth], line : line + 1, :] = xb_ref[row : row + 1]

    @pl.when(parity("gx") == 0)
    def _():
        fill_whole(1)
        fill_partial(-1)

    @pl.when(parity("gx") == 1)
    def _():
        fill_whole(-1)
        fill_partial(1)

    sums = {}
    corner_sums = {}
    for sign in (1, -1):
        block = y_rows(nx) + EDGE_ROWS
        first, second = (0, block) if sign > 0 else (block, 0)
        one, two = lines[sign]
        nothing = jnp.zeros((1, nz), jnp.float32)
        for q in range(19):
            for x in range(nx):
                if VEL[q][1] == 0:
                    ext[q, x + 2, one : one + 1, :] = nothing
                elif VEL[q][1] == sign:
                    ext[q, x + 2, two : two + 1, :] = nothing
        got = jnp.where(
            even_y,
            y_ref[first : first + y_rows(nx)],
            y_ref[second : second + y_rows(nx)],
        )
        sums[sign] = got
        for k, q in enumerate(far(1, sign) + UB):
            for x in range(nx):
                row = (5 + k) * nx + x
                ext[q, x + 2, one : one + 1, :] = got[row : row + 1]
        for k, (q, depth, x) in enumerate(y_edge_entries(sign, nx)):
            line = lines[sign][depth]
            row = 14 * nx + k
            ext[q, x + 2, line : line + 1, :] = got[row : row + 1]
        for sx in (1, -1):
            xs = (ya_ref, yb_ref) if sx > 0 else (yb_ref, ya_ref)
            block = CORNER + EDGE_ROWS
            ys = (0, block) if sign > 0 else (block, 0)
            low, high = [
                jnp.where(even_x, xs[0][r : r + CORNER], xs[1][r : r + CORNER])
                for r in ys
            ]
            got = jnp.where(even_y, low, high)
            corner_sums[sx, sign] = got[0:1]
            for k in range(4):
                line = lines[sign][0]
                ext[19 + k, planes[sx][0], line : line + 1, :] = got[1 + k : 2 + k]
            for q, dx, dy in corner_zeros(sx, sign):
                line = lines[sign][dy]
                ext[q, planes[sx][dx], line : line + 1, :] = nothing
            for k, (q, dx, dy) in enumerate(corner_rows(sx, sign)):
                line = lines[sign][dy]
                ext[q, planes[sx][dx], line : line + 1, :] = got[5 + k : 6 + k]

    def near_cells(q, plane, t, cy):
        if t < tiles:
            row = base + 8 * t + cy
            return ext[q, plane, row : row + 8, :]
        above = base + ny + cy
        below = base - 8 + cy
        return jnp.where(
            sub < 4, ext[q, plane, above : above + 8, :], ext[q, plane, below : below + 8, :]
        )

    def first_level(p, t, kinds, partial=None):
        got = []
        for i in range(19):
            cx, cy, cz = VEL[i]
            got.append(z_shifted(near_cells(i, p + 1 + cx, t, cy), cz))
        ub = [near_cells(19 + k, p + 1, t, 0) for k in range(4)]
        out, kept = adjoint_cell(got, ub[:3], ub[3], 1.0)
        if t == tiles and 1 <= p <= nx:
            for sign, row in ((1, 0), (-1, 7)):
                for k, i in enumerate(far(1, sign)):
                    line = k * nx + p - 1
                    term = sums[sign][line : line + 1]
                    out[i] = out[i] + jnp.where(sub == row, term, 0.0)
        elif t == tiles:
            sx = -1 if p == 0 else 1
            for sign, row in ((1, 0), (-1, 7)):
                i = corner_rows(sx, sign)[0][0]
                out[i] = out[i] + jnp.where(sub == row, corner_sums[sx, sign], 0.0)
        if partial is not None:
            for k, i in enumerate(kinds):
                row = k * ny + 8 * t
                out[i] = out[i] + jnp.where(partial, xb_ref[row : row + 8], 0.0)
        for i in kinds:
            if t < tiles:
                mid[i, p, t * 8 + 8 : t * 8 + 16, :] = out[i]
            elif VEL[i][1] > 0:
                mid[i, p, t * 8 + 8 : t * 8 + 16, :] = out[i]
            elif VEL[i][1] < 0:
                mid[i, p, 0:8, :] = out[i]
        return kept, ub[:3]

    def inside(x, carry):
        for t in range(tiles):
            kept, u = first_level(x + 1, t, range(19))
            rows = slice(t * 8, t * 8 + 8)
            f0, fs, fd, fm, _ = state_of(states_ref, (1, x, rows))
            grad1_ref[x, rows, :] = gradient_cell(kept, f0, fs, fd, fm, u)
        return carry

    lax.fori_loop(0, nx, inside, 0)
    for t in range(tiles):
        first_level(0, t, far(0, -1), even_x)
        first_level(nx + 1, t, far(0, 1), jnp.logical_not(even_x))

    for p in range(nx + 2):
        first_level(p, tiles, far(1, -1) + far(1, 1))

    def second_level(x, carry):
        for t in range(tiles):
            rows = slice(t * 8, t * 8 + 8)
            got = []
            for i in range(19):
                cx, cy, cz = VEL[i]
                low = 8 + 8 * t + cy
                value = z_shifted(mid[i, x + 1 + cx, low : low + 8, :], cz)
                got.append(value)
                pack_ref[i, rows, :] = jnp.where(
                    slot == x, pltpu.roll(value, 4 * x + 2, 1), pack_ref[i, rows, :]
                )
            f0, fs, fd, fm, u = state_of(states_ref, (0, x, rows))
            b = ub_ref[3, x, rows, :]
            out, kept = adjoint_cell(got, u, b, 1.0)
            for i in range(19):
                out_ref[i, x, rows, :] = out[i]
            grad_ref[x, rows, :] = grad1_ref[x, rows, :] + gradient_cell(
                kept, f0, fs, fd, fm, u
            )
        return carry

    lax.fori_loop(0, nx, second_level, 0)

    def tile(t, carry):
        rows = pl.ds(pl.multiple_of(t * 8, 8), 8)
        for i in range(20):
            for out_ref, level, first in ((f0_ref, 0, 0), (f1_ref, 1, 2)):
                if i == 19 and level == 1:
                    continue
                acc = jnp.zeros((8, nz), jnp.float32)
                for x in range(nx):
                    value = (
                        states_ref[level, i, x, rows, :]
                        if i < 19
                        else ub_ref[3, x, rows, :]
                    )
                    p = x + first
                    acc = jnp.where(slot == p, pltpu.roll(value, 4 * p + 2, 1), acc)
                out_ref[i, rows, :] = acc
        return carry

    lax.fori_loop(0, ny // 8, tile, 0)


def edge_kernel(
    zown_ref,
    za_ref,
    zb_ref,
    pack_ref,
    f0_ref,
    f1_ref,
    zout,
    tail_ref,
    zmid,
):
    ny, nz = pack_ref.shape[1:]
    tiles = ny // 8
    height = (tiles + 1) * 8
    even = parity("gz") == 0
    lane = lax.broadcasted_iota(jnp.int32, (8, nz), 1)
    sub = lax.broadcasted_iota(jnp.int32, (8, nz), 0)
    even_lane = lane % 2 == 0
    low_pair = lane % 4 < 2

    last = slice(2 * ny + 3, 2 * ny + 4)
    tail_ref[...] = za_ref[last] + zb_ref[last]

    def swapped(value):
        return jnp.where(even_lane, turn(value, -1), turn(value, 1))

    slab_grad = []
    for t in range(tiles + 1):
        received = []
        for g in range(2):
            row = (g * tiles + t) * 8 if t < tiles else 2 * ny
            va = za_ref[row : row + 8, :]
            vb = zb_ref[row : row + 8, :]
            if t == tiles and g:
                va, vb = [
                    jnp.where(sub < 4, pltpu.roll(v, 7, 0), pltpu.roll(v, 1, 0))
                    for v in (va, vb)
                ]
            received.append((jnp.where(even, va, vb), jnp.where(even, vb, va)))
        (high0, low0), (high1, low1) = received
        pairs = []
        for g in range(4):
            row = (g * (tiles + 1) + t) * 8
            own = zown_ref[row : row + 8]
            if g == 0:
                head, tail = own, low0
            elif g == 1:
                head, tail = high0, own
            elif g == 2:
                head = jnp.where(even_lane, own, turn(high1, 1))
                tail = jnp.where(even_lane, low1, own)
            else:
                head = jnp.where(even_lane, own, high1)
                tail = jnp.where(even_lane, turn(low1, -1), own)
            head = swapped(head)
            tail = swapped(tail)
            pairs.append(
                (
                    jnp.where(low_pair, head, turn(tail, 2)),
                    jnp.where(low_pair, turn(head, -2), tail),
                )
            )
        got = []
        for q in range(NSLOT):
            g, k = ZSLOT[q]
            got.append(turn(pairs[g][k % 2], -32 * (k // 2)))
        out, kept = adjoint_cell(got[:19], got[19:22], got[22], 1.0)
        for i in range(19):
            if t < tiles or VEL[i][1] > 0:
                zmid[i, 8 * t + 8 : 8 * t + 16, :] = out[i]
            elif VEL[i][1] < 0:
                zmid[i, 0:8, :] = out[i]
        if t < tiles:
            f = [f1_ref[i, 8 * t : 8 * t + 8, :] for i in range(19)]
            fs, fd = pairs_of(f)
            fm = moments(f[0], fs, fd)
            grad = gradient_cell(kept, f[0], fs, fd, fm, got[19:22])
            slab_grad.append(turn(grad, -8))

    at = lane % 4
    for t in range(tiles):
        rows = slice(8 * t, 8 * t + 8)
        got = []
        for i in range(19):
            cx, cy, cz = VEL[i]
            value = pack_ref[i, rows, :]
            edge = zmid[i, 8 + 8 * t + cy : 16 + 8 * t + cy, :]
            back = -4 * (2 + cx)
            if cz == 0:
                value = jnp.where((at == 1) | (at == 2), turn(edge, back), value)
            else:
                near_lane = 2 if cz < 0 else 0
                value = jnp.where(at == near_lane, turn(edge, back - 1), value)
                value = jnp.where(at == near_lane + 1, turn(edge, back + 1), value)
            got.append(value)
        f = [f0_ref[i, rows, :] for i in range(19)]
        fs, fd = pairs_of(f)
        fm = moments(f[0], fs, fd)
        inverse = 1.0 / fm["total"]
        u = [one * inverse for one in fm["one"]]
        out, kept = adjoint_cell(got, u, f0_ref[19, rows, :], 1.0)
        for i in range(19):
            zout[i, rows, :] = out[i]
        zout[19, rows, :] = gradient_cell(kept, f[0], fs, fd, fm, u)
        zout[20, rows, :] = slab_grad[t]


def finish_kernel(whole_cells, mask_ref, zout, inner_ref, grad1_ref, inner_grad_ref, *refs):
    tiles_of_drag, (out_hbm, grad_hbm, drag_hbm, out_ref, grad_ref, drag_ref, sems) = (
        refs[:-7],
        refs[-7:],
    )
    nx, ny, nz = mask_ref.shape
    tiles = ny // 8
    lane = lax.broadcasted_iota(jnp.int32, (8, nz), 1)
    outer = (lane < 2) | (lane >= nz - 2)
    ends = (lane < 1) | (lane >= nz - 1)
    copies = []

    def send(src, dst):
        copy = pltpu.make_async_copy(src, dst, sems.at[len(copies)])
        copy.start()
        copies.append(copy)

    for low, high in OUT_GROUPS:
        for i in range(low, high):
            for x in range(nx):
                for t in range(tiles):
                    rows = slice(8 * t, 8 * t + 8)
                    out_ref[i, x, rows, :] = jnp.where(
                        outer,
                        turn(zout[i, rows, :], -2 - 4 * x),
                        inner_ref[i, x, rows, :],
                    )
        send(out_ref.at[low:high], out_hbm.at[low:high])
    for x in range(nx):
        for t in range(tiles):
            rows = slice(8 * t, 8 * t + 8)
            level1 = jnp.where(
                ends, turn(zout[20, rows, :], -2 - 4 * x), grad1_ref[x, rows, :]
            )
            edge = turn(zout[19, rows, :], -2 - 4 * x) + level1
            grad = jnp.where(outer, edge, inner_grad_ref[x, rows, :])
            grad_ref[x, rows, :] = jnp.where(mask_ref[x, rows, :] == 0, grad, 0.0)
    send(grad_ref, grad_hbm)
    total = 0.0
    for ref in tiles_of_drag:
        total = total + jnp.sum(ref[...], axis=0, keepdims=True)
    drag_ref[...] = jnp.sum(total, axis=1, keepdims=True) / whole_cells
    send(drag_ref, drag_hbm)
    for copy in copies:
        copy.wait()


def swaps(count):
    first = [(i, i ^ 1) for i in range(count)]
    second = [(i, (((i + 1) % count) ^ 1) - 1) for i in range(count)]
    second = [(i, j % count) for i, j in second]
    return first, second


VMEM = pl.BlockSpec(memory_space=pltpu.VMEM)
HBM = pl.BlockSpec(memory_space=pltpu.HBM)
PARAMS = pltpu.CompilerParams(vmem_limit_bytes=48 * 2**20)


def call(kernel, inputs, shapes, scratch=(), space=VMEM, micros=0.05, outs=None):
    if space is HBM:
        inputs = [pltpu.with_memory_space_constraint(x, pltpu.HBM) for x in inputs]
    return pl.pallas_call(
        kernel,
        out_shape=[jax.ShapeDtypeStruct(s, jnp.float32) for s in shapes],
        in_specs=[space] * len(inputs),
        out_specs=outs or [VMEM] * len(shapes),
        scratch_shapes=list(scratch),
        compiler_params=PARAMS,
        cost_estimate=pl.CostEstimate(
            flops=0, bytes_accessed=int(3.6e6 * micros), transcendentals=0
        ),
    )(*inputs)


def body(primal_states, adjoint_last, porosity, solid_mask):
    nx, ny, nz = porosity.shape
    gx, gy, gz = [lax.axis_size(axis) for axis in AXES]
    x_first, x_second = swaps(gx)
    y_first, y_second = swaps(gy)
    z_first, z_second = swaps(gz)
    tiles = ny // 8
    height = (tiles + 1) * 8
    f32 = jnp.float32

    def diagonal(message, x_pairs, y_pairs):
        pairs = [(a * gy + c, b * gy + d) for a, b in x_pairs for c, d in y_pairs]
        return lax.ppermute(message, ("gx", "gy"), pairs)

    rows_x = NSLOT * ny + 8
    rows_y = 2 * (y_rows(nx) + EDGE_ROWS) + 8
    rows_c = 2 * (CORNER + EDGE_ROWS)
    rows_z = 2 * ny + 8
    rides = (gx, gy, gz) == (4, 2, 4)
    ub, drag = call(
        state_kernel,
        (primal_states, porosity, solid_mask),
        [(4, nx, ny, nz), (8, nz)],
        [
            pltpu.VMEM((2, 19, nx, ny, nz), f32),
            pltpu.VMEM((nx, ny, nz), f32),
            pltpu.VMEM((nx, ny, nz), jnp.int32),
            pltpu.SemaphoreType.DMA((5,)),
        ],
        HBM,
    )
    cols, y, ya, yb = call(
        pack_y_kernel,
        (adjoint_last, ub, drag),
        [(4 * ny + 8, nz), (rows_y, nz), (rows_c, nz), (rows_c, nz)],
        [pltpu.VMEM((NSLOT, 2 * nx, nz), f32)],
        micros=4,
    )
    (xa,) = call(pack_x_kernel, (adjoint_last, ub, drag), [(rows_x, nz)])
    (xb,) = call(pack_partial_kernel, (adjoint_last, ub), [(14 * ny + 8, nz)])
    xc = lax.ppermute(cols, "gx", x_second)
    xa = lax.ppermute(xa, "gx", x_first)
    if gy == 2:
        y = lax.ppermute(y, "gy", y_first)
        yb = diagonal(yb, x_second, y_first)
        ya = diagonal(ya, x_first, y_first)
    else:

        def both(message, block, send):
            parts = [message[:block], message[block : 2 * block], message[2 * block :]]
            return jnp.concatenate(
                [send(parts[0], y_first), send(parts[1], y_second), parts[2]]
            )

        block = y_rows(nx) + EDGE_ROWS
        y = both(y, block, lambda m, pairs: lax.ppermute(m, "gy", pairs))
        block = CORNER + EDGE_ROWS
        yb = both(yb, block, lambda m, pairs: diagonal(m, x_second, pairs))
        ya = both(ya, block, lambda m, pairs: diagonal(m, x_first, pairs))
    xb, yb = lax.optimization_barrier((xb, yb))
    xb = lax.ppermute(xb, "gx", x_second)

    (columns,) = call(pack_columns_kernel, (cols, xa, xc), [(4 * ny, nz)])
    zown, za, zb, drag_xy = call(
        pack_z_kernel,
        (columns, cols, xa, xc, y, ya, yb),
        [(4 * height, nz), (rows_z, nz), (rows_z, nz), (1, nz)],
        [pltpu.VMEM((4, ny + 32, nz), f32)],
    )
    if rides:
        second = jnp.sum(xc[4 * ny :], axis=0, keepdims=True)
        second = second + yb[DRAG_ROW : DRAG_ROW + 1]
        drag_xy = drag_xy + lax.ppermute(second, "gx", x_first)
        za = za.at[2 * ny + 3 : 2 * ny + 4].set(drag_xy)
        zb = zb.at[2 * ny + 3 : 2 * ny + 4].set(drag_xy)
    zb = lax.ppermute(zb, "gz", z_second)
    za = lax.ppermute(za, "gz", z_first)
    inner, grad1, inner_grad, pack, f0, f1 = call(
        inner_kernel,
        (primal_states, adjoint_last, ub, xa, xb, y, ya, yb),
        [
            (19, nx, ny, nz),
            (nx, ny, nz),
            (nx, ny, nz),
            (19, ny, nz),
            (20, ny, nz),
            (19, ny, nz),
        ],
        [
            pltpu.VMEM((NSLOT, nx + 4, ny + 32, nz), f32),
            pltpu.VMEM((19, nx + 2, height + 8, nz), f32),
        ],
        micros=4,
    )
    if rides:
        zhalf = lax.ppermute(drag_xy, "gz", [(i, i ^ 2) for i in range(gz)])
        drags = (drag_xy, zhalf)
    else:
        drags = (lax.psum(drag, AXES),)

    zout, tails = call(
        edge_kernel,
        (zown, za, zb, pack, f0, f1),
        [(21, ny, nz), (1, nz)],
        [pltpu.VMEM((19, height + 8, nz), f32)],
    )
    if rides:
        drags += (tails,)
    whole_cells = float(nx * ny * nz * gx * gy * gz)
    first, gradient, drag = call(
        functools.partial(finish_kernel, whole_cells),
        (solid_mask, zout, inner, grad1, inner_grad) + drags,
        [(19, nx, ny, nz), (nx, ny, nz), (1, 1)],
        [
            pltpu.VMEM((19, nx, ny, nz), f32),
            pltpu.VMEM((nx, ny, nz), f32),
            pltpu.VMEM((1, 1), f32),
            pltpu.SemaphoreType.DMA((len(OUT_GROUPS) + 2,)),
        ],
        outs=[HBM, HBM, HBM],
    )
    return (first, gradient, drag.reshape(()))


def solution(mesh):
    return jax.shard_map(
        body,
        mesh=mesh,
        in_specs=(
            P(None, None, "gx", "gy", "gz"),
            P(None, "gx", "gy", "gz"),
            P("gx", "gy", "gz"),
            P("gx", "gy", "gz"),
        ),
        out_specs=(P(None, "gx", "gy", "gz"), P("gx", "gy", "gz"), P()),
        check_vma=False,
    )
```

```python
import functools

import jax
import jax.numpy as jnp
import numpy as np
from jax import lax
from jax.experimental import pallas as pl
from jax.experimental.pallas import tpu as pltpu
from jax.sharding import PartitionSpec as P

VEL = (
    (0, 0, 0),
    (1, 0, 0),
    (-1, 0, 0),
    (0, 1, 0),
    (0, -1, 0),
    (0, 0, 1),
    (0, 0, -1),
    (1, 1, 0),
    (-1, -1, 0),
    (1, -1, 0),
    (-1, 1, 0),
    (1, 0, 1),
    (-1, 0, -1),
    (1, 0, -1),
    (-1, 0, 1),
    (0, 1, 1),
    (0, -1, -1),
    (0, 1, -1),
    (0, -1, 1),
)
PAIRS = tuple((i, i + 1) for i in range(1, 19, 2))
AXES = ("gx", "gy", "gz")
UB = (19, 20, 21, 22)


def near(axis, sign):
    return tuple(i for i in range(19) if VEL[i][axis] * sign >= 0) + UB


def far(axis, sign):
    return tuple(i for i in range(19) if VEL[i][axis] == sign)


NSLOT = 23
CORNER = 16
DRAG_ROW = 14
EDGE_ROWS = 8


def y_rows(nx):
    return 14 * nx + 8


ZGROUPS = (
    tuple(i for i in range(19) if VEL[i][2] == -1),
    tuple(i for i in range(19) if VEL[i][2] == 1),
    tuple(i for i in range(19) if VEL[i][2] == 0)[:8],
    tuple(i for i in range(19) if VEL[i][2] == 0)[8:] + UB,
)
ZSLOT = {q: (g, k) for g, group in enumerate(ZGROUPS) for k, q in enumerate(group)}


def pairs_of(values):
    s = [values[a] + values[b] for a, b in PAIRS]
    d = [values[a] - values[b] for a, b in PAIRS]
    return s, d


def moments(v0, s, d):
    sx, sy, sz, sp, sq, sr, ss, st, su = s
    dx, dy, dz, dp, dq, dr, ds, dt, du = d
    ex = sp + sq
    ez = sr + ss
    ey = st + su
    faces = sx + sy + sz
    edges = ex + ez + ey
    exx = ex + ez
    eyy = ex + ey
    ezz = ez + ey
    fx = (dp + dq) + (dr + ds)
    fy = (dp - dq) + (dt + du)
    fz = (dr - ds) + (dt - du)
    return dict(
        rest=v0,
        faces=faces,
        edges=edges,
        total=v0 + faces + edges,
        face1=(dx, dy, dz),
        edge1=(fx, fy, fz),
        one=(dx + fx, dy + fy, dz + fz),
        face2=(sx, sy, sz),
        edge2=(exx, eyy, ezz),
        two=(sx + exx, sy + eyy, sz + ezz),
        cross=(sp - sq, sr - ss, st - su),
    )


def adjoint_cell(g, u, b, drive):
    s, d = pairs_of(g)
    m = moments(g[0], s, d)
    total = m["total"]
    trace = m["faces"] + 2.0 * m["edges"] - (30.0 / 19.0) * total
    p0 = (-1.2 / 19.0) * total - (2.0 / 21.0) * trace
    q = [
        (0.4 / 6.0) * (two - (10.0 / 19.0) * total) + (0.8 / 21.0) * trace
        for two in m["two"]
    ]
    qsum = q[0] + q[1] + q[2]
    qab = [0.1 * c for c in m["cross"]]
    p1 = [-0.12 * one for one in m["one"]]
    h0 = (
        0.4 * m["rest"]
        + (1.2 / 18.0) * m["faces"]
        + (1.2 / 36.0) * m["edges"]
        + p0
        + (1.0 / 3.0) * qsum
    )
    h1 = [
        (1.2 / 18.0) * f + (1.2 / 36.0) * e + (1.0 / 3.0) * p
        for f, e, p in zip(m["face1"], m["edge1"], p1)
    ]
    base = (1.0 / 3.0) * p0 + (1.0 / 9.0) * qsum
    haa = [
        (1.2 / 18.0) * f + (1.2 / 36.0) * e + (2.0 / 9.0) * qa + base
        for f, e, qa in zip(m["face2"], m["edge2"], q)
    ]
    hxy, hxz, hyz = [(2.0 / 45.0) * c for c in m["cross"]]
    ux, uy, uz = u
    v = (
        haa[0] * ux + hxy * uy + hxz * uz,
        hxy * ux + haa[1] * uy + hyz * uz,
        hxz * ux + hyz * uy + haa[2] * uz,
    )
    uv = ux * v[0] + uy * v[1] + uz * v[2]
    uu = ux * ux + uy * uy + uz * uz
    uuh = 1.5 * uu * h0
    a = h0 + uuh - 4.5 * uv
    nb = 1.0 - b
    e0 = nb * (a - p0)
    nq = [nb * x for x in q]
    nxy, nxz, nyz = [nb * x for x in qab]
    o = [
        nb * (3.0 * h1[k] + 9.0 * v[k] - 3.0 * u[k] * h0 - p1[k]) for k in range(3)
    ]
    o[0] = o[0] + b * drive
    alpha = -0.2 * nb
    half_s = 0.5 * (alpha + b)
    half_d = 0.5 * (alpha - b)
    exy = e0 - nq[0] - nq[1]
    exz = e0 - nq[0] - nq[2]
    eyz = e0 - nq[1] - nq[2]
    even = (
        e0 - nq[0],
        e0 - nq[1],
        e0 - nq[2],
        exy - nxy,
        exy + nxy,
        exz - nxz,
        exz + nxz,
        eyz - nyz,
        eyz + nyz,
    )
    odd = (
        o[0],
        o[1],
        o[2],
        o[0] + o[1],
        o[0] - o[1],
        o[0] + o[2],
        o[0] - o[2],
        o[1] + o[2],
        o[1] - o[2],
    )
    out = [(alpha + b) * g[0] + e0]
    for k in range(9):
        even_k = half_s * s[k] + even[k]
        odd_k = half_d * d[k] + odd[k]
        out.append(even_k + odd_k)
        out.append(even_k - odd_k)
    kept = dict(
        s=s, d=d, g0=g[0], p0=p0, p1=p1, q=q, qab=qab, h0=h0, h1=h1, uv=uv, uuh=uuh
    )
    return out, kept


def gradient_cell(kept, f0, fs, fd, fm, u):
    rho = fm["total"]
    even = fs[0] * kept["s"][0]
    odd = fd[0] * kept["d"][0]
    for k in range(1, 9):
        even = even + fs[k] * kept["s"][k]
        odd = odd + fd[k] * kept["d"][k]
    hf = kept["p0"] * rho
    for k in range(3):
        hf = hf + kept["p1"][k] * fm["one"][k] + kept["q"][k] * fm["two"][k]
        hf = hf + kept["qab"][k] * fm["cross"][k]
    uh1 = u[0] * kept["h1"][0] + u[1] * kept["h1"][1] + u[2] * kept["h1"][2]
    hfeq = rho * (kept["h0"] - kept["uuh"] + 3.0 * uh1 + 4.5 * kept["uv"])
    pairs = 1.2 * f0 * kept["g0"] + 0.6 * even - 0.4 * odd
    return pairs + hf - hfeq + fm["one"][0]


def state_of(ref, index):
    f = [ref[(index[0], i) + index[1:]] for i in range(19)]
    s, d = pairs_of(f)
    m = moments(f[0], s, d)
    inverse = 1.0 / m["total"]
    u = [one * inverse for one in m["one"]]
    return f[0], s, d, m, u


def corner_rows(sx, sy):
    both = [i for i in far(0, sx) if VEL[i][1] == sy]
    along_y = [i for i in far(1, sy) if VEL[i][0] == 0]
    along_x = [i for i in far(0, sx) if VEL[i][1] == 0]
    rows = [(i, 0, 0) for i in both + along_y + along_x]
    return rows + [(i, 1, 0) for i in both] + [(i, 0, 1) for i in both]


def corner_zeros(sx, sy):
    rows = [(i, 0, 0) for i in range(19) if VEL[i][0] == 0 and VEL[i][1] == 0]
    rows += [(i, 1, 0) for i in far(0, sx) if VEL[i][1] == 0]
    rows += [(i, 0, 1) for i in far(1, sy) if VEL[i][0] == 0]
    return rows + [(i, 1, 1) for i in far(0, sx) if VEL[i][1] == sy]


CORNERS = ((1, 1), (1, -1), (-1, 1), (-1, -1))


def parity(axis):
    return lax.axis_index(axis) % 2


def cell_rows(adj_ref, ub_ref, q, x, rows):
    return adj_ref[q, x, rows, :] if q < 19 else ub_ref[q - 19, x, rows, :]


def state_kernel(
    states_hbm,
    por_hbm,
    mask_hbm,
    ub_ref,
    drag_ref,
    states_ref,
    por_ref,
    mask_ref,
    sems,
):
    nx, ny, nz = por_ref.shape
    tiles = ny // 8
    copies = [
        pltpu.make_async_copy(src, dst, sems.at[k])
        for k, (src, dst) in enumerate(
            (
                (states_hbm.at[1], states_ref.at[1]),
                (por_hbm, por_ref),
                (mask_hbm, mask_ref),
                (states_hbm.at[0, 1:3], states_ref.at[0, 1:3]),
                (states_hbm.at[0, 7:15], states_ref.at[0, 7:15]),
            )
        )
    ]
    for copy in copies:
        copy.start()
    for copy in copies[:3]:
        copy.wait()

    def cells(x, carry):
        for t in range(tiles):
            rows = slice(8 * t, 8 * t + 8)
            blocking = jnp.where(mask_ref[x, rows, :] == 0, por_ref[x, rows, :], 1.0)
            f0, s, d, m, u = state_of(states_ref, (1, x, rows))
            for k in range(3):
                ub_ref[k, x, rows, :] = u[k]
            ub_ref[3, x, rows, :] = blocking
            carry = carry + blocking * m["one"][0]
        return carry

    drag = lax.fori_loop(0, nx, cells, jnp.zeros((8, nz), jnp.float32))
    for copy in copies[3:]:
        copy.wait()

    def flux_cells(x, carry):
        for t in range(tiles):
            rows = slice(8 * t, 8 * t + 8)
            flux = 0.0
            for a, b in PAIRS:
                if VEL[a][0]:
                    flux = flux + (
                        states_ref[0, a, x, rows, :] - states_ref[0, b, x, rows, :]
                    )
            carry = carry + ub_ref[3, x, rows, :] * flux
        return carry

    drag = lax.fori_loop(0, nx, flux_cells, drag)
    drag_ref[...] = drag


def pack_x_kernel(adj_ref, ub_ref, drag_ref, out_ref):
    nx, ny = adj_ref.shape[1:3]
    out_ref[NSLOT * ny :] = drag_ref[...]

    def fill(sign):
        for names, offset, x in (
            (near(0, sign), 0, 0 if sign > 0 else nx - 1),
            (far(0, sign), 18, 1 if sign > 0 else nx - 2),
        ):
            for k, q in enumerate(names):
                k += offset
                out_ref[k * ny : (k + 1) * ny] = cell_rows(
                    adj_ref, ub_ref, q, x, slice(0, ny)
                )

    pl.when(parity("gx") == 0)(functools.partial(fill, -1))
    pl.when(parity("gx") == 1)(functools.partial(fill, 1))


def y_edge_entries(sign, nx):
    rows = []
    for side in (1, -1):
        x = 0 if side > 0 else nx - 1
        rows += [(i, 0, x) for i in far(0, side) if VEL[i][1] == 0]
        rows += [(i, 1, x) for i in far(0, side) if VEL[i][1] == sign]
    return rows


def edge_entries(sign):
    rows = []
    for side in (1, -1):
        rows += [(i, 0, side) for i in far(1, side) if VEL[i][0] == 0]
        rows += [(i, 1, side) for i in far(1, side) if VEL[i][0] == sign]
    return rows


def pack_partial_kernel(adj_ref, ub_ref, out_ref):
    nx, ny, nz = adj_ref.shape[1:]
    tiles = ny // 8
    sub = lax.broadcasted_iota(jnp.int32, (8, nz), 0)

    def fill(sign):
        here, inside = (0, 1) if sign > 0 else (nx - 1, nx - 2)
        names = far(0, sign)
        for t in range(tiles):
            rows = slice(8 * t, 8 * t + 8)
            got = []
            for i in range(19):
                cx, cy, cz = VEL[i]
                if cx * sign < 0:
                    got.append(jnp.zeros((8, nz), jnp.float32))
                    continue
                x = inside if cx else here
                if t == 0 and cy < 0:
                    value = pltpu.roll(adj_ref[i, x, rows, :], 1, 0)
                    value = jnp.where(sub == 0, 0.0, value)
                elif t == tiles - 1 and cy > 0:
                    value = pltpu.roll(adj_ref[i, x, rows, :], 7, 0)
                    value = jnp.where(sub == 7, 0.0, value)
                else:
                    value = adj_ref[i, x, 8 * t + cy : 8 * t + 8 + cy, :]
                got.append(z_shifted(value, cz))
            u = [ub_ref[k, here, rows, :] for k in range(3)]
            out, _ = adjoint_cell(got, u, ub_ref[3, here, rows, :], 0.0)
            for k, i in enumerate(names):
                out_ref[k * ny + 8 * t : k * ny + 8 * t + 8] = out[i]
        for k, q in enumerate(names + UB):
            k += 5
            out_ref[k * ny : (k + 1) * ny] = cell_rows(
                adj_ref, ub_ref, q, here, slice(0, ny)
            )
        for k, (i, depth, side) in enumerate(edge_entries(sign)):
            y = 0 if side > 0 else ny - 1
            row = 14 * ny + k
            out_ref[row : row + 1] = adj_ref[i, inside if depth else here, y : y + 1, :]

    pl.when(parity("gx") == 0)(functools.partial(fill, 1))
    pl.when(parity("gx") == 1)(functools.partial(fill, -1))


def column_pair(acc, value, pair, q, k, plane):
    start = 32 * (k // 2) + 4 * plane + 2 * (k % 2)
    cz = VEL[q][2] if q < 19 else 0
    return jnp.where(pair == start // 2, turn(value, start + 1 - cz), acc)


def pack_y_kernel(
    adj_ref, ub_ref, drag_ref, cols_ref, y_ref, ya_ref, yb_ref, read_ref
):
    nx, ny, nz = adj_ref.shape[1:]
    pair = lax.broadcasted_iota(jnp.int32, (8, nz), 1) // 2
    for g, group in enumerate(ZGROUPS):
        for t in range(ny // 8):
            acc = jnp.zeros((8, nz), jnp.float32)
            for k, q in enumerate(group):
                for x in range(nx):
                    value = cell_rows(adj_ref, ub_ref, q, x, slice(8 * t, 8 * t + 8))
                    acc = column_pair(acc, value, pair, q, k, x + 2)
            row = g * ny + 8 * t
            cols_ref[row : row + 8] = acc
    y_block = y_rows(nx) + EDGE_ROWS
    corner_block = CORNER + EDGE_ROWS

    def fill_edges(place, sign):
        for g in range(4):
            for d in range(2):
                y = d if sign > 0 else ny - 1 - d
                line = cols_ref[g * ny + y : g * ny + y + 1]
                row = place * y_block + y_rows(nx) + 2 * g + d
                y_ref[row : row + 1] = line
                row = place * corner_block + CORNER + 2 * g + d
                ya_ref[row : row + 1] = line
                yb_ref[row : row + 1] = line

    faces = ((1, 0, 1), (-1, ny - 1, ny - 2))
    for i in range(19):
        cx, cy, _ = VEL[i]
        read_ref[i] = jnp.zeros((2 * nx, nz), jnp.float32)
        for n, (sign, here, inside) in enumerate(faces):
            for x in range(max(0, -cx), min(nx, nx - cx)):
                if cy * sign >= 0:
                    y = inside if cy else here
                    read_ref[i, n * nx + x : n * nx + x + 1, :] = adj_ref[
                        i, x + cx, y : y + 1, :
                    ]
    for k in range(4):
        for n, (sign, here, inside) in enumerate(faces):
            for x in range(nx):
                read_ref[19 + k, n * nx + x : n * nx + x + 1, :] = ub_ref[
                    k, x, here : here + 1, :
                ]
    got = [z_shifted(read_ref[i], VEL[i][2]) for i in range(19)]
    sums, _ = adjoint_cell(
        got, [read_ref[19 + k] for k in range(3)], read_ref[22], 0.0
    )

    def fill_y(place, sign):
        n = 0 if sign > 0 else 1
        _, here, inside = faces[n]
        first = place * y_block
        for k, i in enumerate(far(1, sign)):
            row = first + k * nx
            y_ref[row : row + nx] = sums[i][n * nx : (n + 1) * nx]
        for k, q in enumerate(far(1, sign) + UB):
            for x in range(nx):
                row = first + (5 + k) * nx + x
                y_ref[row : row + 1] = cell_rows(
                    adj_ref, ub_ref, q, x, slice(here, here + 1)
                )
        for k, (i, depth, x) in enumerate(y_edge_entries(sign, nx)):
            y = inside if depth else here
            row = first + 14 * nx + k
            y_ref[row : row + 1] = adj_ref[i, x, y : y + 1, :]

    for i in range(19):
        read_ref[i] = jnp.zeros((2 * nx, nz), jnp.float32)
    for n, (sx, sy) in enumerate(CORNERS):
        xs = (0, 1) if sx > 0 else (nx - 1, nx - 2)
        ys = (0, 1) if sy > 0 else (ny - 1, ny - 2)
        for i, dx, dy in corner_zeros(sx, sy):
            read_ref[i, n : n + 1, :] = adj_ref[i, xs[dx], ys[dy] : ys[dy] + 1, :]
        for k in range(4):
            read_ref[19 + k, n : n + 1, :] = ub_ref[k, xs[0], ys[0] : ys[0] + 1, :]
    got = [z_shifted(read_ref[i], VEL[i][2]) for i in range(19)]
    corner_sums, _ = adjoint_cell(
        got, [read_ref[19 + k] for k in range(3)], read_ref[22], 0.0
    )
    line = jnp.sum(drag_ref[...], axis=0, keepdims=True)

    def fill_corner(out_ref, place, sx, sy):
        xs = (0, 1) if sx > 0 else (nx - 1, nx - 2)
        ys = (0, 1) if sy > 0 else (ny - 1, ny - 2)
        n = CORNERS.index((sx, sy))
        first = place * corner_block
        rows = corner_rows(sx, sy)
        out_ref[first : first + 1] = corner_sums[rows[0][0]][n : n + 1]
        for k in range(4):
            out_ref[first + 1 + k : first + 2 + k] = ub_ref[
                k, xs[0], ys[0] : ys[0] + 1, :
            ]
        for k, (i, dx, dy) in enumerate(rows):
            row = first + 5 + k
            out_ref[row : row + 1] = adj_ref[i, xs[dx], ys[dy] : ys[dy] + 1, :]
        out_ref[first + DRAG_ROW : first + DRAG_ROW + 1] = line
        out_ref[first + DRAG_ROW + 1 : first + CORNER] = jnp.zeros((1, nz), jnp.float32)

    drag = drag_ref[...]
    cols_ref[4 * ny :] = drag
    y_ref[2 * y_block :] = drag
    for py in (0, 1):

        @pl.when(parity("gy") == py)
        def _():
            s0 = 1 if py else -1
            fill_y(0, s0)
            fill_y(1, -s0)
            fill_edges(0, s0)
            fill_edges(1, -s0)

    for px in (0, 1):
        for py in (0, 1):

            @pl.when((parity("gx") == px) & (parity("gy") == py))
            def _():
                sa = 1 if px else -1
                s0 = 1 if py else -1
                for out_ref, sx in ((ya_ref, sa), (yb_ref, -sa)):
                    fill_corner(out_ref, 0, sx, s0)
                    fill_corner(out_ref, 1, sx, -s0)


def pack_columns_kernel(cols_ref, xa_ref, xc_ref, out_ref):
    ny = (cols_ref.shape[0] - 8) // 4
    nz = cols_ref.shape[1]
    tiles = ny // 8
    lane = lax.broadcasted_iota(jnp.int32, (8, nz), 1)
    plane = (lane % 32) // 4
    pair = lane // 2

    def fill_main(sign):
        halo = {}
        for names, offset, p in (
            (near(0, sign), 0, 6 if sign > 0 else 1),
            (far(0, sign), 18, 7 if sign > 0 else 0),
        ):
            for k, q in enumerate(names):
                halo.setdefault(q, []).append((k + offset, p))
        for g, group in enumerate(ZGROUPS):
            for t in range(tiles):
                rows = slice(g * ny + 8 * t, g * ny + 8 * t + 8)
                acc = jnp.where(
                    plane < 2 if sign > 0 else plane > 5,
                    turn(xc_ref[rows], -16 * sign),
                    cols_ref[rows],
                )
                for k, q in enumerate(group):
                    for at, p in halo.get(q, ()):
                        row = at * ny + 8 * t
                        acc = column_pair(acc, xa_ref[row : row + 8], pair, q, k, p)
                    out_ref[rows] = acc

    @pl.when(parity("gx") == 0)
    def _():
        fill_main(1)

    @pl.when(parity("gx") == 1)
    def _():
        fill_main(-1)


def pack_z_kernel(
    main_ref,
    cols_ref,
    xa_ref,
    xc_ref,
    y_ref,
    ya_ref,
    yb_ref,
    zown_ref,
    za_ref,
    zb_ref,
    drag_ref,
    ext,
):
    ny = (cols_ref.shape[0] - 8) // 4
    nz = cols_ref.shape[1]
    tiles = ny // 8
    base = 16
    even_x = parity("gx") == 0
    even_y = parity("gy") == 0
    lane = lax.broadcasted_iota(jnp.int32, (8, nz), 1)
    sub = lax.broadcasted_iota(jnp.int32, (8, nz), 0)
    plane = (lane % 32) // 4
    slot = 2 * (lane // 32) + (lane % 4) // 2

    def along_x(own, va, vb):
        low = turn(jnp.where(even_x, vb, va), -16)
        high = turn(jnp.where(even_x, va, vb), 16)
        return jnp.where(plane < 2, low, jnp.where(plane > 5, high, own))

    for g in range(4):
        for t in range(tiles):
            row = g * ny + 8 * t
            ext[g, base + 8 * t : base + 8 * t + 8, :] = main_ref[row : row + 8]

    y_block = (y_ref.shape[0] - 8) // 2
    corner_block = CORNER + EDGE_ROWS

    def edges(ref, block, place):
        return ref[(place + 1) * block - EDGE_ROWS : (place + 1) * block]

    first, second = [
        along_x(
            edges(y_ref, y_block, place),
            edges(ya_ref, corner_block, place),
            edges(yb_ref, corner_block, place),
        )
        for place in range(2)
    ]
    high = jnp.where(even_y, first, second)
    low = jnp.where(even_y, second, first)
    for g in range(4):
        for d in range(2):
            row = 2 * g + d
            ext[g, base + ny + d : base + ny + d + 1, :] = high[row : row + 1]
            ext[g, base - 1 - d : base - d, :] = low[row : row + 1]

    packed = []
    for g, group in enumerate(ZGROUPS):
        moves = {}
        for k, q in enumerate(group):
            cx, cy, _ = VEL[q] if q < 19 else (0, 0, 0)
            moves.setdefault((cx, cy), []).append(k)
        acc = [jnp.zeros((8, nz), jnp.float32) for t in range(tiles + 1)]
        for (cx, cy), slots in moves.items():
            mask = slot == slots[0]
            for k in slots[1:]:
                mask = mask | (slot == k)
            for t in range(tiles + 1):
                if t < tiles:
                    row = base + 8 * t + cy
                    value = ext[g, row : row + 8, :]
                else:
                    above = base + ny + cy
                    below = base - 8 + cy
                    value = jnp.where(
                        sub < 4, ext[g, above : above + 8, :], ext[g, below : below + 8, :]
                    )
                acc[t] = jnp.where(mask, turn(value, -4 * cx), acc[t])
        packed.append(acc)
        for t in range(tiles + 1):
            row = (g * (tiles + 1) + t) * 8
            zown_ref[row : row + 8, :] = acc[t]
    up_first = parity("gz") == 0
    even_lane = lane % 2 == 0
    for t in range(tiles + 1):
        two, three = packed[2][t], packed[3][t]
        up = (packed[0][t], jnp.where(even_lane, two, pltpu.roll(three, 1, 1)))
        down = (packed[1][t], jnp.where(even_lane, pltpu.roll(two, nz - 1, 1), three))
        if t == tiles:
            up, down = [
                (
                    jnp.where(
                        (sub == 0) | (sub == 7),
                        side[0],
                        jnp.where(
                            sub < 4, pltpu.roll(side[1], 1, 0), pltpu.roll(side[1], 7, 0)
                        ),
                    ),
                )
                for side in (up, down)
            ]
        for g in range(len(up)):
            row = (g * tiles + t) * 8 if t < tiles else 2 * tiles * 8
            za_ref[row : row + 8, :] = jnp.where(up_first, up[g], down[g])
            zb_ref[row : row + 8, :] = jnp.where(up_first, down[g], up[g])
    drag = (cols_ref[4 * ny :] + y_ref[2 * y_block :]) + (
        xa_ref[xa_ref.shape[0] - 8 :] + xc_ref[4 * ny :]
    )
    row = slice(DRAG_ROW, DRAG_ROW + 1)
    drag_ref[...] = jnp.sum(drag, axis=0, keepdims=True) + (ya_ref[row] + yb_ref[row])


OUT_GROUPS = ((0, 6), (6, 12), (12, 17), (17, 19))


def turn(value, shift):
    nz = value.shape[1]
    return pltpu.roll(value, shift % nz, 1) if shift % nz else value


def z_shifted(value, cz):
    return turn(value, -cz) if cz else value


def inner_kernel(
    states_ref,
    adj_ref,
    ub_ref,
    xa_ref,
    xb_ref,
    y_ref,
    ya_ref,
    yb_ref,
    out_ref,
    grad1_ref,
    grad_ref,
    pack_ref,
    f0_ref,
    f1_ref,
    ext,
    mid,
):
    nx, ny, nz = grad_ref.shape
    tiles = ny // 8
    lane = lax.broadcasted_iota(jnp.int32, (8, nz), 1)
    slot = lane // 4
    sub = lax.broadcasted_iota(jnp.int32, (8, nz), 0)
    even_x = parity("gx") == 0
    even_y = parity("gy") == 0
    base = 16

    for q in range(NSLOT):
        for x in range(nx):
            ext[q, x + 2, base : base + ny, :] = (
                adj_ref[q, x] if q < 19 else ub_ref[q - 19, x]
            )
    planes = {1: (nx + 2, nx + 3), -1: (1, 0)}
    lines = {1: (base + ny, base + ny + 1), -1: (base - 1, base - 2)}

    def fill_whole(sign):
        for names, depth, offset in ((near(0, sign), 0, 0), (far(0, sign), 1, 18)):
            for k, q in enumerate(names):
                rows = slice((k + offset) * ny, (k + offset + 1) * ny)
                ext[q, planes[sign][depth], base : base + ny, :] = xa_ref[rows]

    def fill_partial(sign):
        one, two = planes[sign]
        for k, q in enumerate(far(0, sign) + UB):
            ext[q, one, base : base + ny, :] = xb_ref[(5 + k) * ny : (6 + k) * ny]
        nothing = jnp.zeros((ny, nz), jnp.float32)
        for q in range(19):
            if VEL[q][0] == 0:
                ext[q, one, base : base + ny, :] = nothing
            elif VEL[q][0] == sign:
                ext[q, two, base : base + ny, :] = nothing
        for k, (q, depth, side) in enumerate(edge_entries(sign)):
            line = base if side > 0 else base + ny - 1
            row = 14 * ny + k
            ext[q, planes[sign][depth], line : line + 1, :] = xb_ref[row : row + 1]

    @pl.when(parity("gx") == 0)
    def _():
        fill_whole(1)
        fill_partial(-1)

    @pl.when(parity("gx") == 1)
    def _():
        fill_whole(-1)
        fill_partial(1)

    sums = {}
    corner_sums = {}
    for sign in (1, -1):
        block = y_rows(nx) + EDGE_ROWS
        first, second = (0, block) if sign > 0 else (block, 0)
        one, two = lines[sign]
        nothing = jnp.zeros((1, nz), jnp.float32)
        for q in range(19):
            for x in range(nx):
                if VEL[q][1] == 0:
                    ext[q, x + 2, one : one + 1, :] = nothing
                elif VEL[q][1] == sign:
                    ext[q, x + 2, two : two + 1, :] = nothing
        got = jnp.where(
            even_y,
            y_ref[first : first + y_rows(nx)],
            y_ref[second : second + y_rows(nx)],
        )
        sums[sign] = got
        for k, q in enumerate(far(1, sign) + UB):
            for x in range(nx):
                row = (5 + k) * nx + x
                ext[q, x + 2, one : one + 1, :] = got[row : row + 1]
        for k, (q, depth, x) in enumerate(y_edge_entries(sign, nx)):
            line = lines[sign][depth]
            row = 14 * nx + k
            ext[q, x + 2, line : line + 1, :] = got[row : row + 1]
        for sx in (1, -1):
            xs = (ya_ref, yb_ref) if sx > 0 else (yb_ref, ya_ref)
            block = CORNER + EDGE_ROWS
            ys = (0, block) if sign > 0 else (block, 0)
            low, high = [
                jnp.where(even_x, xs[0][r : r + CORNER], xs[1][r : r + CORNER])
                for r in ys
            ]
            got = jnp.where(even_y, low, high)
            corner_sums[sx, sign] = got[0:1]
            for k in range(4):
                line = lines[sign][0]
                ext[19 + k, planes[sx][0], line : line + 1, :] = got[1 + k : 2 + k]
            for q, dx, dy in corner_zeros(sx, sign):
                line = lines[sign][dy]
                ext[q, planes[sx][dx], line : line + 1, :] = nothing
            for k, (q, dx, dy) in enumerate(corner_rows(sx, sign)):
                line = lines[sign][dy]
                ext[q, planes[sx][dx], line : line + 1, :] = got[5 + k : 6 + k]

    def near_cells(q, plane, t, cy):
        if t < tiles:
            row = base + 8 * t + cy
            return ext[q, plane, row : row + 8, :]
        above = base + ny + cy
        below = base - 8 + cy
        return jnp.where(
            sub < 4, ext[q, plane, above : above + 8, :], ext[q, plane, below : below + 8, :]
        )

    def first_level(p, t, kinds, partial=None):
        got = []
        for i in range(19):
            cx, cy, cz = VEL[i]
            got.append(z_shifted(near_cells(i, p + 1 + cx, t, cy), cz))
        ub = [near_cells(19 + k, p + 1, t, 0) for k in range(4)]
        out, kept = adjoint_cell(got, ub[:3], ub[3], 1.0)
        if t == tiles and 1 <= p <= nx:
            for sign, row in ((1, 0), (-1, 7)):
                for k, i in enumerate(far(1, sign)):
                    line = k * nx + p - 1
                    term = sums[sign][line : line + 1]
                    out[i] = out[i] + jnp.where(sub == row, term, 0.0)
        elif t == tiles:
            sx = -1 if p == 0 else 1
            for sign, row in ((1, 0), (-1, 7)):
                i = corner_rows(sx, sign)[0][0]
                out[i] = out[i] + jnp.where(sub == row, corner_sums[sx, sign], 0.0)
        if partial is not None:
            for k, i in enumerate(kinds):
                row = k * ny + 8 * t
                out[i] = out[i] + jnp.where(partial, xb_ref[row : row + 8], 0.0)
        for i in kinds:
            if t < tiles:
                mid[i, p, t * 8 + 8 : t * 8 + 16, :] = out[i]
            elif VEL[i][1] > 0:
                mid[i, p, t * 8 + 8 : t * 8 + 16, :] = out[i]
            elif VEL[i][1] < 0:
                mid[i, p, 0:8, :] = out[i]
        return kept, ub[:3]

    def inside(x, carry):
        for t in range(tiles):
            kept, u = first_level(x + 1, t, range(19))
            rows = slice(t * 8, t * 8 + 8)
            f0, fs, fd, fm, _ = state_of(states_ref, (1, x, rows))
            grad1_ref[x, rows, :] = gradient_cell(kept, f0, fs, fd, fm, u)
        return carry

    lax.fori_loop(0, nx, inside, 0)
    for t in range(tiles):
        first_level(0, t, far(0, -1), even_x)
        first_level(nx + 1, t, far(0, 1), jnp.logical_not(even_x))

    for p in range(nx + 2):
        first_level(p, tiles, far(1, -1) + far(1, 1))

    def second_level(x, carry):
        for t in range(tiles):
            rows = slice(t * 8, t * 8 + 8)
            got = []
            for i in range(19):
                cx, cy, cz = VEL[i]
                low = 8 + 8 * t + cy
                value = z_shifted(mid[i, x + 1 + cx, low : low + 8, :], cz)
                got.append(value)
                pack_ref[i, rows, :] = jnp.where(
                    slot == x, pltpu.roll(value, 4 * x + 2, 1), pack_ref[i, rows, :]
                )
            f0, fs, fd, fm, u = state_of(states_ref, (0, x, rows))
            b = ub_ref[3, x, rows, :]
            out, kept = adjoint_cell(got, u, b, 1.0)
            for i in range(19):
                out_ref[i, x, rows, :] = out[i]
            grad_ref[x, rows, :] = grad1_ref[x, rows, :] + gradient_cell(
                kept, f0, fs, fd, fm, u
            )
        return carry

    lax.fori_loop(0, nx, second_level, 0)

    def tile(t, carry):
        rows = pl.ds(pl.multiple_of(t * 8, 8), 8)
        for i in range(20):
            for out_ref, level, first in ((f0_ref, 0, 0), (f1_ref, 1, 2)):
                if i == 19 and level == 1:
                    continue
                acc = jnp.zeros((8, nz), jnp.float32)
                for x in range(nx):
                    value = (
                        states_ref[level, i, x, rows, :]
                        if i < 19
                        else ub_ref[3, x, rows, :]
                    )
                    p = x + first
                    acc = jnp.where(slot == p, pltpu.roll(value, 4 * p + 2, 1), acc)
                out_ref[i, rows, :] = acc
        return carry

    lax.fori_loop(0, ny // 8, tile, 0)


def edge_kernel(
    zown_ref,
    za_ref,
    zb_ref,
    pack_ref,
    f0_ref,
    f1_ref,
    zout,
    tail_ref,
    zmid,
):
    ny, nz = pack_ref.shape[1:]
    tiles = ny // 8
    height = (tiles + 1) * 8
    even = parity("gz") == 0
    lane = lax.broadcasted_iota(jnp.int32, (8, nz), 1)
    sub = lax.broadcasted_iota(jnp.int32, (8, nz), 0)
    even_lane = lane % 2 == 0
    low_pair = lane % 4 < 2

    last = slice(2 * ny + 3, 2 * ny + 4)
    tail_ref[...] = za_ref[last] + zb_ref[last]

    def swapped(value):
        return jnp.where(even_lane, turn(value, -1), turn(value, 1))

    slab_grad = []
    for t in range(tiles + 1):
        received = []
        for g in range(2):
            row = (g * tiles + t) * 8 if t < tiles else 2 * ny
            va = za_ref[row : row + 8, :]
            vb = zb_ref[row : row + 8, :]
            if t == tiles and g:
                va, vb = [
                    jnp.where(sub < 4, pltpu.roll(v, 7, 0), pltpu.roll(v, 1, 0))
                    for v in (va, vb)
                ]
            received.append((jnp.where(even, va, vb), jnp.where(even, vb, va)))
        (high0, low0), (high1, low1) = received
        pairs = []
        for g in range(4):
            row = (g * (tiles + 1) + t) * 8
            own = zown_ref[row : row + 8]
            if g == 0:
                head, tail = own, low0
            elif g == 1:
                head, tail = high0, own
            elif g == 2:
                head = jnp.where(even_lane, own, turn(high1, 1))
                tail = jnp.where(even_lane, low1, own)
            else:
                head = jnp.where(even_lane, own, high1)
                tail = jnp.where(even_lane, turn(low1, -1), own)
            head = swapped(head)
            tail = swapped(tail)
            pairs.append(
                (
                    jnp.where(low_pair, head, turn(tail, 2)),
                    jnp.where(low_pair, turn(head, -2), tail),
                )
            )
        got = []
        for q in range(NSLOT):
            g, k = ZSLOT[q]
            got.append(turn(pairs[g][k % 2], -32 * (k // 2)))
        out, kept = adjoint_cell(got[:19], got[19:22], got[22], 1.0)
        for i in range(19):
            if t < tiles or VEL[i][1] > 0:
                zmid[i, 8 * t + 8 : 8 * t + 16, :] = out[i]
            elif VEL[i][1] < 0:
                zmid[i, 0:8, :] = out[i]
        if t < tiles:
            f = [f1_ref[i, 8 * t : 8 * t + 8, :] for i in range(19)]
            fs, fd = pairs_of(f)
            fm = moments(f[0], fs, fd)
            grad = gradient_cell(kept, f[0], fs, fd, fm, got[19:22])
            slab_grad.append(turn(grad, -8))

    at = lane % 4
    for t in range(tiles):
        rows = slice(8 * t, 8 * t + 8)
        got = []
        for i in range(19):
            cx, cy, cz = VEL[i]
            value = pack_ref[i, rows, :]
            edge = zmid[i, 8 + 8 * t + cy : 16 + 8 * t + cy, :]
            back = -4 * (2 + cx)
            if cz == 0:
                value = jnp.where((at == 1) | (at == 2), turn(edge, back), value)
            else:
                near_lane = 2 if cz < 0 else 0
                value = jnp.where(at == near_lane, turn(edge, back - 1), value)
                value = jnp.where(at == near_lane + 1, turn(edge, back + 1), value)
            got.append(value)
        f = [f0_ref[i, rows, :] for i in range(19)]
        fs, fd = pairs_of(f)
        fm = moments(f[0], fs, fd)
        inverse = 1.0 / fm["total"]
        u = [one * inverse for one in fm["one"]]
        out, kept = adjoint_cell(got, u, f0_ref[19, rows, :], 1.0)
        for i in range(19):
            zout[i, rows, :] = out[i]
        zout[19, rows, :] = gradient_cell(kept, f[0], fs, fd, fm, u)
        zout[20, rows, :] = slab_grad[t]


def finish_kernel(whole_cells, mask_ref, zout, inner_ref, grad1_ref, inner_grad_ref, *refs):
    tiles_of_drag, (out_hbm, grad_hbm, drag_hbm, out_ref, grad_ref, drag_ref, sems) = (
        refs[:-7],
        refs[-7:],
    )
    nx, ny, nz = mask_ref.shape
    tiles = ny // 8
    lane = lax.broadcasted_iota(jnp.int32, (8, nz), 1)
    outer = (lane < 2) | (lane >= nz - 2)
    ends = (lane < 1) | (lane >= nz - 1)
    copies = []

    def send(src, dst):
        copy = pltpu.make_async_copy(src, dst, sems.at[len(copies)])
        copy.start()
        copies.append(copy)

    for x in range(nx):
        for t in range(tiles):
            rows = slice(8 * t, 8 * t + 8)
            level1 = jnp.where(
                ends, turn(zout[20, rows, :], -2 - 4 * x), grad1_ref[x, rows, :]
            )
            edge = turn(zout[19, rows, :], -2 - 4 * x) + level1
            grad = jnp.where(outer, edge, inner_grad_ref[x, rows, :])
            grad_ref[x, rows, :] = jnp.where(mask_ref[x, rows, :] == 0, grad, 0.0)
    send(grad_ref, grad_hbm)
    total = 0.0
    for ref in tiles_of_drag:
        total = total + jnp.sum(ref[...], axis=0, keepdims=True)
    drag_ref[...] = jnp.sum(total, axis=1, keepdims=True) / whole_cells
    send(drag_ref, drag_hbm)
    for low, high in OUT_GROUPS:
        for i in range(low, high):
            for x in range(nx):
                for t in range(tiles):
                    rows = slice(8 * t, 8 * t + 8)
                    out_ref[i, x, rows, :] = jnp.where(
                        outer,
                        turn(zout[i, rows, :], -2 - 4 * x),
                        inner_ref[i, x, rows, :],
                    )
        send(out_ref.at[low:high], out_hbm.at[low:high])
    for copy in copies:
        copy.wait()


def swaps(count):
    first = [(i, i ^ 1) for i in range(count)]
    second = [(i, (((i + 1) % count) ^ 1) - 1) for i in range(count)]
    second = [(i, j % count) for i, j in second]
    return first, second


VMEM = pl.BlockSpec(memory_space=pltpu.VMEM)
HBM = pl.BlockSpec(memory_space=pltpu.HBM)
PARAMS = pltpu.CompilerParams(vmem_limit_bytes=48 * 2**20)


def call(kernel, inputs, shapes, scratch=(), space=VMEM, micros=0.05, outs=None):
    if space is HBM:
        inputs = [pltpu.with_memory_space_constraint(x, pltpu.HBM) for x in inputs]
    return pl.pallas_call(
        kernel,
        out_shape=[jax.ShapeDtypeStruct(s, jnp.float32) for s in shapes],
        in_specs=[space] * len(inputs),
        out_specs=outs or [VMEM] * len(shapes),
        scratch_shapes=list(scratch),
        compiler_params=PARAMS,
        cost_estimate=pl.CostEstimate(
            flops=0, bytes_accessed=int(3.6e6 * micros), transcendentals=0
        ),
    )(*inputs)


def body(primal_states, adjoint_last, porosity, solid_mask):
    nx, ny, nz = porosity.shape
    gx, gy, gz = [lax.axis_size(axis) for axis in AXES]
    x_first, x_second = swaps(gx)
    y_first, y_second = swaps(gy)
    z_first, z_second = swaps(gz)
    tiles = ny // 8
    height = (tiles + 1) * 8
    f32 = jnp.float32

    def diagonal(message, x_pairs, y_pairs):
        pairs = [(a * gy + c, b * gy + d) for a, b in x_pairs for c, d in y_pairs]
        return lax.ppermute(message, ("gx", "gy"), pairs)

    rows_x = NSLOT * ny + 8
    rows_y = 2 * (y_rows(nx) + EDGE_ROWS) + 8
    rows_c = 2 * (CORNER + EDGE_ROWS)
    rows_z = 2 * ny + 8
    rides = (gx, gy, gz) == (4, 2, 4)
    ub, drag = call(
        state_kernel,
        (primal_states, porosity, solid_mask),
        [(4, nx, ny, nz), (8, nz)],
        [
            pltpu.VMEM((2, 19, nx, ny, nz), f32),
            pltpu.VMEM((nx, ny, nz), f32),
            pltpu.VMEM((nx, ny, nz), jnp.int32),
            pltpu.SemaphoreType.DMA((5,)),
        ],
        HBM,
    )
    cols, y, ya, yb = call(
        pack_y_kernel,
        (adjoint_last, ub, drag),
        [(4 * ny + 8, nz), (rows_y, nz), (rows_c, nz), (rows_c, nz)],
        [pltpu.VMEM((NSLOT, 2 * nx, nz), f32)],
        micros=4,
    )
    (xa,) = call(pack_x_kernel, (adjoint_last, ub, drag), [(rows_x, nz)])
    (xb,) = call(pack_partial_kernel, (adjoint_last, ub), [(14 * ny + 8, nz)])
    xc = lax.ppermute(cols, "gx", x_second)
    xa = lax.ppermute(xa, "gx", x_first)
    if gy == 2:
        y = lax.ppermute(y, "gy", y_first)
        yb = diagonal(yb, x_second, y_first)
        ya = diagonal(ya, x_first, y_first)
    else:

        def both(message, block, send):
            parts = [message[:block], message[block : 2 * block], message[2 * block :]]
            return jnp.concatenate(
                [send(parts[0], y_first), send(parts[1], y_second), parts[2]]
            )

        block = y_rows(nx) + EDGE_ROWS
        y = both(y, block, lambda m, pairs: lax.ppermute(m, "gy", pairs))
        block = CORNER + EDGE_ROWS
        yb = both(yb, block, lambda m, pairs: diagonal(m, x_second, pairs))
        ya = both(ya, block, lambda m, pairs: diagonal(m, x_first, pairs))
    xb, yb = lax.optimization_barrier((xb, yb))
    xb = lax.ppermute(xb, "gx", x_second)

    (columns,) = call(pack_columns_kernel, (cols, xa, xc), [(4 * ny, nz)])
    zown, za, zb, drag_xy = call(
        pack_z_kernel,
        (columns, cols, xa, xc, y, ya, yb),
        [(4 * height, nz), (rows_z, nz), (rows_z, nz), (1, nz)],
        [pltpu.VMEM((4, ny + 32, nz), f32)],
    )
    if rides:
        second = jnp.sum(xc[4 * ny :], axis=0, keepdims=True)
        second = second + yb[DRAG_ROW : DRAG_ROW + 1]
        drag_xy = drag_xy + lax.ppermute(second, "gx", x_first)
        za = za.at[2 * ny + 3 : 2 * ny + 4].set(drag_xy)
        zb = zb.at[2 * ny + 3 : 2 * ny + 4].set(drag_xy)
    zb = lax.ppermute(zb, "gz", z_second)
    za = lax.ppermute(za, "gz", z_first)
    inner, grad1, inner_grad, pack, f0, f1 = call(
        inner_kernel,
        (primal_states, adjoint_last, ub, xa, xb, y, ya, yb),
        [
            (19, nx, ny, nz),
            (nx, ny, nz),
            (nx, ny, nz),
            (19, ny, nz),
            (20, ny, nz),
            (19, ny, nz),
        ],
        [
            pltpu.VMEM((NSLOT, nx + 4, ny + 32, nz), f32),
            pltpu.VMEM((19, nx + 2, height + 8, nz), f32),
        ],
        micros=4,
    )
    if rides:
        zhalf = lax.ppermute(drag_xy, "gz", [(i, i ^ 2) for i in range(gz)])
        drags = (drag_xy, zhalf)
    else:
        drags = (lax.psum(drag, AXES),)

    zout, tails = call(
        edge_kernel,
        (zown, za, zb, pack, f0, f1),
        [(21, ny, nz), (1, nz)],
        [pltpu.VMEM((19, height + 8, nz), f32)],
    )
    if rides:
        drags += (tails,)
    whole_cells = float(nx * ny * nz * gx * gy * gz)
    first, gradient, drag = call(
        functools.partial(finish_kernel, whole_cells),
        (solid_mask, zout, inner, grad1, inner_grad) + drags,
        [(19, nx, ny, nz), (nx, ny, nz), (1, 1)],
        [
            pltpu.VMEM((19, nx, ny, nz), f32),
            pltpu.VMEM((nx, ny, nz), f32),
            pltpu.VMEM((1, 1), f32),
            pltpu.SemaphoreType.DMA((len(OUT_GROUPS) + 2,)),
        ],
        outs=[HBM, HBM, HBM],
    )
    return (first, gradient, drag.reshape(()))


def solution(mesh):
    return jax.shard_map(
        body,
        mesh=mesh,
        in_specs=(
            P(None, None, "gx", "gy", "gz"),
            P(None, "gx", "gy", "gz"),
            P("gx", "gy", "gz"),
            P("gx", "gy", "gz"),
        ),
        out_specs=(P(None, "gx", "gy", "gz"), P("gx", "gy", "gz"), P()),
        check_vma=False,
    )
```

```python
import functools

import jax
import jax.numpy as jnp
import numpy as np
from jax import lax
from jax.experimental import pallas as pl
from jax.experimental.pallas import tpu as pltpu
from jax.sharding import PartitionSpec as P

VEL = (
    (0, 0, 0),
    (1, 0, 0),
    (-1, 0, 0),
    (0, 1, 0),
    (0, -1, 0),
    (0, 0, 1),
    (0, 0, -1),
    (1, 1, 0),
    (-1, -1, 0),
    (1, -1, 0),
    (-1, 1, 0),
    (1, 0, 1),
    (-1, 0, -1),
    (1, 0, -1),
    (-1, 0, 1),
    (0, 1, 1),
    (0, -1, -1),
    (0, 1, -1),
    (0, -1, 1),
)
PAIRS = tuple((i, i + 1) for i in range(1, 19, 2))
AXES = ("gx", "gy", "gz")
UB = (19, 20, 21, 22)


def near(axis, sign):
    return tuple(i for i in range(19) if VEL[i][axis] * sign >= 0) + UB


def far(axis, sign):
    return tuple(i for i in range(19) if VEL[i][axis] == sign)


NSLOT = 23
CORNER = 16
DRAG_ROW = 14
EDGE_ROWS = 8


def y_rows(nx):
    return 14 * nx + 8


ZGROUPS = (
    tuple(i for i in range(19) if VEL[i][2] == -1),
    tuple(i for i in range(19) if VEL[i][2] == 1),
    tuple(i for i in range(19) if VEL[i][2] == 0)[:8],
    tuple(i for i in range(19) if VEL[i][2] == 0)[8:] + UB,
)
ZSLOT = {q: (g, k) for g, group in enumerate(ZGROUPS) for k, q in enumerate(group)}


def pairs_of(values):
    s = [values[a] + values[b] for a, b in PAIRS]
    d = [values[a] - values[b] for a, b in PAIRS]
    return s, d


def moments(v0, s, d):
    sx, sy, sz, sp, sq, sr, ss, st, su = s
    dx, dy, dz, dp, dq, dr, ds, dt, du = d
    ex = sp + sq
    ez = sr + ss
    ey = st + su
    faces = sx + sy + sz
    edges = ex + ez + ey
    exx = ex + ez
    eyy = ex + ey
    ezz = ez + ey
    fx = (dp + dq) + (dr + ds)
    fy = (dp - dq) + (dt + du)
    fz = (dr - ds) + (dt - du)
    return dict(
        rest=v0,
        faces=faces,
        edges=edges,
        total=v0 + faces + edges,
        face1=(dx, dy, dz),
        edge1=(fx, fy, fz),
        one=(dx + fx, dy + fy, dz + fz),
        face2=(sx, sy, sz),
        edge2=(exx, eyy, ezz),
        two=(sx + exx, sy + eyy, sz + ezz),
        cross=(sp - sq, sr - ss, st - su),
    )


def adjoint_cell(g, u, b, drive):
    s, d = pairs_of(g)
    m = moments(g[0], s, d)
    total = m["total"]
    trace = m["faces"] + 2.0 * m["edges"] - (30.0 / 19.0) * total
    p0 = (-1.2 / 19.0) * total - (2.0 / 21.0) * trace
    q = [
        (0.4 / 6.0) * (two - (10.0 / 19.0) * total) + (0.8 / 21.0) * trace
        for two in m["two"]
    ]
    qsum = q[0] + q[1] + q[2]
    qab = [0.1 * c for c in m["cross"]]
    p1 = [-0.12 * one for one in m["one"]]
    h0 = (
        0.4 * m["rest"]
        + (1.2 / 18.0) * m["faces"]
        + (1.2 / 36.0) * m["edges"]
        + p0
        + (1.0 / 3.0) * qsum
    )
    h1 = [
        (1.2 / 18.0) * f + (1.2 / 36.0) * e + (1.0 / 3.0) * p
        for f, e, p in zip(m["face1"], m["edge1"], p1)
    ]
    base = (1.0 / 3.0) * p0 + (1.0 / 9.0) * qsum
    haa = [
        (1.2 / 18.0) * f + (1.2 / 36.0) * e + (2.0 / 9.0) * qa + base
        for f, e, qa in zip(m["face2"], m["edge2"], q)
    ]
    hxy, hxz, hyz = [(2.0 / 45.0) * c for c in m["cross"]]
    ux, uy, uz = u
    v = (
        haa[0] * ux + hxy * uy + hxz * uz,
        hxy * ux + haa[1] * uy + hyz * uz,
        hxz * ux + hyz * uy + haa[2] * uz,
    )
    uv = ux * v[0] + uy * v[1] + uz * v[2]
    uu = ux * ux + uy * uy + uz * uz
    uuh = 1.5 * uu * h0
    a = h0 + uuh - 4.5 * uv
    nb = 1.0 - b
    e0 = nb * (a - p0)
    nq = [nb * x for x in q]
    nxy, nxz, nyz = [nb * x for x in qab]
    o = [
        nb * (3.0 * h1[k] + 9.0 * v[k] - 3.0 * u[k] * h0 - p1[k]) for k in range(3)
    ]
    o[0] = o[0] + b * drive
    alpha = -0.2 * nb
    half_s = 0.5 * (alpha + b)
    half_d = 0.5 * (alpha - b)
    exy = e0 - nq[0] - nq[1]
    exz = e0 - nq[0] - nq[2]
    eyz = e0 - nq[1] - nq[2]
    even = (
        e0 - nq[0],
        e0 - nq[1],
        e0 - nq[2],
        exy - nxy,
        exy + nxy,
        exz - nxz,
        exz + nxz,
        eyz - nyz,
        eyz + nyz,
    )
    odd = (
        o[0],
        o[1],
        o[2],
        o[0] + o[1],
        o[0] - o[1],
        o[0] + o[2],
        o[0] - o[2],
        o[1] + o[2],
        o[1] - o[2],
    )
    out = [(alpha + b) * g[0] + e0]
    for k in range(9):
        even_k = half_s * s[k] + even[k]
        odd_k = half_d * d[k] + odd[k]
        out.append(even_k + odd_k)
        out.append(even_k - odd_k)
    kept = dict(
        s=s, d=d, g0=g[0], p0=p0, p1=p1, q=q, qab=qab, h0=h0, h1=h1, uv=uv, uuh=uuh
    )
    return out, kept


def gradient_cell(kept, f0, fs, fd, fm, u):
    rho = fm["total"]
    even = fs[0] * kept["s"][0]
    odd = fd[0] * kept["d"][0]
    for k in range(1, 9):
        even = even + fs[k] * kept["s"][k]
        odd = odd + fd[k] * kept["d"][k]
    hf = kept["p0"] * rho
    for k in range(3):
        hf = hf + kept["p1"][k] * fm["one"][k] + kept["q"][k] * fm["two"][k]
        hf = hf + kept["qab"][k] * fm["cross"][k]
    uh1 = u[0] * kept["h1"][0] + u[1] * kept["h1"][1] + u[2] * kept["h1"][2]
    hfeq = rho * (kept["h0"] - kept["uuh"] + 3.0 * uh1 + 4.5 * kept["uv"])
    pairs = 1.2 * f0 * kept["g0"] + 0.6 * even - 0.4 * odd
    return pairs + hf - hfeq + fm["one"][0]


def state_of(ref, index):
    f = [ref[(index[0], i) + index[1:]] for i in range(19)]
    s, d = pairs_of(f)
    m = moments(f[0], s, d)
    inverse = 1.0 / m["total"]
    u = [one * inverse for one in m["one"]]
    return f[0], s, d, m, u


def corner_rows(sx, sy):
    both = [i for i in far(0, sx) if VEL[i][1] == sy]
    along_y = [i for i in far(1, sy) if VEL[i][0] == 0]
    along_x = [i for i in far(0, sx) if VEL[i][1] == 0]
    rows = [(i, 0, 0) for i in both + along_y + along_x]
    return rows + [(i, 1, 0) for i in both] + [(i, 0, 1) for i in both]


def corner_zeros(sx, sy):
    rows = [(i, 0, 0) for i in range(19) if VEL[i][0] == 0 and VEL[i][1] == 0]
    rows += [(i, 1, 0) for i in far(0, sx) if VEL[i][1] == 0]
    rows += [(i, 0, 1) for i in far(1, sy) if VEL[i][0] == 0]
    return rows + [(i, 1, 1) for i in far(0, sx) if VEL[i][1] == sy]


CORNERS = ((1, 1), (1, -1), (-1, 1), (-1, -1))


def parity(axis):
    return lax.axis_index(axis) % 2


def cell_rows(adj_ref, ub_ref, q, x, rows):
    return adj_ref[q, x, rows, :] if q < 19 else ub_ref[q - 19, x, rows, :]


def state_kernel(
    states_hbm,
    por_hbm,
    mask_hbm,
    ub_ref,
    drag_ref,
    states_ref,
    por_ref,
    mask_ref,
    sems,
):
    nx, ny, nz = por_ref.shape
    tiles = ny // 8
    copies = [
        pltpu.make_async_copy(src, dst, sems.at[k])
        for k, (src, dst) in enumerate(
            (
                (states_hbm.at[1], states_ref.at[1]),
                (por_hbm, por_ref),
                (mask_hbm, mask_ref),
                (states_hbm.at[0, 1:3], states_ref.at[0, 1:3]),
                (states_hbm.at[0, 7:15], states_ref.at[0, 7:15]),
            )
        )
    ]
    for copy in copies:
        copy.start()
    for copy in copies[:3]:
        copy.wait()

    def cells(x, carry):
        for t in range(tiles):
            rows = slice(8 * t, 8 * t + 8)
            blocking = jnp.where(mask_ref[x, rows, :] == 0, por_ref[x, rows, :], 1.0)
            f0, s, d, m, u = state_of(states_ref, (1, x, rows))
            for k in range(3):
                ub_ref[k, x, rows, :] = u[k]
            ub_ref[3, x, rows, :] = blocking
            carry = carry + blocking * m["one"][0]
        return carry

    drag = lax.fori_loop(0, nx, cells, jnp.zeros((8, nz), jnp.float32))
    for copy in copies[3:]:
        copy.wait()

    def flux_cells(x, carry):
        for t in range(tiles):
            rows = slice(8 * t, 8 * t + 8)
            flux = 0.0
            for a, b in PAIRS:
                if VEL[a][0]:
                    flux = flux + (
                        states_ref[0, a, x, rows, :] - states_ref[0, b, x, rows, :]
                    )
            carry = carry + ub_ref[3, x, rows, :] * flux
        return carry

    drag = lax.fori_loop(0, nx, flux_cells, drag)
    drag_ref[...] = drag


def pack_x_kernel(adj_ref, ub_ref, drag_ref, out_ref):
    nx, ny = adj_ref.shape[1:3]
    out_ref[NSLOT * ny :] = drag_ref[...]

    def fill(sign):
        for names, offset, x in (
            (near(0, sign), 0, 0 if sign > 0 else nx - 1),
            (far(0, sign), 18, 1 if sign > 0 else nx - 2),
        ):
            for k, q in enumerate(names):
                k += offset
                out_ref[k * ny : (k + 1) * ny] = cell_rows(
                    adj_ref, ub_ref, q, x, slice(0, ny)
                )

    pl.when(parity("gx") == 0)(functools.partial(fill, -1))
    pl.when(parity("gx") == 1)(functools.partial(fill, 1))


def y_edge_entries(sign, nx):
    rows = []
    for side in (1, -1):
        x = 0 if side > 0 else nx - 1
        rows += [(i, 0, x) for i in far(0, side) if VEL[i][1] == 0]
        rows += [(i, 1, x) for i in far(0, side) if VEL[i][1] == sign]
    return rows


def edge_entries(sign):
    rows = []
    for side in (1, -1):
        rows += [(i, 0, side) for i in far(1, side) if VEL[i][0] == 0]
        rows += [(i, 1, side) for i in far(1, side) if VEL[i][0] == sign]
    return rows


def pack_partial_kernel(adj_ref, ub_ref, out_ref):
    nx, ny, nz = adj_ref.shape[1:]
    tiles = ny // 8
    sub = lax.broadcasted_iota(jnp.int32, (8, nz), 0)

    def fill(sign):
        here, inside = (0, 1) if sign > 0 else (nx - 1, nx - 2)
        names = far(0, sign)
        for t in range(tiles):
            rows = slice(8 * t, 8 * t + 8)
            got = []
            for i in range(19):
                cx, cy, cz = VEL[i]
                if cx * sign < 0:
                    got.append(jnp.zeros((8, nz), jnp.float32))
                    continue
                x = inside if cx else here
                if t == 0 and cy < 0:
                    value = pltpu.roll(adj_ref[i, x, rows, :], 1, 0)
                    value = jnp.where(sub == 0, 0.0, value)
                elif t == tiles - 1 and cy > 0:
                    value = pltpu.roll(adj_ref[i, x, rows, :], 7, 0)
                    value = jnp.where(sub == 7, 0.0, value)
                else:
                    value = adj_ref[i, x, 8 * t + cy : 8 * t + 8 + cy, :]
                got.append(z_shifted(value, cz))
            u = [ub_ref[k, here, rows, :] for k in range(3)]
            out, _ = adjoint_cell(got, u, ub_ref[3, here, rows, :], 0.0)
            for k, i in enumerate(names):
                out_ref[k * ny + 8 * t : k * ny + 8 * t + 8] = out[i]
        for k, q in enumerate(names + UB):
            k += 5
            out_ref[k * ny : (k + 1) * ny] = cell_rows(
                adj_ref, ub_ref, q, here, slice(0, ny)
            )
        for k, (i, depth, side) in enumerate(edge_entries(sign)):
            y = 0 if side > 0 else ny - 1
            row = 14 * ny + k
            out_ref[row : row + 1] = adj_ref[i, inside if depth else here, y : y + 1, :]

    pl.when(parity("gx") == 0)(functools.partial(fill, 1))
    pl.when(parity("gx") == 1)(functools.partial(fill, -1))


def column_pair(acc, value, pair, q, k, plane):
    start = 32 * (k // 2) + 4 * plane + 2 * (k % 2)
    cz = VEL[q][2] if q < 19 else 0
    return jnp.where(pair == start // 2, turn(value, start + 1 - cz), acc)


def pack_y_kernel(
    adj_ref, ub_ref, drag_ref, cols_ref, y_ref, ya_ref, yb_ref, read_ref
):
    nx, ny, nz = adj_ref.shape[1:]
    pair = lax.broadcasted_iota(jnp.int32, (8, nz), 1) // 2
    for g, group in enumerate(ZGROUPS):
        for t in range(ny // 8):
            acc = jnp.zeros((8, nz), jnp.float32)
            for k, q in enumerate(group):
                for x in range(nx):
                    value = cell_rows(adj_ref, ub_ref, q, x, slice(8 * t, 8 * t + 8))
                    acc = column_pair(acc, value, pair, q, k, x + 2)
            row = g * ny + 8 * t
            cols_ref[row : row + 8] = acc
    y_block = y_rows(nx) + EDGE_ROWS
    corner_block = CORNER + EDGE_ROWS

    def fill_edges(place, sign):
        for g in range(4):
            for d in range(2):
                y = d if sign > 0 else ny - 1 - d
                line = cols_ref[g * ny + y : g * ny + y + 1]
                row = place * y_block + y_rows(nx) + 2 * g + d
                y_ref[row : row + 1] = line
                row = place * corner_block + CORNER + 2 * g + d
                ya_ref[row : row + 1] = line
                yb_ref[row : row + 1] = line

    faces = ((1, 0, 1), (-1, ny - 1, ny - 2))
    for i in range(19):
        cx, cy, _ = VEL[i]
        read_ref[i] = jnp.zeros((2 * nx, nz), jnp.float32)
        for n, (sign, here, inside) in enumerate(faces):
            for x in range(max(0, -cx), min(nx, nx - cx)):
                if cy * sign >= 0:
                    y = inside if cy else here
                    read_ref[i, n * nx + x : n * nx + x + 1, :] = adj_ref[
                        i, x + cx, y : y + 1, :
                    ]
    for k in range(4):
        for n, (sign, here, inside) in enumerate(faces):
            for x in range(nx):
                read_ref[19 + k, n * nx + x : n * nx + x + 1, :] = ub_ref[
                    k, x, here : here + 1, :
                ]
    got = [z_shifted(read_ref[i], VEL[i][2]) for i in range(19)]
    sums, _ = adjoint_cell(
        got, [read_ref[19 + k] for k in range(3)], read_ref[22], 0.0
    )

    def fill_y(place, sign):
        n = 0 if sign > 0 else 1
        _, here, inside = faces[n]
        first = place * y_block
        for k, i in enumerate(far(1, sign)):
            row = first + k * nx
            y_ref[row : row + nx] = sums[i][n * nx : (n + 1) * nx]
        for k, q in enumerate(far(1, sign) + UB):
            for x in range(nx):
                row = first + (5 + k) * nx + x
                y_ref[row : row + 1] = cell_rows(
                    adj_ref, ub_ref, q, x, slice(here, here + 1)
                )
        for k, (i, depth, x) in enumerate(y_edge_entries(sign, nx)):
            y = inside if depth else here
            row = first + 14 * nx + k
            y_ref[row : row + 1] = adj_ref[i, x, y : y + 1, :]

    for i in range(19):
        read_ref[i] = jnp.zeros((2 * nx, nz), jnp.float32)
    for n, (sx, sy) in enumerate(CORNERS):
        xs = (0, 1) if sx > 0 else (nx - 1, nx - 2)
        ys = (0, 1) if sy > 0 else (ny - 1, ny - 2)
        for i, dx, dy in corner_zeros(sx, sy):
            read_ref[i, n : n + 1, :] = adj_ref[i, xs[dx], ys[dy] : ys[dy] + 1, :]
        for k in range(4):
            read_ref[19 + k, n : n + 1, :] = ub_ref[k, xs[0], ys[0] : ys[0] + 1, :]
    got = [z_shifted(read_ref[i], VEL[i][2]) for i in range(19)]
    corner_sums, _ = adjoint_cell(
        got, [read_ref[19 + k] for k in range(3)], read_ref[22], 0.0
    )
    line = jnp.sum(drag_ref[...], axis=0, keepdims=True)

    def fill_corner(out_ref, place, sx, sy):
        xs = (0, 1) if sx > 0 else (nx - 1, nx - 2)
        ys = (0, 1) if sy > 0 else (ny - 1, ny - 2)
        n = CORNERS.index((sx, sy))
        first = place * corner_block
        rows = corner_rows(sx, sy)
        out_ref[first : first + 1] = corner_sums[rows[0][0]][n : n + 1]
        for k in range(4):
            out_ref[first + 1 + k : first + 2 + k] = ub_ref[
                k, xs[0], ys[0] : ys[0] + 1, :
            ]
        for k, (i, dx, dy) in enumerate(rows):
            row = first + 5 + k
            out_ref[row : row + 1] = adj_ref[i, xs[dx], ys[dy] : ys[dy] + 1, :]
        out_ref[first + DRAG_ROW : first + DRAG_ROW + 1] = line
        out_ref[first + DRAG_ROW + 1 : first + CORNER] = jnp.zeros((1, nz), jnp.float32)

    drag = drag_ref[...]
    cols_ref[4 * ny :] = drag
    y_ref[2 * y_block :] = drag
    for py in (0, 1):

        @pl.when(parity("gy") == py)
        def _():
            s0 = 1 if py else -1
            fill_y(0, s0)
            fill_y(1, -s0)
            fill_edges(0, s0)
            fill_edges(1, -s0)

    for px in (0, 1):
        for py in (0, 1):

            @pl.when((parity("gx") == px) & (parity("gy") == py))
            def _():
                sa = 1 if px else -1
                s0 = 1 if py else -1
                for out_ref, sx in ((ya_ref, sa), (yb_ref, -sa)):
                    fill_corner(out_ref, 0, sx, s0)
                    fill_corner(out_ref, 1, sx, -s0)


def pack_columns_kernel(cols_ref, xa_ref, xc_ref, out_ref):
    ny = (cols_ref.shape[0] - 8) // 4
    nz = cols_ref.shape[1]
    tiles = ny // 8
    lane = lax.broadcasted_iota(jnp.int32, (8, nz), 1)
    plane = (lane % 32) // 4
    pair = lane // 2

    def fill_main(sign):
        halo = {}
        for names, offset, p in (
            (near(0, sign), 0, 6 if sign > 0 else 1),
            (far(0, sign), 18, 7 if sign > 0 else 0),
        ):
            for k, q in enumerate(names):
                halo.setdefault(q, []).append((k + offset, p))
        for g, group in enumerate(ZGROUPS):
            for t in range(tiles):
                rows = slice(g * ny + 8 * t, g * ny + 8 * t + 8)
                acc = jnp.where(
                    plane < 2 if sign > 0 else plane > 5,
                    turn(xc_ref[rows], -16 * sign),
                    cols_ref[rows],
                )
                for k, q in enumerate(group):
                    for at, p in halo.get(q, ()):
                        row = at * ny + 8 * t
                        acc = column_pair(acc, xa_ref[row : row + 8], pair, q, k, p)
                    out_ref[rows] = acc

    @pl.when(parity("gx") == 0)
    def _():
        fill_main(1)

    @pl.when(parity("gx") == 1)
    def _():
        fill_main(-1)


def pack_z_kernel(
    main_ref,
    cols_ref,
    xa_ref,
    xc_ref,
    y_ref,
    ya_ref,
    yb_ref,
    zown_ref,
    za_ref,
    zb_ref,
    drag_ref,
    ext,
):
    ny = (cols_ref.shape[0] - 8) // 4
    nz = cols_ref.shape[1]
    tiles = ny // 8
    base = 16
    even_x = parity("gx") == 0
    even_y = parity("gy") == 0
    lane = lax.broadcasted_iota(jnp.int32, (8, nz), 1)
    sub = lax.broadcasted_iota(jnp.int32, (8, nz), 0)
    plane = (lane % 32) // 4
    slot = 2 * (lane // 32) + (lane % 4) // 2

    def along_x(own, va, vb):
        low = turn(jnp.where(even_x, vb, va), -16)
        high = turn(jnp.where(even_x, va, vb), 16)
        return jnp.where(plane < 2, low, jnp.where(plane > 5, high, own))

    for g in range(4):
        for t in range(tiles):
            row = g * ny + 8 * t
            ext[g, base + 8 * t : base + 8 * t + 8, :] = main_ref[row : row + 8]

    y_block = (y_ref.shape[0] - 8) // 2
    corner_block = CORNER + EDGE_ROWS

    def edges(ref, block, place):
        return ref[(place + 1) * block - EDGE_ROWS : (place + 1) * block]

    first, second = [
        along_x(
            edges(y_ref, y_block, place),
            edges(ya_ref, corner_block, place),
            edges(yb_ref, corner_block, place),
        )
        for place in range(2)
    ]
    high = jnp.where(even_y, first, second)
    low = jnp.where(even_y, second, first)
    for g in range(4):
        for d in range(2):
            row = 2 * g + d
            ext[g, base + ny + d : base + ny + d + 1, :] = high[row : row + 1]
            ext[g, base - 1 - d : base - d, :] = low[row : row + 1]

    packed = []
    for g, group in enumerate(ZGROUPS):
        moves = {}
        for k, q in enumerate(group):
            cx, cy, _ = VEL[q] if q < 19 else (0, 0, 0)
            moves.setdefault((cx, cy), []).append(k)
        acc = [jnp.zeros((8, nz), jnp.float32) for t in range(tiles + 1)]
        for (cx, cy), slots in moves.items():
            mask = slot == slots[0]
            for k in slots[1:]:
                mask = mask | (slot == k)
            for t in range(tiles + 1):
                if t < tiles:
                    row = base + 8 * t + cy
                    value = ext[g, row : row + 8, :]
                else:
                    above = base + ny + cy
                    below = base - 8 + cy
                    value = jnp.where(
                        sub < 4, ext[g, above : above + 8, :], ext[g, below : below + 8, :]
                    )
                acc[t] = jnp.where(mask, turn(value, -4 * cx), acc[t])
        packed.append(acc)
        for t in range(tiles + 1):
            row = (g * (tiles + 1) + t) * 8
            zown_ref[row : row + 8, :] = acc[t]
    up_first = parity("gz") == 0
    even_lane = lane % 2 == 0
    for t in range(tiles + 1):
        two, three = packed[2][t], packed[3][t]
        up = (packed[0][t], jnp.where(even_lane, two, pltpu.roll(three, 1, 1)))
        down = (packed[1][t], jnp.where(even_lane, pltpu.roll(two, nz - 1, 1), three))
        if t == tiles:
            up, down = [
                (
                    jnp.where(
                        (sub == 0) | (sub == 7),
                        side[0],
                        jnp.where(
                            sub < 4, pltpu.roll(side[1], 1, 0), pltpu.roll(side[1], 7, 0)
                        ),
                    ),
                )
                for side in (up, down)
            ]
        for g in range(len(up)):
            row = (g * tiles + t) * 8 if t < tiles else 2 * tiles * 8
            za_ref[row : row + 8, :] = jnp.where(up_first, up[g], down[g])
            zb_ref[row : row + 8, :] = jnp.where(up_first, down[g], up[g])
    drag = (cols_ref[4 * ny :] + y_ref[2 * y_block :]) + (
        xa_ref[xa_ref.shape[0] - 8 :] + xc_ref[4 * ny :]
    )
    row = slice(DRAG_ROW, DRAG_ROW + 1)
    drag_ref[...] = jnp.sum(drag, axis=0, keepdims=True) + (ya_ref[row] + yb_ref[row])


OUT_GROUPS = ((0, 6), (6, 12), (12, 17), (17, 19))


def turn(value, shift):
    nz = value.shape[1]
    return pltpu.roll(value, shift % nz, 1) if shift % nz else value


def z_shifted(value, cz):
    return turn(value, -cz) if cz else value


def inner_kernel(
    states_ref,
    adj_ref,
    ub_ref,
    xa_ref,
    xb_ref,
    y_ref,
    ya_ref,
    yb_ref,
    out_ref,
    grad1_ref,
    grad_ref,
    pack_ref,
    f0_ref,
    f1_ref,
    ext,
    mid,
):
    nx, ny, nz = grad_ref.shape
    tiles = ny // 8
    lane = lax.broadcasted_iota(jnp.int32, (8, nz), 1)
    slot = lane // 4
    slot0 = ((lane + 2) % nz) // 4
    sub = lax.broadcasted_iota(jnp.int32, (8, nz), 0)
    even_x = parity("gx") == 0
    even_y = parity("gy") == 0
    base = 16

    for q in range(NSLOT):
        for x in range(nx):
            ext[q, x + 2, base : base + ny, :] = (
                adj_ref[q, x] if q < 19 else ub_ref[q - 19, x]
            )
    planes = {1: (nx + 2, nx + 3), -1: (1, 0)}
    lines = {1: (base + ny, base + ny + 1), -1: (base - 1, base - 2)}

    def fill_whole(sign):
        for names, depth, offset in ((near(0, sign), 0, 0), (far(0, sign), 1, 18)):
            for k, q in enumerate(names):
                rows = slice((k + offset) * ny, (k + offset + 1) * ny)
                ext[q, planes[sign][depth], base : base + ny, :] = xa_ref[rows]

    def fill_partial(sign):
        one, two = planes[sign]
        for k, q in enumerate(far(0, sign) + UB):
            ext[q, one, base : base + ny, :] = xb_ref[(5 + k) * ny : (6 + k) * ny]
        nothing = jnp.zeros((ny, nz), jnp.float32)
        for q in range(19):
            if VEL[q][0] == 0:
                ext[q, one, base : base + ny, :] = nothing
            elif VEL[q][0] == sign:
                ext[q, two, base : base + ny, :] = nothing
        for k, (q, depth, side) in enumerate(edge_entries(sign)):
            line = base if side > 0 else base + ny - 1
            row = 14 * ny + k
            ext[q, planes[sign][depth], line : line + 1, :] = xb_ref[row : row + 1]

    @pl.when(parity("gx") == 0)
    def _():
        fill_whole(1)
        fill_partial(-1)

    @pl.when(parity("gx") == 1)
    def _():
        fill_whole(-1)
        fill_partial(1)

    sums = {}
    corner_sums = {}
    for sign in (1, -1):
        block = y_rows(nx) + EDGE_ROWS
        first, second = (0, block) if sign > 0 else (block, 0)
        one, two = lines[sign]
        nothing = jnp.zeros((1, nz), jnp.float32)
        for q in range(19):
            for x in range(nx):
                if VEL[q][1] == 0:
                    ext[q, x + 2, one : one + 1, :] = nothing
                elif VEL[q][1] == sign:
                    ext[q, x + 2, two : two + 1, :] = nothing
        got = jnp.where(
            even_y,
            y_ref[first : first + y_rows(nx)],
            y_ref[second : second + y_rows(nx)],
        )
        sums[sign] = got
        for k, q in enumerate(far(1, sign) + UB):
            for x in range(nx):
                row = (5 + k) * nx + x
                ext[q, x + 2, one : one + 1, :] = got[row : row + 1]
        for k, (q, depth, x) in enumerate(y_edge_entries(sign, nx)):
            line = lines[sign][depth]
            row = 14 * nx + k
            ext[q, x + 2, line : line + 1, :] = got[row : row + 1]
        for sx in (1, -1):
            xs = (ya_ref, yb_ref) if sx > 0 else (yb_ref, ya_ref)
            block = CORNER + EDGE_ROWS
            ys = (0, block) if sign > 0 else (block, 0)
            low, high = [
                jnp.where(even_x, xs[0][r : r + CORNER], xs[1][r : r + CORNER])
                for r in ys
            ]
            got = jnp.where(even_y, low, high)
            corner_sums[sx, sign] = got[0:1]
            for k in range(4):
                line = lines[sign][0]
                ext[19 + k, planes[sx][0], line : line + 1, :] = got[1 + k : 2 + k]
            for q, dx, dy in corner_zeros(sx, sign):
                line = lines[sign][dy]
                ext[q, planes[sx][dx], line : line + 1, :] = nothing
            for k, (q, dx, dy) in enumerate(corner_rows(sx, sign)):
                line = lines[sign][dy]
                ext[q, planes[sx][dx], line : line + 1, :] = got[5 + k : 6 + k]

    def near_cells(q, plane, t, cy):
        if t < tiles:
            row = base + 8 * t + cy
            return ext[q, plane, row : row + 8, :]
        above = base + ny + cy
        below = base - 8 + cy
        return jnp.where(
            sub < 4, ext[q, plane, above : above + 8, :], ext[q, plane, below : below + 8, :]
        )

    def first_level(p, t, kinds, partial=None):
        got = []
        for i in range(19):
            cx, cy, cz = VEL[i]
            got.append(z_shifted(near_cells(i, p + 1 + cx, t, cy), cz))
        ub = [near_cells(19 + k, p + 1, t, 0) for k in range(4)]
        out, kept = adjoint_cell(got, ub[:3], ub[3], 1.0)
        if t == tiles and 1 <= p <= nx:
            for sign, row in ((1, 0), (-1, 7)):
                for k, i in enumerate(far(1, sign)):
                    line = k * nx + p - 1
                    term = sums[sign][line : line + 1]
                    out[i] = out[i] + jnp.where(sub == row, term, 0.0)
        elif t == tiles:
            sx = -1 if p == 0 else 1
            for sign, row in ((1, 0), (-1, 7)):
                i = corner_rows(sx, sign)[0][0]
                out[i] = out[i] + jnp.where(sub == row, corner_sums[sx, sign], 0.0)
        if partial is not None:
            for k, i in enumerate(kinds):
                row = k * ny + 8 * t
                out[i] = out[i] + jnp.where(partial, xb_ref[row : row + 8], 0.0)
        for i in kinds:
            if t < tiles:
                mid[i, p, t * 8 + 8 : t * 8 + 16, :] = out[i]
            elif VEL[i][1] > 0:
                mid[i, p, t * 8 + 8 : t * 8 + 16, :] = out[i]
            elif VEL[i][1] < 0:
                mid[i, p, 0:8, :] = out[i]
        return kept, ub[:3]

    def inside(x, carry):
        for t in range(tiles):
            kept, u = first_level(x + 1, t, range(19))
            rows = slice(t * 8, t * 8 + 8)
            f0, fs, fd, fm, _ = state_of(states_ref, (1, x, rows))
            grad1_ref[x, rows, :] = gradient_cell(kept, f0, fs, fd, fm, u)
        return carry

    lax.fori_loop(0, nx, inside, 0)
    for t in range(tiles):
        first_level(0, t, far(0, -1), even_x)
        first_level(nx + 1, t, far(0, 1), jnp.logical_not(even_x))

    for p in range(nx + 2):
        first_level(p, tiles, far(1, -1) + far(1, 1))

    def second_level(x, carry):
        for t in range(tiles):
            rows = slice(t * 8, t * 8 + 8)
            got = []
            for i in range(19):
                cx, cy, cz = VEL[i]
                low = 8 + 8 * t + cy
                value = z_shifted(mid[i, x + 1 + cx, low : low + 8, :], cz)
                got.append(value)
                pack_ref[i, rows, :] = jnp.where(
                    slot0 == x, pltpu.roll(value, 4 * x, 1), pack_ref[i, rows, :]
                )
            f0, fs, fd, fm, u = state_of(states_ref, (0, x, rows))
            b = ub_ref[3, x, rows, :]
            out, kept = adjoint_cell(got, u, b, 1.0)
            for i in range(19):
                out_ref[i, x, rows, :] = out[i]
            grad_ref[x, rows, :] = grad1_ref[x, rows, :] + gradient_cell(
                kept, f0, fs, fd, fm, u
            )
        return carry

    lax.fori_loop(0, nx, second_level, 0)

    def tile(t, carry):
        rows = pl.ds(pl.multiple_of(t * 8, 8), 8)
        for i in range(20):
            for out_ref, level, first in ((f0_ref, 0, 0), (f1_ref, 1, 2)):
                if i == 19 and level == 1:
                    continue
                acc = jnp.zeros((8, nz), jnp.float32)
                for x in range(nx):
                    value = (
                        states_ref[level, i, x, rows, :]
                        if i < 19
                        else ub_ref[3, x, rows, :]
                    )
                    p = x + first
                    acc = jnp.where(
                        (slot if level else slot0) == p,
                        turn(value, 4 * p + 2 * level),
                        acc,
                    )
                out_ref[i, rows, :] = acc
        return carry

    lax.fori_loop(0, ny // 8, tile, 0)


def edge_kernel(
    zown_ref,
    za_ref,
    zb_ref,
    pack_ref,
    f0_ref,
    f1_ref,
    zout,
    tail_ref,
    zmid,
):
    ny, nz = pack_ref.shape[1:]
    tiles = ny // 8
    height = (tiles + 1) * 8
    even = parity("gz") == 0
    lane = lax.broadcasted_iota(jnp.int32, (8, nz), 1)
    sub = lax.broadcasted_iota(jnp.int32, (8, nz), 0)
    even_lane = lane % 2 == 0
    low_pair = lane % 4 < 2

    last = slice(2 * ny + 3, 2 * ny + 4)
    tail_ref[...] = za_ref[last] + zb_ref[last]

    def swapped(value):
        return jnp.where(even_lane, turn(value, -1), turn(value, 1))

    slab_grad = []
    for t in range(tiles + 1):
        received = []
        for g in range(2):
            row = (g * tiles + t) * 8 if t < tiles else 2 * ny
            va = za_ref[row : row + 8, :]
            vb = zb_ref[row : row + 8, :]
            if t == tiles and g:
                va, vb = [
                    jnp.where(sub < 4, pltpu.roll(v, 7, 0), pltpu.roll(v, 1, 0))
                    for v in (va, vb)
                ]
            received.append((jnp.where(even, va, vb), jnp.where(even, vb, va)))
        (high0, low0), (high1, low1) = received
        pairs = []
        for g in range(4):
            row = (g * (tiles + 1) + t) * 8
            own = zown_ref[row : row + 8]
            if g == 0:
                head, tail = own, low0
            elif g == 1:
                head, tail = high0, own
            elif g == 2:
                head = jnp.where(even_lane, own, turn(high1, 1))
                tail = jnp.where(even_lane, low1, own)
            else:
                head = jnp.where(even_lane, own, high1)
                tail = jnp.where(even_lane, turn(low1, -1), own)
            head = swapped(head)
            tail = swapped(tail)
            pairs.append(
                (
                    jnp.where(low_pair, head, turn(tail, 2)),
                    jnp.where(low_pair, turn(head, -2), tail),
                )
            )
        got = []
        for q in range(NSLOT):
            g, k = ZSLOT[q]
            got.append(turn(pairs[g][k % 2], -32 * (k // 2)))
        out, kept = adjoint_cell(got[:19], got[19:22], got[22], 1.0)
        for i in range(19):
            if t < tiles or VEL[i][1] > 0:
                zmid[i, 8 * t + 8 : 8 * t + 16, :] = out[i]
            elif VEL[i][1] < 0:
                zmid[i, 0:8, :] = out[i]
        if t < tiles:
            f = [f1_ref[i, 8 * t : 8 * t + 8, :] for i in range(19)]
            fs, fd = pairs_of(f)
            fm = moments(f[0], fs, fd)
            grad = gradient_cell(kept, f[0], fs, fd, fm, got[19:22])
            slab_grad.append(turn(grad, -10))

    at = (lane + 2) % 4
    for t in range(tiles):
        rows = slice(8 * t, 8 * t + 8)
        got = []
        for i in range(19):
            cx, cy, cz = VEL[i]
            value = pack_ref[i, rows, :]
            edge = zmid[i, 8 + 8 * t + cy : 16 + 8 * t + cy, :]
            back = -4 * (2 + cx) - 2
            if cz == 0:
                value = jnp.where((at == 1) | (at == 2), turn(edge, back), value)
            else:
                near_lane = 2 if cz < 0 else 0
                value = jnp.where(at == near_lane, turn(edge, back - 1), value)
                value = jnp.where(at == near_lane + 1, turn(edge, back + 1), value)
            got.append(value)
        f = [f0_ref[i, rows, :] for i in range(19)]
        fs, fd = pairs_of(f)
        fm = moments(f[0], fs, fd)
        inverse = 1.0 / fm["total"]
        u = [one * inverse for one in fm["one"]]
        out, kept = adjoint_cell(got, u, f0_ref[19, rows, :], 1.0)
        for i in range(19):
            zout[i, rows, :] = out[i]
        zout[19, rows, :] = gradient_cell(kept, f[0], fs, fd, fm, u)
        zout[20, rows, :] = slab_grad[t]


def finish_kernel(whole_cells, mask_ref, zout, inner_ref, grad1_ref, inner_grad_ref, *refs):
    tiles_of_drag, (out_hbm, grad_hbm, drag_hbm, out_ref, grad_ref, drag_ref, sems) = (
        refs[:-7],
        refs[-7:],
    )
    nx, ny, nz = mask_ref.shape
    tiles = ny // 8
    lane = lax.broadcasted_iota(jnp.int32, (8, nz), 1)
    outer = (lane < 2) | (lane >= nz - 2)
    ends = (lane < 1) | (lane >= nz - 1)
    copies = []

    def send(src, dst):
        copy = pltpu.make_async_copy(src, dst, sems.at[len(copies)])
        copy.start()
        copies.append(copy)

    for x in range(nx):
        for t in range(tiles):
            rows = slice(8 * t, 8 * t + 8)
            level1 = jnp.where(
                ends, turn(zout[20, rows, :], -4 * x), grad1_ref[x, rows, :]
            )
            edge = turn(zout[19, rows, :], -4 * x) + level1
            grad = jnp.where(outer, edge, inner_grad_ref[x, rows, :])
            grad_ref[x, rows, :] = jnp.where(mask_ref[x, rows, :] == 0, grad, 0.0)
    send(grad_ref, grad_hbm)
    total = 0.0
    for ref in tiles_of_drag:
        total = total + jnp.sum(ref[...], axis=0, keepdims=True)
    drag_ref[...] = jnp.sum(total, axis=1, keepdims=True) / whole_cells
    send(drag_ref, drag_hbm)
    for low, high in OUT_GROUPS:
        for i in range(low, high):
            for x in range(nx):
                for t in range(tiles):
                    rows = slice(8 * t, 8 * t + 8)
                    out_ref[i, x, rows, :] = jnp.where(
                        outer,
                        turn(zout[i, rows, :], -4 * x),
                        inner_ref[i, x, rows, :],
                    )
        send(out_ref.at[low:high], out_hbm.at[low:high])
    for copy in copies:
        copy.wait()


def swaps(count):
    first = [(i, i ^ 1) for i in range(count)]
    second = [(i, (((i + 1) % count) ^ 1) - 1) for i in range(count)]
    second = [(i, j % count) for i, j in second]
    return first, second


VMEM = pl.BlockSpec(memory_space=pltpu.VMEM)
HBM = pl.BlockSpec(memory_space=pltpu.HBM)
PARAMS = pltpu.CompilerParams(vmem_limit_bytes=48 * 2**20)


def call(kernel, inputs, shapes, scratch=(), space=VMEM, micros=0.05, outs=None):
    if space is HBM:
        inputs = [pltpu.with_memory_space_constraint(x, pltpu.HBM) for x in inputs]
    return pl.pallas_call(
        kernel,
        out_shape=[jax.ShapeDtypeStruct(s, jnp.float32) for s in shapes],
        in_specs=[space] * len(inputs),
        out_specs=outs or [VMEM] * len(shapes),
        scratch_shapes=list(scratch),
        compiler_params=PARAMS,
        cost_estimate=pl.CostEstimate(
            flops=0, bytes_accessed=int(3.6e6 * micros), transcendentals=0
        ),
    )(*inputs)


def body(primal_states, adjoint_last, porosity, solid_mask):
    nx, ny, nz = porosity.shape
    gx, gy, gz = [lax.axis_size(axis) for axis in AXES]
    x_first, x_second = swaps(gx)
    y_first, y_second = swaps(gy)
    z_first, z_second = swaps(gz)
    tiles = ny // 8
    height = (tiles + 1) * 8
    f32 = jnp.float32

    def diagonal(message, x_pairs, y_pairs):
        pairs = [(a * gy + c, b * gy + d) for a, b in x_pairs for c, d in y_pairs]
        return lax.ppermute(message, ("gx", "gy"), pairs)

    rows_x = NSLOT * ny + 8
    rows_y = 2 * (y_rows(nx) + EDGE_ROWS) + 8
    rows_c = 2 * (CORNER + EDGE_ROWS)
    rows_z = 2 * ny + 8
    rides = (gx, gy, gz) == (4, 2, 4)
    ub, drag = call(
        state_kernel,
        (primal_states, porosity, solid_mask),
        [(4, nx, ny, nz), (8, nz)],
        [
            pltpu.VMEM((2, 19, nx, ny, nz), f32),
            pltpu.VMEM((nx, ny, nz), f32),
            pltpu.VMEM((nx, ny, nz), jnp.int32),
            pltpu.SemaphoreType.DMA((5,)),
        ],
        HBM,
    )
    cols, y, ya, yb = call(
        pack_y_kernel,
        (adjoint_last, ub, drag),
        [(4 * ny + 8, nz), (rows_y, nz), (rows_c, nz), (rows_c, nz)],
        [pltpu.VMEM((NSLOT, 2 * nx, nz), f32)],
        micros=4,
    )
    (xa,) = call(pack_x_kernel, (adjoint_last, ub, drag), [(rows_x, nz)])
    (xb,) = call(pack_partial_kernel, (adjoint_last, ub), [(14 * ny + 8, nz)])
    xc = lax.ppermute(cols, "gx", x_second)
    xa = lax.ppermute(xa, "gx", x_first)
    if gy == 2:
        y = lax.ppermute(y, "gy", y_first)
        yb = diagonal(yb, x_second, y_first)
        ya = diagonal(ya, x_first, y_first)
    else:

        def both(message, block, send):
            parts = [message[:block], message[block : 2 * block], message[2 * block :]]
            return jnp.concatenate(
                [send(parts[0], y_first), send(parts[1], y_second), parts[2]]
            )

        block = y_rows(nx) + EDGE_ROWS
        y = both(y, block, lambda m, pairs: lax.ppermute(m, "gy", pairs))
        block = CORNER + EDGE_ROWS
        yb = both(yb, block, lambda m, pairs: diagonal(m, x_second, pairs))
        ya = both(ya, block, lambda m, pairs: diagonal(m, x_first, pairs))
    xb, yb = lax.optimization_barrier((xb, yb))
    xb = lax.ppermute(xb, "gx", x_second)

    (columns,) = call(pack_columns_kernel, (cols, xa, xc), [(4 * ny, nz)])
    zown, za, zb, drag_xy = call(
        pack_z_kernel,
        (columns, cols, xa, xc, y, ya, yb),
        [(4 * height, nz), (rows_z, nz), (rows_z, nz), (1, nz)],
        [pltpu.VMEM((4, ny + 32, nz), f32)],
    )
    if rides:
        second = jnp.sum(xc[4 * ny :], axis=0, keepdims=True)
        second = second + yb[DRAG_ROW : DRAG_ROW + 1]
        drag_xy = drag_xy + lax.ppermute(second, "gx", x_first)
        za = za.at[2 * ny + 3 : 2 * ny + 4].set(drag_xy)
        zb = zb.at[2 * ny + 3 : 2 * ny + 4].set(drag_xy)
    zb = lax.ppermute(zb, "gz", z_second)
    za = lax.ppermute(za, "gz", z_first)
    inner, grad1, inner_grad, pack, f0, f1 = call(
        inner_kernel,
        (primal_states, adjoint_last, ub, xa, xb, y, ya, yb),
        [
            (19, nx, ny, nz),
            (nx, ny, nz),
            (nx, ny, nz),
            (19, ny, nz),
            (20, ny, nz),
            (19, ny, nz),
        ],
        [
            pltpu.VMEM((NSLOT, nx + 4, ny + 32, nz), f32),
            pltpu.VMEM((19, nx + 2, height + 8, nz), f32),
        ],
        micros=4,
    )
    if rides:
        zhalf = lax.ppermute(drag_xy, "gz", [(i, i ^ 2) for i in range(gz)])
        drags = (drag_xy, zhalf)
    else:
        drags = (lax.psum(drag, AXES),)

    zout, tails = call(
        edge_kernel,
        (zown, za, zb, pack, f0, f1),
        [(21, ny, nz), (1, nz)],
        [pltpu.VMEM((19, height + 8, nz), f32)],
    )
    if rides:
        drags += (tails,)
    whole_cells = float(nx * ny * nz * gx * gy * gz)
    first, gradient, drag = call(
        functools.partial(finish_kernel, whole_cells),
        (solid_mask, zout, inner, grad1, inner_grad) + drags,
        [(19, nx, ny, nz), (nx, ny, nz), (1, 1)],
        [
            pltpu.VMEM((19, nx, ny, nz), f32),
            pltpu.VMEM((nx, ny, nz), f32),
            pltpu.VMEM((1, 1), f32),
            pltpu.SemaphoreType.DMA((len(OUT_GROUPS) + 2,)),
        ],
        outs=[HBM, HBM, HBM],
    )
    return (first, gradient, drag.reshape(()))


def solution(mesh):
    return jax.shard_map(
        body,
        mesh=mesh,
        in_specs=(
            P(None, None, "gx", "gy", "gz"),
            P(None, "gx", "gy", "gz"),
            P("gx", "gy", "gz"),
            P("gx", "gy", "gz"),
        ),
        out_specs=(P(None, "gx", "gy", "gz"), P("gx", "gy", "gz"), P()),
        check_vma=False,
    )
```
